32 devices in a mesh: dp: 8 (over y, x, core), tensor: 4 (over z).
Axes of the slice: x: 2, y: 2, z: 4, core: 2. Of those that a mesh axis runs over, the one named last changes fastest.
Arguments:
- hidden_in: bfloat16 [8, 1024, 2048], P('dp', 'tensor'), may hold values from -6 to 6
- out_grad: bfloat16 [8, 1024, 2048], P('dp', 'tensor'), may hold values from -6 to 6
- doc_ids: int32 [8, 1024], P('dp'), may hold values from 0 to 1023, as said below
- expert_ids: int32 [8, 1024, 8], P('dp'), may hold values from 0 to 63, all different within a row; in each aligned block of 1024 rows (0 to 1023, 1024 to 2047, ..., all dimensions but the last counted through in order) at most 192 rows name the same one
- prenorm: bfloat16 [2048], P(('dp', 'tensor')), may hold values from 0.099609375 to 1.8984375
- querynorm: bfloat16 [128, 16], P('dp', 'tensor'), may hold values from 0.099609375 to 1.8984375
- keynorm: bfloat16 [128, 16], P('dp', 'tensor'), may hold values from 0.099609375 to 1.8984375
- query_proj: bfloat16 [2048, 2048], P('dp', 'tensor'), may hold values from -0.125 to 0.125
- key_proj: bfloat16 [2048, 2048], P('dp', 'tensor'), may hold values from -0.125 to 0.125
- value_proj: bfloat16 [2048, 2048], P('dp', 'tensor'), may hold values from -0.125 to 0.125
- output_proj: bfloat16 [2048, 2048], P('dp', 'tensor'), may hold values from -1.5 to 1.5
- postnorm: bfloat16 [2048], P(('dp', 'tensor')), may hold values from 0.099609375 to 1.8984375
- router: bfloat16 [2048, 64], P(('dp', 'tensor')), may hold values from -0.0625 to 0.0625
- gate_proj: bfloat16 [64, 2048, 1024], P('dp', None, 'tensor'), may hold values from -0.125 to 0.125
- up_proj: bfloat16 [64, 2048, 1024], P('dp', None, 'tensor'), may hold values from -0.125 to 0.125
- down_proj: bfloat16 [64, 2048, 1024], P('dp', None, 'tensor'), may hold values from -6 to 6
Outputs:
- layer_out: bfloat16 [8, 1024, 2048], P('dp', 'tensor')
- input_grad: bfloat16 [8, 1024, 2048], P('dp', 'tensor')
- prenorm_grad: float32 [2048], P(('dp', 'tensor'))
- querynorm_grad: float32 [128, 16], P('dp', 'tensor')
- keynorm_grad: float32 [128, 16], P('dp', 'tensor')
- query_grad: float32 [2048, 2048], P('dp', 'tensor')
- key_grad: float32 [2048, 2048], P('dp', 'tensor')
- value_grad: float32 [2048, 2048], P('dp', 'tensor')
- output_grad: float32 [2048, 2048], P('dp', 'tensor')
- postnorm_grad: float32 [2048], P(('dp', 'tensor'))
- router_grad: float32 [2048, 64], P(('dp', 'tensor'))
- gate_grad: float32 [64, 2048, 1024], P('dp', None, 'tensor')
- up_grad: float32 [64, 2048, 1024], P('dp', None, 'tensor')
- down_grad: float32 [64, 2048, 1024], P('dp', None, 'tensor')
The draws below stay inside these ranges and needn't reach their ends.
Inputs may be any that keep to these rules, and one draw needn't show every extreme that they name: `expert_ids`: each row names 8 different experts; of the 1024 rows of one sequence at most 192 name any one expert. `doc_ids`: ids never fall along a sequence; the last token of every sequence has id 1024 - 1.
All inputs are finite; a program needn't handle non-finite values.
Results may differ from the reference program's by a relative error of at most 0.02.
Values may be sent and summed in bfloat16 or wider, within the bound.
A program may use at most 704 MiB of HBM per device.

```python
import math
import jax
import jax.numpy as jnp
import numpy as np
from jax import lax

D = 2048
H = 16
HD = 128
F = 1024
E = 64
TOP = 8
SEQ = 1024
SEQS = 8
TOK_DEV = 256
CG = 192


def draw_doc_ids(key, part):
    key = jax.random.fold_in(key, 11)
    first_key, second_key, third_key = jax.random.split(key, 3)
    begin = jax.random.randint(first_key, (SEQS, 1), 0, TOK_DEV // 2 + 1)
    finish = jax.random.randint(second_key, (SEQS, 1), SEQ - TOK_DEV // 2, SEQ + 1)
    cuts = jax.random.randint(third_key, (SEQS, SEQ), 0, 16) == 0
    places = jnp.arange(SEQ)[None, :]
    inside = (places > begin) & (places < finish)
    flags = jnp.where(inside, False, cuts) | (places == begin) | (places == finish)
    flags = flags & (places > 0)
    counts = jnp.cumsum(flags.astype(jnp.int32), axis=1).astype(jnp.int32)
    offset = SEQ - 1 - counts[:, -1:]
    return (counts + offset).astype(jnp.int32)


def block_levels(stream_key, dims, pieces, low, largest):
    factor_of, own = 1.0, jax.random.fold_in(stream_key, 6)
    for dim, parts in pieces:
        steps = jnp.exp(jax.random.uniform(jax.random.fold_in(own, dim), (parts,), jnp.float32, low / len(pieces), largest / len(pieces)))
        factor_of = factor_of * jnp.repeat(steps, dims[dim] // parts).reshape([-1 if axis == dim else 1 for axis in range(len(dims))])
    return factor_of


def shared_out(own_key, own, number, rows, count, top, reach, skew):
    ranking = jax.random.permutation(own_key, count)
    crowded, ordinary = shares(count, rows * top, reach, skew, True), shares(count, rows * top, reach, skew, False)
    places = jnp.arange(count)

    def named(tallies, turn):
        used = int((tallies > 0).sum())
        fixed = max(1, used // 4)
        shifted = fixed + (places - fixed + turn * (used - fixed)) % max(1, count - fixed)
        return jnp.zeros((count,), jnp.int32).at[ranking[jnp.where(places < fixed, places, shifted)]].set(jnp.asarray(tallies, jnp.int32))

    tallies = jnp.where(number % 4 == 0, named(crowded, number // 4), named(ordinary, number - number // 4 - 1))
    mixed = jax.random.permutation(jax.random.fold_in(own, 3), count)
    donor, sink = mixed[0:count // 2 * 2:2], mixed[1:count // 2 * 2:2]
    margin = jnp.minimum(tallies[donor] - 1, reach - tallies[sink]) // 2
    margin = jnp.where((donor == ranking[0]) | (sink == ranking[0]) | (tallies[sink] == 0), 0, jnp.maximum(margin, 0))
    shifted = jax.random.randint(jax.random.fold_in(own, 4), (count // 2,), 0, 1 << 20) % (margin + 1)
    tallies = tallies.at[donor].add(-shifted).at[sink].add(shifted)
    items = jnp.searchsorted(jnp.cumsum(tallies), jnp.arange(rows * top), side="right").astype(jnp.int32)
    grid = items.reshape(top, rows).T
    grid = grid[jax.random.permutation(jax.random.fold_in(own, 1), rows)]
    turn = jax.random.randint(jax.random.fold_in(own, 2), (rows, 1), 0, top)
    return jnp.take_along_axis(grid, (jnp.arange(top)[None, :] + turn) % top, axis=1)


def shares(amount, total, reach, skew, full):
    loads = [(1 << 20) // math.isqrt(rank ** skew) + 1 for rank in range(1, amount + 1)]
    largest = reach if full else min(reach, max(-(-total // amount), total * loads[0] // sum(loads)))
    least = 1 if total - largest >= amount - 1 else 0
    holding, rest = [largest] + [least] * (amount - 1), total - largest - least * (amount - 1)
    while rest > 0:
        movable = [i for i in range(1, amount) if holding[i] < largest] or [i for i in range(1, amount) if holding[i] < reach]
        pool, remaining = sum([loads[i] for i in movable]), rest
        for i in movable:
            addition = min(reach - holding[i], max(1, remaining * loads[i] // pool), rest)
            holding[i] = holding[i] + addition
            rest = rest - addition
    return np.array(holding)


def bell_draw(rng, extent, deviation, limit, pieces=(), kind=jnp.bfloat16):
    entries = jax.random.normal(rng, extent, jnp.float32) * deviation
    if len(pieces) > 0:
        entries = block_levels(rng, extent, pieces, -0.22, 0.18) * entries
    return jnp.clip(entries, min=-limit, max=limit).astype(kind)


def setup_inputs(seed: int = 0) -> dict:
    streams_of = jax.random.split(jax.random.key(seed), 17)
    hidden_in = bell_draw(streams_of[0], (SEQS, SEQ, D), 1.0, 6.0, ((0, 8), (1, 4)))
    out_grad = bell_draw(streams_of[1], (SEQS, SEQ, D), 1.0, 6.0, ((0, 8), (1, 4)))
    doc_ids = draw_doc_ids(jax.random.fold_in(streams_of[16], 71), 0)
    expert_ids_keys = jax.random.split(jax.random.fold_in(streams_of[3], 1), SEQS * SEQ // SEQ)
    expert_ids_turns = jax.random.permutation(jax.random.fold_in(streams_of[3], 3), SEQS * SEQ // SEQ)
    expert_ids = jax.vmap(lambda own, number: shared_out(jax.random.fold_in(streams_of[3], 2), own, number, SEQ, E, TOP, CG, 1))(expert_ids_keys, expert_ids_turns).reshape((SEQS, SEQ, TOP))
    prenorm = jnp.clip(1.0 + 0.18 * jax.random.normal(streams_of[4], (D,), jnp.float32), 0.099609375, 1.8984375).astype(jnp.bfloat16)
    querynorm = jnp.clip(1.0 + 0.18 * jax.random.normal(streams_of[5], (HD, H), jnp.float32), 0.099609375, 1.8984375).astype(jnp.bfloat16)
    keynorm = jnp.clip(1.0 + 0.18 * jax.random.normal(streams_of[6], (HD, H), jnp.float32), 0.099609375, 1.8984375).astype(jnp.bfloat16)
    query_proj = bell_draw(streams_of[7], (D, D), D ** -0.5, 0.125, ((0, 8), (1, 4)))
    key_proj = bell_draw(streams_of[8], (D, D), D ** -0.5, 0.125, ((0, 8), (1, 4)))
    value_proj = bell_draw(streams_of[9], (D, D), D ** -0.5, 0.125, ((0, 8), (1, 4)))
    output_proj = bell_draw(streams_of[10], (D, D), (D // 128) ** -0.5, 1.5, ((0, 8), (1, 4)))
    postnorm = jnp.clip(1.0 + 0.18 * jax.random.normal(streams_of[11], (D,), jnp.float32), 0.099609375, 1.8984375).astype(jnp.bfloat16)
    router = bell_draw(streams_of[12], (D, E), (4 * D) ** -0.5, 0.0625, ((0, 32),))
    gate_proj = bell_draw(streams_of[13], (E, D, F), D ** -0.5, 0.125, ((0, 8), (2, 4)))
    up_proj = bell_draw(streams_of[14], (E, D, F), D ** -0.5, 0.125, ((0, 8), (2, 4)))
    down_proj = bell_draw(streams_of[15], (E, D, F), 1.0, 6.0, ((0, 8), (2, 4)))
    return {"hidden_in": hidden_in, "out_grad": out_grad, "doc_ids": doc_ids, "expert_ids": expert_ids, "prenorm": prenorm, "querynorm": querynorm, "keynorm": keynorm, "query_proj": query_proj, "key_proj": key_proj, "value_proj": value_proj, "output_proj": output_proj, "postnorm": postnorm, "router": router, "gate_proj": gate_proj, "up_proj": up_proj, "down_proj": down_proj}


epsilon = 1e-05
highest = lax.Precision.HIGHEST

@jax.custom_vjp
def low(v):
    return lax.optimization_barrier(v.astype(jnp.bfloat16)).astype(jnp.float32)

@jax.custom_vjp
def low_back(v):
    return v

def low_keep(v):
    return (low(v), None)

def low_pass(kept, grad):
    return (grad,)

def back_keep(v):
    return (v, None)

def back_low(kept, grad):
    return (low(grad),)
low.defvjp(low_keep, low_pass)
low_back.defvjp(back_keep, back_low)

def rms_scale(tensor, gain):
    return tensor * lax.rsqrt(lax.optimization_barrier(jnp.mean(tensor * tensor, -1, keepdims=True)) + epsilon) * gain

def rotate(tensor):
    half = tensor.shape[-1] // 2
    return jnp.concatenate([-tensor[..., half:], tensor[..., :half]], -1)

def rope_tables(length, width):
    positions = jnp.arange(length).astype(jnp.float32)
    rates = 10000.0 ** (-jnp.arange(0, width, 2).astype(jnp.float32) / width)
    angles = positions[:, None] * rates[None, :]
    return (jnp.concatenate([jnp.cos(angles)] * 2, -1), jnp.concatenate([jnp.sin(angles)] * 2, -1))

def forward(hidden, prenorm, querynorm, keynorm, query_proj, key_proj, value_proj, output_proj, postnorm, router, gate_proj, up_proj, down_proj, doc_ids, expert_ids):
    cosine, sine = rope_tables(SEQ, HD)
    scale = HD ** (-0.5)
    query_gain = querynorm.T.reshape(D)
    key_gain = keynorm.T.reshape(D)
    normed = low(rms_scale(hidden, prenorm))

    def sequence(inputs):
        rows, documents = inputs
        query = low_back(jnp.dot(rows, query_proj, precision=highest))
        keys = low_back(jnp.dot(rows, key_proj, precision=highest))
        values = low_back(low(jnp.dot(rows, value_proj, precision=highest)))
        query = rms_scale(query, query_gain).reshape(SEQ, H, HD)
        keys = rms_scale(keys, key_gain).reshape(SEQ, H, HD)
        query = low(query * cosine[:, None] + rotate(query) * sine[:, None])
        keys = low(keys * cosine[:, None] + rotate(keys) * sine[:, None])
        scores = low_back(jnp.einsum('qhd,khd->hqk', query, keys, precision=highest) * scale)
        order = jnp.arange(SEQ)
        allowed = (documents[:, None] == documents[None, :]) & (order[:, None] >= order[None, :])
        scores = jnp.where(allowed[None], scores, -1000000000.0)
        portion = low(jax.nn.softmax(scores, -1))
        mixed = jnp.einsum('hqk,khd->qhd', portion, values.reshape(SEQ, H, HD), precision=highest).reshape(SEQ, D)
        mixed = low_back(low(mixed))
        return low_back(jnp.dot(mixed, output_proj.T, precision=highest))
    attended = lax.map(jax.checkpoint(sequence), (normed, doc_ids))
    residual = hidden + attended
    count = SEQS * SEQ
    flat = low(rms_scale(residual, postnorm)).reshape(count, D)
    logits = jnp.dot(flat, router, precision=highest)
    share = jax.nn.softmax(logits, -1)
    routes = expert_ids.reshape(count, TOP)
    gates = jnp.take_along_axis(share, routes, 1).reshape(-1)
    padded = jnp.concatenate([flat, jnp.zeros((1, D), flat.dtype)], 0)
    gate_pad = jnp.concatenate([gates, jnp.zeros((1,), gates.dtype)], 0)
    chosen = routes.reshape(-1)

    def expert(index):
        pair = jnp.nonzero(chosen == index, size=SEQS * CG, fill_value=count * TOP)[0].astype(jnp.int32)
        tokens = (pair // TOP).astype(jnp.int32)
        rows = padded[tokens]
        gate_pre = low_back(jnp.dot(rows, gate_proj[index], precision=highest))
        up_pre = low_back(jnp.dot(rows, up_proj[index], precision=highest))
        active = low(jax.nn.silu(gate_pre) * up_pre)
        result = low_back(jnp.dot(active, down_proj[index].T, precision=highest))
        return (result * gate_pad[pair][:, None], tokens)
    contrib, tokens = lax.map(jax.checkpoint(expert), jnp.arange(E).astype(jnp.int32))
    mixture = jnp.zeros((count + 1, D), contrib.dtype).at[tokens.reshape(-1)].add(contrib.reshape(-1, D))[:count]
    return residual + mixture.reshape(SEQS, SEQ, D)

def reference(hidden_in, out_grad, doc_ids, expert_ids, prenorm, querynorm, keynorm, query_proj, key_proj, value_proj, output_proj, postnorm, router, gate_proj, up_proj, down_proj):
    floats = [value.astype(jnp.float32) for value in (hidden_in, prenorm, querynorm, keynorm, query_proj, key_proj, value_proj, output_proj, postnorm, router, gate_proj, up_proj, down_proj)]

    def wrapped(*values):
        return forward(*values, doc_ids, expert_ids)
    result, pullback = jax.vjp(wrapped, *floats)
    grads = pullback(out_grad.astype(jnp.float32))
    return (result.astype(jnp.bfloat16), grads[0].astype(jnp.bfloat16), grads[1], grads[2], grads[3], grads[4], grads[5], grads[6], grads[7], grads[8], grads[9], grads[10], grads[11], grads[12])
```

```python
import functools

import jax
import jax.numpy as jnp
from jax import lax
from jax.experimental import pallas as pl
from jax.experimental.pallas import tpu as pltpu
from jax.sharding import PartitionSpec as P

D = 2048
HD = 128
E = 64
TOP = 8
CG = 192


epsilon = 1e-05
masked_score = -1000000000.0


def as_sent(value):
    return jax.tree.map(lambda a: a.astype(jnp.bfloat16) if a.dtype == jnp.float32 else a, value)


def rope_tables(length, width):
    positions = jnp.arange(length).astype(jnp.float32)
    rates = 10000.0 ** (-jnp.arange(0, width, 2).astype(jnp.float32) / width)
    angles = positions[:, None] * rates[None, :]
    return (jnp.concatenate([jnp.cos(angles)] * 2, -1), jnp.concatenate([jnp.sin(angles)] * 2, -1))


def rotate(tensor):
    half = tensor.shape[-1] // 2
    return jnp.concatenate([-tensor[..., half:], tensor[..., :half]], -1)


def rotate_back(tensor):
    half = tensor.shape[-1] // 2
    return jnp.concatenate([tensor[..., half:], -tensor[..., :half]], -1)


def gather_tokens(parts):
    return jax.tree.map(
        lambda part, own: part.astype(own.dtype),
        lax.all_gather(as_sent(parts), "tensor", axis=0, tiled=True),
        parts,
    )


def sum_tokens(part):
    return lax.psum_scatter(
        part.astype(jnp.bfloat16), "tensor", scatter_dimension=0, tiled=True
    ).astype(jnp.float32)


def sum_all(part):
    return sum_tokens(lax.psum_scatter(part, "dp", scatter_dimension=0, tiled=True))


def sum_heads(parts):
    return lax.psum((parts[0], parts[1]), "tensor")


def norm_back(grad, value, inverse, gain, width):
    scaled = grad * gain
    inner = jnp.sum(scaled * value, -1, keepdims=True)
    return inverse * scaled - value * inverse**3 * inner / width


def block_scores(query, keys, documents, start, block, scale):
    row_place = start + jnp.arange(block)
    col_place = jnp.arange(documents.shape[0])
    allowed = (documents[:, None] == documents[None, :]) & (
        row_place[:, None] >= col_place[None, :]
    )
    scores = jnp.einsum("qhd,khd->hqk", query, keys, preferred_element_type=jnp.float32) * scale
    return (jnp.where(allowed[None], scores, masked_score), query)


def attend_forward(query, keys, values, documents, block, scale):
    count = query.shape[0] // block

    def one(index):
        scores, rows = block_scores(query, keys, documents, index * block, block, scale)
        peak = jnp.max(scores, -1, keepdims=True)
        weights = jnp.exp(scores - peak)
        total = jnp.sum(weights, -1, keepdims=True)
        portion = (weights / total).astype(jnp.bfloat16)
        mixed = jnp.einsum("hqk,khd->qhd", portion, values, preferred_element_type=jnp.float32)
        return (mixed.astype(jnp.bfloat16), peak + jnp.log(total))

    mixed, logsum = lax.map(one, jnp.arange(count))
    return (mixed.reshape(query.shape), logsum)


def attend_backward(query, keys, values, documents, logsum, grad_mixed, block, scale):
    count = query.shape[0] // block

    def one(index):
        start = index * block
        scores, rows = block_scores(query, keys, documents, start, block, scale)
        portion = jnp.exp(scores - logsum[index])
        grad_portion = jnp.einsum(
            "qhd,khd->hqk", grad_mixed, values, preferred_element_type=jnp.float32
        )
        center = jnp.sum(portion * grad_portion, -1, keepdims=True)
        grad_scores = (portion * (grad_portion - center)).astype(jnp.bfloat16)
        grad_values = jnp.einsum(
            "hqk,qhd->khd",
            portion.astype(jnp.bfloat16),
            grad_mixed,
            preferred_element_type=jnp.float32,
        )
        grad_query = (
            jnp.einsum("hqk,khd->qhd", grad_scores, keys, preferred_element_type=jnp.float32)
            * scale
        )
        grad_keys = (
            jnp.einsum("hqk,qhd->khd", grad_scores, rows, preferred_element_type=jnp.float32)
            * scale
        )
        return (grad_query, grad_keys, grad_values)

    grad_query, grad_keys, grad_values = lax.map(one, jnp.arange(count))
    return (grad_query.reshape(query.shape), jnp.sum(grad_keys, 0), jnp.sum(grad_values, 0))


TB = 256
GR = 16
TILE = 256
SLOTS = 512
EXTRA = 2 * E
VMEM = 60 * 1024 * 1024


def ceil_to(value, unit):
    return (value + unit - 1) // unit * unit


def nt_dot(a, b):
    return lax.dot_general(a, b, (((1,), (1,)), ((), ())), preferred_element_type=jnp.float32)


def tn_dot(a, b):
    return lax.dot_general(a, b, (((0,), (0,)), ((), ())), preferred_element_type=jnp.float32)


def nn_dot(a, b):
    return jnp.dot(a, b, preferred_element_type=jnp.float32)


def pair(value):
    high = value.astype(jnp.bfloat16)
    low = (value - high.astype(jnp.float32)).astype(jnp.bfloat16)
    return high, low


def unpair(value):
    value = value.astype(jnp.float32)
    return value[:, :E] + value[:, E:]


def excl_cumsum(value, axis):
    return jnp.cumsum(value, axis) - value


class Plan:
    def __init__(self, tokens, seq_len, local):
        seqs = tokens // seq_len
        self.tokens, self.local = tokens, local
        self.blocks = tokens // TB
        per_seq = seq_len // TB
        worst = min(CG + (GR - 1) * per_seq, seq_len)
        self.cap = ceil_to(seqs * worst // GR * GR, TILE)
        groups = (seqs * local * CG + self.blocks * local * (GR - 1)) // GR
        self.items = groups * GR // TILE + self.blocks
        self.joins = groups * GR // SLOTS + self.blocks
        self.tiles = self.cap // TILE


def routing(plan, routes, base):
    local, blocks = plan.local, plan.blocks
    mine = base + jnp.arange(local)
    picked = jnp.any(routes[:, :, None] == mine[None, None, :], 1)
    grid = picked.reshape(blocks, TB, local)
    ones = grid.astype(jnp.bfloat16)
    earlier = (jnp.arange(TB)[:, None] > jnp.arange(TB)[None, :]).astype(jnp.bfloat16)
    rank = jnp.einsum("ts,bse->bte", earlier, ones, preferred_element_type=jnp.float32).astype(
        jnp.int32
    )
    count = jnp.sum(grid.astype(jnp.int32), 1)
    groups = (count + GR - 1) // GR
    inner = excl_cumsum(groups, 1)
    total = jnp.sum(groups, 1)
    outer = excl_cumsum(groups, 0)
    expert_rows = jnp.sum(groups, 0) * GR
    place = jnp.where(grid, inner[:, None, :] * GR + rank, -1)

    def items(size, unit):
        steps = jnp.maximum((total * GR + unit - 1) // unit, 1)
        first = excl_cumsum(steps, 0)
        used = jnp.sum(steps)
        index = jnp.minimum(jnp.arange(size), used - 1)
        block = jnp.sum((first[None, :] <= index[:, None]).astype(jnp.int32), 1) - 1
        here = block[:, None] == jnp.arange(blocks)[None, :]
        part = index - jnp.sum(jnp.where(here, first[None, :], 0), 1)
        last = part == jnp.sum(jnp.where(here, steps[None, :], 0), 1) - 1
        return first, used, block, part, last.astype(jnp.int32), here

    first, used, block, part, _, _ = items(plan.items, TILE)
    slots = plan.cap // GR
    spot = jnp.arange(slots)[None, :, None]
    low = outer.T[:, None, :]
    inside = (spot >= low) & (spot < low + groups.T[:, None, :])
    origin = first[None, :] * (TILE // GR) + inner.T
    source = jnp.sum(jnp.where(inside, origin[:, None, :] + spot - low, 0), 2)
    _, joined, jblock, jpart, jlast, here = items(plan.joins, SLOTS)

    def at_block(table):
        return jnp.sum(jnp.where(here[:, :, None], table[None], 0), 1)[:, None, :]

    wide = SLOTS // GR
    spot = (jpart[:, None] * wide + jnp.arange(wide)[None, :])[:, :, None]
    low, many, begin = at_block(inner), at_block(groups), at_block(outer)
    inside = (spot >= low) & (spot < low + many)
    target = jnp.sum(
        jnp.where(inside, (jnp.arange(local) * slots)[None, None, :] + begin + spot - low, 0), 2
    )
    return dict(
        place=place,
        used=used[None],
        block=block,
        part=part,
        source=source.reshape(-1),
        expert_rows=expert_rows,
        expert_tiles=jnp.maximum((expert_rows + TILE - 1) // TILE, 1),
        joined=joined[None],
        jblock=jblock,
        jpart=jpart,
        jlast=jlast,
        target=target.reshape(-1),
    )


def dispatch_kernel(used, block, part, post, grad, router, place, rows, share, held):
    step = pl.program_id(0)
    local = place.shape[1]

    @pl.when(step < used[0])
    def _():
        @pl.when(part[step] == 0)
        def _():
            portion = jax.nn.softmax(nn_dot(post[...], router[...]), -1)
            high, low = pair(portion)
            both = jnp.concatenate([high, low], 1)
            held[...] = both
            share[...] = both

        slot = lax.broadcasted_iota(jnp.int32, (TILE, TB), 0) + part[step] * TILE
        hit = slot == place[0, 0:1, :]
        for one in range(1, local):
            hit = hit | (slot == place[0, one : one + 1, :])
        pick = jnp.where(hit, 1.0, 0.0).astype(jnp.bfloat16)
        rows[:, :D] = nn_dot(pick, post[...]).astype(jnp.bfloat16)
        rows[:, D : 2 * D] = nn_dot(pick, grad[...]).astype(jnp.bfloat16)
        rows[:, 2 * D :] = nn_dot(pick, held[...]).astype(jnp.bfloat16)


def dispatch(plan, route, post, grad, router):
    wide = 2 * D + EXTRA
    place = route["place"].transpose(0, 2, 1)

    def at_block(step, used, block, part):
        return (block[step], 0)

    return pl.pallas_call(
        dispatch_kernel,
        grid_spec=pltpu.PrefetchScalarGridSpec(
            num_scalar_prefetch=3,
            grid=(plan.items,),
            in_specs=[
                pl.BlockSpec((TB, D), at_block),
                pl.BlockSpec((TB, D), at_block),
                pl.BlockSpec((D, E), lambda step, used, block, part: (0, 0)),
                pl.BlockSpec((1, plan.local, TB), lambda s, used, block, part: (block[s], 0, 0)),
            ],
            out_specs=[
                pl.BlockSpec(
                    (TILE, wide), lambda s, used, block, part: (jnp.minimum(s, used[0] - 1), 0)
                ),
                pl.BlockSpec((TB, EXTRA), at_block),
            ],
            scratch_shapes=[pltpu.VMEM((TB, EXTRA), jnp.bfloat16)],
        ),
        out_shape=[
            jax.ShapeDtypeStruct((plan.items * TILE, wide), jnp.bfloat16),
            jax.ShapeDtypeStruct((plan.tokens, EXTRA), jnp.bfloat16),
        ],
        compiler_params=pltpu.CompilerParams(vmem_limit_bytes=VMEM),
        cost_estimate=pl.CostEstimate(
            flops=2 * plan.items * TILE * TB * wide,
            bytes_accessed=4 * plan.items * TILE * wide,
            transcendentals=0,
        ),
        name="dispatch",
    )(route["used"], route["block"], route["part"], post, grad, router, place)


def expert_kernel(source, tiles, filled, base, *refs):
    count = TILE // GR
    parts = refs[:count]
    w_gate, w_up, w_down, result, gate_out, up_out, down_out = refs[count : count + 7]
    gate_sum, up_sum, down_sum = refs[count + 7 :]
    expert, step = pl.program_id(0), pl.program_id(1)

    @pl.when(step == 0)
    def _():
        gate_sum[...] = jnp.zeros_like(gate_sum)
        up_sum[...] = jnp.zeros_like(up_sum)
        down_sum[...] = jnp.zeros_like(down_sum)

    @pl.when(step < tiles[expert])
    def _():
        number = base[0] + expert
        real = lax.broadcasted_iota(jnp.int32, (TILE, 1), 0) < filled[expert] - step * TILE

        def take(begin, end):
            value = jnp.concatenate([part[:, begin:end] for part in parts], 0)
            return jnp.where(real, value, jnp.zeros_like(value))

        rows, upstream, shares = take(0, D), take(D, 2 * D), take(2 * D, 2 * D + EXTRA)
        lane = lax.broadcasted_iota(jnp.int32, (TILE, EXTRA), 1)
        own = (lane == number) | (lane == number + E)
        gate = jnp.sum(jnp.where(own, shares.astype(jnp.float32), 0.0), -1, keepdims=True)
        gate_pre = nn_dot(rows, w_gate[0])
        up_pre = nn_dot(rows, w_up[0])
        plain = nn_dot(upstream, w_down[0])
        squash = jax.nn.sigmoid(gate_pre)
        swish = gate_pre * squash
        active = (swish * up_pre).astype(jnp.bfloat16).astype(jnp.float32)
        change = jnp.sum(active * plain, -1, keepdims=True)
        grad_active = gate * plain
        grad_gate = (grad_active * up_pre * squash * (1.0 + gate_pre * (1.0 - squash))).astype(
            jnp.bfloat16
        )
        grad_up = (grad_active * swish).astype(jnp.bfloat16)
        scaled = (gate * active).astype(jnp.bfloat16)
        result[:, :D] = nt_dot(scaled, w_down[0]).astype(jnp.bfloat16)
        result[:, D : 2 * D] = (nt_dot(grad_gate, w_gate[0]) + nt_dot(grad_up, w_up[0])).astype(
            jnp.bfloat16
        )
        high, low = pair(change)
        result[:, 2 * D :] = jnp.where(
            lane == number,
            high.astype(jnp.float32),
            jnp.where(lane == number + E, low.astype(jnp.float32), 0.0),
        ).astype(jnp.bfloat16)
        gate_sum[...] += tn_dot(grad_gate, rows)
        up_sum[...] += tn_dot(grad_up, rows)
        down_sum[...] += tn_dot(scaled, upstream)

    @pl.when(step == pl.num_programs(1) - 1)
    def _():
        gate_out[0] = gate_sum[...].T
        up_out[0] = up_sum[...].T
        down_out[0] = down_sum[...].T


def experts(plan, route, base, rows, w_gate, w_up, w_down):
    wide = 2 * D + EXTRA
    width = w_gate.shape[2]
    count = TILE // GR
    slots = plan.cap // GR

    def group_at(index):
        def place(expert, step, source, tiles, filled, base):
            tile = jnp.minimum(step, tiles[expert] - 1)
            return (source[expert * slots + tile * count + index], 0)

        return pl.BlockSpec((GR, wide), place)

    def whole(expert, step, source, tiles, filled, base):
        return (expert, 0, 0)

    def tile_at(expert, step, source, tiles, filled, base):
        return (expert * plan.tiles + jnp.minimum(step, tiles[expert] - 1), 0)

    weight = pl.BlockSpec((1, D, width), whole)
    total = plan.local * plan.cap
    return pl.pallas_call(
        expert_kernel,
        grid_spec=pltpu.PrefetchScalarGridSpec(
            num_scalar_prefetch=4,
            grid=(plan.local, plan.tiles),
            in_specs=[group_at(index) for index in range(count)] + [weight] * 3,
            out_specs=[pl.BlockSpec((TILE, wide), tile_at)] + [weight] * 3,
            scratch_shapes=[pltpu.VMEM((width, D), jnp.float32)] * 3,
        ),
        out_shape=[jax.ShapeDtypeStruct((total, wide), jnp.bfloat16)]
        + [jax.ShapeDtypeStruct((plan.local, D, width), jnp.float32)] * 3,
        compiler_params=pltpu.CompilerParams(vmem_limit_bytes=VMEM),
        cost_estimate=pl.CostEstimate(
            flops=18 * total * D * width * 5 // 8,
            bytes_accessed=4 * total * wide * 5 // 8,
            transcendentals=0,
        ),
        name="experts",
    )(
        route["source"],
        route["expert_tiles"],
        route["expert_rows"],
        base[None],
        *([rows] * count),
        w_gate,
        w_up,
        w_down,
    )


def combine_kernel(joined, block, part, last, target, *refs):
    count = SLOTS // GR
    groups = refs[:count]
    place, share, post, router, out, grad, router_out, sums = refs[count:]
    step = pl.program_id(0)
    local = place.shape[1]

    @pl.when(step == 0)
    def _():
        router_out[...] = jnp.zeros_like(router_out)

    @pl.when(step < joined[0])
    def _():
        slot = lax.broadcasted_iota(jnp.int32, (TB, SLOTS), 1) + part[step] * SLOTS
        hit = slot == place[:, 0:1]
        for one in range(1, local):
            hit = hit | (slot == place[:, one : one + 1])
        pick = jnp.where(hit, 1.0, 0.0).astype(jnp.bfloat16)

        def term(begin, end):
            return nn_dot(pick, jnp.concatenate([group[:, begin:end] for group in groups], 0))

        def finish(value):
            change = unpair_wide(value(2 * D, 2 * D + EXTRA))
            portion = unpair(share[...])
            moved = portion * (change - jnp.sum(change * portion, -1, keepdims=True))
            moved = moved.astype(jnp.bfloat16)
            out[...] = value(0, D).astype(jnp.bfloat16)
            grad[...] = (value(D, 2 * D) + nt_dot(moved, router[...])).astype(jnp.bfloat16)
            router_out[...] += tn_dot(moved, post[...])

        single = (part[step] == 0) & (last[step] == 1)

        @pl.when(single)
        def _():
            finish(term)

        @pl.when(jnp.logical_not(single))
        def _():
            @pl.when(part[step] == 0)
            def _():
                sums[...] = jnp.zeros_like(sums)

            sums[...] += term(0, 2 * D + EXTRA)

            @pl.when(last[step] == 1)
            def _():
                finish(lambda begin, end: sums[:, begin:end])


def unpair_wide(value):
    return value[:, :E] + value[:, E:]


def combine(plan, route, results, share, post, router):
    wide = 2 * D + EXTRA
    count = SLOTS // GR

    def group_at(index):
        def place(step, joined, block, part, last, target):
            return (target[step * count + index], 0)

        return pl.BlockSpec((GR, wide), place)

    def at_block(step, joined, block, part, last, target):
        return (block[step], 0)

    def fixed(step, joined, block, part, last, target):
        return (0, 0)

    return pl.pallas_call(
        combine_kernel,
        grid_spec=pltpu.PrefetchScalarGridSpec(
            num_scalar_prefetch=5,
            grid=(plan.joins,),
            in_specs=[group_at(index) for index in range(count)]
            + [
                pl.BlockSpec((TB, plan.local), at_block),
                pl.BlockSpec((TB, EXTRA), at_block),
                pl.BlockSpec((TB, D), at_block),
                pl.BlockSpec((D, E), fixed),
            ],
            out_specs=[
                pl.BlockSpec((TB, D), at_block),
                pl.BlockSpec((TB, D), at_block),
                pl.BlockSpec((E, D), fixed),
            ],
            scratch_shapes=[pltpu.VMEM((TB, wide), jnp.float32)],
        ),
        out_shape=[
            jax.ShapeDtypeStruct((plan.tokens, D), jnp.bfloat16),
            jax.ShapeDtypeStruct((plan.tokens, D), jnp.bfloat16),
            jax.ShapeDtypeStruct((E, D), jnp.float32),
        ],
        compiler_params=pltpu.CompilerParams(vmem_limit_bytes=VMEM),
        cost_estimate=pl.CostEstimate(
            flops=2 * plan.joins * SLOTS * TB * wide,
            bytes_accessed=4 * plan.tokens * wide,
            transcendentals=0,
        ),
        name="combine",
    )(
        route["joined"],
        route["jblock"],
        route["jpart"],
        route["jlast"],
        route["target"],
        *([results] * count),
        route["place"].reshape(plan.tokens, plan.local),
        share,
        post,
        router,
    )


def body(
    hidden_in,
    out_grad,
    doc_ids,
    expert_ids,
    prenorm,
    querynorm,
    keynorm,
    query_proj,
    key_proj,
    value_proj,
    output_proj,
    postnorm,
    router,
    gate_proj,
    up_proj,
    down_proj,
):
    residual = hidden_in[0].astype(jnp.float32)
    upstream = out_grad[0]
    documents = doc_ids[0]
    routes = expert_ids[0]
    shard = residual.shape[0]
    seq_len = documents.shape[0]
    mesh_dp = lax.axis_size("dp")
    block = min(seq_len, 1024)
    scale = HD ** (-0.5)
    cosine, sine = rope_tables(seq_len, HD)
    router_full, pre_gain, post_gain = (
        lax.all_gather(router, ("dp", "tensor"), axis=0, tiled=True),
        lax.all_gather(prenorm, ("dp", "tensor"), axis=0, tiled=True),
        lax.all_gather(postnorm, ("dp", "tensor"), axis=0, tiled=True),
    )
    pre_gain = pre_gain.astype(jnp.float32)
    post_gain = post_gain.astype(jnp.float32)
    w_query, w_key, w_value, w_output, gain_query, gain_key = (
        lax.all_gather(query_proj, "dp", axis=0, tiled=True),
        lax.all_gather(key_proj, "dp", axis=0, tiled=True),
        lax.all_gather(value_proj, "dp", axis=0, tiled=True),
        lax.all_gather(output_proj, "dp", axis=0, tiled=True),
        lax.all_gather(querynorm, "dp", axis=0, tiled=True),
        lax.all_gather(keynorm, "dp", axis=0, tiled=True),
    )
    heads = w_query.shape[1] // HD
    query_scale = gain_query.astype(jnp.float32).T.reshape(-1)
    key_scale = gain_key.astype(jnp.float32).T.reshape(-1)
    inv_pre = lax.rsqrt(jnp.mean(residual * residual, -1, keepdims=True) + epsilon)
    normed = (residual * inv_pre * pre_gain).astype(jnp.bfloat16)
    (group_normed,) = gather_tokens((normed,))
    plan = Plan(mesh_dp * seq_len, seq_len, gate_proj.shape[0])
    base = (lax.axis_index("dp") * plan.local).astype(jnp.int32)
    all_routes = lax.all_gather(routes, "dp", axis=0, tiled=True)
    all_grad = lax.all_gather(upstream, ("dp", "tensor"), axis=0, tiled=True)
    route = routing(plan, all_routes, base)
    query = jnp.dot(group_normed, w_query, preferred_element_type=jnp.float32)
    keys = jnp.dot(group_normed, w_key, preferred_element_type=jnp.float32)
    values = jnp.dot(group_normed, w_value, preferred_element_type=jnp.float32).astype(jnp.bfloat16)
    query_sq, key_sq = sum_heads(
        (jnp.sum(query * query, -1, keepdims=True), jnp.sum(keys * keys, -1, keepdims=True))
    )
    inv_query = lax.rsqrt(query_sq / D + epsilon)
    inv_key = lax.rsqrt(key_sq / D + epsilon)
    query_heads = (query * inv_query * query_scale).reshape(seq_len, heads, HD)
    key_heads = (keys * inv_key * key_scale).reshape(seq_len, heads, HD)
    query_rot = (query_heads * cosine[:, None] + rotate(query_heads) * sine[:, None]).astype(
        jnp.bfloat16
    )
    key_rot = (key_heads * cosine[:, None] + rotate(key_heads) * sine[:, None]).astype(jnp.bfloat16)
    value_heads = values.reshape(seq_len, heads, HD)
    mixed, logsum = attend_forward(query_rot, key_rot, value_heads, documents, block, scale)
    mixed_flat = mixed.reshape(seq_len, heads * HD)
    attn_term = lax.dot_general(
        mixed_flat, w_output, (((1,), (1,)), ((), ())), preferred_element_type=jnp.float32
    )
    attn_local = sum_tokens(attn_term)
    middle = residual + attn_local
    inv_post = lax.rsqrt(jnp.mean(middle * middle, -1, keepdims=True) + epsilon)
    post_normed = (middle * inv_post * post_gain).astype(jnp.bfloat16)
    all_post = lax.all_gather(post_normed, ("dp", "tensor"), axis=0, tiled=True)
    rows = dispatch(plan, route, all_post, all_grad, router_full)
    results, gate_weight_grad, up_weight_grad, down_weight_grad = experts(
        plan, route, base, rows[0], gate_proj, up_proj, down_proj
    )
    moe_term, grad_term, router_part = combine(
        plan, route, results, rows[1], all_post, router_full
    )
    moe_local = sum_all(moe_term)
    grad_post = sum_all(grad_term)
    router_part = router_part.T
    layer_out = (middle + moe_local).astype(jnp.bfloat16)[None]
    post_gain_part = jnp.sum(grad_post * middle * inv_post, 0)
    grad_middle = upstream.astype(jnp.float32) + norm_back(
        grad_post, middle, inv_post, post_gain, D
    )
    (group_change,) = gather_tokens((grad_middle.astype(jnp.bfloat16),))
    grad_mixed = jnp.dot(group_change, w_output, preferred_element_type=jnp.float32).astype(
        jnp.bfloat16
    )
    output_part = lax.dot_general(
        group_change, mixed_flat, (((0,), (0,)), ((), ())), preferred_element_type=jnp.float32
    )
    grad_query_rot, grad_key_rot, grad_value_heads = attend_backward(
        query_rot,
        key_rot,
        value_heads,
        documents,
        logsum,
        grad_mixed.reshape(seq_len, heads, HD),
        block,
        scale,
    )
    grad_query_flat = (
        grad_query_rot * cosine[:, None] + rotate_back(grad_query_rot * sine[:, None])
    ).reshape(seq_len, -1)
    grad_key_flat = (
        grad_key_rot * cosine[:, None] + rotate_back(grad_key_rot * sine[:, None])
    ).reshape(seq_len, -1)
    query_inner, key_inner = sum_heads(
        (
            jnp.sum(grad_query_flat * query_scale * query, -1, keepdims=True),
            jnp.sum(grad_key_flat * key_scale * keys, -1, keepdims=True),
        )
    )
    grad_query = (
        inv_query * query_scale * grad_query_flat - query * inv_query**3 * query_inner / D
    ).astype(jnp.bfloat16)
    grad_key = (inv_key * key_scale * grad_key_flat - keys * inv_key**3 * key_inner / D).astype(
        jnp.bfloat16
    )
    query_gain_part = jnp.sum(grad_query_flat * query * inv_query, 0).reshape(heads, HD).T
    key_gain_part = jnp.sum(grad_key_flat * keys * inv_key, 0).reshape(heads, HD).T
    grad_value = grad_value_heads.reshape(seq_len, -1).astype(jnp.bfloat16)
    query_part = lax.dot_general(
        group_normed, grad_query, (((0,), (0,)), ((), ())), preferred_element_type=jnp.float32
    )
    key_part = lax.dot_general(
        group_normed, grad_key, (((0,), (0,)), ((), ())), preferred_element_type=jnp.float32
    )
    value_part = lax.dot_general(
        group_normed, grad_value, (((0,), (0,)), ((), ())), preferred_element_type=jnp.float32
    )
    normed_term = lax.dot_general(
        grad_query, w_query, (((1,), (1,)), ((), ())), preferred_element_type=jnp.float32
    )
    normed_term = normed_term + lax.dot_general(
        grad_key, w_key, (((1,), (1,)), ((), ())), preferred_element_type=jnp.float32
    )
    normed_term = normed_term + lax.dot_general(
        grad_value, w_value, (((1,), (1,)), ((), ())), preferred_element_type=jnp.float32
    )
    grad_normed = sum_tokens(normed_term)
    pre_gain_part = jnp.sum(grad_normed * residual * inv_pre, 0)
    input_grad = (grad_middle + norm_back(grad_normed, residual, inv_pre, pre_gain, D)).astype(
        jnp.bfloat16
    )[None]
    attn_sums = (
        lax.psum_scatter(
            query_part.astype(jnp.bfloat16), "dp", scatter_dimension=0, tiled=True
        ).astype(jnp.float32),
        lax.psum_scatter(
            key_part.astype(jnp.bfloat16), "dp", scatter_dimension=0, tiled=True
        ).astype(jnp.float32),
        lax.psum_scatter(
            value_part.astype(jnp.bfloat16), "dp", scatter_dimension=0, tiled=True
        ).astype(jnp.float32),
        lax.psum_scatter(
            output_part.astype(jnp.bfloat16), "dp", scatter_dimension=0, tiled=True
        ).astype(jnp.float32),
        lax.psum_scatter(
            query_gain_part.astype(jnp.bfloat16), "dp", scatter_dimension=0, tiled=True
        ).astype(jnp.float32),
        lax.psum_scatter(
            key_gain_part.astype(jnp.bfloat16), "dp", scatter_dimension=0, tiled=True
        ).astype(jnp.float32),
    )
    small_sums = (
        lax.psum_scatter(router_part, ("dp", "tensor"), scatter_dimension=0, tiled=True),
        lax.psum_scatter(pre_gain_part, ("dp", "tensor"), scatter_dimension=0, tiled=True),
        lax.psum_scatter(post_gain_part, ("dp", "tensor"), scatter_dimension=0, tiled=True),
    )
    return (
        layer_out,
        input_grad,
        small_sums[1],
        attn_sums[4],
        attn_sums[5],
        attn_sums[0],
        attn_sums[1],
        attn_sums[2],
        attn_sums[3],
        small_sums[2],
        small_sums[0],
        gate_weight_grad,
        up_weight_grad,
        down_weight_grad,
    )


def solution(mesh):
    in_specs = (
        P("dp", "tensor", None),
        P("dp", "tensor", None),
        P("dp", None),
        P("dp", None, None),
        P(("dp", "tensor")),
        P("dp", "tensor"),
        P("dp", "tensor"),
        P("dp", "tensor"),
        P("dp", "tensor"),
        P("dp", "tensor"),
        P("dp", "tensor"),
        P(("dp", "tensor")),
        P(("dp", "tensor"), None),
        P("dp", None, "tensor"),
        P("dp", None, "tensor"),
        P("dp", None, "tensor"),
    )
    out_specs = (
        P("dp", "tensor", None),
        P("dp", "tensor", None),
        P(("dp", "tensor")),
        P("dp", "tensor"),
        P("dp", "tensor"),
        P("dp", "tensor"),
        P("dp", "tensor"),
        P("dp", "tensor"),
        P("dp", "tensor"),
        P(("dp", "tensor")),
        P(("dp", "tensor"), None),
        P("dp", None, "tensor"),
        P("dp", None, "tensor"),
        P("dp", None, "tensor"),
    )
    return jax.shard_map(body, mesh=mesh, in_specs=in_specs, out_specs=out_specs, check_vma=False)
```

```python
import functools

import jax
import jax.numpy as jnp
from jax import lax
from jax.experimental import pallas as pl
from jax.experimental.pallas import tpu as pltpu
from jax.sharding import PartitionSpec as P

D = 2048
HD = 128
E = 64
TOP = 8
CG = 192


epsilon = 1e-05
masked_score = -1000000000.0


def rope_tables(length, width):
    positions = jnp.arange(length).astype(jnp.float32)
    rates = 10000.0 ** (-jnp.arange(0, width, 2).astype(jnp.float32) / width)
    angles = positions[:, None] * rates[None, :]
    return (jnp.concatenate([jnp.cos(angles)] * 2, -1), jnp.concatenate([jnp.sin(angles)] * 2, -1))


def rotate(tensor):
    half = tensor.shape[-1] // 2
    return jnp.concatenate([-tensor[..., half:], tensor[..., :half]], -1)


def rotate_back(tensor):
    half = tensor.shape[-1] // 2
    return jnp.concatenate([tensor[..., half:], -tensor[..., :half]], -1)


def sum_heads(parts):
    return lax.psum((parts[0], parts[1]), "tensor")


def norm_back(grad, value, inverse, gain, width):
    scaled = grad * gain
    inner = jnp.sum(scaled * value, -1, keepdims=True)
    return inverse * scaled - value * inverse**3 * inner / width


def block_scores(query, keys, documents, start, block, scale):
    row_place = start + jnp.arange(block)
    col_place = jnp.arange(documents.shape[0])
    allowed = (documents[:, None] == documents[None, :]) & (
        row_place[:, None] >= col_place[None, :]
    )
    scores = jnp.einsum("qhd,khd->hqk", query, keys, preferred_element_type=jnp.float32) * scale
    return (jnp.where(allowed[None], scores, masked_score), query)


def attend_forward(query, keys, values, documents, block, scale):
    count = query.shape[0] // block

    def one(index):
        scores, rows = block_scores(query, keys, documents, index * block, block, scale)
        peak = jnp.max(scores, -1, keepdims=True)
        weights = jnp.exp(scores - peak)
        total = jnp.sum(weights, -1, keepdims=True)
        portion = (weights / total).astype(jnp.bfloat16)
        mixed = jnp.einsum("hqk,khd->qhd", portion, values, preferred_element_type=jnp.float32)
        return (mixed.astype(jnp.bfloat16), peak + jnp.log(total))

    mixed, logsum = lax.map(one, jnp.arange(count))
    return (mixed.reshape(query.shape), logsum)


def attend_backward(query, keys, values, documents, logsum, grad_mixed, block, scale):
    count = query.shape[0] // block

    def one(index):
        start = index * block
        scores, rows = block_scores(query, keys, documents, start, block, scale)
        portion = jnp.exp(scores - logsum[index])
        grad_portion = jnp.einsum(
            "qhd,khd->hqk", grad_mixed, values, preferred_element_type=jnp.float32
        )
        center = jnp.sum(portion * grad_portion, -1, keepdims=True)
        grad_scores = (portion * (grad_portion - center)).astype(jnp.bfloat16)
        grad_values = jnp.einsum(
            "hqk,qhd->khd",
            portion.astype(jnp.bfloat16),
            grad_mixed,
            preferred_element_type=jnp.float32,
        )
        grad_query = (
            jnp.einsum("hqk,khd->qhd", grad_scores, keys, preferred_element_type=jnp.float32)
            * scale
        )
        grad_keys = (
            jnp.einsum("hqk,qhd->khd", grad_scores, rows, preferred_element_type=jnp.float32)
            * scale
        )
        return (grad_query, grad_keys, grad_values)

    grad_query, grad_keys, grad_values = lax.map(one, jnp.arange(count))
    return (grad_query.reshape(query.shape), jnp.sum(grad_keys, 0), jnp.sum(grad_values, 0))


MESH = pl.DeviceIdType.MESH
VMEM = 60 * 1024 * 1024


def transfer(microseconds):
    return pl.CostEstimate(flops=0, bytes_accessed=microseconds * 3_000_000, transcendentals=0)


def flip(index, bit):
    return index + bit - 2 * bit * ((index // bit) % 2)


def send(source, target, send_sem, recv_sem, device):
    return pltpu.make_async_remote_copy(
        src_ref=source,
        dst_ref=target,
        send_sem=send_sem,
        recv_sem=recv_sem,
        device_id=device,
        device_id_type=MESH,
    )


def greet(devices, extra=()):
    barrier = pltpu.get_barrier_semaphore()
    for device in devices:
        pl.semaphore_signal(barrier, inc=1, device_id=device, device_id_type=MESH)
    for there, device in extra:

        @pl.when(there)
        def _(device=device):
            pl.semaphore_signal(barrier, inc=1, device_id=device, device_id_type=MESH)

    count = len(devices)
    for there, _ in extra:
        count = count + jnp.where(there, 1, 0)
    pl.semaphore_wait(barrier, count)


def both_ways(n):
    spot = lax.axis_index("tensor")
    return spot, (
        (spot < n - 1, {"tensor": jnp.minimum(spot + 1, n - 1)}),
        (spot > 0, {"tensor": jnp.maximum(spot - 1, 0)}),
    )


def shard_at(spot, way, distance, n):
    number = spot - distance if way == 0 else spot + distance
    return (number >= 0) & (number < n), jnp.clip(number, 0, n - 1)


def chain_gather_kernel(n, pieces, own, _later, out, _passed, local_sem, send_sem, recv_sem):
    spot, sides = both_ways(n)
    rows = own.shape[0] // pieces
    greet([], sides)
    keep = pltpu.make_async_copy(own, out.at[spot], local_sem)
    keep.start()

    def copy(way, distance, piece):
        there, number = shard_at(spot, way, distance, n)
        part = pl.ds(piece * rows, rows)
        source = own.at[part] if distance == 0 else out.at[number, part]
        return there & sides[way][0], send(
            source,
            out.at[number, part],
            send_sem.at[way, distance, piece],
            recv_sem.at[way, distance, piece],
            sides[way][1],
        )

    def arrived(way, distance, piece):
        there, number = shard_at(spot, way, distance, n)
        part = pl.ds(piece * rows, rows)

        @pl.when(there)
        def _():
            send(
                out.at[number, part],
                out.at[number, part],
                send_sem.at[way, distance - 1, piece],
                recv_sem.at[way, distance - 1, piece],
                sides[way][1],
            ).wait_recv()

    for distance in range(n):
        for piece in range(pieces):
            for way in (0, 1):
                if distance:
                    arrived(way, distance, piece)
                if distance < n - 1:
                    go, one = copy(way, distance, piece)

                    @pl.when(go)
                    def _(one=one):
                        one.start()

    keep.wait()
    for distance in range(n - 1):
        for piece in range(pieces):
            for way in (0, 1):
                go, one = copy(way, distance, piece)

                @pl.when(go)
                def _(one=one):
                    one.wait_send()


def chain_gather(own, later, number, pieces=4):
    n = lax.axis_size("tensor")
    rows, width = own.shape
    anywhere = pl.BlockSpec(memory_space=pl.ANY)
    out, later = pl.pallas_call(
        functools.partial(chain_gather_kernel, n, pieces),
        out_shape=[
            jax.ShapeDtypeStruct((n, rows, width), own.dtype),
            jax.ShapeDtypeStruct(later.shape, later.dtype),
        ],
        in_specs=[anywhere] * 2,
        out_specs=[anywhere] * 2,
        input_output_aliases={1: 1},
        scratch_shapes=[
            pltpu.SemaphoreType.DMA,
            pltpu.SemaphoreType.DMA((2, n - 1, pieces)),
            pltpu.SemaphoreType.DMA((2, n - 1, pieces)),
        ],
        compiler_params=pltpu.CompilerParams(collective_id=number, has_side_effects=True),
        cost_estimate=transfer(65),
        name="chain_gather",
    )(own, later)
    return out.reshape(n * rows, width), later


def add_into(target, source, rows, start=0, source_start=0):
    step = 16

    def body(index, carry):
        at = pl.ds(pl.multiple_of(start + index * step, step), step)
        come = pl.ds(pl.multiple_of(source_start + index * step, step), step)
        target[at, :] = (
            target[at, :].astype(jnp.float32) + source[come, :].astype(jnp.float32)
        ).astype(target.dtype)
        return carry

    lax.fori_loop(0, rows // step, body, 0)


def chain_sum_kernel(n, pieces, part, _later, out, _passed, held, send_sem, recv_sem):
    spot, sides = both_ways(n)
    rows = out.shape[0] // pieces
    greet([], sides)

    def copy(way, far, piece, mine):
        number = spot + far if way == 0 else spot - far
        there = (number >= 0) & (number < n)
        number = jnp.clip(number, 0, n - 1)
        at = pl.ds(piece * rows, rows)
        source = part.at[number, at]
        return there, number, send(
            source if mine else held.at[way, far, at],
            held.at[way, far - 1, at],
            send_sem.at[way, far - 1, piece],
            recv_sem.at[way, far - 1, piece],
            sides[way][1],
        )

    def arrived(way, far, piece):
        at = pl.ds(piece * rows, rows)
        send(
            held.at[way, far, at],
            held.at[way, far, at],
            send_sem.at[way, far, piece],
            recv_sem.at[way, far, piece],
            sides[way][1],
        ).wait_recv()

    for far in range(n - 1, 0, -1):
        for piece in range(pieces):
            for way in (0, 1):
                behind = sides[1 - way][0]
                there, number, first = copy(way, far, piece, True)

                @pl.when(there & jnp.logical_not(behind))
                def _(first=first):
                    first.start()

                if far < n - 1:
                    _, _, onward = copy(way, far, piece, False)

                    @pl.when(there & behind)
                    def _(way=way, far=far, piece=piece, number=number, onward=onward):
                        arrived(way, far, piece)
                        add_into(
                            held.at[way, far], part.at[number], rows, piece * rows, piece * rows
                        )
                        onward.start()

    for piece in range(pieces):
        at = pl.ds(piece * rows, rows)

        def body(index, carry):
            here = pl.ds(pl.multiple_of(piece * rows + index * 16, 16), 16)
            out[here, :] = part[spot, here, :].astype(jnp.float32)
            return carry

        lax.fori_loop(0, rows // 16, body, 0)
        for way in (0, 1):

            @pl.when(sides[1 - way][0])
            def _(way=way):
                arrived(way, 0, piece)
                add_into(out, held.at[way, 0], rows, piece * rows, piece * rows)

    for far in range(n - 1, 0, -1):
        for piece in range(pieces):
            for way in (0, 1):
                there, _, one = copy(way, far, piece, True)

                @pl.when(there)
                def _(one=one):
                    one.wait_send()


def chain_sum(part, later, number, pieces=4):
    n = lax.axis_size("tensor")
    width = part.shape[1]
    rows = part.shape[0] // n
    anywhere = pl.BlockSpec(memory_space=pl.ANY)
    inside = pl.BlockSpec(memory_space=pltpu.VMEM)
    return pl.pallas_call(
        functools.partial(chain_sum_kernel, n, pieces),
        out_shape=[
            jax.ShapeDtypeStruct((rows, width), jnp.float32),
            jax.ShapeDtypeStruct(later.shape, later.dtype),
        ],
        in_specs=[inside, anywhere],
        out_specs=[inside, anywhere],
        input_output_aliases={1: 1},
        scratch_shapes=[
            pltpu.VMEM((2, n - 1, rows, width), part.dtype),
            pltpu.SemaphoreType.DMA((2, n - 1, pieces)),
            pltpu.SemaphoreType.DMA((2, n - 1, pieces)),
        ],
        compiler_params=pltpu.CompilerParams(
            collective_id=number, has_side_effects=True, vmem_limit_bytes=VMEM
        ),
        cost_estimate=transfer(65),
        name="chain_sum",
    )(part.reshape(n, rows, width), later)


def box_devices():
    me = lax.axis_index("dp")
    return me, {bit: {"dp": flip(me, bit)} for bit in (1, 2, 4)}


def box_gather_kernel(n, own, out, local_sem, z_send, z_recv, near_send, near_recv, on_send, on_recv, side_send, side_recv):
    spot, sides = both_ways(n)
    me, near = box_devices()
    half = own.shape[0] // 2
    greet([near[1], near[2], near[4]], sides)
    keep = pltpu.make_async_copy(own, out.at[me, spot], local_sem)
    keep.start()
    sends = []

    def piece(seq, shard, part):
        return out.at[seq, shard, pl.ds(part * half, half)]

    def start(condition, one):
        sends.append((condition, one))

        @pl.when(condition)
        def _():
            one.start()

    def await_piece(condition, target, recv):
        @pl.when(condition)
        def _():
            send(target, target, side_send.at[0, 0, 0], recv, near[1]).wait_recv()

    def to_side(condition, slot, seq, shard, part, source):
        start(condition, send(source, piece(seq, shard, part), side_send.at[slot, shard, part], side_recv.at[slot, shard, part], near[1]))

    def mine(way, distance):
        there, shard = shard_at(spot, way, distance, n)
        for part in (0, 1):
            if distance:
                await_piece(there, piece(me, shard, part), z_recv.at[way, distance - 1, part])
            source = piece(me, shard, part) if distance else own.at[pl.ds(part * half, half)]
            for out_way in (0, 1) if distance == 0 else (way,):
                if distance < n - 1:
                    start(there & sides[out_way][0], send(source, piece(me, shard, part), z_send.at[out_way, distance, part], z_recv.at[out_way, distance, part], sides[out_way][1]))
            for axis, bit in ((0, 2), (1, 4)):
                start(there, send(source, piece(me, shard, part), near_send.at[axis, shard, part], near_recv.at[axis, shard, part], near[bit]))
            to_side(there, 0, me, shard, part, source)

    def nearby(way, distance):
        there, shard = shard_at(spot, way, distance, n)
        for part in (0, 1):
            for axis, bit in ((0, 2), (1, 4)):
                seq = flip(me, bit)
                source = piece(seq, shard, part)
                await_piece(there, source, near_recv.at[axis, shard, part])
                if part == axis:
                    start(there, send(source, source, on_send.at[1 - axis, shard], on_recv.at[1 - axis, shard], near[6 - bit]))
                to_side(there, 1 + axis, seq, shard, part, source)

    def far(way, distance):
        there, shard = shard_at(spot, way, distance, n)
        seq = flip(flip(me, 2), 4)
        for part in (0, 1):
            source = piece(seq, shard, part)
            await_piece(there, source, on_recv.at[1 - part, shard])
            to_side(there, 3, seq, shard, part, source)

    for step in range(n + 2):
        for task, delay in ((mine, 0), (nearby, 1), (far, 2)):
            distance = step - delay
            if 0 <= distance < n:
                for way in (0, 1) if distance else (0,):
                    task(way, distance)
    for shard in range(n):
        for part in (0, 1):
            for slot, bit in enumerate((0, 2, 4, 6)):
                seq = flip(me, 1)
                for one in (2, 4):
                    if bit & one:
                        seq = flip(seq, one)
                await_piece(spot >= 0, piece(seq, shard, part), side_recv.at[slot, shard, part])
    keep.wait()
    for condition, one in sends:

        @pl.when(condition)
        def _(one=one):
            one.wait_send()


def box_gather(own):
    n = lax.axis_size("tensor")
    rows, width = own.shape
    sem = pltpu.SemaphoreType.DMA
    out = pl.pallas_call(
        functools.partial(box_gather_kernel, n),
        out_shape=jax.ShapeDtypeStruct((8, n, rows, width), own.dtype),
        in_specs=[pl.BlockSpec(memory_space=pl.ANY)],
        out_specs=pl.BlockSpec(memory_space=pl.ANY),
        scratch_shapes=[sem]
        + [sem((2, n - 1, 2))] * 2
        + [sem((2, n, 2))] * 2
        + [sem((2, n))] * 2
        + [sem((4, n, 2))] * 2,
        compiler_params=pltpu.CompilerParams(collective_id=3, has_side_effects=True),
        cost_estimate=transfer(140),
        name="box_gather",
    )(own)
    return out.reshape(8 * n * rows, width)


def order_of(spot, n):
    table = [sorted(range(n), key=lambda s: -abs(s - j)) for j in range(n)]
    result = []
    for step in range(n):
        value = jnp.int32(table[0][step])
        for j in range(1, n):
            value = jnp.where(spot == j, table[j][step], value)
        result.append(value)
    return result


def box_sum_kernel(n, part, _later, out, _passed, side, local, on, near, chain, local_sem, side_send, side_recv, on_send, on_recv, near_send, near_recv, z_send, z_recv):
    spot, sides = both_ways(n)
    me, close = box_devices()
    half = out.shape[0] // 2
    rows = out.shape[0]
    greet([close[1], close[2], close[4]], sides)
    order = order_of(spot, n)
    bits = (6, 2, 4, 0)
    sends = []

    def seq_of(index, bit):
        for one in (2, 4):
            if bit & one:
                index = flip(index, one)
        return index

    def start(one, condition=None):
        sends.append((condition, one))
        if condition is None:
            one.start()
        else:

            @pl.when(condition)
            def _():
                one.start()

    def await_at(target, recv):
        send(target, target, side_send.at[0, 0], recv, close[1]).wait_recv()

    def loads(chip, shard):
        return pltpu.make_async_copy(part.at[seq_of(me, bits[chip]), shard], local.at[chip, shard], local_sem.at[chip, shard])

    for shard in order:
        for chip in range(4):
            start(send(part.at[seq_of(flip(me, 1), bits[chip]), shard], side.at[chip, shard], side_send.at[chip, shard], side_recv.at[chip, shard], close[1]))
            loads(chip, shard).start()

    def merge(chip, shard):
        await_at(side.at[chip, shard], side_recv.at[chip, shard])
        loads(chip, shard).wait()
        add_into(side.at[chip, shard], local.at[chip, shard], rows)

    def first(step):
        shard = order[step]
        merge(0, shard)
        for axis, bit in ((0, 2), (1, 4)):
            at = pl.ds(axis * half, half)
            start(send(side.at[0, shard, at], on.at[axis, shard], on_send.at[axis, shard], on_recv.at[axis, shard], close[bit]))
        merge(1, shard)
        merge(2, shard)

    def second(step):
        shard = order[step]
        for axis, bit in ((0, 2), (1, 4)):
            other = 2 - axis
            await_at(on.at[axis, shard], on_recv.at[axis, shard])
            add_into(side.at[other, shard], on.at[axis, shard], half, axis * half, 0)
            start(send(side.at[other, shard], near.at[1 - axis, shard], near_send.at[1 - axis, shard], near_recv.at[1 - axis, shard], close[6 - bit]))
        merge(3, shard)

    def third(step):
        shard = order[step]
        for axis in (0, 1):
            await_at(near.at[axis, shard], near_recv.at[axis, shard])
            add_into(side.at[3, shard], near.at[axis, shard], rows)

    def fourth(step):
        shard = order[step]
        if step < n - 1:
            for way in (0, 1):
                ahead = shard > spot if way == 0 else shard < spot
                distance = jnp.clip(shard - spot if way == 0 else spot - shard, 1, n - 1)

                @pl.when(ahead & sides[1 - way][0])
                def _(way=way, distance=distance):
                    slot = jnp.minimum(distance, n - 2)
                    await_at(chain.at[way, slot], z_recv.at[way, slot])
                    add_into(side.at[3, shard], chain.at[way, slot], rows)

                start(send(side.at[3, shard], chain.at[way, distance - 1], z_send.at[way, distance - 1], z_recv.at[way, distance - 1], sides[way][1]), ahead)
        else:

            def body(index, carry):
                at = pl.ds(pl.multiple_of(index * 16, 16), 16)
                out[at, :] = side[3, spot, at, :].astype(jnp.float32)
                return carry

            lax.fori_loop(0, rows // 16, body, 0)
            for way in (0, 1):

                @pl.when(sides[1 - way][0])
                def _(way=way):
                    await_at(chain.at[way, 0], z_recv.at[way, 0])
                    add_into(out, chain.at[way, 0], rows)

    for step in range(n + 3):
        for task, delay in ((first, 0), (second, 1), (third, 2), (fourth, 3)):
            if 0 <= step - delay < n:
                task(step - delay)
    for condition, one in sends:
        if condition is None:
            one.wait_send()
        else:

            @pl.when(condition)
            def _(one=one):
                one.wait_send()


def box_sum(part, later):
    n = lax.axis_size("tensor")
    width = part.shape[1]
    rows = part.shape[0] // (8 * n)
    sem = pltpu.SemaphoreType.DMA
    kind = part.dtype
    anywhere = pl.BlockSpec(memory_space=pl.ANY)
    return pl.pallas_call(
        functools.partial(box_sum_kernel, n),
        out_shape=[
            jax.ShapeDtypeStruct((rows, width), jnp.float32),
            jax.ShapeDtypeStruct(later.shape, later.dtype),
        ],
        in_specs=[anywhere] * 2,
        out_specs=[pl.BlockSpec(memory_space=pltpu.VMEM), anywhere],
        input_output_aliases={1: 1},
        scratch_shapes=[
            pltpu.VMEM((4, n, rows, width), kind),
            pltpu.VMEM((4, n, rows, width), kind),
            pltpu.VMEM((2, n, rows // 2, width), kind),
            pltpu.VMEM((2, n, rows, width), kind),
            pltpu.VMEM((2, n - 1, rows, width), kind),
            sem((4, n)),
            sem((4, n)),
            sem((4, n)),
            sem((2, n)),
            sem((2, n)),
            sem((2, n)),
            sem((2, n)),
            sem((2, n - 1)),
            sem((2, n - 1)),
        ],
        compiler_params=pltpu.CompilerParams(
            collective_id=4, has_side_effects=True, vmem_limit_bytes=VMEM
        ),
        cost_estimate=transfer(165),
        name="box_sum",
    )(part.reshape(8, n, rows, width), later)


def everyone(n):
    count = lax.axis_size("dp") * n
    me = lax.axis_index("dp") * n + lax.axis_index("tensor")

    def device(number):
        return {"dp": number // n, "tensor": number % n}

    return count, me, device


def greet_all(count, me, device):
    barrier = pltpu.get_barrier_semaphore()

    def signal(step, carry):
        pl.semaphore_signal(barrier, inc=1, device_id=device(lax.rem(me + step, count)), device_id_type=MESH)
        return carry

    lax.fori_loop(1, count, signal, 0)
    pl.semaphore_wait(barrier, count - 1)


def spread_kernel(n, own, out, send_sem, recv_sem):
    count, me, device = everyone(n)
    greet_all(count, me, device)
    out[me] = own[...]

    def copy(step):
        return send(own, out.at[me], send_sem.at[step], recv_sem.at[step], device(lax.rem(me + step, count)))

    def go(step, carry):
        copy(step).start()
        return carry

    def end(step, carry):
        copy(step).wait_send()
        come = lax.rem(me - step + count, count)
        send(own, out.at[come], send_sem.at[step], recv_sem.at[step], device(come)).wait_recv()
        return carry

    lax.fori_loop(1, count, go, 0)
    lax.fori_loop(1, count, end, 0)


def spread(own):
    n = lax.axis_size("tensor")
    count = lax.axis_size("dp") * n
    sem = pltpu.SemaphoreType.DMA
    return pl.pallas_call(
        functools.partial(spread_kernel, n),
        out_shape=jax.ShapeDtypeStruct((count,) + own.shape, own.dtype),
        in_specs=[pl.BlockSpec(memory_space=pltpu.VMEM)],
        out_specs=pl.BlockSpec(memory_space=pltpu.VMEM),
        scratch_shapes=[sem((count,)), sem((count,))],
        compiler_params=pltpu.CompilerParams(
            collective_id=5, has_side_effects=True, vmem_limit_bytes=VMEM
        ),
        cost_estimate=transfer(10),
        name="spread",
    )(own)


def sum_spread_kernel(n, part, out, held, send_sem, recv_sem):
    count, me, device = everyone(n)
    greet_all(count, me, device)
    out[...] = part[me]

    def copy(step):
        to = lax.rem(me + step, count)
        return send(part.at[to], held.at[me], send_sem.at[step], recv_sem.at[step], device(to))

    def go(step, carry):
        copy(step).start()
        return carry

    def end(step, carry):
        come = lax.rem(me - step + count, count)
        send(part.at[0], held.at[come], send_sem.at[step], recv_sem.at[step], device(come)).wait_recv()
        out[...] += held[come]
        copy(step).wait_send()
        return carry

    lax.fori_loop(1, count, go, 0)
    lax.fori_loop(1, count, end, 0)


def sum_spread(part):
    n = lax.axis_size("tensor")
    count = lax.axis_size("dp") * n
    sem = pltpu.SemaphoreType.DMA
    return pl.pallas_call(
        functools.partial(sum_spread_kernel, n),
        out_shape=jax.ShapeDtypeStruct(part.shape[1:], part.dtype),
        in_specs=[pl.BlockSpec(memory_space=pltpu.VMEM)],
        out_specs=pl.BlockSpec(memory_space=pltpu.VMEM),
        scratch_shapes=[pltpu.VMEM(part.shape, part.dtype), sem((count,)), sem((count,))],
        compiler_params=pltpu.CompilerParams(
            collective_id=6, has_side_effects=True, vmem_limit_bytes=VMEM
        ),
        cost_estimate=transfer(20),
        name="sum_spread",
    )(part)


TB = 256
GR = 16
TILE = 256
SLOTS = 512
EXTRA = 2 * E
def ceil_to(value, unit):
    return (value + unit - 1) // unit * unit


def nt_dot(a, b):
    return lax.dot_general(a, b, (((1,), (1,)), ((), ())), preferred_element_type=jnp.float32)


def tn_dot(a, b):
    return lax.dot_general(a, b, (((0,), (0,)), ((), ())), preferred_element_type=jnp.float32)


def nn_dot(a, b):
    return jnp.dot(a, b, preferred_element_type=jnp.float32)


def pair(value):
    high = value.astype(jnp.bfloat16)
    low = (value - high.astype(jnp.float32)).astype(jnp.bfloat16)
    return high, low


def unpair(value):
    value = value.astype(jnp.float32)
    return value[:, :E] + value[:, E:]


def excl_cumsum(value, axis):
    return jnp.cumsum(value, axis) - value


class Plan:
    def __init__(self, tokens, seq_len, local):
        seqs = tokens // seq_len
        self.tokens, self.local = tokens, local
        self.blocks = tokens // TB
        per_seq = seq_len // TB
        worst = min(CG + (GR - 1) * per_seq, seq_len)
        self.cap = ceil_to(seqs * worst // GR * GR, TILE)
        groups = (seqs * local * CG + self.blocks * local * (GR - 1)) // GR
        self.items = groups * GR // TILE + self.blocks
        self.joins = groups * GR // SLOTS + self.blocks
        self.tiles = self.cap // TILE


def routing(plan, routes, base):
    local, blocks = plan.local, plan.blocks
    mine = base + jnp.arange(local)
    picked = jnp.any(routes[:, :, None] == mine[None, None, :], 1)
    grid = picked.reshape(blocks, TB, local)
    ones = grid.astype(jnp.bfloat16)
    earlier = (jnp.arange(TB)[:, None] > jnp.arange(TB)[None, :]).astype(jnp.bfloat16)
    rank = jnp.einsum("ts,bse->bte", earlier, ones, preferred_element_type=jnp.float32).astype(
        jnp.int32
    )
    count = jnp.sum(grid.astype(jnp.int32), 1)
    groups = (count + GR - 1) // GR
    inner = excl_cumsum(groups, 1)
    total = jnp.sum(groups, 1)
    outer = excl_cumsum(groups, 0)
    expert_rows = jnp.sum(groups, 0) * GR
    place = jnp.where(grid, inner[:, None, :] * GR + rank, -1)

    def items(size, unit):
        steps = jnp.maximum((total * GR + unit - 1) // unit, 1)
        first = excl_cumsum(steps, 0)
        used = jnp.sum(steps)
        index = jnp.minimum(jnp.arange(size), used - 1)
        block = jnp.sum((first[None, :] <= index[:, None]).astype(jnp.int32), 1) - 1
        here = block[:, None] == jnp.arange(blocks)[None, :]
        part = index - jnp.sum(jnp.where(here, first[None, :], 0), 1)
        last = part == jnp.sum(jnp.where(here, steps[None, :], 0), 1) - 1
        return first, used, block, part, last.astype(jnp.int32), here

    first, used, block, part, _, _ = items(plan.items, TILE)
    slots = plan.cap // GR
    spot = jnp.arange(slots)[None, :, None]
    low = outer.T[:, None, :]
    inside = (spot >= low) & (spot < low + groups.T[:, None, :])
    origin = first[None, :] * (TILE // GR) + inner.T
    source = jnp.sum(jnp.where(inside, origin[:, None, :] + spot - low, 0), 2)
    _, joined, jblock, jpart, jlast, here = items(plan.joins, SLOTS)

    def at_block(table):
        return jnp.sum(jnp.where(here[:, :, None], table[None], 0), 1)[:, None, :]

    wide = SLOTS // GR
    spot = (jpart[:, None] * wide + jnp.arange(wide)[None, :])[:, :, None]
    low, many, begin = at_block(inner), at_block(groups), at_block(outer)
    inside = (spot >= low) & (spot < low + many)
    target = jnp.sum(
        jnp.where(inside, (jnp.arange(local) * slots)[None, None, :] + begin + spot - low, 0), 2
    )
    return dict(
        place=place,
        used=used[None],
        block=block,
        part=part,
        source=source.reshape(-1),
        expert_rows=expert_rows,
        expert_tiles=jnp.maximum((expert_rows + TILE - 1) // TILE, 1),
        joined=joined[None],
        jblock=jblock,
        jpart=jpart,
        jlast=jlast,
        target=target.reshape(-1),
    )


def dispatch_kernel(used, block, part, post, grad, router, place, rows, share, held):
    step = pl.program_id(0)
    local = place.shape[1]

    @pl.when(step < used[0])
    def _():
        @pl.when(part[step] == 0)
        def _():
            portion = jax.nn.softmax(nn_dot(post[...], router[...]), -1)
            high, low = pair(portion)
            both = jnp.concatenate([high, low], 1)
            held[...] = both
            share[...] = both

        slot = lax.broadcasted_iota(jnp.int32, (TILE, TB), 0) + part[step] * TILE
        hit = slot == place[0, 0:1, :]
        for one in range(1, local):
            hit = hit | (slot == place[0, one : one + 1, :])
        pick = jnp.where(hit, 1.0, 0.0).astype(jnp.bfloat16)
        rows[:, :D] = nn_dot(pick, post[...]).astype(jnp.bfloat16)
        rows[:, D : 2 * D] = nn_dot(pick, grad[...]).astype(jnp.bfloat16)
        rows[:, 2 * D :] = nn_dot(pick, held[...]).astype(jnp.bfloat16)


def dispatch(plan, route, post, grad, router):
    wide = 2 * D + EXTRA
    place = route["place"].transpose(0, 2, 1)

    def at_block(step, used, block, part):
        return (block[step], 0)

    return pl.pallas_call(
        dispatch_kernel,
        grid_spec=pltpu.PrefetchScalarGridSpec(
            num_scalar_prefetch=3,
            grid=(plan.items,),
            in_specs=[
                pl.BlockSpec((TB, D), at_block),
                pl.BlockSpec((TB, D), at_block),
                pl.BlockSpec((D, E), lambda step, used, block, part: (0, 0)),
                pl.BlockSpec((1, plan.local, TB), lambda s, used, block, part: (block[s], 0, 0)),
            ],
            out_specs=[
                pl.BlockSpec(
                    (TILE, wide), lambda s, used, block, part: (jnp.minimum(s, used[0] - 1), 0)
                ),
                pl.BlockSpec((TB, EXTRA), at_block),
            ],
            scratch_shapes=[pltpu.VMEM((TB, EXTRA), jnp.bfloat16)],
        ),
        out_shape=[
            jax.ShapeDtypeStruct((plan.items * TILE, wide), jnp.bfloat16),
            jax.ShapeDtypeStruct((plan.tokens, EXTRA), jnp.bfloat16),
        ],
        compiler_params=pltpu.CompilerParams(vmem_limit_bytes=VMEM),
        cost_estimate=pl.CostEstimate(
            flops=2 * plan.items * TILE * TB * wide,
            bytes_accessed=4 * plan.items * TILE * wide,
            transcendentals=0,
        ),
        name="dispatch",
    )(route["used"], route["block"], route["part"], post, grad, router, place)


def expert_kernel(source, tiles, filled, base, *refs):
    count = TILE // GR
    parts = refs[:count]
    w_gate, w_up, w_down, result, gate_out, up_out, down_out = refs[count : count + 7]
    gate_sum, up_sum, down_sum = refs[count + 7 :]
    expert, step = pl.program_id(0), pl.program_id(1)

    @pl.when(step == 0)
    def _():
        gate_sum[...] = jnp.zeros_like(gate_sum)
        up_sum[...] = jnp.zeros_like(up_sum)
        down_sum[...] = jnp.zeros_like(down_sum)

    @pl.when(step < tiles[expert])
    def _():
        number = base[0] + expert
        real = lax.broadcasted_iota(jnp.int32, (TILE, 1), 0) < filled[expert] - step * TILE

        def take(begin, end):
            value = jnp.concatenate([part[:, begin:end] for part in parts], 0)
            return jnp.where(real, value, jnp.zeros_like(value))

        rows, upstream, shares = take(0, D), take(D, 2 * D), take(2 * D, 2 * D + EXTRA)
        lane = lax.broadcasted_iota(jnp.int32, (TILE, EXTRA), 1)
        own = (lane == number) | (lane == number + E)
        gate = jnp.sum(jnp.where(own, shares.astype(jnp.float32), 0.0), -1, keepdims=True)
        gate_pre = nn_dot(rows, w_gate[0])
        up_pre = nn_dot(rows, w_up[0])
        plain = nn_dot(upstream, w_down[0])
        squash = jax.nn.sigmoid(gate_pre)
        swish = gate_pre * squash
        active = (swish * up_pre).astype(jnp.bfloat16).astype(jnp.float32)
        change = jnp.sum(active * plain, -1, keepdims=True)
        grad_active = gate * plain
        grad_gate = (grad_active * up_pre * squash * (1.0 + gate_pre * (1.0 - squash))).astype(
            jnp.bfloat16
        )
        grad_up = (grad_active * swish).astype(jnp.bfloat16)
        scaled = (gate * active).astype(jnp.bfloat16)
        result[:, :D] = nt_dot(scaled, w_down[0]).astype(jnp.bfloat16)
        result[:, D : 2 * D] = (nt_dot(grad_gate, w_gate[0]) + nt_dot(grad_up, w_up[0])).astype(
            jnp.bfloat16
        )
        high, low = pair(change)
        result[:, 2 * D :] = jnp.where(
            lane == number,
            high.astype(jnp.float32),
            jnp.where(lane == number + E, low.astype(jnp.float32), 0.0),
        ).astype(jnp.bfloat16)
        gate_sum[...] += tn_dot(grad_gate, rows)
        up_sum[...] += tn_dot(grad_up, rows)
        down_sum[...] += tn_dot(scaled, upstream)

    @pl.when(step == pl.num_programs(1) - 1)
    def _():
        gate_out[0] = gate_sum[...].T
        up_out[0] = up_sum[...].T
        down_out[0] = down_sum[...].T


def experts(plan, route, base, rows, w_gate, w_up, w_down):
    wide = 2 * D + EXTRA
    width = w_gate.shape[2]
    count = TILE // GR
    slots = plan.cap // GR

    def group_at(index):
        def place(expert, step, source, tiles, filled, base):
            tile = jnp.minimum(step, tiles[expert] - 1)
            return (source[expert * slots + tile * count + index], 0)

        return pl.BlockSpec((GR, wide), place)

    def whole(expert, step, source, tiles, filled, base):
        return (expert, 0, 0)

    def tile_at(expert, step, source, tiles, filled, base):
        return (expert * plan.tiles + jnp.minimum(step, tiles[expert] - 1), 0)

    weight = pl.BlockSpec((1, D, width), whole)
    total = plan.local * plan.cap
    return pl.pallas_call(
        expert_kernel,
        grid_spec=pltpu.PrefetchScalarGridSpec(
            num_scalar_prefetch=4,
            grid=(plan.local, plan.tiles),
            in_specs=[group_at(index) for index in range(count)] + [weight] * 3,
            out_specs=[pl.BlockSpec((TILE, wide), tile_at)] + [weight] * 3,
            scratch_shapes=[pltpu.VMEM((width, D), jnp.float32)] * 3,
        ),
        out_shape=[jax.ShapeDtypeStruct((total, wide), jnp.bfloat16)]
        + [jax.ShapeDtypeStruct((plan.local, D, width), jnp.float32)] * 3,
        compiler_params=pltpu.CompilerParams(vmem_limit_bytes=VMEM),
        cost_estimate=pl.CostEstimate(
            flops=18 * total * D * width * 5 // 8,
            bytes_accessed=4 * total * wide * 5 // 8,
            transcendentals=0,
        ),
        name="experts",
    )(
        route["source"],
        route["expert_tiles"],
        route["expert_rows"],
        base[None],
        *([rows] * count),
        w_gate,
        w_up,
        w_down,
    )


def combine_kernel(joined, block, part, last, target, *refs):
    count = SLOTS // GR
    groups = refs[:count]
    place, share, post, router, out, grad, router_out, sums = refs[count:]
    step = pl.program_id(0)
    local = place.shape[1]

    @pl.when(step == 0)
    def _():
        router_out[...] = jnp.zeros_like(router_out)

    @pl.when(step < joined[0])
    def _():
        slot = lax.broadcasted_iota(jnp.int32, (TB, SLOTS), 1) + part[step] * SLOTS
        hit = slot == place[:, 0:1]
        for one in range(1, local):
            hit = hit | (slot == place[:, one : one + 1])
        pick = jnp.where(hit, 1.0, 0.0).astype(jnp.bfloat16)

        def term(begin, end):
            return nn_dot(pick, jnp.concatenate([group[:, begin:end] for group in groups], 0))

        def finish(value):
            change = unpair_wide(value(2 * D, 2 * D + EXTRA))
            portion = unpair(share[...])
            moved = portion * (change - jnp.sum(change * portion, -1, keepdims=True))
            moved = moved.astype(jnp.bfloat16)
            out[...] = value(0, D).astype(jnp.bfloat16)
            grad[...] = (value(D, 2 * D) + nt_dot(moved, router[...])).astype(jnp.bfloat16)
            router_out[...] += tn_dot(moved, post[...])

        single = (part[step] == 0) & (last[step] == 1)

        @pl.when(single)
        def _():
            finish(term)

        @pl.when(jnp.logical_not(single))
        def _():
            @pl.when(part[step] == 0)
            def _():
                sums[...] = jnp.zeros_like(sums)

            sums[...] += term(0, 2 * D + EXTRA)

            @pl.when(last[step] == 1)
            def _():
                finish(lambda begin, end: sums[:, begin:end])


def unpair_wide(value):
    return value[:, :E] + value[:, E:]


def combine(plan, route, results, share, post, router):
    wide = 2 * D + EXTRA
    count = SLOTS // GR

    def group_at(index):
        def place(step, joined, block, part, last, target):
            return (target[step * count + index], 0)

        return pl.BlockSpec((GR, wide), place)

    def at_block(step, joined, block, part, last, target):
        return (block[step], 0)

    def fixed(step, joined, block, part, last, target):
        return (0, 0)

    return pl.pallas_call(
        combine_kernel,
        grid_spec=pltpu.PrefetchScalarGridSpec(
            num_scalar_prefetch=5,
            grid=(plan.joins,),
            in_specs=[group_at(index) for index in range(count)]
            + [
                pl.BlockSpec((TB, plan.local), at_block),
                pl.BlockSpec((TB, EXTRA), at_block),
                pl.BlockSpec((TB, D), at_block),
                pl.BlockSpec((D, E), fixed),
            ],
            out_specs=[
                pl.BlockSpec((TB, D), at_block),
                pl.BlockSpec((TB, D), at_block),
                pl.BlockSpec((E, D), fixed),
            ],
            scratch_shapes=[pltpu.VMEM((TB, wide), jnp.float32)],
        ),
        out_shape=[
            jax.ShapeDtypeStruct((plan.tokens, D), jnp.bfloat16),
            jax.ShapeDtypeStruct((plan.tokens, D), jnp.bfloat16),
            jax.ShapeDtypeStruct((E, D), jnp.float32),
        ],
        compiler_params=pltpu.CompilerParams(vmem_limit_bytes=VMEM),
        cost_estimate=pl.CostEstimate(
            flops=2 * plan.joins * SLOTS * TB * wide,
            bytes_accessed=4 * plan.tokens * wide,
            transcendentals=0,
        ),
        name="combine",
    )(
        route["joined"],
        route["jblock"],
        route["jpart"],
        route["jlast"],
        route["target"],
        *([results] * count),
        route["place"].reshape(plan.tokens, plan.local),
        share,
        post,
        router,
    )


def gather_all(own):
    if lax.axis_size("dp") == 8:
        return box_gather(own)
    return lax.all_gather(
        lax.all_gather(own, "tensor", axis=0, tiled=True), "dp", axis=0, tiled=True
    )


def gather_slowly(own):
    if lax.axis_size("dp") == 8:
        return lax.all_gather(own, ("dp", "tensor"), axis=0, tiled=True)
    return gather_all(own)


def sum_all(part, later):
    if lax.axis_size("dp") == 8:
        return box_sum(part, later)
    return chain_sum(lax.psum_scatter(part, "dp", scatter_dimension=0, tiled=True), later, 9)


def fill(value, rows, columns):
    return jnp.pad(value, ((0, rows - value.shape[0]), (0, columns - value.shape[1])))


def share_small(router, prenorm, postnorm, querynorm, keynorm, routes):
    n = lax.axis_size("tensor")
    rank = lax.axis_index("tensor")
    rows = router.shape[0]
    head = ceil_to(max(rows, querynorm.shape[0]), 16)
    heads = querynorm.shape[1]
    block = jnp.concatenate(
        [
            fill(router, head, E),
            fill(prenorm[:, None], head, 1),
            fill(postnorm[:, None], head, 1),
            fill(querynorm, head, heads),
            fill(keynorm, head, heads),
        ],
        1,
    )
    part = routes.shape[0] // n
    own = lax.dynamic_slice_in_dim(routes, rank * part, part, 0)
    own = own.astype(jnp.bfloat16).reshape(-1, 128)
    tail = ceil_to(own.shape[0], 16)
    everything = spread(jnp.concatenate([fill(block, head, 128), fill(own, tail, 128)], 0))
    mine = everything.reshape(-1, n, head + tail, 128)[:, rank]
    at = E + 2
    return (
        everything[:, :rows, :E].reshape(-1, E),
        everything[:, :rows, E].reshape(-1).astype(jnp.float32),
        everything[:, :rows, E + 1].reshape(-1).astype(jnp.float32),
        mine[:, : querynorm.shape[0], at : at + heads].reshape(-1, heads),
        mine[:, : querynorm.shape[0], at + heads : at + 2 * heads].reshape(-1, heads),
        everything[:, head : head + own.shape[0]].reshape(-1, TOP).astype(jnp.int32),
    )


def body(
    hidden_in,
    out_grad,
    doc_ids,
    expert_ids,
    prenorm,
    querynorm,
    keynorm,
    query_proj,
    key_proj,
    value_proj,
    output_proj,
    postnorm,
    router,
    gate_proj,
    up_proj,
    down_proj,
):
    residual = hidden_in[0].astype(jnp.float32)
    upstream = out_grad[0]
    documents = doc_ids[0]
    routes = expert_ids[0]
    shard = residual.shape[0]
    seq_len = documents.shape[0]
    mesh_dp = lax.axis_size("dp")
    block = min(seq_len, 1024)
    scale = HD ** (-0.5)
    cosine, sine = rope_tables(seq_len, HD)
    router_full, pre_gain, post_gain, gain_query, gain_key, all_routes = share_small(
        router, prenorm, postnorm, querynorm, keynorm, routes
    )
    weights = lax.all_gather(
        jnp.concatenate([query_proj, key_proj, value_proj, output_proj], 1),
        "dp",
        axis=0,
        tiled=True,
    )
    w_query, w_key, w_value, w_output = jnp.split(weights, 4, 1)
    heads = w_query.shape[1] // HD
    query_scale = gain_query.astype(jnp.float32).T.reshape(-1)
    key_scale = gain_key.astype(jnp.float32).T.reshape(-1)
    inv_pre = lax.rsqrt(jnp.mean(residual * residual, -1, keepdims=True) + epsilon)
    group_hidden, later = chain_gather(hidden_in[0], upstream, 1)
    group_hidden = group_hidden.astype(jnp.float32)
    group_inv = lax.rsqrt(jnp.mean(group_hidden * group_hidden, -1, keepdims=True) + epsilon)
    group_normed = (group_hidden * group_inv * pre_gain).astype(jnp.bfloat16)
    plan = Plan(mesh_dp * seq_len, seq_len, gate_proj.shape[0])
    base = (lax.axis_index("dp") * plan.local).astype(jnp.int32)
    all_grad = gather_slowly(later)
    route = routing(plan, all_routes, base)
    query = jnp.dot(group_normed, w_query, preferred_element_type=jnp.float32)
    keys = jnp.dot(group_normed, w_key, preferred_element_type=jnp.float32)
    values = jnp.dot(group_normed, w_value, preferred_element_type=jnp.float32).astype(jnp.bfloat16)
    query_sq, key_sq = sum_heads(
        (jnp.sum(query * query, -1, keepdims=True), jnp.sum(keys * keys, -1, keepdims=True))
    )
    inv_query = lax.rsqrt(query_sq / D + epsilon)
    inv_key = lax.rsqrt(key_sq / D + epsilon)
    query_heads = (query * inv_query * query_scale).reshape(seq_len, heads, HD)
    key_heads = (keys * inv_key * key_scale).reshape(seq_len, heads, HD)
    query_rot = (query_heads * cosine[:, None] + rotate(query_heads) * sine[:, None]).astype(
        jnp.bfloat16
    )
    key_rot = (key_heads * cosine[:, None] + rotate(key_heads) * sine[:, None]).astype(jnp.bfloat16)
    value_heads = values.reshape(seq_len, heads, HD)
    mixed, logsum = attend_forward(query_rot, key_rot, value_heads, documents, block, scale)
    mixed_flat = mixed.reshape(seq_len, heads * HD)
    attn_term = lax.dot_general(
        mixed_flat, w_output, (((1,), (1,)), ((), ())), preferred_element_type=jnp.float32
    )
    attn_local, later = chain_sum(attn_term.astype(jnp.bfloat16), later, 7)
    middle = residual + attn_local
    inv_post = lax.rsqrt(jnp.mean(middle * middle, -1, keepdims=True) + epsilon)
    post_normed = (middle * inv_post * post_gain).astype(jnp.bfloat16)
    all_post = gather_all(post_normed)
    rows = dispatch(plan, route, all_post, all_grad, router_full)
    results, gate_weight_grad, up_weight_grad, down_weight_grad = experts(
        plan, route, base, rows[0], gate_proj, up_proj, down_proj
    )
    moe_term, grad_term, router_part = combine(
        plan, route, results, rows[1], all_post, router_full
    )
    grad_post, moe_term = sum_all(grad_term, moe_term)
    moe_term = lax.psum_scatter(moe_term, "dp", scatter_dimension=0, tiled=True)
    moe_local = lax.psum_scatter(moe_term, "tensor", scatter_dimension=0, tiled=True)
    router_part = router_part.T
    post_gain_part = jnp.sum(grad_post * middle * inv_post, 0)
    grad_middle = upstream.astype(jnp.float32) + norm_back(
        grad_post, middle, inv_post, post_gain, D
    )
    group_change, _ = chain_gather(grad_middle.astype(jnp.bfloat16), later, 2)
    grad_mixed = jnp.dot(group_change, w_output, preferred_element_type=jnp.float32).astype(
        jnp.bfloat16
    )
    output_part = lax.dot_general(
        group_change, mixed_flat, (((0,), (0,)), ((), ())), preferred_element_type=jnp.float32
    )
    grad_query_rot, grad_key_rot, grad_value_heads = attend_backward(
        query_rot,
        key_rot,
        value_heads,
        documents,
        logsum,
        grad_mixed.reshape(seq_len, heads, HD),
        block,
        scale,
    )
    grad_query_flat = (
        grad_query_rot * cosine[:, None] + rotate_back(grad_query_rot * sine[:, None])
    ).reshape(seq_len, -1)
    grad_key_flat = (
        grad_key_rot * cosine[:, None] + rotate_back(grad_key_rot * sine[:, None])
    ).reshape(seq_len, -1)
    query_inner, key_inner = sum_heads(
        (
            jnp.sum(grad_query_flat * query_scale * query, -1, keepdims=True),
            jnp.sum(grad_key_flat * key_scale * keys, -1, keepdims=True),
        )
    )
    grad_query = (
        inv_query * query_scale * grad_query_flat - query * inv_query**3 * query_inner / D
    ).astype(jnp.bfloat16)
    grad_key = (inv_key * key_scale * grad_key_flat - keys * inv_key**3 * key_inner / D).astype(
        jnp.bfloat16
    )
    query_gain_part = jnp.sum(grad_query_flat * query * inv_query, 0).reshape(heads, HD).T
    key_gain_part = jnp.sum(grad_key_flat * keys * inv_key, 0).reshape(heads, HD).T
    grad_value = grad_value_heads.reshape(seq_len, -1).astype(jnp.bfloat16)
    query_part = lax.dot_general(
        group_normed, grad_query, (((0,), (0,)), ((), ())), preferred_element_type=jnp.float32
    )
    key_part = lax.dot_general(
        group_normed, grad_key, (((0,), (0,)), ((), ())), preferred_element_type=jnp.float32
    )
    value_part = lax.dot_general(
        group_normed, grad_value, (((0,), (0,)), ((), ())), preferred_element_type=jnp.float32
    )
    normed_term = lax.dot_general(
        grad_query, w_query, (((1,), (1,)), ((), ())), preferred_element_type=jnp.float32
    )
    normed_term = normed_term + lax.dot_general(
        grad_key, w_key, (((1,), (1,)), ((), ())), preferred_element_type=jnp.float32
    )
    normed_term = normed_term + lax.dot_general(
        grad_value, w_value, (((1,), (1,)), ((), ())), preferred_element_type=jnp.float32
    )
    grad_normed, middle = chain_sum(normed_term.astype(jnp.bfloat16), middle, 8)
    layer_out = (middle + moe_local.astype(jnp.float32)).astype(jnp.bfloat16)[None]
    pre_gain_part = jnp.sum(grad_normed * residual * inv_pre, 0)
    input_grad = (grad_middle + norm_back(grad_normed, residual, inv_pre, pre_gain, D)).astype(
        jnp.bfloat16
    )[None]
    own_rows = D // mesh_dp
    gains = jnp.concatenate([query_gain_part, key_gain_part], 1).astype(jnp.bfloat16)
    gains = jnp.pad(
        gains.reshape(mesh_dp, -1, 2 * heads),
        ((0, 0), (0, own_rows - HD // mesh_dp), (0, 128 - 2 * heads)),
    )
    attn_sums = lax.psum_scatter(
        jnp.concatenate(
            [
                part.astype(jnp.bfloat16)
                for part in (query_part, key_part, value_part, output_part)
            ]
            + [gains.reshape(D, 128)],
            1,
        ),
        "dp",
        scatter_dimension=0,
        tiled=True,
    ).astype(jnp.float32)
    query_grad, key_grad, value_grad, output_grad, gain_grads = jnp.split(
        attn_sums, [heads * HD * count for count in (1, 2, 3, 4)], 1
    )
    gain_grads = gain_grads[: HD // mesh_dp]
    small = jnp.concatenate(
        [
            router_part,
            pre_gain_part[:, None],
            post_gain_part[:, None],
            jnp.zeros((D, 128 - E - 2), jnp.float32),
        ],
        1,
    )
    small = sum_spread(small.reshape(-1, router.shape[0], 128))
    return (
        layer_out,
        input_grad,
        small[:, E],
        gain_grads[:, :heads],
        gain_grads[:, heads : 2 * heads],
        query_grad,
        key_grad,
        value_grad,
        output_grad,
        small[:, E + 1],
        small[:, :E],
        gate_weight_grad,
        up_weight_grad,
        down_weight_grad,
    )


def solution(mesh):
    in_specs = (
        P("dp", "tensor", None),
        P("dp", "tensor", None),
        P("dp", None),
        P("dp", None, None),
        P(("dp", "tensor")),
        P("dp", "tensor"),
        P("dp", "tensor"),
        P("dp", "tensor"),
        P("dp", "tensor"),
        P("dp", "tensor"),
        P("dp", "tensor"),
        P(("dp", "tensor")),
        P(("dp", "tensor"), None),
        P("dp", None, "tensor"),
        P("dp", None, "tensor"),
        P("dp", None, "tensor"),
    )
    out_specs = (
        P("dp", "tensor", None),
        P("dp", "tensor", None),
        P(("dp", "tensor")),
        P("dp", "tensor"),
        P("dp", "tensor"),
        P("dp", "tensor"),
        P("dp", "tensor"),
        P("dp", "tensor"),
        P("dp", "tensor"),
        P(("dp", "tensor")),
        P(("dp", "tensor"), None),
        P("dp", None, "tensor"),
        P("dp", None, "tensor"),
        P("dp", None, "tensor"),
    )
    return jax.shard_map(body, mesh=mesh, in_specs=in_specs, out_specs=out_specs, check_vma=False)
```

```python
import functools

import jax
import jax.numpy as jnp
from jax import lax
from jax.experimental import pallas as pl
from jax.experimental.pallas import tpu as pltpu
from jax.sharding import PartitionSpec as P

D = 2048
HD = 128
E = 64
TOP = 8
CG = 192


epsilon = 1e-05
masked_score = -1000000000.0


def rope_tables(length, width):
    positions = jnp.arange(length).astype(jnp.float32)
    rates = 10000.0 ** (-jnp.arange(0, width, 2).astype(jnp.float32) / width)
    angles = positions[:, None] * rates[None, :]
    return (jnp.concatenate([jnp.cos(angles)] * 2, -1), jnp.concatenate([jnp.sin(angles)] * 2, -1))


def rotate(tensor):
    half = tensor.shape[-1] // 2
    return jnp.concatenate([-tensor[..., half:], tensor[..., :half]], -1)


def rotate_back(tensor):
    half = tensor.shape[-1] // 2
    return jnp.concatenate([tensor[..., half:], -tensor[..., :half]], -1)


def sum_heads(parts):
    return lax.psum((parts[0], parts[1]), "tensor")


def norm_back(grad, value, inverse, gain, width):
    scaled = grad * gain
    inner = jnp.sum(scaled * value, -1, keepdims=True)
    return inverse * scaled - value * inverse**3 * inner / width


def block_scores(query, keys, documents, start, block, scale):
    row_place = start + jnp.arange(block)
    col_place = jnp.arange(documents.shape[0])
    allowed = (documents[:, None] == documents[None, :]) & (
        row_place[:, None] >= col_place[None, :]
    )
    scores = jnp.einsum("qhd,khd->hqk", query, keys, preferred_element_type=jnp.float32) * scale
    return (jnp.where(allowed[None], scores, masked_score), query)


def attend_forward(query, keys, values, documents, block, scale):
    count = query.shape[0] // block

    def one(index):
        scores, rows = block_scores(query, keys, documents, index * block, block, scale)
        peak = jnp.max(scores, -1, keepdims=True)
        weights = jnp.exp(scores - peak)
        total = jnp.sum(weights, -1, keepdims=True)
        portion = (weights / total).astype(jnp.bfloat16)
        mixed = jnp.einsum("hqk,khd->qhd", portion, values, preferred_element_type=jnp.float32)
        return (mixed.astype(jnp.bfloat16), peak + jnp.log(total))

    mixed, logsum = lax.map(one, jnp.arange(count))
    return (mixed.reshape(query.shape), logsum)


def attend_backward(query, keys, values, documents, logsum, grad_mixed, block, scale):
    count = query.shape[0] // block

    def one(index):
        start = index * block
        scores, rows = block_scores(query, keys, documents, start, block, scale)
        portion = jnp.exp(scores - logsum[index])
        grad_portion = jnp.einsum(
            "qhd,khd->hqk", grad_mixed, values, preferred_element_type=jnp.float32
        )
        center = jnp.sum(portion * grad_portion, -1, keepdims=True)
        grad_scores = (portion * (grad_portion - center)).astype(jnp.bfloat16)
        grad_values = jnp.einsum(
            "hqk,qhd->khd",
            portion.astype(jnp.bfloat16),
            grad_mixed,
            preferred_element_type=jnp.float32,
        )
        grad_query = (
            jnp.einsum("hqk,khd->qhd", grad_scores, keys, preferred_element_type=jnp.float32)
            * scale
        )
        grad_keys = (
            jnp.einsum("hqk,qhd->khd", grad_scores, rows, preferred_element_type=jnp.float32)
            * scale
        )
        return (grad_query, grad_keys, grad_values)

    grad_query, grad_keys, grad_values = lax.map(one, jnp.arange(count))
    return (grad_query.reshape(query.shape), jnp.sum(grad_keys, 0), jnp.sum(grad_values, 0))


MESH = pl.DeviceIdType.MESH
VMEM = 60 * 1024 * 1024


def transfer(microseconds):
    return pl.CostEstimate(flops=0, bytes_accessed=microseconds * 3_000_000, transcendentals=0)


def flip(index, bit):
    return index + bit - 2 * bit * ((index // bit) % 2)


def send(source, target, send_sem, recv_sem, device):
    return pltpu.make_async_remote_copy(
        src_ref=source,
        dst_ref=target,
        send_sem=send_sem,
        recv_sem=recv_sem,
        device_id=device,
        device_id_type=MESH,
    )


def greet(devices, extra=()):
    barrier = pltpu.get_barrier_semaphore()
    for device in devices:
        pl.semaphore_signal(barrier, inc=1, device_id=device, device_id_type=MESH)
    for there, device in extra:

        @pl.when(there)
        def _(device=device):
            pl.semaphore_signal(barrier, inc=1, device_id=device, device_id_type=MESH)

    count = len(devices)
    for there, _ in extra:
        count = count + jnp.where(there, 1, 0)
    pl.semaphore_wait(barrier, count)


def both_ways(n):
    spot = lax.axis_index("tensor")
    return spot, (
        (spot < n - 1, {"tensor": jnp.minimum(spot + 1, n - 1)}),
        (spot > 0, {"tensor": jnp.maximum(spot - 1, 0)}),
    )


def shard_at(spot, way, distance, n):
    number = spot - distance if way == 0 else spot + distance
    return (number >= 0) & (number < n), jnp.clip(number, 0, n - 1)


def chain_gather_kernel(n, pieces, own, _later, *refs):
    if len(refs) > 5:
        small, out, _passed, everything, local_sem, send_sem, recv_sem, all_send, all_recv = refs
        finish = spread_start(n, small, everything, all_send, all_recv)
    else:
        out, _passed, local_sem, send_sem, recv_sem = refs
        finish = None
    spot, sides = both_ways(n)
    rows = own.shape[0] // pieces
    if finish is None:
        greet([], sides)
    keep = pltpu.make_async_copy(own, out.at[spot], local_sem)
    keep.start()

    def copy(way, distance, piece):
        there, number = shard_at(spot, way, distance, n)
        part = pl.ds(piece * rows, rows)
        source = own.at[part] if distance == 0 else out.at[number, part]
        return there & sides[way][0], send(
            source,
            out.at[number, part],
            send_sem.at[way, distance, piece],
            recv_sem.at[way, distance, piece],
            sides[way][1],
        )

    def arrived(way, distance, piece):
        there, number = shard_at(spot, way, distance, n)
        part = pl.ds(piece * rows, rows)

        @pl.when(there)
        def _():
            send(
                out.at[number, part],
                out.at[number, part],
                send_sem.at[way, distance - 1, piece],
                recv_sem.at[way, distance - 1, piece],
                sides[way][1],
            ).wait_recv()

    for distance in range(n):
        for piece in range(pieces):
            for way in (0, 1):
                if distance:
                    arrived(way, distance, piece)
                if distance < n - 1:
                    go, one = copy(way, distance, piece)

                    @pl.when(go)
                    def _(one=one):
                        one.start()

    keep.wait()
    for distance in range(n - 1):
        for piece in range(pieces):
            for way in (0, 1):
                go, one = copy(way, distance, piece)

                @pl.when(go)
                def _(one=one):
                    one.wait_send()

    if finish is not None:
        finish()


def chain_gather(own, later, number, small=None, pieces=4):
    n = lax.axis_size("tensor")
    rows, width = own.shape
    anywhere = pl.BlockSpec(memory_space=pl.ANY)
    inside = pl.BlockSpec(memory_space=pltpu.VMEM)
    sem = pltpu.SemaphoreType.DMA
    outs = [
        jax.ShapeDtypeStruct((n, rows, width), own.dtype),
        jax.ShapeDtypeStruct(later.shape, later.dtype),
    ]
    more, sems = [], []
    if small is not None:
        count = lax.axis_size("dp") * n
        outs.append(jax.ShapeDtypeStruct((count,) + small.shape, small.dtype))
        more, sems = [small], [sem((count,)), sem((count,))]
    out, *rest = pl.pallas_call(
        functools.partial(chain_gather_kernel, n, pieces),
        out_shape=outs,
        in_specs=[anywhere] * 2 + [inside] * len(more),
        out_specs=[anywhere] * 2 + [inside] * len(more),
        input_output_aliases={1: 1},
        scratch_shapes=[sem, sem((2, n - 1, pieces)), sem((2, n - 1, pieces))] + sems,
        compiler_params=pltpu.CompilerParams(
            collective_id=number, has_side_effects=True, vmem_limit_bytes=VMEM
        ),
        cost_estimate=transfer(65),
        name="chain_gather",
    )(own, later, *more)
    return (out.reshape(n * rows, width), *rest)


def add_into(target, source, rows, start=0, source_start=0):
    step = 16

    def body(index, carry):
        at = pl.ds(pl.multiple_of(start + index * step, step), step)
        come = pl.ds(pl.multiple_of(source_start + index * step, step), step)
        target[at, :] = (
            target[at, :].astype(jnp.float32) + source[come, :].astype(jnp.float32)
        ).astype(target.dtype)
        return carry

    lax.fori_loop(0, rows // step, body, 0)


def chain_sum_kernel(n, pieces, part, _later, out, _passed, held, send_sem, recv_sem):
    spot, sides = both_ways(n)
    greet([], sides)
    onward, finish, drain = chain_steps(n, pieces, part, out, held, send_sem, recv_sem)
    for far in range(n - 1, 0, -1):
        onward(far)
    finish()
    drain()


def chain_steps(n, pieces, part, out, held, send_sem, recv_sem):
    spot, sides = both_ways(n)
    rows = out.shape[0] // pieces

    def copy(way, far, piece, mine):
        number = spot + far if way == 0 else spot - far
        there = (number >= 0) & (number < n)
        number = jnp.clip(number, 0, n - 1)
        at = pl.ds(piece * rows, rows)
        source = part.at[number, at]
        return there, number, send(
            source if mine else held.at[way, far, at],
            held.at[way, far - 1, at],
            send_sem.at[way, far - 1, piece],
            recv_sem.at[way, far - 1, piece],
            sides[way][1],
        )

    def arrived(way, far, piece):
        at = pl.ds(piece * rows, rows)
        send(
            held.at[way, far, at],
            held.at[way, far, at],
            send_sem.at[way, far, piece],
            recv_sem.at[way, far, piece],
            sides[way][1],
        ).wait_recv()

    def onward(far):
        for piece in range(pieces):
            for way in (0, 1):
                behind = sides[1 - way][0]
                there, number, first = copy(way, far, piece, True)

                @pl.when(there & jnp.logical_not(behind))
                def _(first=first):
                    first.start()

                if far < n - 1:
                    _, _, again = copy(way, far, piece, False)

                    @pl.when(there & behind)
                    def _(way=way, piece=piece, number=number, again=again):
                        arrived(way, far, piece)
                        add_into(
                            held.at[way, far], part.at[number], rows, piece * rows, piece * rows
                        )
                        again.start()

    def finish():
        for piece in range(pieces):

            def body(index, carry, piece=piece):
                here = pl.ds(pl.multiple_of(piece * rows + index * 16, 16), 16)
                out[here, :] = part[spot, here, :].astype(jnp.float32)
                return carry

            lax.fori_loop(0, rows // 16, body, 0)
            for way in (0, 1):

                @pl.when(sides[1 - way][0])
                def _(way=way, piece=piece):
                    arrived(way, 0, piece)
                    add_into(out, held.at[way, 0], rows, piece * rows, piece * rows)

    def drain():
        for far in range(n - 1, 0, -1):
            for piece in range(pieces):
                for way in (0, 1):
                    there, _, one = copy(way, far, piece, True)

                    @pl.when(there)
                    def _(one=one):
                        one.wait_send()

    return onward, finish, drain


def chain_sum(part, later, number, pieces=4):
    n = lax.axis_size("tensor")
    width = part.shape[1]
    rows = part.shape[0] // n
    anywhere = pl.BlockSpec(memory_space=pl.ANY)
    inside = pl.BlockSpec(memory_space=pltpu.VMEM)
    return pl.pallas_call(
        functools.partial(chain_sum_kernel, n, pieces),
        out_shape=[
            jax.ShapeDtypeStruct((rows, width), jnp.float32),
            jax.ShapeDtypeStruct(later.shape, later.dtype),
        ],
        in_specs=[inside, anywhere],
        out_specs=[inside, anywhere],
        input_output_aliases={1: 1},
        scratch_shapes=[
            pltpu.VMEM((2, n - 1, rows, width), part.dtype),
            pltpu.SemaphoreType.DMA((2, n - 1, pieces)),
            pltpu.SemaphoreType.DMA((2, n - 1, pieces)),
        ],
        compiler_params=pltpu.CompilerParams(
            collective_id=number, has_side_effects=True, vmem_limit_bytes=VMEM
        ),
        cost_estimate=transfer(65),
        name="chain_sum",
    )(part.reshape(n, rows, width), later)


def box_devices():
    me = lax.axis_index("dp")
    return me, {bit: {"dp": flip(me, bit)} for bit in (1, 2, 4)}


def box_gather_kernel(n, own, out, local_sem, z_send, z_recv, near_send, near_recv, on_send, on_recv, side_send, side_recv):
    spot, sides = both_ways(n)
    me, near = box_devices()
    half = own.shape[0] // 2
    greet([near[1], near[2], near[4]], sides)
    keep = pltpu.make_async_copy(own, out.at[me, spot], local_sem)
    keep.start()
    sends = []

    def piece(seq, shard, part):
        return out.at[seq, shard, pl.ds(part * half, half)]

    def start(condition, one):
        sends.append((condition, one))

        @pl.when(condition)
        def _():
            one.start()

    def await_piece(condition, target, recv):
        @pl.when(condition)
        def _():
            send(target, target, side_send.at[0, 0, 0], recv, near[1]).wait_recv()

    def to_side(condition, slot, seq, shard, part, source):
        start(condition, send(source, piece(seq, shard, part), side_send.at[slot, shard, part], side_recv.at[slot, shard, part], near[1]))

    def mine(way, distance):
        there, shard = shard_at(spot, way, distance, n)
        for part in (0, 1):
            if distance:
                await_piece(there, piece(me, shard, part), z_recv.at[way, distance - 1, part])
            source = piece(me, shard, part) if distance else own.at[pl.ds(part * half, half)]
            for out_way in (0, 1) if distance == 0 else (way,):
                if distance < n - 1:
                    start(there & sides[out_way][0], send(source, piece(me, shard, part), z_send.at[out_way, distance, part], z_recv.at[out_way, distance, part], sides[out_way][1]))
            for axis, bit in ((0, 2), (1, 4)):
                start(there, send(source, piece(me, shard, part), near_send.at[axis, shard, part], near_recv.at[axis, shard, part], near[bit]))
            to_side(there, 0, me, shard, part, source)

    def nearby(way, distance):
        there, shard = shard_at(spot, way, distance, n)
        for part in (0, 1):
            for axis, bit in ((0, 2), (1, 4)):
                seq = flip(me, bit)
                source = piece(seq, shard, part)
                await_piece(there, source, near_recv.at[axis, shard, part])
                if part == axis:
                    start(there, send(source, source, on_send.at[1 - axis, shard], on_recv.at[1 - axis, shard], near[6 - bit]))
                to_side(there, 1 + axis, seq, shard, part, source)

    def far(way, distance):
        there, shard = shard_at(spot, way, distance, n)
        seq = flip(flip(me, 2), 4)
        for part in (0, 1):
            source = piece(seq, shard, part)
            await_piece(there, source, on_recv.at[1 - part, shard])
            to_side(there, 3, seq, shard, part, source)

    for step in range(n + 2):
        for task, delay in ((mine, 0), (nearby, 1), (far, 2)):
            distance = step - delay
            if 0 <= distance < n:
                for way in (0, 1) if distance else (0,):
                    task(way, distance)
    for shard in range(n):
        for part in (0, 1):
            for slot, bit in enumerate((0, 2, 4, 6)):
                seq = flip(me, 1)
                for one in (2, 4):
                    if bit & one:
                        seq = flip(seq, one)
                await_piece(spot >= 0, piece(seq, shard, part), side_recv.at[slot, shard, part])
    keep.wait()
    for condition, one in sends:

        @pl.when(condition)
        def _(one=one):
            one.wait_send()


def box_gather(own):
    n = lax.axis_size("tensor")
    rows, width = own.shape
    sem = pltpu.SemaphoreType.DMA
    out = pl.pallas_call(
        functools.partial(box_gather_kernel, n),
        out_shape=jax.ShapeDtypeStruct((8, n, rows, width), own.dtype),
        in_specs=[pl.BlockSpec(memory_space=pl.ANY)],
        out_specs=pl.BlockSpec(memory_space=pl.ANY),
        scratch_shapes=[sem]
        + [sem((2, n - 1, 2))] * 2
        + [sem((2, n, 2))] * 2
        + [sem((2, n))] * 2
        + [sem((4, n, 2))] * 2,
        compiler_params=pltpu.CompilerParams(collective_id=3, has_side_effects=True),
        cost_estimate=transfer(75),
        name="box_gather",
    )(own)
    return out.reshape(8 * n * rows, width)


def order_of(spot, n):
    table = [sorted(range(n), key=lambda s: -abs(s - j)) for j in range(n)]
    result = []
    for step in range(n):
        value = jnp.int32(table[0][step])
        for j in range(1, n):
            value = jnp.where(spot == j, table[j][step], value)
        result.append(value)
    return result


def box_steps(n, pieces, part_at, final, side, local, on, near, chain, local_sem, side_send, side_recv, on_send, on_recv, near_send, near_recv, z_send, z_recv):
    spot, sides = both_ways(n)
    me, close = box_devices()
    rows = side.shape[2]
    half = rows // 2
    bits = (6, 2, 4, 0)
    sends = []

    def seq_of(index, bit):
        for one in (2, 4):
            if bit & one:
                index = flip(index, one)
        return index

    def start(one, condition=None):
        sends.append((condition, one))
        if condition is None:
            one.start()
        else:

            @pl.when(condition)
            def _():
                one.start()

    def await_at(target, recv):
        send(target, target, side_send.at[0, 0], recv, close[1]).wait_recv()

    def loads(chip, shard):
        return pltpu.make_async_copy(
            part_at(seq_of(me, bits[chip]), shard), local.at[chip, shard], local_sem.at[chip, shard]
        )

    def merge(chip, shard):
        await_at(side.at[chip, shard], side_recv.at[chip, shard])
        loads(chip, shard).wait()
        add_into(side.at[chip, shard], local.at[chip, shard], rows)

    def begin():
        for shard, _ in pieces:
            for chip in range(4):
                start(
                    send(
                        part_at(seq_of(flip(me, 1), bits[chip]), shard),
                        side.at[chip, shard],
                        side_send.at[chip, shard],
                        side_recv.at[chip, shard],
                        close[1],
                    )
                )
                loads(chip, shard).start()

    def first(step):
        shard = pieces[step][0]
        merge(0, shard)
        for axis, bit in ((0, 2), (1, 4)):
            start(
                send(
                    side.at[0, shard, pl.ds(axis * half, half)],
                    on.at[axis, shard],
                    on_send.at[axis, shard],
                    on_recv.at[axis, shard],
                    close[bit],
                )
            )
        merge(1, shard)
        merge(2, shard)

    def second(step):
        shard = pieces[step][0]
        for axis, bit in ((0, 2), (1, 4)):
            other = 2 - axis
            await_at(on.at[axis, shard], on_recv.at[axis, shard])
            add_into(side.at[other, shard], on.at[axis, shard], half, axis * half, 0)
            start(
                send(
                    side.at[other, shard],
                    near.at[1 - axis, shard],
                    near_send.at[1 - axis, shard],
                    near_recv.at[1 - axis, shard],
                    close[6 - bit],
                )
            )
        merge(3, shard)

    def third(step):
        shard = pieces[step][0]
        for axis in (0, 1):
            await_at(near.at[axis, shard], near_recv.at[axis, shard])
            add_into(side.at[3, shard], near.at[axis, shard], rows)

    def fourth(step):
        shard, kind = pieces[step]
        if kind == "far":
            for way in (0, 1):
                ahead = shard > spot if way == 0 else shard < spot
                distance = jnp.clip(shard - spot if way == 0 else spot - shard, 1, n - 1)

                @pl.when(ahead & sides[1 - way][0])
                def _(way=way, distance=distance):
                    slot = jnp.minimum(distance, n - 2)
                    await_at(chain.at[way, slot], z_recv.at[way, slot])
                    add_into(side.at[3, shard], chain.at[way, slot], rows)

                start(
                    send(
                        side.at[3, shard],
                        chain.at[way, distance - 1],
                        z_send.at[way, distance - 1],
                        z_recv.at[way, distance - 1],
                        sides[way][1],
                    ),
                    ahead,
                )
            return
        out = final(step)

        def body(index, carry):
            at = pl.ds(pl.multiple_of(index * 16, 16), 16)
            out[at, :] = side[3, shard, at, :].astype(jnp.float32)
            return carry

        lax.fori_loop(0, rows // 16, body, 0)
        if kind == "own":
            for way in (0, 1):

                @pl.when(sides[1 - way][0])
                def _(way=way):
                    await_at(chain.at[way, 0], z_recv.at[way, 0])
                    add_into(out, chain.at[way, 0], rows)

    def drain():
        for condition, one in sends:
            if condition is None:
                one.wait_send()
            else:

                @pl.when(condition)
                def _(one=one):
                    one.wait_send()

    return begin, first, second, third, fourth, drain


def greet_box(n):
    _, sides = both_ways(n)
    _, close = box_devices()
    greet([close[1], close[2], close[4]], sides)


def box_scratch(n, pieces, rows, width, kind):
    sem = pltpu.SemaphoreType.DMA
    return [
        pltpu.VMEM((4, pieces, rows, width), kind),
        pltpu.VMEM((4, pieces, rows, width), kind),
        pltpu.VMEM((2, pieces, rows // 2, width), kind),
        pltpu.VMEM((2, pieces, rows, width), kind),
        pltpu.VMEM((2, n - 1, rows, width), kind),
        sem((4, pieces)),
        sem((4, pieces)),
        sem((4, pieces)),
        sem((2, pieces)),
        sem((2, pieces)),
        sem((2, pieces)),
        sem((2, pieces)),
        sem((2, n - 1)),
        sem((2, n - 1)),
    ]


def box_sum_kernel(n, passing, part, tokens, *refs):
    out, token_out = refs[passing : passing + 2]
    held, send_sem, recv_sem, *scratch = refs[2 * passing + 2 :]
    onward, finish, end = chain_steps(n, 4, tokens, token_out, held, send_sem, recv_sem)
    spot, _ = both_ways(n)
    greet_box(n)
    order = order_of(spot, n)
    pieces = [(shard, "far") for shard in order[:-1]] + [(order[-1], "own")]
    begin, *tasks, drain = box_steps(
        n, pieces, lambda seq, shard: part.at[seq, shard], lambda step: out, *scratch
    )
    begin()
    for step in range(n + 3):
        if step < n - 1:
            onward(n - 1 - step)
        for delay, task in enumerate(tasks):
            if 0 <= step - delay < n:
                task(step - delay)
    finish()
    end()
    drain()


def closing_kernel(n, tokens, part, _later, out, weights, _passed, *scratch):
    spot, _ = both_ways(n)
    greet_box(n)
    held, send_sem, recv_sem = scratch[:3]
    onward, finish, end = chain_steps(n, 4, tokens, out, held, send_sem, recv_sem)
    order = order_of(spot, n)
    flat = weights.shape[0] - 1
    pieces = [(shard, "far") for shard in order[:-1]]
    pieces += [(n + index, "flat") for index in range(flat)] + [(order[-1], "own")]
    targets = [None] * (n - 1) + [weights.at[1 + index] for index in range(flat)] + [weights.at[0]]
    begin, first, second, third, fourth, drain = box_steps(
        n, pieces, lambda seq, shard: part.at[shard, seq], lambda step: targets[step], *scratch[3:]
    )
    begin()
    onward(n - 1)
    count = len(pieces)
    far = n - 2
    for task in (first, second, third, fourth):
        for step in range(count):
            task(step)
        if far:
            onward(far)
            far -= 1
    for left in range(far, 0, -1):
        onward(left)
    finish()
    end()
    drain()


def closing(tokens, part, later):
    n = lax.axis_size("tensor")
    pieces, _, rows, width = part.shape
    sem = pltpu.SemaphoreType.DMA
    inside = pl.BlockSpec(memory_space=pltpu.VMEM)
    anywhere = pl.BlockSpec(memory_space=pl.ANY)
    return pl.pallas_call(
        functools.partial(closing_kernel, n),
        out_shape=[
            jax.ShapeDtypeStruct(tokens.shape[1:], jnp.float32),
            jax.ShapeDtypeStruct((pieces - n + 1, rows, width), jnp.float32),
            jax.ShapeDtypeStruct(later.shape, later.dtype),
        ],
        in_specs=[inside, anywhere, anywhere],
        out_specs=[inside, inside, anywhere],
        input_output_aliases={2: 2},
        scratch_shapes=[
            pltpu.VMEM((2, n - 1) + tokens.shape[1:], tokens.dtype),
            sem((2, n - 1, 4)),
            sem((2, n - 1, 4)),
        ]
        + box_scratch(n, pieces, rows, width, part.dtype),
        compiler_params=pltpu.CompilerParams(
            collective_id=8, has_side_effects=True, vmem_limit_bytes=VMEM
        ),
        cost_estimate=transfer(80),
        name="closing",
    )(tokens, part, later)


def swap_kernel(n, part, _later, out, _passed, local_sem, send_sem, recv_sem):
    spot = lax.axis_index("tensor")
    greet([{"tensor": lax.rem(spot + step, n)} for step in range(1, n)])
    keep = pltpu.make_async_copy(part.at[spot], out.at[spot], local_sem)
    keep.start()

    def copy(step):
        to = lax.rem(spot + step, n)
        return send(
            part.at[to], out.at[spot], send_sem.at[step], recv_sem.at[step], {"tensor": to}
        )

    for step in range(1, n):
        copy(step).start()
    keep.wait()
    for step in range(1, n):
        come = lax.rem(spot - step + n, n)
        send(
            part.at[come], out.at[come], send_sem.at[step], recv_sem.at[step], {"tensor": come}
        ).wait_recv()
        copy(step).wait_send()


def swap(part, later, number):
    n = lax.axis_size("tensor")
    sem = pltpu.SemaphoreType.DMA
    anywhere = pl.BlockSpec(memory_space=pl.ANY)
    return pl.pallas_call(
        functools.partial(swap_kernel, n),
        out_shape=[
            jax.ShapeDtypeStruct(part.shape, part.dtype),
            jax.ShapeDtypeStruct(later.shape, later.dtype),
        ],
        in_specs=[anywhere] * 2,
        out_specs=[anywhere] * 2,
        input_output_aliases={1: 1},
        scratch_shapes=[sem, sem((n,)), sem((n,))],
        compiler_params=pltpu.CompilerParams(
            collective_id=number, has_side_effects=True, vmem_limit_bytes=VMEM
        ),
        cost_estimate=transfer(25),
        name="swap",
    )(part, later)


def box_sum(part, tokens, later):
    n = lax.axis_size("tensor")
    width = part.shape[1]
    rows = part.shape[0] // (8 * n)
    kind = part.dtype
    anywhere = pl.BlockSpec(memory_space=pl.ANY)
    inside = pl.BlockSpec(memory_space=pltpu.VMEM)
    tokens = tokens.reshape(n, -1, width)
    sem = pltpu.SemaphoreType.DMA
    out, token_out, *later = pl.pallas_call(
        functools.partial(box_sum_kernel, n, len(later)),
        out_shape=[
            jax.ShapeDtypeStruct((rows, width), jnp.float32),
            jax.ShapeDtypeStruct(tokens.shape[1:], jnp.float32),
        ]
        + [jax.ShapeDtypeStruct(one.shape, one.dtype) for one in later],
        in_specs=[anywhere, inside] + [anywhere] * len(later),
        out_specs=[inside] * 2 + [anywhere] * len(later),
        input_output_aliases={2 + index: 2 + index for index in range(len(later))},
        scratch_shapes=[
            pltpu.VMEM((2, n - 1) + tokens.shape[1:], tokens.dtype),
            sem((2, n - 1, 4)),
            sem((2, n - 1, 4)),
        ]
        + box_scratch(n, n, rows, width, kind),
        compiler_params=pltpu.CompilerParams(
            collective_id=4, has_side_effects=True, vmem_limit_bytes=VMEM
        ),
        cost_estimate=transfer(90),
        name="box_sum",
    )(part.reshape(8, n, rows, width), tokens, *later)
    return out, token_out, later


def everyone(n):
    count = lax.axis_size("dp") * n
    me = lax.axis_index("dp") * n + lax.axis_index("tensor")

    def device(number):
        return {"dp": number // n, "tensor": number % n}

    return count, me, device


def greet_all(count, me, device):
    barrier = pltpu.get_barrier_semaphore()

    def signal(step, carry):
        pl.semaphore_signal(barrier, inc=1, device_id=device(lax.rem(me + step, count)), device_id_type=MESH)
        return carry

    lax.fori_loop(1, count, signal, 0)
    pl.semaphore_wait(barrier, count - 1)


def spread_start(n, own, out, send_sem, recv_sem):
    count, me, device = everyone(n)
    greet_all(count, me, device)
    out[me] = own[...]

    def copy(step):
        to = device(lax.rem(me + step, count))
        return send(own, out.at[me], send_sem.at[step], recv_sem.at[step], to)

    def go(step, carry):
        copy(step).start()
        return carry

    def end(step, carry):
        copy(step).wait_send()
        come = lax.rem(me - step + count, count)
        send(own, out.at[come], send_sem.at[step], recv_sem.at[step], device(come)).wait_recv()
        return carry

    lax.fori_loop(1, count, go, 0)
    return lambda: lax.fori_loop(1, count, end, 0)


def sum_spread_kernel(n, part, out, held, send_sem, recv_sem):
    count, me, device = everyone(n)
    greet_all(count, me, device)
    out[...] = part[me]

    def copy(step):
        to = lax.rem(me + step, count)
        return send(part.at[to], held.at[me], send_sem.at[step], recv_sem.at[step], device(to))

    def go(step, carry):
        copy(step).start()
        return carry

    def end(step, carry):
        come = lax.rem(me - step + count, count)
        send(part.at[0], held.at[come], send_sem.at[step], recv_sem.at[step], device(come)).wait_recv()
        out[...] += held[come]
        copy(step).wait_send()
        return carry

    lax.fori_loop(1, count, go, 0)
    lax.fori_loop(1, count, end, 0)


def sum_spread(part):
    n = lax.axis_size("tensor")
    count = lax.axis_size("dp") * n
    sem = pltpu.SemaphoreType.DMA
    return pl.pallas_call(
        functools.partial(sum_spread_kernel, n),
        out_shape=jax.ShapeDtypeStruct(part.shape[1:], part.dtype),
        in_specs=[pl.BlockSpec(memory_space=pltpu.VMEM)],
        out_specs=pl.BlockSpec(memory_space=pltpu.VMEM),
        scratch_shapes=[pltpu.VMEM(part.shape, part.dtype), sem((count,)), sem((count,))],
        compiler_params=pltpu.CompilerParams(
            collective_id=6, has_side_effects=True, vmem_limit_bytes=VMEM
        ),
        cost_estimate=transfer(20),
        name="sum_spread",
    )(part)


TB = 256
GR = 16
TILE = 256
EXTRA = 2 * E
def ceil_to(value, unit):
    return (value + unit - 1) // unit * unit


def nt_dot(a, b):
    return lax.dot_general(a, b, (((1,), (1,)), ((), ())), preferred_element_type=jnp.float32)


def tn_dot(a, b):
    return lax.dot_general(a, b, (((0,), (0,)), ((), ())), preferred_element_type=jnp.float32)


def nn_dot(a, b):
    return jnp.dot(a, b, preferred_element_type=jnp.float32)


def pair(value):
    high = value.astype(jnp.bfloat16)
    low = (value - high.astype(jnp.float32)).astype(jnp.bfloat16)
    return high, low


def unpair(value):
    value = value.astype(jnp.float32)
    return value[:, :E] + value[:, E:]


def excl_cumsum(value, axis):
    return jnp.cumsum(value, axis) - value


class Plan:
    def __init__(self, tokens, seq_len, local):
        seqs = tokens // seq_len
        self.tokens, self.local = tokens, local
        self.blocks = tokens // TB
        per_seq = seq_len // TB
        worst = min(CG + (GR - 1) * per_seq, seq_len)
        self.cap = ceil_to(seqs * worst // GR * GR, TILE)
        groups = (seqs * local * CG + self.blocks * local * (GR - 1)) // GR
        self.slots = ceil_to(TB * TOP * local // E + local * GR, 64)
        self.items = groups * GR // self.slots + self.blocks
        self.tiles = self.cap // TILE


def pick_at(here, table):
    return jnp.sum(jnp.where(here, table[None, :], 0), 1)


def steps_of(size, steps):
    first = excl_cumsum(steps, 0)
    used = jnp.sum(steps)
    index = jnp.minimum(jnp.arange(size), used - 1)
    owner = jnp.sum((first[None, :] <= index[:, None]).astype(jnp.int32), 1) - 1
    here = owner[:, None] == jnp.arange(steps.shape[0])[None, :]
    part = index - pick_at(here, first)
    last = (part == pick_at(here, steps) - 1).astype(jnp.int32)
    return first, used, owner, part, last, here


def routing(plan, routes, base):
    local, blocks = plan.local, plan.blocks
    mine = base + jnp.arange(local)
    picked = jnp.any(routes[:, :, None] == mine[None, None, :], 1)
    grid = picked.reshape(blocks, TB, local)
    ones = grid.astype(jnp.bfloat16)
    earlier = (jnp.arange(TB)[:, None] > jnp.arange(TB)[None, :]).astype(jnp.bfloat16)
    rank = jnp.einsum("ts,bse->bte", earlier, ones, preferred_element_type=jnp.float32).astype(
        jnp.int32
    )
    count = jnp.sum(grid.astype(jnp.int32), 1)
    groups = (count + GR - 1) // GR
    inner = excl_cumsum(groups, 1)
    total = jnp.sum(groups, 1)
    outer = excl_cumsum(groups, 0)
    expert_rows = jnp.sum(groups, 0) * GR
    place = jnp.where(grid, inner[:, None, :] * GR + rank, -1)
    items = jnp.maximum((total * GR + plan.slots - 1) // plan.slots, 1)
    first, used, block, part, last, here = steps_of(plan.items, items)
    wide, slots = plan.slots // GR, plan.cap // GR
    spot = jnp.arange(slots)[None, :, None]
    low = outer.T[:, None, :]
    inside = (spot >= low) & (spot < low + groups.T[:, None, :])
    origin = first[None, :] * wide + inner.T
    source = jnp.sum(jnp.where(inside, origin[:, None, :] + spot - low, 0), 2)
    tiles = jnp.maximum((expert_rows + TILE - 1) // TILE, 1)
    _, tiles_used, owner, tile, tile_last, _ = steps_of(local * plan.tiles, tiles)

    def at_block(table):
        return jnp.sum(jnp.where(here[:, :, None], table[None], 0), 1)[:, None, :]

    spot = (part[:, None] * wide + jnp.arange(wide)[None, :])[:, :, None]
    low, many, begin = at_block(inner), at_block(groups), at_block(outer)
    inside = (spot >= low) & (spot < low + many)
    target = jnp.sum(
        jnp.where(inside, (jnp.arange(local) * slots)[None, None, :] + begin + spot - low, 0), 2
    )
    return dict(
        place=place,
        used=used[None],
        block=block,
        part=part,
        last=last,
        source=source.reshape(-1),
        filled=expert_rows,
        tiles_used=tiles_used[None],
        owner=owner,
        tile=tile,
        tile_last=tile_last,
        target=target.reshape(-1),
    )


def while_used(step, used, *refs):
    @pl.when(pl.program_id(0) < used[0])
    def _():
        step(used, *refs)


def dispatch_step(used, block, part, post, grad, router, place, rows, share, held):
    step = pl.program_id(0)
    local = place.shape[1]
    slots = rows.shape[0]

    @pl.when(part[step] == 0)
    def _():
        portion = jax.nn.softmax(nn_dot(post[...], router[...]), -1)
        high, low = pair(portion)
        both = jnp.concatenate([high, low], 1)
        held[...] = both
        share[...] = both

    slot = lax.broadcasted_iota(jnp.int32, (slots, TB), 0) + part[step] * slots
    hit = slot == place[0, 0:1, :]
    for one in range(1, local):
        hit = hit | (slot == place[0, one : one + 1, :])
    pick = jnp.where(hit, 1.0, 0.0).astype(jnp.bfloat16)
    rows[:, :D] = nn_dot(pick, post[...]).astype(jnp.bfloat16)
    rows[:, D : 2 * D] = nn_dot(pick, grad[...]).astype(jnp.bfloat16)
    rows[:, 2 * D :] = nn_dot(pick, held[...]).astype(jnp.bfloat16)


def dispatch(plan, route, post, grad, router):
    wide = 2 * D + EXTRA
    place = route["place"].transpose(0, 2, 1)

    def at_block(step, used, block, part):
        return (block[step], 0)

    return pl.pallas_call(
        functools.partial(while_used, dispatch_step),
        grid_spec=pltpu.PrefetchScalarGridSpec(
            num_scalar_prefetch=3,
            grid=(plan.items,),
            in_specs=[
                pl.BlockSpec((TB, D), at_block),
                pl.BlockSpec((TB, D), at_block),
                pl.BlockSpec((D, E), lambda step, used, block, part: (0, 0)),
                pl.BlockSpec((1, plan.local, TB), lambda step, used, block, part: (block[step], 0, 0)),
            ],
            out_specs=[
                pl.BlockSpec((plan.slots, wide), lambda step, used, block, part: (jnp.minimum(step, used[0] - 1), 0)),
                pl.BlockSpec((TB, EXTRA), at_block),
            ],
            scratch_shapes=[pltpu.VMEM((TB, EXTRA), jnp.bfloat16)],
        ),
        out_shape=[
            jax.ShapeDtypeStruct((plan.items * plan.slots, wide), jnp.bfloat16),
            jax.ShapeDtypeStruct((plan.tokens, EXTRA), jnp.bfloat16),
        ],
        compiler_params=pltpu.CompilerParams(vmem_limit_bytes=VMEM),
        cost_estimate=transfer(45),
        name="dispatch",
    )(route["used"], route["block"], route["part"], post, grad, router, place)


def fetch_groups(table, rows, held, sems, step, count):
    slot = lax.rem(step, 2)
    for index in range(count):
        group = table[step * count + index]
        pltpu.make_async_copy(
            rows.at[pl.ds(pl.multiple_of(group * GR, GR), GR)],
            held.at[slot, pl.ds(index * GR, GR)],
            sems.at[slot],
        ).start()


def await_groups(rows, held, sems, step, count):
    slot = lax.rem(step, 2)
    pltpu.make_async_copy(rows.at[pl.ds(0, count * GR)], held.at[slot], sems.at[slot]).wait()


def next_groups(used, table, rows, held, sems, count):
    step = pl.program_id(0)

    @pl.when(step == 0)
    def _():
        fetch_groups(table, rows, held, sems, step, count)

    @pl.when(step + 1 < used[0])
    def _():
        fetch_groups(table, rows, held, sems, step + 1, count)

    await_groups(rows, held, sems, step, count)
    return lax.rem(step, 2)


def expert_step(
    used, source, owner, tile, last, filled, base, all_rows, w_gate, w_up, w_down, *refs
):
    *before, result, gate_out, up_out, down_out, held, sems, gate_sum, up_sum, down_sum = refs
    step = pl.program_id(0)
    count = TILE // GR
    slot = next_groups(used, source, all_rows, held, sems, count)
    expert, part = owner[step], tile[step]

    @pl.when(part == 0)
    def _():
        gate_sum[...] = jnp.zeros_like(gate_sum)
        up_sum[...] = jnp.zeros_like(up_sum)
        down_sum[...] = jnp.zeros_like(down_sum)

    @pl.when(last[step] == 1)
    def _():
        def clear(index, carry):
            at = pl.ds(pl.multiple_of(index * GR, GR), GR)
            held[slot, at, :] = jnp.zeros((GR, held.shape[2]), held.dtype)
            return carry

        lax.fori_loop((filled[expert] - part * TILE) // GR, count, clear, 0)

    number = base[0] + expert
    rows, upstream = held[slot, :, :D], held[slot, :, D : 2 * D]
    shares = held[slot, :, 2 * D :]
    lane = lax.broadcasted_iota(jnp.int32, (TILE, EXTRA), 1)
    own = (lane == number) | (lane == number + E)
    gate = jnp.sum(jnp.where(own, shares.astype(jnp.float32), 0.0), -1, keepdims=True)
    gate_pre = nn_dot(rows, w_gate[0])
    up_pre = nn_dot(rows, w_up[0])
    plain = nn_dot(upstream, w_down[0])
    squash = jax.nn.sigmoid(gate_pre)
    swish = gate_pre * squash
    active = (swish * up_pre).astype(jnp.bfloat16).astype(jnp.float32)
    change = jnp.sum(active * plain, -1, keepdims=True)
    grad_active = gate * plain
    grad_gate = (grad_active * up_pre * squash * (1.0 + gate_pre * (1.0 - squash))).astype(
        jnp.bfloat16
    )
    grad_up = (grad_active * swish).astype(jnp.bfloat16)
    scaled = (gate * active).astype(jnp.bfloat16)
    result[:, :D] = nt_dot(scaled, w_down[0]).astype(jnp.bfloat16)
    result[:, D : 2 * D] = (nt_dot(grad_gate, w_gate[0]) + nt_dot(grad_up, w_up[0])).astype(
        jnp.bfloat16
    )
    high, low = pair(change)
    result[:, 2 * D :] = jnp.where(
        lane == number,
        high.astype(jnp.float32),
        jnp.where(lane == number + E, low.astype(jnp.float32), 0.0),
    ).astype(jnp.bfloat16)
    gate_sum[...] += tn_dot(grad_gate, rows)
    up_sum[...] += tn_dot(grad_up, rows)
    down_sum[...] += tn_dot(scaled, upstream)

    @pl.when(last[step] == 1)
    def _():
        for index, (out, total) in enumerate(
            ((gate_out, gate_sum), (up_out, up_sum), (down_out, down_sum))
        ):
            out[0] = total[...].T + before[index][0] if before else total[...].T


def experts(plan, route, base, rows, w_gate, w_up, w_down, before):
    wide = 2 * D + EXTRA
    width = w_gate.shape[2]
    slots, count = plan.cap // GR, TILE // GR
    table = route["source"].reshape(plan.local * plan.tiles, count)
    number = route["owner"] * (slots // count) + route["tile"]
    table = table[number].reshape(-1)

    def whole(step, used, table, owner, tile, last, filled, base):
        return (owner[step], 0, 0)

    def tile_at(step, used, table, owner, tile, last, filled, base):
        return (owner[step] * plan.tiles + tile[step], 0)

    weight = pl.BlockSpec((1, D, width), whole)
    total = plan.local * plan.cap
    return pl.pallas_call(
        functools.partial(while_used, expert_step),
        grid_spec=pltpu.PrefetchScalarGridSpec(
            num_scalar_prefetch=7,
            grid=(plan.local * plan.tiles,),
            in_specs=[pl.BlockSpec(memory_space=pl.ANY)] + [weight] * (3 + len(before)),
            out_specs=[pl.BlockSpec((TILE, wide), tile_at)] + [weight] * 3,
            scratch_shapes=[
                pltpu.VMEM((2, TILE, wide), jnp.bfloat16),
                pltpu.SemaphoreType.DMA((2,)),
            ]
            + [pltpu.VMEM((width, D), jnp.float32)] * 3,
        ),
        out_shape=[jax.ShapeDtypeStruct((total, wide), jnp.bfloat16)]
        + [jax.ShapeDtypeStruct((plan.local, D, width), jnp.float32)] * 3,
        compiler_params=pltpu.CompilerParams(vmem_limit_bytes=VMEM),
        input_output_aliases={11 + index: 1 + index for index in range(len(before))},
        cost_estimate=transfer(80),
        name="experts",
    )(
        route["tiles_used"],
        table,
        route["owner"],
        route["tile"],
        route["tile_last"],
        route["filled"],
        base[None],
        rows,
        w_gate,
        w_up,
        w_down,
        *before,
    )


def combine_step(
    used, target, block, part, last, results, place, share, post, router, *refs
):
    held, sems, sums = refs[-3:]
    passing = (len(refs) - 6) // 2
    out, grad, router_out = refs[passing : passing + 3]
    step = pl.program_id(0)
    local = place.shape[1]
    slots = held.shape[1]

    at = next_groups(used, target, results, held, sems, slots // GR)

    @pl.when(step == 0)
    def _():
        router_out[...] = jnp.zeros_like(router_out)

    slot = lax.broadcasted_iota(jnp.int32, (TB, slots), 1) + part[step] * slots
    hit = slot == place[:, 0:1]
    for one in range(1, local):
        hit = hit | (slot == place[:, one : one + 1])
    pick = jnp.where(hit, 1.0, 0.0).astype(jnp.bfloat16)

    def term(begin, end):
        return nn_dot(pick, held[at, :, begin:end])

    def finish(value):
        change = unpair(value(2 * D, 2 * D + EXTRA))
        portion = unpair(share[...])
        moved = portion * (change - jnp.sum(change * portion, -1, keepdims=True))
        moved = moved.astype(jnp.bfloat16)
        out[...] = value(0, D).astype(jnp.bfloat16)
        grad[...] = (value(D, 2 * D) + nt_dot(moved, router[...])).astype(jnp.bfloat16)
        router_out[...] += tn_dot(moved, post[...])

    single = (part[step] == 0) & (last[step] == 1)

    @pl.when(single)
    def _():
        finish(term)

    @pl.when(jnp.logical_not(single))
    def _():
        @pl.when(part[step] == 0)
        def _():
            sums[...] = jnp.zeros_like(sums)

        sums[...] += term(0, 2 * D + EXTRA)

        @pl.when(last[step] == 1)
        def _():
            finish(lambda begin, end: sums[:, begin:end])


def combine(plan, route, results, share, post, router, later):
    wide = 2 * D + EXTRA

    def at_block(step, used, target, block, part, last):
        return (block[step], 0)

    def fixed(step, used, target, block, part, last):
        return (0, 0)

    return pl.pallas_call(
        functools.partial(while_used, combine_step),
        grid_spec=pltpu.PrefetchScalarGridSpec(
            num_scalar_prefetch=5,
            grid=(plan.items,),
            in_specs=[
                pl.BlockSpec(memory_space=pl.ANY),
                pl.BlockSpec((TB, plan.local), at_block),
                pl.BlockSpec((TB, EXTRA), at_block),
                pl.BlockSpec((TB, D), at_block),
                pl.BlockSpec((D, E), fixed),
            ]
            + [pl.BlockSpec(memory_space=pl.ANY)] * len(later),
            out_specs=[
                pl.BlockSpec((TB, D), at_block),
                pl.BlockSpec((TB, D), at_block),
                pl.BlockSpec((E, D), fixed),
            ]
            + [pl.BlockSpec(memory_space=pl.ANY)] * len(later),
            scratch_shapes=[
                pltpu.VMEM((2, plan.slots, wide), jnp.bfloat16),
                pltpu.SemaphoreType.DMA((2,)),
                pltpu.VMEM((TB, wide), jnp.float32),
            ],
        ),
        out_shape=[
            jax.ShapeDtypeStruct((plan.tokens, D), jnp.bfloat16),
            jax.ShapeDtypeStruct((plan.tokens, D), jnp.bfloat16),
            jax.ShapeDtypeStruct((E, D), jnp.float32),
        ]
        + [jax.ShapeDtypeStruct(one.shape, one.dtype) for one in later],
        input_output_aliases={10 + index: 3 + index for index in range(len(later))},
        compiler_params=pltpu.CompilerParams(vmem_limit_bytes=VMEM),
        cost_estimate=transfer(50),
        name="combine",
    )(
        route["used"],
        route["target"],
        route["block"],
        route["part"],
        route["last"],
        results,
        route["place"].reshape(plan.tokens, plan.local),
        share,
        post,
        router,
        *later,
    )


def gather_all(own):
    if lax.axis_size("dp") == 8:
        return box_gather(own)
    return lax.all_gather(
        lax.all_gather(own, "tensor", axis=0, tiled=True), "dp", axis=0, tiled=True
    )


def gather_slowly(own):
    if lax.axis_size("dp") == 8:
        return lax.all_gather(own, ("dp", "tensor"), axis=0, tiled=True)
    return gather_all(own)


def gather_output(own):
    n = lax.axis_size("tensor")
    if lax.axis_size("dp") == 8:
        everything = lax.all_gather(own, ("dp", "tensor"), axis=0, tiled=False)
        everything = everything.reshape((8, n) + own.shape).transpose(1, 0, 2, 3)
        return everything.reshape(n, -1, own.shape[1])
    part = lax.all_gather(own, "dp", axis=0, tiled=True)
    return lax.all_gather(part, "tensor", axis=0, tiled=False)


def sum_last(tokens, parts, later):
    n = lax.axis_size("tensor")
    if lax.axis_size("dp") == 8:
        return closing(
            tokens.reshape(n, -1, tokens.shape[1]),
            parts.reshape(parts.shape[0], 8, -1, parts.shape[2]),
            later,
        )
    tokens, later = chain_sum(tokens, later, 8)
    parts = lax.psum_scatter(parts, "dp", scatter_dimension=1, tiled=True)
    own = lax.psum_scatter(parts[:n], "tensor", scatter_dimension=0, tiled=True)
    return tokens, jnp.concatenate([own, parts[n:]]).astype(jnp.float32), later


def sum_all(part, tokens, later):
    if lax.axis_size("dp") == 8:
        return box_sum(part, tokens, later)
    tokens = lax.psum_scatter(tokens, "tensor", scatter_dimension=0, tiled=True)
    return sum_slowly(part).astype(jnp.float32), tokens.astype(jnp.float32), later


def sum_slowly(part):
    part = lax.psum_scatter(part, "dp", scatter_dimension=0, tiled=True)
    return lax.psum_scatter(part, "tensor", scatter_dimension=0, tiled=True)


def fill(value, rows, columns):
    return jnp.pad(value, ((0, rows - value.shape[0]), (0, columns - value.shape[1])))


def pack_small(router, prenorm, postnorm, querynorm, keynorm, routes):
    n = lax.axis_size("tensor")
    rank = lax.axis_index("tensor")
    rows = router.shape[0]
    head = ceil_to(max(rows, querynorm.shape[0]), 16)
    heads = querynorm.shape[1]
    block = jnp.concatenate(
        [
            fill(router, head, E),
            fill(prenorm[:, None], head, 1),
            fill(postnorm[:, None], head, 1),
            fill(querynorm, head, heads),
            fill(keynorm, head, heads),
        ],
        1,
    )
    part = routes.shape[0] // n
    own = lax.dynamic_slice_in_dim(routes, rank * part, part, 0)
    own = own.astype(jnp.bfloat16).reshape(-1, 128)
    tail = ceil_to(own.shape[0], 16)
    return jnp.concatenate([fill(block, head, 128), fill(own, tail, 128)], 0)


def unpack_small(everything, router, querynorm, routes):
    n = lax.axis_size("tensor")
    rank = lax.axis_index("tensor")
    rows, heads = router.shape[0], querynorm.shape[1]
    head = ceil_to(max(rows, querynorm.shape[0]), 16)
    part = routes.size // n // 128
    total = everything.shape[1]
    mine = everything.reshape(-1, n, total, 128)[:, rank]
    at = E + 2
    return (
        everything[:, :rows, :E].reshape(-1, E),
        everything[:, :rows, E].reshape(-1).astype(jnp.float32),
        everything[:, :rows, E + 1].reshape(-1).astype(jnp.float32),
        mine[:, : querynorm.shape[0], at : at + heads].reshape(-1, heads),
        mine[:, : querynorm.shape[0], at + heads : at + 2 * heads].reshape(-1, heads),
        everything[:, head : head + part].reshape(-1, TOP).astype(jnp.int32),
    )


def body(
    hidden_in,
    out_grad,
    doc_ids,
    expert_ids,
    prenorm,
    querynorm,
    keynorm,
    query_proj,
    key_proj,
    value_proj,
    output_proj,
    postnorm,
    router,
    gate_proj,
    up_proj,
    down_proj,
):
    residual = hidden_in[0].astype(jnp.float32)
    upstream = out_grad[0]
    documents = doc_ids[0]
    routes = expert_ids[0]
    shard = residual.shape[0]
    seq_len = documents.shape[0]
    mesh_dp = lax.axis_size("dp")
    block = min(seq_len, 1024)
    scale = HD ** (-0.5)
    cosine, sine = rope_tables(seq_len, HD)
    small = pack_small(router, prenorm, postnorm, querynorm, keynorm, routes)
    group_hidden, later, everything = chain_gather(
        hidden_in[0], upstream[: shard // 2], 1, small
    )
    router_full, pre_gain, post_gain, gain_query, gain_key, all_routes = unpack_small(
        everything, router, querynorm, routes
    )
    weights = lax.all_gather(
        jnp.concatenate([query_proj, key_proj, value_proj], 1),
        "dp",
        axis=0,
        tiled=True,
    )
    w_query, w_key, w_value = jnp.split(weights, 3, 1)
    w_output = gather_output(output_proj)
    heads = w_query.shape[1] // HD
    query_scale = gain_query.astype(jnp.float32).T.reshape(-1)
    key_scale = gain_key.astype(jnp.float32).T.reshape(-1)
    inv_pre = lax.rsqrt(jnp.mean(residual * residual, -1, keepdims=True) + epsilon)
    group_hidden = group_hidden.astype(jnp.float32)
    group_inv = lax.rsqrt(jnp.mean(group_hidden * group_hidden, -1, keepdims=True) + epsilon)
    group_normed = (group_hidden * group_inv * pre_gain).astype(jnp.bfloat16)
    n = lax.axis_size("tensor")
    few = shard // 2
    plan = Plan(mesh_dp * n * few, n * few, gate_proj.shape[0])
    base = (lax.axis_index("dp") * plan.local).astype(jnp.int32)
    all_routes = all_routes.reshape(mesh_dp, n, 2, few, TOP)
    route = [
        routing(plan, all_routes[:, :, index].reshape(-1, TOP), base) for index in range(2)
    ]
    all_grad = [gather_slowly(later)]
    query = jnp.dot(group_normed, w_query, preferred_element_type=jnp.float32)
    keys = jnp.dot(group_normed, w_key, preferred_element_type=jnp.float32)
    values = jnp.dot(group_normed, w_value, preferred_element_type=jnp.float32).astype(jnp.bfloat16)
    query_sq, key_sq = sum_heads(
        (jnp.sum(query * query, -1, keepdims=True), jnp.sum(keys * keys, -1, keepdims=True))
    )
    inv_query = lax.rsqrt(query_sq / D + epsilon)
    inv_key = lax.rsqrt(key_sq / D + epsilon)
    query_heads = (query * inv_query * query_scale).reshape(seq_len, heads, HD)
    key_heads = (keys * inv_key * key_scale).reshape(seq_len, heads, HD)
    query_rot = (query_heads * cosine[:, None] + rotate(query_heads) * sine[:, None]).astype(
        jnp.bfloat16
    )
    key_rot = (key_heads * cosine[:, None] + rotate(key_heads) * sine[:, None]).astype(jnp.bfloat16)
    value_heads = values.reshape(seq_len, heads, HD)
    mixed, logsum = attend_forward(query_rot, key_rot, value_heads, documents, block, scale)
    mixed_flat = mixed.reshape(seq_len, heads * HD)
    mixed_own, later = swap(mixed_flat.reshape(n, shard, heads * HD), upstream[few:], 7)
    all_grad.append(gather_slowly(later))
    attn_local = sum(nt_dot(mixed_own[index], w_output[index]) for index in range(n))
    middle = residual + attn_local
    inv_post = lax.rsqrt(jnp.mean(middle * middle, -1, keepdims=True) + epsilon)
    post_normed = (middle * inv_post * post_gain).astype(jnp.bfloat16)
    all_post = [gather_all(post_normed[:few]), gather_slowly(post_normed[few:])]
    grads, outs, backs, router_parts = [], [], [], []
    for index in range(2):
        rows, portion = dispatch(plan, route[index], all_post[index], all_grad[index], router_full)
        results, *grads = experts(
            plan, route[index], base, rows, gate_proj, up_proj, down_proj, grads
        )
        later = [all_post[1], all_grad[1]] if index == 0 else []
        out, back, router_part, *later = combine(
            plan, route[index], results, portion, all_post[index], router_full, later
        )
        if index == 0:
            all_post[1], all_grad[1] = later
        outs.append(out)
        backs.append(back)
        router_parts.append(router_part)
    gate_weight_grad, up_weight_grad, down_weight_grad = grads
    early = lax.psum_scatter(backs[0], "dp", scatter_dimension=0, tiled=True)
    late, early, outs = sum_all(backs[1], early, outs)
    grad_post = jnp.concatenate([early, late], 0)
    moe_local = jnp.concatenate([sum_slowly(out) for out in outs], 0)
    router_part = router_parts[0] + router_parts[1]
    router_part = router_part.T
    post_gain_part = jnp.sum(grad_post * middle * inv_post, 0)
    grad_middle = upstream.astype(jnp.float32) + norm_back(
        grad_post, middle, inv_post, post_gain, D
    )
    change = grad_middle.astype(jnp.bfloat16)
    grad_mixed, _ = swap(
        jnp.stack([nn_dot(change, w_output[index]).astype(jnp.bfloat16) for index in range(n)]),
        jnp.zeros((16, 128), jnp.bfloat16),
        2,
    )
    output_parts = [tn_dot(change, mixed_own[index]).astype(jnp.bfloat16) for index in range(n)]
    grad_query_rot, grad_key_rot, grad_value_heads = attend_backward(
        query_rot,
        key_rot,
        value_heads,
        documents,
        logsum,
        grad_mixed.reshape(seq_len, heads, HD),
        block,
        scale,
    )
    grad_query_flat = (
        grad_query_rot * cosine[:, None] + rotate_back(grad_query_rot * sine[:, None])
    ).reshape(seq_len, -1)
    grad_key_flat = (
        grad_key_rot * cosine[:, None] + rotate_back(grad_key_rot * sine[:, None])
    ).reshape(seq_len, -1)
    query_inner, key_inner = sum_heads(
        (
            jnp.sum(grad_query_flat * query_scale * query, -1, keepdims=True),
            jnp.sum(grad_key_flat * key_scale * keys, -1, keepdims=True),
        )
    )
    grad_query = (
        inv_query * query_scale * grad_query_flat - query * inv_query**3 * query_inner / D
    ).astype(jnp.bfloat16)
    grad_key = (inv_key * key_scale * grad_key_flat - keys * inv_key**3 * key_inner / D).astype(
        jnp.bfloat16
    )
    query_gain_part = jnp.sum(grad_query_flat * query * inv_query, 0).reshape(heads, HD).T
    key_gain_part = jnp.sum(grad_key_flat * keys * inv_key, 0).reshape(heads, HD).T
    grad_value = grad_value_heads.reshape(seq_len, -1).astype(jnp.bfloat16)
    query_part = lax.dot_general(
        group_normed, grad_query, (((0,), (0,)), ((), ())), preferred_element_type=jnp.float32
    )
    key_part = lax.dot_general(
        group_normed, grad_key, (((0,), (0,)), ((), ())), preferred_element_type=jnp.float32
    )
    value_part = lax.dot_general(
        group_normed, grad_value, (((0,), (0,)), ((), ())), preferred_element_type=jnp.float32
    )
    normed_term = lax.dot_general(
        grad_query, w_query, (((1,), (1,)), ((), ())), preferred_element_type=jnp.float32
    )
    normed_term = normed_term + lax.dot_general(
        grad_key, w_key, (((1,), (1,)), ((), ())), preferred_element_type=jnp.float32
    )
    normed_term = normed_term + lax.dot_general(
        grad_value, w_value, (((1,), (1,)), ((), ())), preferred_element_type=jnp.float32
    )
    grad_normed, weight_sums, middle = sum_last(
        normed_term.astype(jnp.bfloat16),
        jnp.stack(
            output_parts + [part.astype(jnp.bfloat16) for part in (query_part, key_part, value_part)]
        ),
        middle,
    )
    layer_out = (middle + moe_local.astype(jnp.float32)).astype(jnp.bfloat16)[None]
    pre_gain_part = jnp.sum(grad_normed * residual * inv_pre, 0)
    input_grad = (grad_middle + norm_back(grad_normed, residual, inv_pre, pre_gain, D)).astype(
        jnp.bfloat16
    )[None]
    gains = jnp.concatenate([query_gain_part, key_gain_part], 1).reshape(mesh_dp, 1, -1, 2 * heads)
    mine = jnp.arange(n)[None, :, None, None] == lax.axis_index("tensor")
    gains = jnp.pad(
        jnp.where(mine, gains, 0.0),
        ((0, 0), (0, 0), (0, max(router.shape[0] - HD // mesh_dp, 0)), (0, 0)),
    ).reshape(D, 2 * heads)
    small = jnp.concatenate(
        [
            router_part,
            pre_gain_part[:, None],
            post_gain_part[:, None],
            gains,
            jnp.zeros((D, 128 - E - 2 - 2 * heads), jnp.float32),
        ],
        1,
    )
    small = sum_spread(small.reshape(-1, router.shape[0], 128))
    gain_grads = small[: HD // mesh_dp, E + 2 : E + 2 + 2 * heads]
    return (
        layer_out,
        input_grad,
        small[:, E],
        gain_grads[:, :heads],
        gain_grads[:, heads : 2 * heads],
        weight_sums[1],
        weight_sums[2],
        weight_sums[3],
        weight_sums[0],
        small[:, E + 1],
        small[:, :E],
        gate_weight_grad,
        up_weight_grad,
        down_weight_grad,
    )


def solution(mesh):
    in_specs = (
        P("dp", "tensor", None),
        P("dp", "tensor", None),
        P("dp", None),
        P("dp", None, None),
        P(("dp", "tensor")),
        P("dp", "tensor"),
        P("dp", "tensor"),
        P("dp", "tensor"),
        P("dp", "tensor"),
        P("dp", "tensor"),
        P("dp", "tensor"),
        P(("dp", "tensor")),
        P(("dp", "tensor"), None),
        P("dp", None, "tensor"),
        P("dp", None, "tensor"),
        P("dp", None, "tensor"),
    )
    out_specs = (
        P("dp", "tensor", None),
        P("dp", "tensor", None),
        P(("dp", "tensor")),
        P("dp", "tensor"),
        P("dp", "tensor"),
        P("dp", "tensor"),
        P("dp", "tensor"),
        P("dp", "tensor"),
        P("dp", "tensor"),
        P(("dp", "tensor")),
        P(("dp", "tensor"), None),
        P("dp", None, "tensor"),
        P("dp", None, "tensor"),
        P("dp", None, "tensor"),
    )
    return jax.shard_map(body, mesh=mesh, in_specs=in_specs, out_specs=out_specs, check_vma=False)
```

```python
import functools

import jax
import jax.numpy as jnp
from jax import lax
from jax.experimental import pallas as pl
from jax.experimental.pallas import tpu as pltpu
from jax.sharding import PartitionSpec as P

D = 2048
HD = 128
E = 64
TOP = 8
CG = 192


epsilon = 1e-05
masked_score = -1000000000.0


def rope_tables(length, width):
    positions = jnp.arange(length).astype(jnp.float32)
    rates = 10000.0 ** (-jnp.arange(0, width, 2).astype(jnp.float32) / width)
    angles = positions[:, None] * rates[None, :]
    return (jnp.concatenate([jnp.cos(angles)] * 2, -1), jnp.concatenate([jnp.sin(angles)] * 2, -1))


def rotate(tensor):
    half = tensor.shape[-1] // 2
    return jnp.concatenate([-tensor[..., half:], tensor[..., :half]], -1)


def rotate_back(tensor):
    half = tensor.shape[-1] // 2
    return jnp.concatenate([tensor[..., half:], -tensor[..., :half]], -1)


def sum_heads(parts):
    return lax.psum((parts[0], parts[1]), "tensor")


def norm_back(grad, value, inverse, gain, width):
    scaled = grad * gain
    inner = jnp.sum(scaled * value, -1, keepdims=True)
    return inverse * scaled - value * inverse**3 * inner / width


def block_scores(query, keys, documents, start, block, scale):
    row_place = start + jnp.arange(block)
    col_place = jnp.arange(documents.shape[0])
    allowed = (documents[:, None] == documents[None, :]) & (
        row_place[:, None] >= col_place[None, :]
    )
    scores = jnp.einsum("qhd,khd->hqk", query, keys, preferred_element_type=jnp.float32) * scale
    return (jnp.where(allowed[None], scores, masked_score), query)


def attend_forward(query, keys, values, documents, block, scale):
    count = query.shape[0] // block

    def one(index):
        scores, rows = block_scores(query, keys, documents, index * block, block, scale)
        peak = jnp.max(scores, -1, keepdims=True)
        weights = jnp.exp(scores - peak)
        total = jnp.sum(weights, -1, keepdims=True)
        portion = (weights / total).astype(jnp.bfloat16)
        mixed = jnp.einsum("hqk,khd->qhd", portion, values, preferred_element_type=jnp.float32)
        return (mixed.astype(jnp.bfloat16), peak + jnp.log(total))

    mixed, logsum = lax.map(one, jnp.arange(count))
    return (mixed.reshape(query.shape), logsum)


def attend_backward(query, keys, values, documents, logsum, grad_mixed, block, scale):
    count = query.shape[0] // block

    def one(index):
        start = index * block
        scores, rows = block_scores(query, keys, documents, start, block, scale)
        portion = jnp.exp(scores - logsum[index])
        grad_portion = jnp.einsum(
            "qhd,khd->hqk", grad_mixed, values, preferred_element_type=jnp.float32
        )
        center = jnp.sum(portion * grad_portion, -1, keepdims=True)
        grad_scores = (portion * (grad_portion - center)).astype(jnp.bfloat16)
        grad_values = jnp.einsum(
            "hqk,qhd->khd",
            portion.astype(jnp.bfloat16),
            grad_mixed,
            preferred_element_type=jnp.float32,
        )
        grad_query = (
            jnp.einsum("hqk,khd->qhd", grad_scores, keys, preferred_element_type=jnp.float32)
            * scale
        )
        grad_keys = (
            jnp.einsum("hqk,qhd->khd", grad_scores, rows, preferred_element_type=jnp.float32)
            * scale
        )
        return (grad_query, grad_keys, grad_values)

    grad_query, grad_keys, grad_values = lax.map(one, jnp.arange(count))
    return (grad_query.reshape(query.shape), jnp.sum(grad_keys, 0), jnp.sum(grad_values, 0))


MESH = pl.DeviceIdType.MESH
VMEM = 60 * 1024 * 1024


def transfer(microseconds):
    return pl.CostEstimate(flops=0, bytes_accessed=microseconds * 3_000_000, transcendentals=0)


def flip(index, bit):
    return index + bit - 2 * bit * ((index // bit) % 2)


def send(source, target, send_sem, recv_sem, device):
    return pltpu.make_async_remote_copy(
        src_ref=source,
        dst_ref=target,
        send_sem=send_sem,
        recv_sem=recv_sem,
        device_id=device,
        device_id_type=MESH,
    )


def greet(devices, extra=()):
    barrier = pltpu.get_barrier_semaphore()
    for device in devices:
        pl.semaphore_signal(barrier, inc=1, device_id=device, device_id_type=MESH)
    for there, device in extra:

        @pl.when(there)
        def _(device=device):
            pl.semaphore_signal(barrier, inc=1, device_id=device, device_id_type=MESH)

    count = len(devices)
    for there, _ in extra:
        count = count + jnp.where(there, 1, 0)
    pl.semaphore_wait(barrier, count)


def both_ways(n):
    spot = lax.axis_index("tensor")
    return spot, (
        (spot < n - 1, {"tensor": jnp.minimum(spot + 1, n - 1)}),
        (spot > 0, {"tensor": jnp.maximum(spot - 1, 0)}),
    )


def shard_at(spot, way, distance, n):
    number = spot - distance if way == 0 else spot + distance
    return (number >= 0) & (number < n), jnp.clip(number, 0, n - 1)


def chain_gather_kernel(n, pieces, passing, own, *refs):
    refs = refs[passing:]
    if len(refs) > passing + 4:
        small, out, everything, *sems = refs[0], refs[1], refs[2 + passing], *refs[3 + passing :]
        local_sem, send_sem, recv_sem, all_send, all_recv = sems
        finish = spread_start(n, small, everything, all_send, all_recv)
    else:
        out, (local_sem, send_sem, recv_sem) = refs[0], refs[1 + passing :]
        finish = None
    spot, sides = both_ways(n)
    rows = own.shape[0] // pieces
    if finish is None:
        greet([], sides)
    keep = pltpu.make_async_copy(own, out.at[spot], local_sem)
    keep.start()

    def copy(way, distance, piece):
        there, number = shard_at(spot, way, distance, n)
        part = pl.ds(piece * rows, rows)
        source = own.at[part] if distance == 0 else out.at[number, part]
        return there & sides[way][0], send(
            source,
            out.at[number, part],
            send_sem.at[way, distance, piece],
            recv_sem.at[way, distance, piece],
            sides[way][1],
        )

    def arrived(way, distance, piece):
        there, number = shard_at(spot, way, distance, n)
        part = pl.ds(piece * rows, rows)

        @pl.when(there)
        def _():
            send(
                out.at[number, part],
                out.at[number, part],
                send_sem.at[way, distance - 1, piece],
                recv_sem.at[way, distance - 1, piece],
                sides[way][1],
            ).wait_recv()

    for distance in range(n):
        for piece in range(pieces):
            for way in (0, 1):
                if distance:
                    arrived(way, distance, piece)
                if distance < n - 1:
                    go, one = copy(way, distance, piece)

                    @pl.when(go)
                    def _(one=one):
                        one.start()

    keep.wait()
    for distance in range(n - 1):
        for piece in range(pieces):
            for way in (0, 1):
                go, one = copy(way, distance, piece)

                @pl.when(go)
                def _(one=one):
                    one.wait_send()

    if finish is not None:
        finish()


def chain_gather(own, later, number, small=None, pieces=4):
    n = lax.axis_size("tensor")
    rows, width = own.shape
    anywhere = pl.BlockSpec(memory_space=pl.ANY)
    inside = pl.BlockSpec(memory_space=pltpu.VMEM)
    sem = pltpu.SemaphoreType.DMA
    outs = [jax.ShapeDtypeStruct((n, rows, width), own.dtype)]
    outs += [jax.ShapeDtypeStruct(one.shape, one.dtype) for one in later]
    more, sems = [], []
    if small is not None:
        count = lax.axis_size("dp") * n
        outs.append(jax.ShapeDtypeStruct((count,) + small.shape, small.dtype))
        more, sems = [small], [sem((count,)), sem((count,))]
    plain = [anywhere] * (1 + len(later)) + [inside] * len(more)
    out, *rest = pl.pallas_call(
        functools.partial(chain_gather_kernel, n, pieces, len(later)),
        out_shape=outs,
        in_specs=plain,
        out_specs=plain,
        input_output_aliases={1 + index: 1 + index for index in range(len(later))},
        scratch_shapes=[sem, sem((2, n - 1, pieces)), sem((2, n - 1, pieces))] + sems,
        compiler_params=pltpu.CompilerParams(
            collective_id=number, has_side_effects=True, vmem_limit_bytes=VMEM
        ),
        cost_estimate=transfer(65),
        name="chain_gather",
    )(own, *later, *more)
    return (out.reshape(n * rows, width), *rest)


def add_into(target, source, rows, start=0, source_start=0):
    step = 16

    def body(index, carry):
        at = pl.ds(pl.multiple_of(start + index * step, step), step)
        come = pl.ds(pl.multiple_of(source_start + index * step, step), step)
        target[at, :] = (
            target[at, :].astype(jnp.float32) + source[come, :].astype(jnp.float32)
        ).astype(target.dtype)
        return carry

    lax.fori_loop(0, rows // step, body, 0)


def chain_sum_kernel(n, pieces, part, _later, out, _passed, held, send_sem, recv_sem):
    spot, sides = both_ways(n)
    greet([], sides)
    onward, finish, drain = chain_steps(n, pieces, part, out, held, send_sem, recv_sem)
    for far in range(n - 1, 0, -1):
        onward(far)
    finish()
    drain()


def chain_steps(n, pieces, part, out, held, send_sem, recv_sem):
    spot, sides = both_ways(n)
    rows = out.shape[0] // pieces

    def copy(way, far, piece, mine):
        number = spot + far if way == 0 else spot - far
        there = (number >= 0) & (number < n)
        number = jnp.clip(number, 0, n - 1)
        at = pl.ds(piece * rows, rows)
        source = part.at[number, at]
        return there, number, send(
            source if mine else held.at[way, far, at],
            held.at[way, far - 1, at],
            send_sem.at[way, far - 1, piece],
            recv_sem.at[way, far - 1, piece],
            sides[way][1],
        )

    def arrived(way, far, piece):
        at = pl.ds(piece * rows, rows)
        send(
            held.at[way, far, at],
            held.at[way, far, at],
            send_sem.at[way, far, piece],
            recv_sem.at[way, far, piece],
            sides[way][1],
        ).wait_recv()

    def onward(far):
        for piece in range(pieces):
            for way in (0, 1):
                behind = sides[1 - way][0]
                there, number, first = copy(way, far, piece, True)

                @pl.when(there & jnp.logical_not(behind))
                def _(first=first):
                    first.start()

                if far < n - 1:
                    _, _, again = copy(way, far, piece, False)

                    @pl.when(there & behind)
                    def _(way=way, piece=piece, number=number, again=again):
                        arrived(way, far, piece)
                        add_into(
                            held.at[way, far], part.at[number], rows, piece * rows, piece * rows
                        )
                        again.start()

    def finish():
        for piece in range(pieces):

            def body(index, carry, piece=piece):
                here = pl.ds(pl.multiple_of(piece * rows + index * 16, 16), 16)
                out[here, :] = part[spot, here, :].astype(jnp.float32)
                return carry

            lax.fori_loop(0, rows // 16, body, 0)
            for way in (0, 1):

                @pl.when(sides[1 - way][0])
                def _(way=way, piece=piece):
                    arrived(way, 0, piece)
                    add_into(out, held.at[way, 0], rows, piece * rows, piece * rows)

    def drain():
        for far in range(n - 1, 0, -1):
            for piece in range(pieces):
                for way in (0, 1):
                    there, _, one = copy(way, far, piece, True)

                    @pl.when(there)
                    def _(one=one):
                        one.wait_send()

    return onward, finish, drain


def chain_sum(part, later, number, pieces=4):
    n = lax.axis_size("tensor")
    width = part.shape[1]
    rows = part.shape[0] // n
    anywhere = pl.BlockSpec(memory_space=pl.ANY)
    inside = pl.BlockSpec(memory_space=pltpu.VMEM)
    return pl.pallas_call(
        functools.partial(chain_sum_kernel, n, pieces),
        out_shape=[
            jax.ShapeDtypeStruct((rows, width), jnp.float32),
            jax.ShapeDtypeStruct(later.shape, later.dtype),
        ],
        in_specs=[inside, anywhere],
        out_specs=[inside, anywhere],
        input_output_aliases={1: 1},
        scratch_shapes=[
            pltpu.VMEM((2, n - 1, rows, width), part.dtype),
            pltpu.SemaphoreType.DMA((2, n - 1, pieces)),
            pltpu.SemaphoreType.DMA((2, n - 1, pieces)),
        ],
        compiler_params=pltpu.CompilerParams(
            collective_id=number, has_side_effects=True, vmem_limit_bytes=VMEM
        ),
        cost_estimate=transfer(65),
        name="chain_sum",
    )(part.reshape(n, rows, width), later)


def box_devices():
    me = lax.axis_index("dp")
    return me, {bit: {"dp": flip(me, bit)} for bit in (1, 2, 4)}


def box_gather_kernel(n, own, out, local_sem, z_send, z_recv, near_send, near_recv, on_send, on_recv, side_send, side_recv):
    spot, sides = both_ways(n)
    me, near = box_devices()
    half = own.shape[0] // 2
    greet([near[1], near[2], near[4]], sides)
    keep = pltpu.make_async_copy(own, out.at[me, spot], local_sem)
    keep.start()
    sends = []

    def piece(seq, shard, part):
        return out.at[seq, shard, pl.ds(part * half, half)]

    def start(condition, one):
        sends.append((condition, one))

        @pl.when(condition)
        def _():
            one.start()

    def await_piece(condition, target, recv):
        @pl.when(condition)
        def _():
            send(target, target, side_send.at[0, 0, 0], recv, near[1]).wait_recv()

    def to_side(condition, slot, seq, shard, part, source):
        start(condition, send(source, piece(seq, shard, part), side_send.at[slot, shard, part], side_recv.at[slot, shard, part], near[1]))

    def mine(way, distance):
        there, shard = shard_at(spot, way, distance, n)
        for part in (0, 1):
            if distance:
                await_piece(there, piece(me, shard, part), z_recv.at[way, distance - 1, part])
            source = piece(me, shard, part) if distance else own.at[pl.ds(part * half, half)]
            for out_way in (0, 1) if distance == 0 else (way,):
                if distance < n - 1:
                    start(there & sides[out_way][0], send(source, piece(me, shard, part), z_send.at[out_way, distance, part], z_recv.at[out_way, distance, part], sides[out_way][1]))
            for axis, bit in ((0, 2), (1, 4)):
                start(there, send(source, piece(me, shard, part), near_send.at[axis, shard, part], near_recv.at[axis, shard, part], near[bit]))
            to_side(there, 0, me, shard, part, source)

    def nearby(way, distance):
        there, shard = shard_at(spot, way, distance, n)
        for part in (0, 1):
            for axis, bit in ((0, 2), (1, 4)):
                seq = flip(me, bit)
                source = piece(seq, shard, part)
                await_piece(there, source, near_recv.at[axis, shard, part])
                if part == axis:
                    start(there, send(source, source, on_send.at[1 - axis, shard], on_recv.at[1 - axis, shard], near[6 - bit]))
                to_side(there, 1 + axis, seq, shard, part, source)

    def far(way, distance):
        there, shard = shard_at(spot, way, distance, n)
        seq = flip(flip(me, 2), 4)
        for part in (0, 1):
            source = piece(seq, shard, part)
            await_piece(there, source, on_recv.at[1 - part, shard])
            to_side(there, 3, seq, shard, part, source)

    for step in range(n + 2):
        for task, delay in ((mine, 0), (nearby, 1), (far, 2)):
            distance = step - delay
            if 0 <= distance < n:
                for way in (0, 1) if distance else (0,):
                    task(way, distance)
    for shard in range(n):
        for part in (0, 1):
            for slot, bit in enumerate((0, 2, 4, 6)):
                seq = flip(me, 1)
                for one in (2, 4):
                    if bit & one:
                        seq = flip(seq, one)
                await_piece(spot >= 0, piece(seq, shard, part), side_recv.at[slot, shard, part])
    keep.wait()
    for condition, one in sends:

        @pl.when(condition)
        def _(one=one):
            one.wait_send()


def box_gather(own):
    n = lax.axis_size("tensor")
    rows, width = own.shape
    sem = pltpu.SemaphoreType.DMA
    out = pl.pallas_call(
        functools.partial(box_gather_kernel, n),
        out_shape=jax.ShapeDtypeStruct((8, n, rows, width), own.dtype),
        in_specs=[pl.BlockSpec(memory_space=pl.ANY)],
        out_specs=pl.BlockSpec(memory_space=pl.ANY),
        scratch_shapes=[sem]
        + [sem((2, n - 1, 2))] * 2
        + [sem((2, n, 2))] * 2
        + [sem((2, n))] * 2
        + [sem((4, n, 2))] * 2,
        compiler_params=pltpu.CompilerParams(collective_id=3, has_side_effects=True),
        cost_estimate=transfer(75),
        name="box_gather",
    )(own)
    return out.reshape(8 * n * rows, width)


def order_of(spot, n):
    table = [sorted(range(n), key=lambda s: -abs(s - j)) for j in range(n)]
    result = []
    for step in range(n):
        value = jnp.int32(table[0][step])
        for j in range(1, n):
            value = jnp.where(spot == j, table[j][step], value)
        result.append(value)
    return result


def box_steps(n, pieces, part_at, final, side, local, on, near, chain, local_sem, side_send, side_recv, on_send, on_recv, near_send, near_recv, z_send, z_recv):
    spot, sides = both_ways(n)
    me, close = box_devices()
    rows = side.shape[2]
    half = rows // 2
    bits = (6, 2, 4, 0)
    sends = []

    def seq_of(index, bit):
        for one in (2, 4):
            if bit & one:
                index = flip(index, one)
        return index

    def start(one, condition=None):
        sends.append((condition, one))
        if condition is None:
            one.start()
        else:

            @pl.when(condition)
            def _():
                one.start()

    def await_at(target, recv):
        send(target, target, side_send.at[0, 0], recv, close[1]).wait_recv()

    def loads(chip, shard):
        return pltpu.make_async_copy(
            part_at(seq_of(me, bits[chip]), shard), local.at[chip, shard], local_sem.at[chip, shard]
        )

    def merge(chip, shard):
        await_at(side.at[chip, shard], side_recv.at[chip, shard])
        loads(chip, shard).wait()
        add_into(side.at[chip, shard], local.at[chip, shard], rows)

    def begin():
        for shard, _ in pieces:
            for chip in range(4):
                start(
                    send(
                        part_at(seq_of(flip(me, 1), bits[chip]), shard),
                        side.at[chip, shard],
                        side_send.at[chip, shard],
                        side_recv.at[chip, shard],
                        close[1],
                    )
                )
                loads(chip, shard).start()

    def first(step):
        shard = pieces[step][0]
        merge(0, shard)
        for axis, bit in ((0, 2), (1, 4)):
            start(
                send(
                    side.at[0, shard, pl.ds(axis * half, half)],
                    on.at[axis, shard],
                    on_send.at[axis, shard],
                    on_recv.at[axis, shard],
                    close[bit],
                )
            )
        merge(1, shard)
        merge(2, shard)

    def second(step):
        shard = pieces[step][0]
        for axis, bit in ((0, 2), (1, 4)):
            other = 2 - axis
            await_at(on.at[axis, shard], on_recv.at[axis, shard])
            add_into(side.at[other, shard], on.at[axis, shard], half, axis * half, 0)
            start(
                send(
                    side.at[other, shard],
                    near.at[1 - axis, shard],
                    near_send.at[1 - axis, shard],
                    near_recv.at[1 - axis, shard],
                    close[6 - bit],
                )
            )
        merge(3, shard)

    def third(step):
        shard = pieces[step][0]
        for axis in (0, 1):
            await_at(near.at[axis, shard], near_recv.at[axis, shard])
            add_into(side.at[3, shard], near.at[axis, shard], rows)

    def fourth(step):
        shard, kind = pieces[step]
        if kind == "far":
            for way in (0, 1):
                ahead = shard > spot if way == 0 else shard < spot
                distance = jnp.clip(shard - spot if way == 0 else spot - shard, 1, n - 1)

                @pl.when(ahead & sides[1 - way][0])
                def _(way=way, distance=distance):
                    slot = jnp.minimum(distance, n - 2)
                    await_at(chain.at[way, slot], z_recv.at[way, slot])
                    add_into(side.at[3, shard], chain.at[way, slot], rows)

                start(
                    send(
                        side.at[3, shard],
                        chain.at[way, distance - 1],
                        z_send.at[way, distance - 1],
                        z_recv.at[way, distance - 1],
                        sides[way][1],
                    ),
                    ahead,
                )
            return
        out = final(step)

        def body(index, carry):
            at = pl.ds(pl.multiple_of(index * 16, 16), 16)
            out[at, :] = side[3, shard, at, :].astype(jnp.float32)
            return carry

        lax.fori_loop(0, rows // 16, body, 0)
        if kind == "own":
            for way in (0, 1):

                @pl.when(sides[1 - way][0])
                def _(way=way):
                    await_at(chain.at[way, 0], z_recv.at[way, 0])
                    add_into(out, chain.at[way, 0], rows)

    def drain():
        for condition, one in sends:
            if condition is None:
                one.wait_send()
            else:

                @pl.when(condition)
                def _(one=one):
                    one.wait_send()

    return begin, first, second, third, fourth, drain


def greet_box(n):
    _, sides = both_ways(n)
    _, close = box_devices()
    greet([close[1], close[2], close[4]], sides)


def box_scratch(n, pieces, rows, width, kind):
    sem = pltpu.SemaphoreType.DMA
    return [
        pltpu.VMEM((4, pieces, rows, width), kind),
        pltpu.VMEM((4, pieces, rows, width), kind),
        pltpu.VMEM((2, pieces, rows // 2, width), kind),
        pltpu.VMEM((2, pieces, rows, width), kind),
        pltpu.VMEM((2, n - 1, rows, width), kind),
        sem((4, pieces)),
        sem((4, pieces)),
        sem((4, pieces)),
        sem((2, pieces)),
        sem((2, pieces)),
        sem((2, pieces)),
        sem((2, pieces)),
        sem((2, n - 1)),
        sem((2, n - 1)),
    ]


def box_sum_kernel(n, passing, part, tokens, *refs):
    out, token_out = refs[passing : passing + 2]
    held, send_sem, recv_sem, *scratch = refs[2 * passing + 2 :]
    onward, finish, end = chain_steps(n, 4, tokens, token_out, held, send_sem, recv_sem)
    spot, _ = both_ways(n)
    greet_box(n)
    order = order_of(spot, n)
    pieces = [(shard, "far") for shard in order[:-1]] + [(order[-1], "own")]
    begin, *tasks, drain = box_steps(
        n, pieces, lambda seq, shard: part.at[seq, shard], lambda step: out, *scratch
    )
    begin()
    for step in range(n + 3):
        if step < n - 1:
            onward(n - 1 - step)
        for delay, task in enumerate(tasks):
            if 0 <= step - delay < n:
                task(step - delay)
    finish()
    end()
    drain()


def closing_kernel(n, tokens, part, _later, out, weights, _passed, *scratch):
    spot, _ = both_ways(n)
    greet_box(n)
    held, send_sem, recv_sem = scratch[:3]
    onward, finish, end = chain_steps(n, 4, tokens, out, held, send_sem, recv_sem)
    order = order_of(spot, n)
    flat = weights.shape[0] - 1
    pieces = [(shard, "far") for shard in order[:-1]]
    pieces += [(n + index, "flat") for index in range(flat)] + [(order[-1], "own")]
    targets = [None] * (n - 1) + [weights.at[1 + index] for index in range(flat)] + [weights.at[0]]
    begin, first, second, third, fourth, drain = box_steps(
        n, pieces, lambda seq, shard: part.at[shard, seq], lambda step: targets[step], *scratch[3:]
    )
    begin()
    onward(n - 1)
    count = len(pieces)
    far = n - 2
    for task in (first, second, third, fourth):
        for step in range(count):
            task(step)
        if far:
            onward(far)
            far -= 1
    for left in range(far, 0, -1):
        onward(left)
    finish()
    end()
    drain()


def closing(tokens, part, later):
    n = lax.axis_size("tensor")
    pieces, _, rows, width = part.shape
    sem = pltpu.SemaphoreType.DMA
    inside = pl.BlockSpec(memory_space=pltpu.VMEM)
    anywhere = pl.BlockSpec(memory_space=pl.ANY)
    return pl.pallas_call(
        functools.partial(closing_kernel, n),
        out_shape=[
            jax.ShapeDtypeStruct(tokens.shape[1:], jnp.float32),
            jax.ShapeDtypeStruct((pieces - n + 1, rows, width), jnp.float32),
            jax.ShapeDtypeStruct(later.shape, later.dtype),
        ],
        in_specs=[inside, anywhere, anywhere],
        out_specs=[inside, inside, anywhere],
        input_output_aliases={2: 2},
        scratch_shapes=[
            pltpu.VMEM((2, n - 1) + tokens.shape[1:], tokens.dtype),
            sem((2, n - 1, 4)),
            sem((2, n - 1, 4)),
        ]
        + box_scratch(n, pieces, rows, width, part.dtype),
        compiler_params=pltpu.CompilerParams(
            collective_id=8, has_side_effects=True, vmem_limit_bytes=VMEM
        ),
        cost_estimate=transfer(80),
        name="closing",
    )(tokens, part, later)


def swap_kernel(n, part, _later, out, _passed, local_sem, send_sem, recv_sem):
    spot = lax.axis_index("tensor")
    greet([{"tensor": lax.rem(spot + step, n)} for step in range(1, n)])
    keep = pltpu.make_async_copy(part.at[spot], out.at[spot], local_sem)
    keep.start()

    def copy(step):
        to = lax.rem(spot + step, n)
        return send(
            part.at[to], out.at[spot], send_sem.at[step], recv_sem.at[step], {"tensor": to}
        )

    for step in range(1, n):
        copy(step).start()
    keep.wait()
    for step in range(1, n):
        come = lax.rem(spot - step + n, n)
        send(
            part.at[come], out.at[come], send_sem.at[step], recv_sem.at[step], {"tensor": come}
        ).wait_recv()
        copy(step).wait_send()


def swap(part, later, number):
    n = lax.axis_size("tensor")
    sem = pltpu.SemaphoreType.DMA
    anywhere = pl.BlockSpec(memory_space=pl.ANY)
    return pl.pallas_call(
        functools.partial(swap_kernel, n),
        out_shape=[
            jax.ShapeDtypeStruct(part.shape, part.dtype),
            jax.ShapeDtypeStruct(later.shape, later.dtype),
        ],
        in_specs=[anywhere] * 2,
        out_specs=[anywhere] * 2,
        input_output_aliases={1: 1},
        scratch_shapes=[sem, sem((n,)), sem((n,))],
        compiler_params=pltpu.CompilerParams(
            collective_id=number, has_side_effects=True, vmem_limit_bytes=VMEM
        ),
        cost_estimate=transfer(25),
        name="swap",
    )(part, later)


def box_sum(part, tokens, later):
    n = lax.axis_size("tensor")
    width = part.shape[1]
    rows = part.shape[0] // (8 * n)
    kind = part.dtype
    anywhere = pl.BlockSpec(memory_space=pl.ANY)
    inside = pl.BlockSpec(memory_space=pltpu.VMEM)
    tokens = tokens.reshape(n, -1, width)
    sem = pltpu.SemaphoreType.DMA
    out, token_out, *later = pl.pallas_call(
        functools.partial(box_sum_kernel, n, len(later)),
        out_shape=[
            jax.ShapeDtypeStruct((rows, width), jnp.float32),
            jax.ShapeDtypeStruct(tokens.shape[1:], jnp.float32),
        ]
        + [jax.ShapeDtypeStruct(one.shape, one.dtype) for one in later],
        in_specs=[anywhere, inside] + [anywhere] * len(later),
        out_specs=[inside] * 2 + [anywhere] * len(later),
        input_output_aliases={2 + index: 2 + index for index in range(len(later))},
        scratch_shapes=[
            pltpu.VMEM((2, n - 1) + tokens.shape[1:], tokens.dtype),
            sem((2, n - 1, 4)),
            sem((2, n - 1, 4)),
        ]
        + box_scratch(n, n, rows, width, kind),
        compiler_params=pltpu.CompilerParams(
            collective_id=4, has_side_effects=True, vmem_limit_bytes=VMEM
        ),
        cost_estimate=transfer(90),
        name="box_sum",
    )(part.reshape(8, n, rows, width), tokens, *later)
    return out, token_out, later


def everyone(n):
    count = lax.axis_size("dp") * n
    me = lax.axis_index("dp") * n + lax.axis_index("tensor")

    def device(number):
        return {"dp": number // n, "tensor": number % n}

    return count, me, device


def greet_all(count, me, device):
    barrier = pltpu.get_barrier_semaphore()

    def signal(step, carry):
        pl.semaphore_signal(barrier, inc=1, device_id=device(lax.rem(me + step, count)), device_id_type=MESH)
        return carry

    lax.fori_loop(1, count, signal, 0)
    pl.semaphore_wait(barrier, count - 1)


def spread_start(n, own, out, send_sem, recv_sem):
    count, me, device = everyone(n)
    greet_all(count, me, device)
    out[me] = own[...]

    def copy(step):
        to = device(lax.rem(me + step, count))
        return send(own, out.at[me], send_sem.at[step], recv_sem.at[step], to)

    def go(step, carry):
        copy(step).start()
        return carry

    def end(step, carry):
        copy(step).wait_send()
        come = lax.rem(me - step + count, count)
        send(own, out.at[come], send_sem.at[step], recv_sem.at[step], device(come)).wait_recv()
        return carry

    lax.fori_loop(1, count, go, 0)
    return lambda: lax.fori_loop(1, count, end, 0)


def sum_spread_kernel(n, part, out, held, send_sem, recv_sem):
    count, me, device = everyone(n)
    greet_all(count, me, device)
    out[...] = part[me]

    def copy(step):
        to = lax.rem(me + step, count)
        return send(part.at[to], held.at[me], send_sem.at[step], recv_sem.at[step], device(to))

    def go(step, carry):
        copy(step).start()
        return carry

    def end(step, carry):
        come = lax.rem(me - step + count, count)
        send(part.at[0], held.at[come], send_sem.at[step], recv_sem.at[step], device(come)).wait_recv()
        out[...] += held[come]
        copy(step).wait_send()
        return carry

    lax.fori_loop(1, count, go, 0)
    lax.fori_loop(1, count, end, 0)


def sum_spread(part):
    n = lax.axis_size("tensor")
    count = lax.axis_size("dp") * n
    sem = pltpu.SemaphoreType.DMA
    return pl.pallas_call(
        functools.partial(sum_spread_kernel, n),
        out_shape=jax.ShapeDtypeStruct(part.shape[1:], part.dtype),
        in_specs=[pl.BlockSpec(memory_space=pltpu.VMEM)],
        out_specs=pl.BlockSpec(memory_space=pltpu.VMEM),
        scratch_shapes=[pltpu.VMEM(part.shape, part.dtype), sem((count,)), sem((count,))],
        compiler_params=pltpu.CompilerParams(
            collective_id=6, has_side_effects=True, vmem_limit_bytes=VMEM
        ),
        cost_estimate=transfer(20),
        name="sum_spread",
    )(part)


TB = 256
GR = 16
TILE = 256
EXTRA = 2 * E
def ceil_to(value, unit):
    return (value + unit - 1) // unit * unit


def nt_dot(a, b):
    return lax.dot_general(a, b, (((1,), (1,)), ((), ())), preferred_element_type=jnp.float32)


def tn_dot(a, b):
    return lax.dot_general(a, b, (((0,), (0,)), ((), ())), preferred_element_type=jnp.float32)


def nn_dot(a, b):
    return jnp.dot(a, b, preferred_element_type=jnp.float32)


def pair(value):
    high = value.astype(jnp.bfloat16)
    low = (value - high.astype(jnp.float32)).astype(jnp.bfloat16)
    return high, low


def unpair(value):
    value = value.astype(jnp.float32)
    return value[:, :E] + value[:, E:]


def excl_cumsum(value, axis):
    return jnp.cumsum(value, axis) - value


class Plan:
    def __init__(self, tokens, seq_len, local):
        seqs = tokens // seq_len
        self.tokens, self.local = tokens, local
        self.blocks = tokens // TB
        per_seq = seq_len // TB
        worst = min(CG + (GR - 1) * per_seq, seq_len)
        self.cap = ceil_to(seqs * worst // GR * GR, TILE)
        groups = (seqs * local * CG + self.blocks * local * (GR - 1)) // GR
        self.slots = ceil_to(TB * TOP * local // E + local * GR, 64)
        self.items = groups * GR // self.slots + self.blocks
        self.tiles = self.cap // TILE


def pick_at(here, table):
    return jnp.sum(jnp.where(here, table[None, :], 0), 1)


def steps_of(size, steps):
    first = excl_cumsum(steps, 0)
    used = jnp.sum(steps)
    index = jnp.minimum(jnp.arange(size), used - 1)
    owner = jnp.sum((first[None, :] <= index[:, None]).astype(jnp.int32), 1) - 1
    here = owner[:, None] == jnp.arange(steps.shape[0])[None, :]
    part = index - pick_at(here, first)
    last = (part == pick_at(here, steps) - 1).astype(jnp.int32)
    return first, used, owner, part, last, here


def routing(plan, routes, base):
    local, blocks = plan.local, plan.blocks
    mine = base + jnp.arange(local)
    picked = jnp.any(routes[:, :, None] == mine[None, None, :], 1)
    grid = picked.reshape(blocks, TB, local)
    ones = grid.astype(jnp.bfloat16)
    earlier = (jnp.arange(TB)[:, None] > jnp.arange(TB)[None, :]).astype(jnp.bfloat16)
    rank = jnp.einsum("ts,bse->bte", earlier, ones, preferred_element_type=jnp.float32).astype(
        jnp.int32
    )
    count = jnp.sum(grid.astype(jnp.int32), 1)
    groups = (count + GR - 1) // GR
    inner = excl_cumsum(groups, 1)
    total = jnp.sum(groups, 1)
    outer = excl_cumsum(groups, 0)
    expert_rows = jnp.sum(groups, 0) * GR
    place = jnp.where(grid, inner[:, None, :] * GR + rank, -1)
    items = jnp.maximum((total * GR + plan.slots - 1) // plan.slots, 1)
    first, used, block, part, last, here = steps_of(plan.items, items)
    wide, slots = plan.slots // GR, plan.cap // GR
    spot = jnp.arange(slots)[None, :, None]
    low = outer.T[:, None, :]
    inside = (spot >= low) & (spot < low + groups.T[:, None, :])
    origin = first[None, :] * wide + inner.T
    source = jnp.sum(jnp.where(inside, origin[:, None, :] + spot - low, 0), 2)
    tiles = jnp.maximum((expert_rows + TILE - 1) // TILE, 1)
    _, tiles_used, owner, tile, tile_last, _ = steps_of(local * plan.tiles, tiles)

    def at_block(table):
        return jnp.sum(jnp.where(here[:, :, None], table[None], 0), 1)[:, None, :]

    spot = (part[:, None] * wide + jnp.arange(wide)[None, :])[:, :, None]
    low, many, begin = at_block(inner), at_block(groups), at_block(outer)
    inside = (spot >= low) & (spot < low + many)
    target = jnp.sum(
        jnp.where(inside, (jnp.arange(local) * slots)[None, None, :] + begin + spot - low, 0), 2
    )
    return dict(
        place=place,
        used=used[None],
        block=block,
        part=part,
        last=last,
        source=source.reshape(-1),
        filled=expert_rows,
        tiles_used=tiles_used[None],
        owner=owner,
        tile=tile,
        tile_last=tile_last,
        target=target.reshape(-1),
    )


def while_used(step, used, *refs):
    @pl.when(pl.program_id(0) < used[0])
    def _():
        step(used, *refs)


def dispatch_step(used, block, part, post, grad, router, place, *refs):
    rows, share, held = refs[len(refs) // 2 - 1], refs[len(refs) // 2], refs[-1]
    step = pl.program_id(0)
    local = place.shape[1]
    slots = rows.shape[0]

    @pl.when(part[step] == 0)
    def _():
        portion = jax.nn.softmax(nn_dot(post[...], router[...]), -1)
        high, low = pair(portion)
        both = jnp.concatenate([high, low], 1)
        held[...] = both
        share[...] = both

    slot = lax.broadcasted_iota(jnp.int32, (slots, TB), 0) + part[step] * slots
    hit = slot == place[0, 0:1, :]
    for one in range(1, local):
        hit = hit | (slot == place[0, one : one + 1, :])
    pick = jnp.where(hit, 1.0, 0.0).astype(jnp.bfloat16)
    rows[:, :D] = nn_dot(pick, post[...]).astype(jnp.bfloat16)
    rows[:, D : 2 * D] = nn_dot(pick, grad[...]).astype(jnp.bfloat16)
    rows[:, 2 * D :] = nn_dot(pick, held[...]).astype(jnp.bfloat16)


def dispatch(plan, route, post, grad, router, later):
    wide = 2 * D + EXTRA
    place = route["place"].transpose(0, 2, 1)

    def at_block(step, used, block, part):
        return (block[step], 0)

    return pl.pallas_call(
        functools.partial(while_used, dispatch_step),
        grid_spec=pltpu.PrefetchScalarGridSpec(
            num_scalar_prefetch=3,
            grid=(plan.items,),
            in_specs=[
                pl.BlockSpec((TB, D), at_block),
                pl.BlockSpec((TB, D), at_block),
                pl.BlockSpec((D, E), lambda step, used, block, part: (0, 0)),
                pl.BlockSpec((1, plan.local, TB), lambda step, used, block, part: (block[step], 0, 0)),
            ]
            + [pl.BlockSpec(memory_space=pl.ANY)] * len(later),
            out_specs=[
                pl.BlockSpec((plan.slots, wide), lambda step, used, block, part: (jnp.minimum(step, used[0] - 1), 0)),
                pl.BlockSpec((TB, EXTRA), at_block),
            ]
            + [pl.BlockSpec(memory_space=pl.ANY)] * len(later),
            scratch_shapes=[pltpu.VMEM((TB, EXTRA), jnp.bfloat16)],
        ),
        out_shape=[
            jax.ShapeDtypeStruct((plan.items * plan.slots, wide), jnp.bfloat16),
            jax.ShapeDtypeStruct((plan.tokens, EXTRA), jnp.bfloat16),
        ]
        + [jax.ShapeDtypeStruct(one.shape, one.dtype) for one in later],
        input_output_aliases={7 + index: 2 + index for index in range(len(later))},
        compiler_params=pltpu.CompilerParams(vmem_limit_bytes=VMEM),
        cost_estimate=transfer(45),
        name="dispatch",
    )(route["used"], route["block"], route["part"], post, grad, router, place, *later)


def fetch_groups(table, rows, held, sems, step, count):
    slot = lax.rem(step, 2)
    for index in range(count):
        group = table[step * count + index]
        pltpu.make_async_copy(
            rows.at[pl.ds(pl.multiple_of(group * GR, GR), GR)],
            held.at[slot, pl.ds(index * GR, GR)],
            sems.at[slot],
        ).start()


def await_groups(rows, held, sems, step, count):
    slot = lax.rem(step, 2)
    pltpu.make_async_copy(rows.at[pl.ds(0, count * GR)], held.at[slot], sems.at[slot]).wait()


def next_groups(used, table, rows, held, sems, count):
    step = pl.program_id(0)

    @pl.when(step == 0)
    def _():
        fetch_groups(table, rows, held, sems, step, count)

    @pl.when(step + 1 < used[0])
    def _():
        fetch_groups(table, rows, held, sems, step + 1, count)

    await_groups(rows, held, sems, step, count)
    return lax.rem(step, 2)


def expert_step(
    used, source, owner, tile, last, filled, base, all_rows, w_gate, w_up, w_down, *refs
):
    *before, result, gate_out, up_out, down_out, held, sems, gate_sum, up_sum, down_sum = refs
    step = pl.program_id(0)
    count = TILE // GR
    slot = next_groups(used, source, all_rows, held, sems, count)
    expert, part = owner[step], tile[step]

    @pl.when(part == 0)
    def _():
        gate_sum[...] = jnp.zeros_like(gate_sum)
        up_sum[...] = jnp.zeros_like(up_sum)
        down_sum[...] = jnp.zeros_like(down_sum)

    @pl.when(last[step] == 1)
    def _():
        def clear(index, carry):
            at = pl.ds(pl.multiple_of(index * GR, GR), GR)
            held[slot, at, :] = jnp.zeros((GR, held.shape[2]), held.dtype)
            return carry

        lax.fori_loop((filled[expert] - part * TILE) // GR, count, clear, 0)

    number = base[0] + expert
    rows, upstream = held[slot, :, :D], held[slot, :, D : 2 * D]
    shares = held[slot, :, 2 * D :]
    lane = lax.broadcasted_iota(jnp.int32, (TILE, EXTRA), 1)
    own = (lane == number) | (lane == number + E)
    gate = jnp.sum(jnp.where(own, shares.astype(jnp.float32), 0.0), -1, keepdims=True)
    gate_pre = nn_dot(rows, w_gate[0])
    up_pre = nn_dot(rows, w_up[0])
    plain = nn_dot(upstream, w_down[0])
    squash = jax.nn.sigmoid(gate_pre)
    swish = gate_pre * squash
    active = (swish * up_pre).astype(jnp.bfloat16).astype(jnp.float32)
    change = jnp.sum(active * plain, -1, keepdims=True)
    grad_active = gate * plain
    grad_gate = (grad_active * up_pre * squash * (1.0 + gate_pre * (1.0 - squash))).astype(
        jnp.bfloat16
    )
    grad_up = (grad_active * swish).astype(jnp.bfloat16)
    scaled = (gate * active).astype(jnp.bfloat16)
    result[:, :D] = nt_dot(scaled, w_down[0]).astype(jnp.bfloat16)
    result[:, D : 2 * D] = (nt_dot(grad_gate, w_gate[0]) + nt_dot(grad_up, w_up[0])).astype(
        jnp.bfloat16
    )
    high, low = pair(change)
    result[:, 2 * D :] = jnp.where(
        lane == number,
        high.astype(jnp.float32),
        jnp.where(lane == number + E, low.astype(jnp.float32), 0.0),
    ).astype(jnp.bfloat16)
    gate_sum[...] += tn_dot(grad_gate, rows)
    up_sum[...] += tn_dot(grad_up, rows)
    down_sum[...] += tn_dot(scaled, upstream)

    @pl.when(last[step] == 1)
    def _():
        for index, (out, total) in enumerate(
            ((gate_out, gate_sum), (up_out, up_sum), (down_out, down_sum))
        ):
            out[0] = total[...].T + before[index][0] if before else total[...].T


def experts(plan, route, base, rows, w_gate, w_up, w_down, before):
    wide = 2 * D + EXTRA
    width = w_gate.shape[2]
    slots, count = plan.cap // GR, TILE // GR
    table = route["source"].reshape(plan.local * plan.tiles, count)
    number = route["owner"] * (slots // count) + route["tile"]
    table = table[number].reshape(-1)

    def whole(step, used, table, owner, tile, last, filled, base):
        return (owner[step], 0, 0)

    def tile_at(step, used, table, owner, tile, last, filled, base):
        return (owner[step] * plan.tiles + tile[step], 0)

    weight = pl.BlockSpec((1, D, width), whole)
    total = plan.local * plan.cap
    return pl.pallas_call(
        functools.partial(while_used, expert_step),
        grid_spec=pltpu.PrefetchScalarGridSpec(
            num_scalar_prefetch=7,
            grid=(plan.local * plan.tiles,),
            in_specs=[pl.BlockSpec(memory_space=pl.ANY)] + [weight] * (3 + len(before)),
            out_specs=[pl.BlockSpec((TILE, wide), tile_at)] + [weight] * 3,
            scratch_shapes=[
                pltpu.VMEM((2, TILE, wide), jnp.bfloat16),
                pltpu.SemaphoreType.DMA((2,)),
            ]
            + [pltpu.VMEM((width, D), jnp.float32)] * 3,
        ),
        out_shape=[jax.ShapeDtypeStruct((total, wide), jnp.bfloat16)]
        + [jax.ShapeDtypeStruct((plan.local, D, width), jnp.float32)] * 3,
        compiler_params=pltpu.CompilerParams(vmem_limit_bytes=VMEM),
        input_output_aliases={11 + index: 1 + index for index in range(len(before))},
        cost_estimate=transfer(80),
        name="experts",
    )(
        route["tiles_used"],
        table,
        route["owner"],
        route["tile"],
        route["tile_last"],
        route["filled"],
        base[None],
        rows,
        w_gate,
        w_up,
        w_down,
        *before,
    )


def combine_step(
    used, target, block, part, last, results, place, share, post, router, *refs
):
    held, sems, sums = refs[-3:]
    passing = (len(refs) - 6) // 2
    out, grad, router_out = refs[passing : passing + 3]
    step = pl.program_id(0)
    local = place.shape[1]
    slots = held.shape[1]

    at = next_groups(used, target, results, held, sems, slots // GR)

    @pl.when(step == 0)
    def _():
        router_out[...] = jnp.zeros_like(router_out)

    slot = lax.broadcasted_iota(jnp.int32, (TB, slots), 1) + part[step] * slots
    hit = slot == place[:, 0:1]
    for one in range(1, local):
        hit = hit | (slot == place[:, one : one + 1])
    pick = jnp.where(hit, 1.0, 0.0).astype(jnp.bfloat16)

    def term(begin, end):
        return nn_dot(pick, held[at, :, begin:end])

    def finish(value):
        change = unpair(value(2 * D, 2 * D + EXTRA))
        portion = unpair(share[...])
        moved = portion * (change - jnp.sum(change * portion, -1, keepdims=True))
        moved = moved.astype(jnp.bfloat16)
        out[...] = value(0, D).astype(jnp.bfloat16)
        grad[...] = (value(D, 2 * D) + nt_dot(moved, router[...])).astype(jnp.bfloat16)
        router_out[...] += tn_dot(moved, post[...])

    single = (part[step] == 0) & (last[step] == 1)

    @pl.when(single)
    def _():
        finish(term)

    @pl.when(jnp.logical_not(single))
    def _():
        @pl.when(part[step] == 0)
        def _():
            sums[...] = jnp.zeros_like(sums)

        sums[...] += term(0, 2 * D + EXTRA)

        @pl.when(last[step] == 1)
        def _():
            finish(lambda begin, end: sums[:, begin:end])


def combine(plan, route, results, share, post, router, later):
    wide = 2 * D + EXTRA

    def at_block(step, used, target, block, part, last):
        return (block[step], 0)

    def fixed(step, used, target, block, part, last):
        return (0, 0)

    return pl.pallas_call(
        functools.partial(while_used, combine_step),
        grid_spec=pltpu.PrefetchScalarGridSpec(
            num_scalar_prefetch=5,
            grid=(plan.items,),
            in_specs=[
                pl.BlockSpec(memory_space=pl.ANY),
                pl.BlockSpec((TB, plan.local), at_block),
                pl.BlockSpec((TB, EXTRA), at_block),
                pl.BlockSpec((TB, D), at_block),
                pl.BlockSpec((D, E), fixed),
            ]
            + [pl.BlockSpec(memory_space=pl.ANY)] * len(later),
            out_specs=[
                pl.BlockSpec((TB, D), at_block),
                pl.BlockSpec((TB, D), at_block),
                pl.BlockSpec((E, D), fixed),
            ]
            + [pl.BlockSpec(memory_space=pl.ANY)] * len(later),
            scratch_shapes=[
                pltpu.VMEM((2, plan.slots, wide), jnp.bfloat16),
                pltpu.SemaphoreType.DMA((2,)),
                pltpu.VMEM((TB, wide), jnp.float32),
            ],
        ),
        out_shape=[
            jax.ShapeDtypeStruct((plan.tokens, D), jnp.bfloat16),
            jax.ShapeDtypeStruct((plan.tokens, D), jnp.bfloat16),
            jax.ShapeDtypeStruct((E, D), jnp.float32),
        ]
        + [jax.ShapeDtypeStruct(one.shape, one.dtype) for one in later],
        input_output_aliases={10 + index: 3 + index for index in range(len(later))},
        compiler_params=pltpu.CompilerParams(vmem_limit_bytes=VMEM),
        cost_estimate=transfer(50),
        name="combine",
    )(
        route["used"],
        route["target"],
        route["block"],
        route["part"],
        route["last"],
        results,
        route["place"].reshape(plan.tokens, plan.local),
        share,
        post,
        router,
        *later,
    )


def gather_all(own):
    if lax.axis_size("dp") == 8:
        return box_gather(own)
    return lax.all_gather(
        lax.all_gather(own, "tensor", axis=0, tiled=True), "dp", axis=0, tiled=True
    )


def gather_slowly(own):
    if lax.axis_size("dp") == 8:
        return lax.all_gather(own, ("dp", "tensor"), axis=0, tiled=True)
    return gather_all(own)


def gather_output(own):
    n = lax.axis_size("tensor")
    if lax.axis_size("dp") == 8:
        everything = lax.all_gather(own, ("dp", "tensor"), axis=0, tiled=False)
        everything = everything.reshape((8, n) + own.shape).transpose(1, 0, 2, 3)
        return everything.reshape(n, -1, own.shape[1])
    part = lax.all_gather(own, "dp", axis=0, tiled=True)
    return lax.all_gather(part, "tensor", axis=0, tiled=False)


def sum_last(tokens, parts, later):
    n = lax.axis_size("tensor")
    if lax.axis_size("dp") == 8:
        return closing(
            tokens.reshape(n, -1, tokens.shape[1]),
            parts.reshape(parts.shape[0], 8, -1, parts.shape[2]),
            later,
        )
    tokens, later = chain_sum(tokens, later, 8)
    parts = lax.psum_scatter(parts, "dp", scatter_dimension=1, tiled=True)
    own = lax.psum_scatter(parts[:n], "tensor", scatter_dimension=0, tiled=True)
    return tokens, jnp.concatenate([own, parts[n:]]).astype(jnp.float32), later


def sum_all(part, tokens, later):
    if lax.axis_size("dp") == 8:
        return box_sum(part, tokens, later)
    tokens = lax.psum_scatter(tokens, "tensor", scatter_dimension=0, tiled=True)
    return sum_slowly(part).astype(jnp.float32), tokens.astype(jnp.float32), later


def sum_slowly(part):
    part = lax.psum_scatter(part, "dp", scatter_dimension=0, tiled=True)
    return lax.psum_scatter(part, "tensor", scatter_dimension=0, tiled=True)


def fill(value, rows, columns):
    return jnp.pad(value, ((0, rows - value.shape[0]), (0, columns - value.shape[1])))


def pack_small(router, prenorm, postnorm, querynorm, keynorm, routes):
    n = lax.axis_size("tensor")
    rank = lax.axis_index("tensor")
    rows = router.shape[0]
    head = ceil_to(max(rows, querynorm.shape[0]), 16)
    heads = querynorm.shape[1]
    block = jnp.concatenate(
        [
            fill(router, head, E),
            fill(prenorm[:, None], head, 1),
            fill(postnorm[:, None], head, 1),
            fill(querynorm, head, heads),
            fill(keynorm, head, heads),
        ],
        1,
    )
    part = routes.shape[0] // n
    own = lax.dynamic_slice_in_dim(routes, rank * part, part, 0)
    own = own.astype(jnp.bfloat16).reshape(-1, 128)
    tail = ceil_to(own.shape[0], 16)
    return jnp.concatenate([fill(block, head, 128), fill(own, tail, 128)], 0)


def unpack_small(everything, router, querynorm, routes):
    n = lax.axis_size("tensor")
    rank = lax.axis_index("tensor")
    rows, heads = router.shape[0], querynorm.shape[1]
    head = ceil_to(max(rows, querynorm.shape[0]), 16)
    part = routes.size // n // 128
    total = everything.shape[1]
    mine = everything.reshape(-1, n, total, 128)[:, rank]
    at = E + 2
    return (
        everything[:, :rows, :E].reshape(-1, E),
        everything[:, :rows, E].reshape(-1).astype(jnp.float32),
        everything[:, :rows, E + 1].reshape(-1).astype(jnp.float32),
        mine[:, : querynorm.shape[0], at : at + heads].reshape(-1, heads),
        mine[:, : querynorm.shape[0], at + heads : at + 2 * heads].reshape(-1, heads),
        everything[:, head : head + part].reshape(-1, TOP).astype(jnp.int32),
    )


def body(
    hidden_in,
    out_grad,
    doc_ids,
    expert_ids,
    prenorm,
    querynorm,
    keynorm,
    query_proj,
    key_proj,
    value_proj,
    output_proj,
    postnorm,
    router,
    gate_proj,
    up_proj,
    down_proj,
):
    residual = hidden_in[0].astype(jnp.float32)
    upstream = out_grad[0]
    documents = doc_ids[0]
    routes = expert_ids[0]
    shard = residual.shape[0]
    seq_len = documents.shape[0]
    mesh_dp = lax.axis_size("dp")
    block = min(seq_len, 1024)
    scale = HD ** (-0.5)
    cosine, sine = rope_tables(seq_len, HD)
    small = pack_small(router, prenorm, postnorm, querynorm, keynorm, routes)
    group_hidden, later, output_late, everything = chain_gather(
        hidden_in[0], [upstream[: shard // 2], output_proj], 1, small
    )
    router_full, pre_gain, post_gain, gain_query, gain_key, all_routes = unpack_small(
        everything, router, querynorm, routes
    )
    weights = lax.all_gather(
        jnp.concatenate([query_proj, key_proj, value_proj], 1),
        "dp",
        axis=0,
        tiled=True,
    )
    w_query, w_key, w_value = jnp.split(weights, 3, 1)
    w_output = gather_output(output_late)
    heads = w_query.shape[1] // HD
    query_scale = gain_query.astype(jnp.float32).T.reshape(-1)
    key_scale = gain_key.astype(jnp.float32).T.reshape(-1)
    inv_pre = lax.rsqrt(jnp.mean(residual * residual, -1, keepdims=True) + epsilon)
    group_hidden = group_hidden.astype(jnp.float32)
    group_inv = lax.rsqrt(jnp.mean(group_hidden * group_hidden, -1, keepdims=True) + epsilon)
    group_normed = (group_hidden * group_inv * pre_gain).astype(jnp.bfloat16)
    n = lax.axis_size("tensor")
    few = shard // 2
    plan = Plan(mesh_dp * n * few, n * few, gate_proj.shape[0])
    base = (lax.axis_index("dp") * plan.local).astype(jnp.int32)
    all_routes = all_routes.reshape(mesh_dp, n, 2, few, TOP)
    route = [
        routing(plan, all_routes[:, :, index].reshape(-1, TOP), base) for index in range(2)
    ]
    all_grad = [gather_slowly(later)]
    query = jnp.dot(group_normed, w_query, preferred_element_type=jnp.float32)
    keys = jnp.dot(group_normed, w_key, preferred_element_type=jnp.float32)
    values = jnp.dot(group_normed, w_value, preferred_element_type=jnp.float32).astype(jnp.bfloat16)
    query_sq, key_sq = sum_heads(
        (jnp.sum(query * query, -1, keepdims=True), jnp.sum(keys * keys, -1, keepdims=True))
    )
    inv_query = lax.rsqrt(query_sq / D + epsilon)
    inv_key = lax.rsqrt(key_sq / D + epsilon)
    query_heads = (query * inv_query * query_scale).reshape(seq_len, heads, HD)
    key_heads = (keys * inv_key * key_scale).reshape(seq_len, heads, HD)
    query_rot = (query_heads * cosine[:, None] + rotate(query_heads) * sine[:, None]).astype(
        jnp.bfloat16
    )
    key_rot = (key_heads * cosine[:, None] + rotate(key_heads) * sine[:, None]).astype(jnp.bfloat16)
    value_heads = values.reshape(seq_len, heads, HD)
    mixed, logsum = attend_forward(query_rot, key_rot, value_heads, documents, block, scale)
    mixed_flat = mixed.reshape(seq_len, heads * HD)
    mixed_own, later = swap(mixed_flat.reshape(n, shard, heads * HD), upstream[few:], 7)
    all_grad.append(gather_slowly(later))
    attn_local = sum(nt_dot(mixed_own[index], w_output[index]) for index in range(n))
    middle = residual + attn_local
    inv_post = lax.rsqrt(jnp.mean(middle * middle, -1, keepdims=True) + epsilon)
    post_normed = (middle * inv_post * post_gain).astype(jnp.bfloat16)
    all_post = [gather_all(post_normed[:few]), gather_slowly(post_normed[few:])]
    grads, outs, backs, router_parts = [], [], [], []
    for index in range(2):
        rows, portion, *outs = dispatch(
            plan, route[index], all_post[index], all_grad[index], router_full, outs
        )
        results, *grads = experts(
            plan, route[index], base, rows, gate_proj, up_proj, down_proj, grads
        )
        if index == 0:
            later = [all_post[1], all_grad[1]]
        else:
            later = [lax.psum_scatter(backs[0], "dp", scatter_dimension=0, tiled=True)]
        out, back, router_part, *later = combine(
            plan, route[index], results, portion, all_post[index], router_full, later
        )
        if index == 0:
            all_post[1], all_grad[1] = later
        else:
            early = later[0]
        outs.append(out)
        backs.append(back)
        router_parts.append(router_part)
    gate_weight_grad, up_weight_grad, down_weight_grad = grads
    first_out = lax.psum_scatter(outs[0], "dp", scatter_dimension=0, tiled=True)
    early = jnp.concatenate(
        [early.reshape(n, few, D), first_out.reshape(n, few, D)], 1
    ).reshape(-1, D)
    late, early, outs = sum_all(backs[1], early, outs[1:])
    early, first_out = early[:few], early[few:].astype(jnp.bfloat16)
    grad_post = jnp.concatenate([early, late], 0)
    moe_local = jnp.concatenate([first_out, sum_slowly(outs[0])], 0)
    router_part = router_parts[0] + router_parts[1]
    router_part = router_part.T
    post_gain_part = jnp.sum(grad_post * middle * inv_post, 0)
    grad_middle = upstream.astype(jnp.float32) + norm_back(
        grad_post, middle, inv_post, post_gain, D
    )
    change = grad_middle.astype(jnp.bfloat16)
    grad_mixed, _ = swap(
        jnp.stack([nn_dot(change, w_output[index]).astype(jnp.bfloat16) for index in range(n)]),
        jnp.zeros((16, 128), jnp.bfloat16),
        2,
    )
    output_parts = [tn_dot(change, mixed_own[index]).astype(jnp.bfloat16) for index in range(n)]
    grad_query_rot, grad_key_rot, grad_value_heads = attend_backward(
        query_rot,
        key_rot,
        value_heads,
        documents,
        logsum,
        grad_mixed.reshape(seq_len, heads, HD),
        block,
        scale,
    )
    grad_query_flat = (
        grad_query_rot * cosine[:, None] + rotate_back(grad_query_rot * sine[:, None])
    ).reshape(seq_len, -1)
    grad_key_flat = (
        grad_key_rot * cosine[:, None] + rotate_back(grad_key_rot * sine[:, None])
    ).reshape(seq_len, -1)
    query_inner, key_inner = sum_heads(
        (
            jnp.sum(grad_query_flat * query_scale * query, -1, keepdims=True),
            jnp.sum(grad_key_flat * key_scale * keys, -1, keepdims=True),
        )
    )
    grad_query = (
        inv_query * query_scale * grad_query_flat - query * inv_query**3 * query_inner / D
    ).astype(jnp.bfloat16)
    grad_key = (inv_key * key_scale * grad_key_flat - keys * inv_key**3 * key_inner / D).astype(
        jnp.bfloat16
    )
    query_gain_part = jnp.sum(grad_query_flat * query * inv_query, 0).reshape(heads, HD).T
    key_gain_part = jnp.sum(grad_key_flat * keys * inv_key, 0).reshape(heads, HD).T
    grad_value = grad_value_heads.reshape(seq_len, -1).astype(jnp.bfloat16)
    query_part = lax.dot_general(
        group_normed, grad_query, (((0,), (0,)), ((), ())), preferred_element_type=jnp.float32
    )
    key_part = lax.dot_general(
        group_normed, grad_key, (((0,), (0,)), ((), ())), preferred_element_type=jnp.float32
    )
    value_part = lax.dot_general(
        group_normed, grad_value, (((0,), (0,)), ((), ())), preferred_element_type=jnp.float32
    )
    normed_term = lax.dot_general(
        grad_query, w_query, (((1,), (1,)), ((), ())), preferred_element_type=jnp.float32
    )
    normed_term = normed_term + lax.dot_general(
        grad_key, w_key, (((1,), (1,)), ((), ())), preferred_element_type=jnp.float32
    )
    normed_term = normed_term + lax.dot_general(
        grad_value, w_value, (((1,), (1,)), ((), ())), preferred_element_type=jnp.float32
    )
    grad_normed, weight_sums, middle = sum_last(
        normed_term.astype(jnp.bfloat16),
        jnp.stack(
            output_parts + [part.astype(jnp.bfloat16) for part in (query_part, key_part, value_part)]
        ),
        middle,
    )
    layer_out = (middle + moe_local.astype(jnp.float32)).astype(jnp.bfloat16)[None]
    pre_gain_part = jnp.sum(grad_normed * residual * inv_pre, 0)
    input_grad = (grad_middle + norm_back(grad_normed, residual, inv_pre, pre_gain, D)).astype(
        jnp.bfloat16
    )[None]
    gains = jnp.concatenate([query_gain_part, key_gain_part], 1).reshape(mesh_dp, 1, -1, 2 * heads)
    mine = jnp.arange(n)[None, :, None, None] == lax.axis_index("tensor")
    gains = jnp.pad(
        jnp.where(mine, gains, 0.0),
        ((0, 0), (0, 0), (0, max(router.shape[0] - HD // mesh_dp, 0)), (0, 0)),
    ).reshape(D, 2 * heads)
    small = jnp.concatenate(
        [
            router_part,
            pre_gain_part[:, None],
            post_gain_part[:, None],
            gains,
            jnp.zeros((D, 128 - E - 2 - 2 * heads), jnp.float32),
        ],
        1,
    )
    small = sum_spread(small.reshape(-1, router.shape[0], 128))
    gain_grads = small[: HD // mesh_dp, E + 2 : E + 2 + 2 * heads]
    return (
        layer_out,
        input_grad,
        small[:, E],
        gain_grads[:, :heads],
        gain_grads[:, heads : 2 * heads],
        weight_sums[1],
        weight_sums[2],
        weight_sums[3],
        weight_sums[0],
        small[:, E + 1],
        small[:, :E],
        gate_weight_grad,
        up_weight_grad,
        down_weight_grad,
    )


def solution(mesh):
    in_specs = (
        P("dp", "tensor", None),
        P("dp", "tensor", None),
        P("dp", None),
        P("dp", None, None),
        P(("dp", "tensor")),
        P("dp", "tensor"),
        P("dp", "tensor"),
        P("dp", "tensor"),
        P("dp", "tensor"),
        P("dp", "tensor"),
        P("dp", "tensor"),
        P(("dp", "tensor")),
        P(("dp", "tensor"), None),
        P("dp", None, "tensor"),
        P("dp", None, "tensor"),
        P("dp", None, "tensor"),
    )
    out_specs = (
        P("dp", "tensor", None),
        P("dp", "tensor", None),
        P(("dp", "tensor")),
        P("dp", "tensor"),
        P("dp", "tensor"),
        P("dp", "tensor"),
        P("dp", "tensor"),
        P("dp", "tensor"),
        P("dp", "tensor"),
        P(("dp", "tensor")),
        P(("dp", "tensor"), None),
        P("dp", None, "tensor"),
        P("dp", None, "tensor"),
        P("dp", None, "tensor"),
    )
    return jax.shard_map(body, mesh=mesh, in_specs=in_specs, out_specs=out_specs, check_vma=False)
```

```python
import functools

import jax
import jax.numpy as jnp
from jax import lax
from jax.experimental import pallas as pl
from jax.experimental.pallas import tpu as pltpu
from jax.sharding import PartitionSpec as P

D = 2048
HD = 128
E = 64
TOP = 8
CG = 192


epsilon = 1e-05
masked_score = -1000000000.0


def rope_tables(length, width):
    positions = jnp.arange(length).astype(jnp.float32)
    rates = 10000.0 ** (-jnp.arange(0, width, 2).astype(jnp.float32) / width)
    angles = positions[:, None] * rates[None, :]
    return (jnp.concatenate([jnp.cos(angles)] * 2, -1), jnp.concatenate([jnp.sin(angles)] * 2, -1))


def rotate(tensor):
    half = tensor.shape[-1] // 2
    return jnp.concatenate([-tensor[..., half:], tensor[..., :half]], -1)


def rotate_back(tensor):
    half = tensor.shape[-1] // 2
    return jnp.concatenate([tensor[..., half:], -tensor[..., :half]], -1)


def sum_heads(parts):
    return lax.psum((parts[0], parts[1]), "tensor")


def norm_back(grad, value, inverse, gain, width):
    scaled = grad * gain
    inner = jnp.sum(scaled * value, -1, keepdims=True)
    return inverse * scaled - value * inverse**3 * inner / width


def block_scores(query, keys, documents, start, block, scale):
    row_place = start + jnp.arange(block)
    col_place = jnp.arange(documents.shape[0])
    allowed = (documents[:, None] == documents[None, :]) & (
        row_place[:, None] >= col_place[None, :]
    )
    scores = jnp.einsum("qhd,khd->hqk", query, keys, preferred_element_type=jnp.float32) * scale
    return (jnp.where(allowed[None], scores, masked_score), query)


def attend_forward(query, keys, values, documents, block, scale):
    count = query.shape[0] // block

    def one(index):
        scores, rows = block_scores(query, keys, documents, index * block, block, scale)
        peak = jnp.max(scores, -1, keepdims=True)
        weights = jnp.exp(scores - peak)
        total = jnp.sum(weights, -1, keepdims=True)
        portion = (weights / total).astype(jnp.bfloat16)
        mixed = jnp.einsum("hqk,khd->qhd", portion, values, preferred_element_type=jnp.float32)
        return (mixed.astype(jnp.bfloat16), peak + jnp.log(total))

    mixed, logsum = lax.map(one, jnp.arange(count))
    return (mixed.reshape(query.shape), logsum)


def attend_backward(query, keys, values, documents, logsum, grad_mixed, block, scale):
    count = query.shape[0] // block

    def one(index):
        start = index * block
        scores, rows = block_scores(query, keys, documents, start, block, scale)
        portion = jnp.exp(scores - logsum[index])
        grad_portion = jnp.einsum(
            "qhd,khd->hqk", grad_mixed, values, preferred_element_type=jnp.float32
        )
        center = jnp.sum(portion * grad_portion, -1, keepdims=True)
        grad_scores = (portion * (grad_portion - center)).astype(jnp.bfloat16)
        grad_values = jnp.einsum(
            "hqk,qhd->khd",
            portion.astype(jnp.bfloat16),
            grad_mixed,
            preferred_element_type=jnp.float32,
        )
        grad_query = (
            jnp.einsum("hqk,khd->qhd", grad_scores, keys, preferred_element_type=jnp.float32)
            * scale
        )
        grad_keys = (
            jnp.einsum("hqk,qhd->khd", grad_scores, rows, preferred_element_type=jnp.float32)
            * scale
        )
        return (grad_query, grad_keys, grad_values)

    grad_query, grad_keys, grad_values = lax.map(one, jnp.arange(count))
    return (grad_query.reshape(query.shape), jnp.sum(grad_keys, 0), jnp.sum(grad_values, 0))


MESH = pl.DeviceIdType.MESH
VMEM = 60 * 1024 * 1024


def transfer(microseconds):
    return pl.CostEstimate(flops=0, bytes_accessed=microseconds * 3_000_000, transcendentals=0)


def flip(index, bit):
    return index + bit - 2 * bit * ((index // bit) % 2)


def send(source, target, send_sem, recv_sem, device):
    return pltpu.make_async_remote_copy(
        src_ref=source,
        dst_ref=target,
        send_sem=send_sem,
        recv_sem=recv_sem,
        device_id=device,
        device_id_type=MESH,
    )


def greet(devices, extra=()):
    barrier = pltpu.get_barrier_semaphore()
    for device in devices:
        pl.semaphore_signal(barrier, inc=1, device_id=device, device_id_type=MESH)
    for there, device in extra:

        @pl.when(there)
        def _(device=device):
            pl.semaphore_signal(barrier, inc=1, device_id=device, device_id_type=MESH)

    count = len(devices)
    for there, _ in extra:
        count = count + jnp.where(there, 1, 0)
    pl.semaphore_wait(barrier, count)


def both_ways(n):
    spot = lax.axis_index("tensor")
    return spot, (
        (spot < n - 1, {"tensor": jnp.minimum(spot + 1, n - 1)}),
        (spot > 0, {"tensor": jnp.maximum(spot - 1, 0)}),
    )


def shard_at(spot, way, distance, n):
    number = spot - distance if way == 0 else spot + distance
    return (number >= 0) & (number < n), jnp.clip(number, 0, n - 1)


def chain_gather_kernel(n, pieces, passing, own, *refs):
    refs = refs[passing:]
    if len(refs) > passing + 4:
        small, out, everything, *sems = refs[0], refs[1], refs[2 + passing], *refs[3 + passing :]
        local_sem, send_sem, recv_sem, all_send, all_recv = sems
        finish = spread_start(n, small, everything, all_send, all_recv)
    else:
        out, (local_sem, send_sem, recv_sem) = refs[0], refs[1 + passing :]
        finish = None
    spot, sides = both_ways(n)
    rows = own.shape[0] // pieces
    if finish is None:
        greet([], sides)
    keep = pltpu.make_async_copy(own, out.at[spot], local_sem)
    keep.start()

    def copy(way, distance, piece):
        there, number = shard_at(spot, way, distance, n)
        part = pl.ds(piece * rows, rows)
        source = own.at[part] if distance == 0 else out.at[number, part]
        return there & sides[way][0], send(
            source,
            out.at[number, part],
            send_sem.at[way, distance, piece],
            recv_sem.at[way, distance, piece],
            sides[way][1],
        )

    def arrived(way, distance, piece):
        there, number = shard_at(spot, way, distance, n)
        part = pl.ds(piece * rows, rows)

        @pl.when(there)
        def _():
            send(
                out.at[number, part],
                out.at[number, part],
                send_sem.at[way, distance - 1, piece],
                recv_sem.at[way, distance - 1, piece],
                sides[way][1],
            ).wait_recv()

    for distance in range(n):
        for piece in range(pieces):
            for way in (0, 1):
                if distance:
                    arrived(way, distance, piece)
                if distance < n - 1:
                    go, one = copy(way, distance, piece)

                    @pl.when(go)
                    def _(one=one):
                        one.start()

    keep.wait()
    for distance in range(n - 1):
        for piece in range(pieces):
            for way in (0, 1):
                go, one = copy(way, distance, piece)

                @pl.when(go)
                def _(one=one):
                    one.wait_send()

    if finish is not None:
        finish()


def chain_gather(own, later, number, small=None, pieces=4):
    n = lax.axis_size("tensor")
    rows, width = own.shape
    anywhere = pl.BlockSpec(memory_space=pl.ANY)
    inside = pl.BlockSpec(memory_space=pltpu.VMEM)
    sem = pltpu.SemaphoreType.DMA
    outs = [jax.ShapeDtypeStruct((n, rows, width), own.dtype)]
    outs += [jax.ShapeDtypeStruct(one.shape, one.dtype) for one in later]
    more, sems = [], []
    if small is not None:
        count = lax.axis_size("dp") * n
        outs.append(jax.ShapeDtypeStruct((count,) + small.shape, small.dtype))
        more, sems = [small], [sem((count,)), sem((count,))]
    plain = [anywhere] * (1 + len(later)) + [inside] * len(more)
    out, *rest = pl.pallas_call(
        functools.partial(chain_gather_kernel, n, pieces, len(later)),
        out_shape=outs,
        in_specs=plain,
        out_specs=plain,
        input_output_aliases={1 + index: 1 + index for index in range(len(later))},
        scratch_shapes=[sem, sem((2, n - 1, pieces)), sem((2, n - 1, pieces))] + sems,
        compiler_params=pltpu.CompilerParams(
            collective_id=number, has_side_effects=True, vmem_limit_bytes=VMEM
        ),
        cost_estimate=transfer(65),
        name="chain_gather",
    )(own, *later, *more)
    return (out.reshape(n * rows, width), *rest)


def add_into(target, source, rows, start=0, source_start=0):
    step = 16

    def body(index, carry):
        at = pl.ds(pl.multiple_of(start + index * step, step), step)
        come = pl.ds(pl.multiple_of(source_start + index * step, step), step)
        target[at, :] = (
            target[at, :].astype(jnp.float32) + source[come, :].astype(jnp.float32)
        ).astype(target.dtype)
        return carry

    lax.fori_loop(0, rows // step, body, 0)


def chain_sum_kernel(n, pieces, part, _later, out, _passed, held, send_sem, recv_sem):
    spot, sides = both_ways(n)
    greet([], sides)
    onward, finish, drain = chain_steps(n, pieces, part, out, held, send_sem, recv_sem)
    for far in range(n - 1, 0, -1):
        onward(far)
    finish()
    drain()


def chain_steps(n, pieces, part, out, held, send_sem, recv_sem):
    spot, sides = both_ways(n)
    rows = out.shape[0] // pieces

    def copy(way, far, piece, mine):
        number = spot + far if way == 0 else spot - far
        there = (number >= 0) & (number < n)
        number = jnp.clip(number, 0, n - 1)
        at = pl.ds(piece * rows, rows)
        source = part.at[number, at]
        return there, number, send(
            source if mine else held.at[way, far, at],
            held.at[way, far - 1, at],
            send_sem.at[way, far - 1, piece],
            recv_sem.at[way, far - 1, piece],
            sides[way][1],
        )

    def arrived(way, far, piece):
        at = pl.ds(piece * rows, rows)
        send(
            held.at[way, far, at],
            held.at[way, far, at],
            send_sem.at[way, far, piece],
            recv_sem.at[way, far, piece],
            sides[way][1],
        ).wait_recv()

    def onward(far):
        for piece in range(pieces):
            for way in (0, 1):
                behind = sides[1 - way][0]
                there, number, first = copy(way, far, piece, True)

                @pl.when(there & jnp.logical_not(behind))
                def _(first=first):
                    first.start()

                if far < n - 1:
                    _, _, again = copy(way, far, piece, False)

                    @pl.when(there & behind)
                    def _(way=way, piece=piece, number=number, again=again):
                        arrived(way, far, piece)
                        add_into(
                            held.at[way, far], part.at[number], rows, piece * rows, piece * rows
                        )
                        again.start()

    def finish():
        for piece in range(pieces):

            def body(index, carry, piece=piece):
                here = pl.ds(pl.multiple_of(piece * rows + index * 16, 16), 16)
                out[here, :] = part[spot, here, :].astype(jnp.float32)
                return carry

            lax.fori_loop(0, rows // 16, body, 0)
            for way in (0, 1):

                @pl.when(sides[1 - way][0])
                def _(way=way, piece=piece):
                    arrived(way, 0, piece)
                    add_into(out, held.at[way, 0], rows, piece * rows, piece * rows)

    def drain():
        for far in range(n - 1, 0, -1):
            for piece in range(pieces):
                for way in (0, 1):
                    there, _, one = copy(way, far, piece, True)

                    @pl.when(there)
                    def _(one=one):
                        one.wait_send()

    return onward, finish, drain


def chain_sum(part, later, number, pieces=4):
    n = lax.axis_size("tensor")
    width = part.shape[1]
    rows = part.shape[0] // n
    anywhere = pl.BlockSpec(memory_space=pl.ANY)
    inside = pl.BlockSpec(memory_space=pltpu.VMEM)
    return pl.pallas_call(
        functools.partial(chain_sum_kernel, n, pieces),
        out_shape=[
            jax.ShapeDtypeStruct((rows, width), jnp.float32),
            jax.ShapeDtypeStruct(later.shape, later.dtype),
        ],
        in_specs=[inside, anywhere],
        out_specs=[inside, anywhere],
        input_output_aliases={1: 1},
        scratch_shapes=[
            pltpu.VMEM((2, n - 1, rows, width), part.dtype),
            pltpu.SemaphoreType.DMA((2, n - 1, pieces)),
            pltpu.SemaphoreType.DMA((2, n - 1, pieces)),
        ],
        compiler_params=pltpu.CompilerParams(
            collective_id=number, has_side_effects=True, vmem_limit_bytes=VMEM
        ),
        cost_estimate=transfer(65),
        name="chain_sum",
    )(part.reshape(n, rows, width), later)


def box_devices():
    me = lax.axis_index("dp")
    return me, {bit: {"dp": flip(me, bit)} for bit in (1, 2, 4)}


def box_gather_kernel(n, own, first, second, local_sem, z_send, z_recv, near_send, near_recv, on_send, on_recv, side_send, side_recv):
    spot, sides = both_ways(n)
    me, near = box_devices()
    half = own.shape[0] // 2
    greet([near[1], near[2], near[4]], sides)
    keep = [
        pltpu.make_async_copy(
            own.at[pl.ds(part * half, half)], (first, second)[part].at[me, spot], local_sem.at[part]
        )
        for part in (0, 1)
    ]
    for one in keep:
        one.start()
    sends = []

    def piece(seq, shard, part):
        return (first, second)[part].at[seq, shard]

    def start(condition, one):
        sends.append((condition, one))

        @pl.when(condition)
        def _():
            one.start()

    def await_piece(condition, target, recv):
        @pl.when(condition)
        def _():
            send(target, target, side_send.at[0, 0, 0], recv, near[1]).wait_recv()

    def to_side(condition, slot, seq, shard, part, source):
        start(condition, send(source, piece(seq, shard, part), side_send.at[slot, shard, part], side_recv.at[slot, shard, part], near[1]))

    def mine(way, distance):
        there, shard = shard_at(spot, way, distance, n)
        for part in (0, 1):
            if distance:
                await_piece(there, piece(me, shard, part), z_recv.at[way, distance - 1, part])
            source = piece(me, shard, part) if distance else own.at[pl.ds(part * half, half)]
            for out_way in (0, 1) if distance == 0 else (way,):
                if distance < n - 1:
                    start(there & sides[out_way][0], send(source, piece(me, shard, part), z_send.at[out_way, distance, part], z_recv.at[out_way, distance, part], sides[out_way][1]))
            for axis, bit in ((0, 2), (1, 4)):
                start(there, send(source, piece(me, shard, part), near_send.at[axis, shard, part], near_recv.at[axis, shard, part], near[bit]))
            to_side(there, 0, me, shard, part, source)

    def nearby(way, distance):
        there, shard = shard_at(spot, way, distance, n)
        for part in (0, 1):
            for axis, bit in ((0, 2), (1, 4)):
                seq = flip(me, bit)
                source = piece(seq, shard, part)
                await_piece(there, source, near_recv.at[axis, shard, part])
                if part == axis:
                    start(there, send(source, source, on_send.at[1 - axis, shard], on_recv.at[1 - axis, shard], near[6 - bit]))
                to_side(there, 1 + axis, seq, shard, part, source)

    def far(way, distance):
        there, shard = shard_at(spot, way, distance, n)
        seq = flip(flip(me, 2), 4)
        for part in (0, 1):
            source = piece(seq, shard, part)
            await_piece(there, source, on_recv.at[1 - part, shard])
            to_side(there, 3, seq, shard, part, source)

    for step in range(n + 2):
        for task, delay in ((mine, 0), (nearby, 1), (far, 2)):
            distance = step - delay
            if 0 <= distance < n:
                for way in (0, 1) if distance else (0,):
                    task(way, distance)
    for shard in range(n):
        for part in (0, 1):
            for slot, bit in enumerate((0, 2, 4, 6)):
                seq = flip(me, 1)
                for one in (2, 4):
                    if bit & one:
                        seq = flip(seq, one)
                await_piece(spot >= 0, piece(seq, shard, part), side_recv.at[slot, shard, part])
    for one in keep:
        one.wait()
    for condition, one in sends:

        @pl.when(condition)
        def _(one=one):
            one.wait_send()


def box_gather(own):
    n = lax.axis_size("tensor")
    rows, width = own.shape
    sem = pltpu.SemaphoreType.DMA
    out = pl.pallas_call(
        functools.partial(box_gather_kernel, n),
        out_shape=[jax.ShapeDtypeStruct((8, n, rows // 2, width), own.dtype)] * 2,
        in_specs=[pl.BlockSpec(memory_space=pl.ANY)],
        out_specs=[pl.BlockSpec(memory_space=pl.ANY)] * 2,
        scratch_shapes=[sem((2,))]
        + [sem((2, n - 1, 2))] * 2
        + [sem((2, n, 2))] * 2
        + [sem((2, n))] * 2
        + [sem((4, n, 2))] * 2,
        compiler_params=pltpu.CompilerParams(collective_id=3, has_side_effects=True),
        cost_estimate=transfer(140),
        name="box_gather",
    )(own)
    return [half.reshape(4 * n * rows, width) for half in out]


def order_of(spot, n):
    table = [sorted(range(n), key=lambda s: -abs(s - j)) for j in range(n)]
    result = []
    for step in range(n):
        value = jnp.int32(table[0][step])
        for j in range(1, n):
            value = jnp.where(spot == j, table[j][step], value)
        result.append(value)
    return result


def box_steps(n, pieces, part_at, final, side, local, on, near, chain, local_sem, side_send, side_recv, on_send, on_recv, near_send, near_recv, z_send, z_recv):
    spot, sides = both_ways(n)
    me, close = box_devices()
    rows = side.shape[2]
    half = rows // 2
    bits = (6, 2, 4, 0)
    sends = []

    def seq_of(index, bit):
        for one in (2, 4):
            if bit & one:
                index = flip(index, one)
        return index

    def start(one, condition=None):
        sends.append((condition, one))
        if condition is None:
            one.start()
        else:

            @pl.when(condition)
            def _():
                one.start()

    def await_at(target, recv):
        send(target, target, side_send.at[0, 0], recv, close[1]).wait_recv()

    def loads(chip, shard):
        return pltpu.make_async_copy(
            part_at(seq_of(me, bits[chip]), shard), local.at[chip, shard], local_sem.at[chip, shard]
        )

    def merge(chip, shard):
        await_at(side.at[chip, shard], side_recv.at[chip, shard])
        loads(chip, shard).wait()
        add_into(side.at[chip, shard], local.at[chip, shard], rows)

    def begin():
        for shard, _ in pieces:
            for chip in range(4):
                start(
                    send(
                        part_at(seq_of(flip(me, 1), bits[chip]), shard),
                        side.at[chip, shard],
                        side_send.at[chip, shard],
                        side_recv.at[chip, shard],
                        close[1],
                    )
                )
                loads(chip, shard).start()

    def first(step):
        shard = pieces[step][0]
        merge(0, shard)
        for axis, bit in ((0, 2), (1, 4)):
            start(
                send(
                    side.at[0, shard, pl.ds(axis * half, half)],
                    on.at[axis, shard],
                    on_send.at[axis, shard],
                    on_recv.at[axis, shard],
                    close[bit],
                )
            )
        merge(1, shard)
        merge(2, shard)

    def second(step):
        shard = pieces[step][0]
        for axis, bit in ((0, 2), (1, 4)):
            other = 2 - axis
            await_at(on.at[axis, shard], on_recv.at[axis, shard])
            add_into(side.at[other, shard], on.at[axis, shard], half, axis * half, 0)
            start(
                send(
                    side.at[other, shard],
                    near.at[1 - axis, shard],
                    near_send.at[1 - axis, shard],
                    near_recv.at[1 - axis, shard],
                    close[6 - bit],
                )
            )
        merge(3, shard)

    def third(step):
        shard = pieces[step][0]
        for axis in (0, 1):
            await_at(near.at[axis, shard], near_recv.at[axis, shard])
            add_into(side.at[3, shard], near.at[axis, shard], rows)

    def fourth(step):
        shard, kind = pieces[step]
        if kind == "far":
            for way in (0, 1):
                ahead = shard > spot if way == 0 else shard < spot
                distance = jnp.clip(shard - spot if way == 0 else spot - shard, 1, n - 1)

                @pl.when(ahead & sides[1 - way][0])
                def _(way=way, distance=distance):
                    slot = jnp.minimum(distance, n - 2)
                    await_at(chain.at[way, slot], z_recv.at[way, slot])
                    add_into(side.at[3, shard], chain.at[way, slot], rows)

                start(
                    send(
                        side.at[3, shard],
                        chain.at[way, distance - 1],
                        z_send.at[way, distance - 1],
                        z_recv.at[way, distance - 1],
                        sides[way][1],
                    ),
                    ahead,
                )
            return
        out = final(step)

        def body(index, carry):
            at = pl.ds(pl.multiple_of(index * 16, 16), 16)
            out[at, :] = side[3, shard, at, :].astype(jnp.float32)
            return carry

        lax.fori_loop(0, rows // 16, body, 0)
        if kind == "own":
            for way in (0, 1):

                @pl.when(sides[1 - way][0])
                def _(way=way):
                    await_at(chain.at[way, 0], z_recv.at[way, 0])
                    add_into(out, chain.at[way, 0], rows)

    def drain():
        for condition, one in sends:
            if condition is None:
                one.wait_send()
            else:

                @pl.when(condition)
                def _(one=one):
                    one.wait_send()

    return begin, first, second, third, fourth, drain


def greet_box(n):
    _, sides = both_ways(n)
    _, close = box_devices()
    greet([close[1], close[2], close[4]], sides)


def box_scratch(n, pieces, rows, width, kind):
    sem = pltpu.SemaphoreType.DMA
    return [
        pltpu.VMEM((4, pieces, rows, width), kind),
        pltpu.VMEM((4, pieces, rows, width), kind),
        pltpu.VMEM((2, pieces, rows // 2, width), kind),
        pltpu.VMEM((2, pieces, rows, width), kind),
        pltpu.VMEM((2, n - 1, rows, width), kind),
        sem((4, pieces)),
        sem((4, pieces)),
        sem((4, pieces)),
        sem((2, pieces)),
        sem((2, pieces)),
        sem((2, pieces)),
        sem((2, pieces)),
        sem((2, n - 1)),
        sem((2, n - 1)),
    ]


def box_sum_kernel(n, passing, part, tokens, *refs):
    out, token_out = refs[passing : passing + 2]
    held, send_sem, recv_sem, *scratch = refs[2 * passing + 2 :]
    onward, finish, end = chain_steps(n, 4, tokens, token_out, held, send_sem, recv_sem)
    spot, _ = both_ways(n)
    greet_box(n)
    order = order_of(spot, n)
    pieces = [(shard, "far") for shard in order[:-1]] + [(order[-1], "own")]
    begin, *tasks, drain = box_steps(
        n, pieces, lambda seq, shard: part.at[seq, shard], lambda step: out, *scratch
    )
    begin()
    for step in range(n + 3):
        if step < n - 1:
            onward(n - 1 - step)
        for delay, task in enumerate(tasks):
            if 0 <= step - delay < n:
                task(step - delay)
    finish()
    end()
    drain()


def closing_kernel(n, tokens, part, _later, out, weights, _passed, *scratch):
    spot, _ = both_ways(n)
    greet_box(n)
    held, send_sem, recv_sem = scratch[:3]
    onward, finish, end = chain_steps(n, 4, tokens, out, held, send_sem, recv_sem)
    order = order_of(spot, n)
    flat = weights.shape[0] - 1
    pieces = [(shard, "far") for shard in order[:-1]]
    pieces += [(n + index, "flat") for index in range(flat)] + [(order[-1], "own")]
    targets = [None] * (n - 1) + [weights.at[1 + index] for index in range(flat)] + [weights.at[0]]
    begin, first, second, third, fourth, drain = box_steps(
        n, pieces, lambda seq, shard: part.at[shard, seq], lambda step: targets[step], *scratch[3:]
    )
    begin()
    onward(n - 1)
    count = len(pieces)
    far = n - 2
    for task in (first, second, third, fourth):
        for step in range(count):
            task(step)
        if far:
            onward(far)
            far -= 1
    for left in range(far, 0, -1):
        onward(left)
    finish()
    end()
    drain()


def closing(tokens, part, later):
    n = lax.axis_size("tensor")
    pieces, _, rows, width = part.shape
    sem = pltpu.SemaphoreType.DMA
    inside = pl.BlockSpec(memory_space=pltpu.VMEM)
    anywhere = pl.BlockSpec(memory_space=pl.ANY)
    return pl.pallas_call(
        functools.partial(closing_kernel, n),
        out_shape=[
            jax.ShapeDtypeStruct(tokens.shape[1:], jnp.float32),
            jax.ShapeDtypeStruct((pieces - n + 1, rows, width), jnp.float32),
            jax.ShapeDtypeStruct(later.shape, later.dtype),
        ],
        in_specs=[inside, anywhere, anywhere],
        out_specs=[inside, inside, anywhere],
        input_output_aliases={2: 2},
        scratch_shapes=[
            pltpu.VMEM((2, n - 1) + tokens.shape[1:], tokens.dtype),
            sem((2, n - 1, 4)),
            sem((2, n - 1, 4)),
        ]
        + box_scratch(n, pieces, rows, width, part.dtype),
        compiler_params=pltpu.CompilerParams(
            collective_id=8, has_side_effects=True, vmem_limit_bytes=VMEM
        ),
        cost_estimate=transfer(80),
        name="closing",
    )(tokens, part, later)


def swap_kernel(n, part, _later, out, _passed, local_sem, send_sem, recv_sem):
    spot = lax.axis_index("tensor")
    greet([{"tensor": lax.rem(spot + step, n)} for step in range(1, n)])
    keep = pltpu.make_async_copy(part.at[spot], out.at[spot], local_sem)
    keep.start()

    def copy(step):
        to = lax.rem(spot + step, n)
        return send(
            part.at[to], out.at[spot], send_sem.at[step], recv_sem.at[step], {"tensor": to}
        )

    for step in range(1, n):
        copy(step).start()
    keep.wait()
    for step in range(1, n):
        come = lax.rem(spot - step + n, n)
        send(
            part.at[come], out.at[come], send_sem.at[step], recv_sem.at[step], {"tensor": come}
        ).wait_recv()
        copy(step).wait_send()


def swap(part, later, number):
    n = lax.axis_size("tensor")
    sem = pltpu.SemaphoreType.DMA
    anywhere = pl.BlockSpec(memory_space=pl.ANY)
    return pl.pallas_call(
        functools.partial(swap_kernel, n),
        out_shape=[
            jax.ShapeDtypeStruct(part.shape, part.dtype),
            jax.ShapeDtypeStruct(later.shape, later.dtype),
        ],
        in_specs=[anywhere] * 2,
        out_specs=[anywhere] * 2,
        input_output_aliases={1: 1},
        scratch_shapes=[sem, sem((n,)), sem((n,))],
        compiler_params=pltpu.CompilerParams(
            collective_id=number, has_side_effects=True, vmem_limit_bytes=VMEM
        ),
        cost_estimate=transfer(25),
        name="swap",
    )(part, later)


def box_sum(part, tokens, later):
    n = lax.axis_size("tensor")
    width = part.shape[1]
    rows = part.shape[0] // (8 * n)
    kind = part.dtype
    anywhere = pl.BlockSpec(memory_space=pl.ANY)
    inside = pl.BlockSpec(memory_space=pltpu.VMEM)
    tokens = tokens.reshape(n, -1, width)
    sem = pltpu.SemaphoreType.DMA
    out, token_out, *later = pl.pallas_call(
        functools.partial(box_sum_kernel, n, len(later)),
        out_shape=[
            jax.ShapeDtypeStruct((rows, width), jnp.float32),
            jax.ShapeDtypeStruct(tokens.shape[1:], jnp.float32),
        ]
        + [jax.ShapeDtypeStruct(one.shape, one.dtype) for one in later],
        in_specs=[anywhere, inside] + [anywhere] * len(later),
        out_specs=[inside] * 2 + [anywhere] * len(later),
        input_output_aliases={2 + index: 2 + index for index in range(len(later))},
        scratch_shapes=[
            pltpu.VMEM((2, n - 1) + tokens.shape[1:], tokens.dtype),
            sem((2, n - 1, 4)),
            sem((2, n - 1, 4)),
        ]
        + box_scratch(n, n, rows, width, kind),
        compiler_params=pltpu.CompilerParams(
            collective_id=4, has_side_effects=True, vmem_limit_bytes=VMEM
        ),
        cost_estimate=transfer(90),
        name="box_sum",
    )(part.reshape(8, n, rows, width), tokens, *later)
    return out, token_out, later


def everyone(n):
    count = lax.axis_size("dp") * n
    me = lax.axis_index("dp") * n + lax.axis_index("tensor")

    def device(number):
        return {"dp": number // n, "tensor": number % n}

    return count, me, device


def greet_all(count, me, device):
    barrier = pltpu.get_barrier_semaphore()

    def signal(step, carry):
        pl.semaphore_signal(barrier, inc=1, device_id=device(lax.rem(me + step, count)), device_id_type=MESH)
        return carry

    lax.fori_loop(1, count, signal, 0)
    pl.semaphore_wait(barrier, count - 1)


def spread_start(n, own, out, send_sem, recv_sem):
    count, me, device = everyone(n)
    greet_all(count, me, device)
    out[me] = own[...]

    def copy(step):
        to = device(lax.rem(me + step, count))
        return send(own, out.at[me], send_sem.at[step], recv_sem.at[step], to)

    def go(step, carry):
        copy(step).start()
        return carry

    def end(step, carry):
        copy(step).wait_send()
        come = lax.rem(me - step + count, count)
        send(own, out.at[come], send_sem.at[step], recv_sem.at[step], device(come)).wait_recv()
        return carry

    lax.fori_loop(1, count, go, 0)
    return lambda: lax.fori_loop(1, count, end, 0)


def sum_spread_kernel(n, part, out, held, send_sem, recv_sem):
    count, me, device = everyone(n)
    greet_all(count, me, device)
    out[...] = part[me]

    def copy(step):
        to = lax.rem(me + step, count)
        return send(part.at[to], held.at[me], send_sem.at[step], recv_sem.at[step], device(to))

    def go(step, carry):
        copy(step).start()
        return carry

    def end(step, carry):
        come = lax.rem(me - step + count, count)
        send(part.at[0], held.at[come], send_sem.at[step], recv_sem.at[step], device(come)).wait_recv()
        out[...] += held[come]
        copy(step).wait_send()
        return carry

    lax.fori_loop(1, count, go, 0)
    lax.fori_loop(1, count, end, 0)


def sum_spread(part):
    n = lax.axis_size("tensor")
    count = lax.axis_size("dp") * n
    sem = pltpu.SemaphoreType.DMA
    return pl.pallas_call(
        functools.partial(sum_spread_kernel, n),
        out_shape=jax.ShapeDtypeStruct(part.shape[1:], part.dtype),
        in_specs=[pl.BlockSpec(memory_space=pltpu.VMEM)],
        out_specs=pl.BlockSpec(memory_space=pltpu.VMEM),
        scratch_shapes=[pltpu.VMEM(part.shape, part.dtype), sem((count,)), sem((count,))],
        compiler_params=pltpu.CompilerParams(
            collective_id=6, has_side_effects=True, vmem_limit_bytes=VMEM
        ),
        cost_estimate=transfer(20),
        name="sum_spread",
    )(part)


TB = 256
GR = 16
TILE = 256
EXTRA = 2 * E
def ceil_to(value, unit):
    return (value + unit - 1) // unit * unit


def nt_dot(a, b):
    return lax.dot_general(a, b, (((1,), (1,)), ((), ())), preferred_element_type=jnp.float32)


def tn_dot(a, b):
    return lax.dot_general(a, b, (((0,), (0,)), ((), ())), preferred_element_type=jnp.float32)


def nn_dot(a, b):
    return jnp.dot(a, b, preferred_element_type=jnp.float32)


def pair(value):
    high = value.astype(jnp.bfloat16)
    low = (value - high.astype(jnp.float32)).astype(jnp.bfloat16)
    return high, low


def unpair(value):
    value = value.astype(jnp.float32)
    return value[:, :E] + value[:, E:]


def excl_cumsum(value, axis):
    return jnp.cumsum(value, axis) - value


class Plan:
    def __init__(self, tokens, seq_len, local):
        seqs = tokens // seq_len
        self.tokens, self.local = tokens, local
        self.blocks = tokens // TB
        per_seq = seq_len // TB
        worst = min(CG + (GR - 1) * per_seq, seq_len)
        self.cap = ceil_to(seqs * worst // GR * GR, TILE)
        groups = (seqs * local * CG + self.blocks * local * (GR - 1)) // GR
        self.slots = ceil_to(TB * TOP * local // E + local * GR, 64)
        self.items = groups * GR // self.slots + self.blocks
        self.tiles = self.cap // TILE


def pick_at(here, table):
    return jnp.sum(jnp.where(here, table[None, :], 0), 1)


def steps_of(size, steps):
    first = excl_cumsum(steps, 0)
    used = jnp.sum(steps)
    index = jnp.minimum(jnp.arange(size), used - 1)
    owner = jnp.sum((first[None, :] <= index[:, None]).astype(jnp.int32), 1) - 1
    here = owner[:, None] == jnp.arange(steps.shape[0])[None, :]
    part = index - pick_at(here, first)
    last = (part == pick_at(here, steps) - 1).astype(jnp.int32)
    return first, used, owner, part, last, here


def routing(plan, routes, base):
    local, blocks = plan.local, plan.blocks
    mine = base + jnp.arange(local)
    picked = jnp.any(routes[:, :, None] == mine[None, None, :], 1)
    grid = picked.reshape(blocks, TB, local)
    ones = grid.astype(jnp.bfloat16)
    earlier = (jnp.arange(TB)[:, None] > jnp.arange(TB)[None, :]).astype(jnp.bfloat16)
    rank = jnp.einsum("ts,bse->bte", earlier, ones, preferred_element_type=jnp.float32).astype(
        jnp.int32
    )
    count = jnp.sum(grid.astype(jnp.int32), 1)
    groups = (count + GR - 1) // GR
    inner = excl_cumsum(groups, 1)
    total = jnp.sum(groups, 1)
    outer = excl_cumsum(groups, 0)
    expert_rows = jnp.sum(groups, 0) * GR
    place = jnp.where(grid, inner[:, None, :] * GR + rank, -1)
    items = jnp.maximum((total * GR + plan.slots - 1) // plan.slots, 1)
    first, used, block, part, last, here = steps_of(plan.items, items)
    wide, slots = plan.slots // GR, plan.cap // GR
    spot = jnp.arange(slots)[None, :, None]
    low = outer.T[:, None, :]
    inside = (spot >= low) & (spot < low + groups.T[:, None, :])
    origin = first[None, :] * wide + inner.T
    source = jnp.sum(jnp.where(inside, origin[:, None, :] + spot - low, 0), 2)
    tiles = jnp.maximum((expert_rows + TILE - 1) // TILE, 1)
    _, tiles_used, owner, tile, tile_last, _ = steps_of(local * plan.tiles, tiles)

    def at_block(table):
        return jnp.sum(jnp.where(here[:, :, None], table[None], 0), 1)[:, None, :]

    spot = (part[:, None] * wide + jnp.arange(wide)[None, :])[:, :, None]
    low, many, begin = at_block(inner), at_block(groups), at_block(outer)
    inside = (spot >= low) & (spot < low + many)
    target = jnp.sum(
        jnp.where(inside, (jnp.arange(local) * slots)[None, None, :] + begin + spot - low, 0), 2
    )
    return dict(
        place=place,
        used=used[None],
        block=block,
        part=part,
        last=last,
        source=source.reshape(-1),
        filled=expert_rows,
        tiles_used=tiles_used[None],
        owner=owner,
        tile=tile,
        tile_last=tile_last,
        target=target.reshape(-1),
    )


def while_used(step, used, *refs):
    @pl.when(pl.program_id(0) < used[0])
    def _():
        step(used, *refs)


def dispatch_step(used, block, part, post, grad, router, place, *refs):
    rows, share, held = refs[len(refs) // 2 - 1], refs[len(refs) // 2], refs[-1]
    step = pl.program_id(0)
    local = place.shape[1]
    slots = rows.shape[0]

    @pl.when(part[step] == 0)
    def _():
        portion = jax.nn.softmax(nn_dot(post[...], router[...]), -1)
        high, low = pair(portion)
        both = jnp.concatenate([high, low], 1)
        held[...] = both
        share[...] = both

    slot = lax.broadcasted_iota(jnp.int32, (slots, TB), 0) + part[step] * slots
    hit = slot == place[0, 0:1, :]
    for one in range(1, local):
        hit = hit | (slot == place[0, one : one + 1, :])
    pick = jnp.where(hit, 1.0, 0.0).astype(jnp.bfloat16)
    rows[:, :D] = nn_dot(pick, post[...]).astype(jnp.bfloat16)
    rows[:, D : 2 * D] = nn_dot(pick, grad[...]).astype(jnp.bfloat16)
    rows[:, 2 * D :] = nn_dot(pick, held[...]).astype(jnp.bfloat16)


def dispatch(plan, route, post, grad, router, later):
    wide = 2 * D + EXTRA
    place = route["place"].transpose(0, 2, 1)

    def at_block(step, used, block, part):
        return (block[step], 0)

    return pl.pallas_call(
        functools.partial(while_used, dispatch_step),
        grid_spec=pltpu.PrefetchScalarGridSpec(
            num_scalar_prefetch=3,
            grid=(plan.items,),
            in_specs=[
                pl.BlockSpec((TB, D), at_block),
                pl.BlockSpec((TB, D), at_block),
                pl.BlockSpec((D, E), lambda step, used, block, part: (0, 0)),
                pl.BlockSpec((1, plan.local, TB), lambda step, used, block, part: (block[step], 0, 0)),
            ]
            + [pl.BlockSpec(memory_space=pl.ANY)] * len(later),
            out_specs=[
                pl.BlockSpec((plan.slots, wide), lambda step, used, block, part: (jnp.minimum(step, used[0] - 1), 0)),
                pl.BlockSpec((TB, EXTRA), at_block),
            ]
            + [pl.BlockSpec(memory_space=pl.ANY)] * len(later),
            scratch_shapes=[pltpu.VMEM((TB, EXTRA), jnp.bfloat16)],
        ),
        out_shape=[
            jax.ShapeDtypeStruct((plan.items * plan.slots, wide), jnp.bfloat16),
            jax.ShapeDtypeStruct((plan.tokens, EXTRA), jnp.bfloat16),
        ]
        + [jax.ShapeDtypeStruct(one.shape, one.dtype) for one in later],
        input_output_aliases={7 + index: 2 + index for index in range(len(later))},
        compiler_params=pltpu.CompilerParams(vmem_limit_bytes=VMEM),
        cost_estimate=transfer(45),
        name="dispatch",
    )(route["used"], route["block"], route["part"], post, grad, router, place, *later)


def fetch_groups(table, rows, held, sems, step, count):
    slot = lax.rem(step, 2)
    for index in range(count):
        group = table[step * count + index]
        pltpu.make_async_copy(
            rows.at[pl.ds(pl.multiple_of(group * GR, GR), GR)],
            held.at[slot, pl.ds(index * GR, GR)],
            sems.at[slot],
        ).start()


def await_groups(rows, held, sems, step, count):
    slot = lax.rem(step, 2)
    pltpu.make_async_copy(rows.at[pl.ds(0, count * GR)], held.at[slot], sems.at[slot]).wait()


def next_groups(used, table, rows, held, sems, count):
    step = pl.program_id(0)

    @pl.when(step == 0)
    def _():
        fetch_groups(table, rows, held, sems, step, count)

    @pl.when(step + 1 < used[0])
    def _():
        fetch_groups(table, rows, held, sems, step + 1, count)

    await_groups(rows, held, sems, step, count)
    return lax.rem(step, 2)


def expert_step(
    used, source, owner, tile, last, filled, base, all_rows, w_gate, w_up, w_down, *refs
):
    *before, result, gate_out, up_out, down_out, held, sems, gate_sum, up_sum, down_sum = refs
    step = pl.program_id(0)
    count = TILE // GR
    slot = next_groups(used, source, all_rows, held, sems, count)
    expert, part = owner[step], tile[step]

    @pl.when(part == 0)
    def _():
        gate_sum[...] = jnp.zeros_like(gate_sum)
        up_sum[...] = jnp.zeros_like(up_sum)
        down_sum[...] = jnp.zeros_like(down_sum)

    @pl.when(last[step] == 1)
    def _():
        def clear(index, carry):
            at = pl.ds(pl.multiple_of(index * GR, GR), GR)
            held[slot, at, :] = jnp.zeros((GR, held.shape[2]), held.dtype)
            return carry

        lax.fori_loop((filled[expert] - part * TILE) // GR, count, clear, 0)

    number = base[0] + expert
    rows, upstream = held[slot, :, :D], held[slot, :, D : 2 * D]
    shares = held[slot, :, 2 * D :]
    lane = lax.broadcasted_iota(jnp.int32, (TILE, EXTRA), 1)
    own = (lane == number) | (lane == number + E)
    gate = jnp.sum(jnp.where(own, shares.astype(jnp.float32), 0.0), -1, keepdims=True)
    gate_pre = nn_dot(rows, w_gate[0])
    up_pre = nn_dot(rows, w_up[0])
    plain = nn_dot(upstream, w_down[0])
    squash = jax.nn.sigmoid(gate_pre)
    swish = gate_pre * squash
    active = (swish * up_pre).astype(jnp.bfloat16).astype(jnp.float32)
    change = jnp.sum(active * plain, -1, keepdims=True)
    grad_active = gate * plain
    grad_gate = (grad_active * up_pre * squash * (1.0 + gate_pre * (1.0 - squash))).astype(
        jnp.bfloat16
    )
    grad_up = (grad_active * swish).astype(jnp.bfloat16)
    scaled = (gate * active).astype(jnp.bfloat16)
    result[:, :D] = nt_dot(scaled, w_down[0]).astype(jnp.bfloat16)
    result[:, D : 2 * D] = (nt_dot(grad_gate, w_gate[0]) + nt_dot(grad_up, w_up[0])).astype(
        jnp.bfloat16
    )
    high, low = pair(change)
    result[:, 2 * D :] = jnp.where(
        lane == number,
        high.astype(jnp.float32),
        jnp.where(lane == number + E, low.astype(jnp.float32), 0.0),
    ).astype(jnp.bfloat16)
    gate_sum[...] += tn_dot(grad_gate, rows)
    up_sum[...] += tn_dot(grad_up, rows)
    down_sum[...] += tn_dot(scaled, upstream)

    @pl.when(last[step] == 1)
    def _():
        for index, (out, total) in enumerate(
            ((gate_out, gate_sum), (up_out, up_sum), (down_out, down_sum))
        ):
            out[0] = total[...].T + before[index][0] if before else total[...].T


def experts(plan, route, base, rows, w_gate, w_up, w_down, before):
    wide = 2 * D + EXTRA
    width = w_gate.shape[2]
    slots, count = plan.cap // GR, TILE // GR
    table = route["source"].reshape(plan.local * plan.tiles, count)
    number = route["owner"] * (slots // count) + route["tile"]
    table = table[number].reshape(-1)

    def whole(step, used, table, owner, tile, last, filled, base):
        return (owner[step], 0, 0)

    def tile_at(step, used, table, owner, tile, last, filled, base):
        return (owner[step] * plan.tiles + tile[step], 0)

    weight = pl.BlockSpec((1, D, width), whole)
    total = plan.local * plan.cap
    return pl.pallas_call(
        functools.partial(while_used, expert_step),
        grid_spec=pltpu.PrefetchScalarGridSpec(
            num_scalar_prefetch=7,
            grid=(plan.local * plan.tiles,),
            in_specs=[pl.BlockSpec(memory_space=pl.ANY)] + [weight] * (3 + len(before)),
            out_specs=[pl.BlockSpec((TILE, wide), tile_at)] + [weight] * 3,
            scratch_shapes=[
                pltpu.VMEM((2, TILE, wide), jnp.bfloat16),
                pltpu.SemaphoreType.DMA((2,)),
            ]
            + [pltpu.VMEM((width, D), jnp.float32)] * 3,
        ),
        out_shape=[jax.ShapeDtypeStruct((total, wide), jnp.bfloat16)]
        + [jax.ShapeDtypeStruct((plan.local, D, width), jnp.float32)] * 3,
        compiler_params=pltpu.CompilerParams(vmem_limit_bytes=VMEM),
        input_output_aliases={11 + index: 1 + index for index in range(len(before))},
        cost_estimate=transfer(80),
        name="experts",
    )(
        route["tiles_used"],
        table,
        route["owner"],
        route["tile"],
        route["tile_last"],
        route["filled"],
        base[None],
        rows,
        w_gate,
        w_up,
        w_down,
        *before,
    )


def combine_step(
    used, target, block, part, last, results, place, share, post, router, *refs
):
    held, sems, sums = refs[-3:]
    passing = (len(refs) - 6) // 2
    out, grad, router_out = refs[passing : passing + 3]
    step = pl.program_id(0)
    local = place.shape[1]
    slots = held.shape[1]

    at = next_groups(used, target, results, held, sems, slots // GR)

    @pl.when(step == 0)
    def _():
        router_out[...] = jnp.zeros_like(router_out)

    slot = lax.broadcasted_iota(jnp.int32, (TB, slots), 1) + part[step] * slots
    hit = slot == place[:, 0:1]
    for one in range(1, local):
        hit = hit | (slot == place[:, one : one + 1])
    pick = jnp.where(hit, 1.0, 0.0).astype(jnp.bfloat16)

    def term(begin, end):
        return nn_dot(pick, held[at, :, begin:end])

    def finish(value):
        change = unpair(value(2 * D, 2 * D + EXTRA))
        portion = unpair(share[...])
        moved = portion * (change - jnp.sum(change * portion, -1, keepdims=True))
        moved = moved.astype(jnp.bfloat16)
        out[...] = value(0, D).astype(jnp.bfloat16)
        grad[...] = (value(D, 2 * D) + nt_dot(moved, router[...])).astype(jnp.bfloat16)
        router_out[...] += tn_dot(moved, post[...])

    single = (part[step] == 0) & (last[step] == 1)

    @pl.when(single)
    def _():
        finish(term)

    @pl.when(jnp.logical_not(single))
    def _():
        @pl.when(part[step] == 0)
        def _():
            sums[...] = jnp.zeros_like(sums)

        sums[...] += term(0, 2 * D + EXTRA)

        @pl.when(last[step] == 1)
        def _():
            finish(lambda begin, end: sums[:, begin:end])


def combine(plan, route, results, share, post, router, later):
    wide = 2 * D + EXTRA

    def at_block(step, used, target, block, part, last):
        return (block[step], 0)

    def fixed(step, used, target, block, part, last):
        return (0, 0)

    return pl.pallas_call(
        functools.partial(while_used, combine_step),
        grid_spec=pltpu.PrefetchScalarGridSpec(
            num_scalar_prefetch=5,
            grid=(plan.items,),
            in_specs=[
                pl.BlockSpec(memory_space=pl.ANY),
                pl.BlockSpec((TB, plan.local), at_block),
                pl.BlockSpec((TB, EXTRA), at_block),
                pl.BlockSpec((TB, D), at_block),
                pl.BlockSpec((D, E), fixed),
            ]
            + [pl.BlockSpec(memory_space=pl.ANY)] * len(later),
            out_specs=[
                pl.BlockSpec((TB, D), at_block),
                pl.BlockSpec((TB, D), at_block),
                pl.BlockSpec((E, D), fixed),
            ]
            + [pl.BlockSpec(memory_space=pl.ANY)] * len(later),
            scratch_shapes=[
                pltpu.VMEM((2, plan.slots, wide), jnp.bfloat16),
                pltpu.SemaphoreType.DMA((2,)),
                pltpu.VMEM((TB, wide), jnp.float32),
            ],
        ),
        out_shape=[
            jax.ShapeDtypeStruct((plan.tokens, D), jnp.bfloat16),
            jax.ShapeDtypeStruct((plan.tokens, D), jnp.bfloat16),
            jax.ShapeDtypeStruct((E, D), jnp.float32),
        ]
        + [jax.ShapeDtypeStruct(one.shape, one.dtype) for one in later],
        input_output_aliases={10 + index: 3 + index for index in range(len(later))},
        compiler_params=pltpu.CompilerParams(vmem_limit_bytes=VMEM),
        cost_estimate=transfer(50),
        name="combine",
    )(
        route["used"],
        route["target"],
        route["block"],
        route["part"],
        route["last"],
        results,
        route["place"].reshape(plan.tokens, plan.local),
        share,
        post,
        router,
        *later,
    )


def gather_halves(own):
    if lax.axis_size("dp") == 8:
        return box_gather(own)
    few = own.shape[0] // 2
    return [gather_slowly(own[:few]), gather_slowly(own[few:])]


def gather_slowly(own):
    if lax.axis_size("dp") == 8:
        return lax.all_gather(own, ("dp", "tensor"), axis=0, tiled=True)
    return lax.all_gather(
        lax.all_gather(own, "tensor", axis=0, tiled=True), "dp", axis=0, tiled=True
    )


def gather_output(own):
    n = lax.axis_size("tensor")
    if lax.axis_size("dp") == 8:
        everything = lax.all_gather(own, ("dp", "tensor"), axis=0, tiled=False)
        everything = everything.reshape((8, n) + own.shape).transpose(1, 0, 2, 3)
        return everything.reshape(n, -1, own.shape[1])
    part = lax.all_gather(own, "dp", axis=0, tiled=True)
    return lax.all_gather(part, "tensor", axis=0, tiled=False)


def sum_last(tokens, parts, later):
    n = lax.axis_size("tensor")
    if lax.axis_size("dp") == 8:
        return closing(
            tokens.reshape(n, -1, tokens.shape[1]),
            parts.reshape(parts.shape[0], 8, -1, parts.shape[2]),
            later,
        )
    tokens, later = chain_sum(tokens, later, 8)
    parts = lax.psum_scatter(parts, "dp", scatter_dimension=1, tiled=True)
    own = lax.psum_scatter(parts[:n], "tensor", scatter_dimension=0, tiled=True)
    return tokens, jnp.concatenate([own, parts[n:]]).astype(jnp.float32), later


def sum_all(part, tokens, later):
    if lax.axis_size("dp") == 8:
        return box_sum(part, tokens, later)
    tokens = lax.psum_scatter(tokens, "tensor", scatter_dimension=0, tiled=True)
    return sum_slowly(part).astype(jnp.float32), tokens.astype(jnp.float32), later


def sum_slowly(part):
    part = lax.psum_scatter(part, "dp", scatter_dimension=0, tiled=True)
    return lax.psum_scatter(part, "tensor", scatter_dimension=0, tiled=True)


def fill(value, rows, columns):
    return jnp.pad(value, ((0, rows - value.shape[0]), (0, columns - value.shape[1])))


def pack_small(router, prenorm, postnorm, querynorm, keynorm, routes):
    n = lax.axis_size("tensor")
    rank = lax.axis_index("tensor")
    rows = router.shape[0]
    head = ceil_to(max(rows, querynorm.shape[0]), 16)
    heads = querynorm.shape[1]
    block = jnp.concatenate(
        [
            fill(router, head, E),
            fill(prenorm[:, None], head, 1),
            fill(postnorm[:, None], head, 1),
            fill(querynorm, head, heads),
            fill(keynorm, head, heads),
        ],
        1,
    )
    part = routes.shape[0] // n
    own = lax.dynamic_slice_in_dim(routes, rank * part, part, 0)
    own = own.astype(jnp.bfloat16).reshape(-1, 128)
    tail = ceil_to(own.shape[0], 16)
    return jnp.concatenate([fill(block, head, 128), fill(own, tail, 128)], 0)


def unpack_small(everything, router, querynorm, routes):
    n = lax.axis_size("tensor")
    rank = lax.axis_index("tensor")
    rows, heads = router.shape[0], querynorm.shape[1]
    head = ceil_to(max(rows, querynorm.shape[0]), 16)
    part = routes.size // n // 128
    total = everything.shape[1]
    mine = everything.reshape(-1, n, total, 128)[:, rank]
    at = E + 2
    return (
        everything[:, :rows, :E].reshape(-1, E),
        everything[:, :rows, E].reshape(-1).astype(jnp.float32),
        everything[:, :rows, E + 1].reshape(-1).astype(jnp.float32),
        mine[:, : querynorm.shape[0], at : at + heads].reshape(-1, heads),
        mine[:, : querynorm.shape[0], at + heads : at + 2 * heads].reshape(-1, heads),
        everything[:, head : head + part].reshape(-1, TOP).astype(jnp.int32),
    )


def body(
    hidden_in,
    out_grad,
    doc_ids,
    expert_ids,
    prenorm,
    querynorm,
    keynorm,
    query_proj,
    key_proj,
    value_proj,
    output_proj,
    postnorm,
    router,
    gate_proj,
    up_proj,
    down_proj,
):
    residual = hidden_in[0].astype(jnp.float32)
    upstream = out_grad[0]
    documents = doc_ids[0]
    routes = expert_ids[0]
    shard = residual.shape[0]
    seq_len = documents.shape[0]
    mesh_dp = lax.axis_size("dp")
    block = min(seq_len, 1024)
    scale = HD ** (-0.5)
    cosine, sine = rope_tables(seq_len, HD)
    small = pack_small(router, prenorm, postnorm, querynorm, keynorm, routes)
    group_hidden, later, output_late, everything = chain_gather(
        hidden_in[0], [upstream[: shard // 2], output_proj], 1, small
    )
    router_full, pre_gain, post_gain, gain_query, gain_key, all_routes = unpack_small(
        everything, router, querynorm, routes
    )
    weights = lax.all_gather(
        jnp.concatenate([query_proj, key_proj, value_proj], 1),
        "dp",
        axis=0,
        tiled=True,
    )
    w_query, w_key, w_value = jnp.split(weights, 3, 1)
    w_output = gather_output(output_late)
    heads = w_query.shape[1] // HD
    query_scale = gain_query.astype(jnp.float32).T.reshape(-1)
    key_scale = gain_key.astype(jnp.float32).T.reshape(-1)
    inv_pre = lax.rsqrt(jnp.mean(residual * residual, -1, keepdims=True) + epsilon)
    group_hidden = group_hidden.astype(jnp.float32)
    group_inv = lax.rsqrt(jnp.mean(group_hidden * group_hidden, -1, keepdims=True) + epsilon)
    group_normed = (group_hidden * group_inv * pre_gain).astype(jnp.bfloat16)
    n = lax.axis_size("tensor")
    few = shard // 2
    plan = Plan(mesh_dp * n * few, n * few, gate_proj.shape[0])
    base = (lax.axis_index("dp") * plan.local).astype(jnp.int32)
    all_routes = all_routes.reshape(mesh_dp, n, 2, few, TOP)
    both = jnp.moveaxis(all_routes, 2, 0).reshape(2, -1, TOP)
    both = jax.vmap(lambda routes: routing(plan, routes, base))(both)
    route = [{name: value[index] for name, value in both.items()} for index in range(2)]
    all_grad = [gather_slowly(later)]
    query = jnp.dot(group_normed, w_query, preferred_element_type=jnp.float32)
    keys = jnp.dot(group_normed, w_key, preferred_element_type=jnp.float32)
    values = jnp.dot(group_normed, w_value, preferred_element_type=jnp.float32).astype(jnp.bfloat16)
    query_sq, key_sq = sum_heads(
        (jnp.sum(query * query, -1, keepdims=True), jnp.sum(keys * keys, -1, keepdims=True))
    )
    inv_query = lax.rsqrt(query_sq / D + epsilon)
    inv_key = lax.rsqrt(key_sq / D + epsilon)
    query_heads = (query * inv_query * query_scale).reshape(seq_len, heads, HD)
    key_heads = (keys * inv_key * key_scale).reshape(seq_len, heads, HD)
    query_rot = (query_heads * cosine[:, None] + rotate(query_heads) * sine[:, None]).astype(
        jnp.bfloat16
    )
    key_rot = (key_heads * cosine[:, None] + rotate(key_heads) * sine[:, None]).astype(jnp.bfloat16)
    value_heads = values.reshape(seq_len, heads, HD)
    mixed, logsum = attend_forward(query_rot, key_rot, value_heads, documents, block, scale)
    mixed_flat = mixed.reshape(seq_len, heads * HD)
    mixed_own, later = swap(mixed_flat.reshape(n, shard, heads * HD), upstream[few:], 7)
    all_grad.append(gather_slowly(later))
    attn_local = sum(nt_dot(mixed_own[index], w_output[index]) for index in range(n))
    middle = residual + attn_local
    inv_post = lax.rsqrt(jnp.mean(middle * middle, -1, keepdims=True) + epsilon)
    post_normed = (middle * inv_post * post_gain).astype(jnp.bfloat16)
    all_post = gather_halves(post_normed)
    grads, outs, backs, router_parts = [], [], [], []
    for index in range(2):
        rows, portion, *outs = dispatch(
            plan, route[index], all_post[index], all_grad[index], router_full, outs
        )
        results, *grads = experts(
            plan, route[index], base, rows, gate_proj, up_proj, down_proj, grads
        )
        if index == 0:
            later = [all_grad[1]]
        else:
            later = [lax.psum_scatter(backs[0], "dp", scatter_dimension=0, tiled=True)]
        out, back, router_part, *later = combine(
            plan, route[index], results, portion, all_post[index], router_full, later
        )
        if index == 0:
            all_grad[1] = later[0]
        else:
            early = later[0]
        outs.append(out)
        backs.append(back)
        router_parts.append(router_part)
    gate_weight_grad, up_weight_grad, down_weight_grad = grads
    first_out = lax.psum_scatter(outs[0], "dp", scatter_dimension=0, tiled=True)
    late, early, outs = sum_all(backs[1], early, outs[1:])
    grad_post = jnp.concatenate([early, late], 0)
    second_out = lax.psum_scatter(outs[0], "dp", scatter_dimension=0, tiled=True)
    router_part = router_parts[0] + router_parts[1]
    router_part = router_part.T
    post_gain_part = jnp.sum(grad_post * middle * inv_post, 0)
    grad_middle = upstream.astype(jnp.float32) + norm_back(
        grad_post, middle, inv_post, post_gain, D
    )
    change = grad_middle.astype(jnp.bfloat16)
    grad_mixed, first_out = swap(
        jnp.stack([nn_dot(change, w_output[index]).astype(jnp.bfloat16) for index in range(n)]),
        first_out,
        2,
    )
    moe_local = lax.psum_scatter(
        jnp.concatenate(
            [first_out.reshape(n, few, D), second_out.reshape(n, few, D)], 1
        ).reshape(-1, D),
        "tensor",
        scatter_dimension=0,
        tiled=True,
    )
    output_parts = [tn_dot(change, mixed_own[index]).astype(jnp.bfloat16) for index in range(n)]
    grad_query_rot, grad_key_rot, grad_value_heads = attend_backward(
        query_rot,
        key_rot,
        value_heads,
        documents,
        logsum,
        grad_mixed.reshape(seq_len, heads, HD),
        block,
        scale,
    )
    grad_query_flat = (
        grad_query_rot * cosine[:, None] + rotate_back(grad_query_rot * sine[:, None])
    ).reshape(seq_len, -1)
    grad_key_flat = (
        grad_key_rot * cosine[:, None] + rotate_back(grad_key_rot * sine[:, None])
    ).reshape(seq_len, -1)
    query_inner, key_inner = sum_heads(
        (
            jnp.sum(grad_query_flat * query_scale * query, -1, keepdims=True),
            jnp.sum(grad_key_flat * key_scale * keys, -1, keepdims=True),
        )
    )
    grad_query = (
        inv_query * query_scale * grad_query_flat - query * inv_query**3 * query_inner / D
    ).astype(jnp.bfloat16)
    grad_key = (inv_key * key_scale * grad_key_flat - keys * inv_key**3 * key_inner / D).astype(
        jnp.bfloat16
    )
    query_gain_part = jnp.sum(grad_query_flat * query * inv_query, 0).reshape(heads, HD).T
    key_gain_part = jnp.sum(grad_key_flat * keys * inv_key, 0).reshape(heads, HD).T
    grad_value = grad_value_heads.reshape(seq_len, -1).astype(jnp.bfloat16)
    query_part = lax.dot_general(
        group_normed, grad_query, (((0,), (0,)), ((), ())), preferred_element_type=jnp.float32
    )
    key_part = lax.dot_general(
        group_normed, grad_key, (((0,), (0,)), ((), ())), preferred_element_type=jnp.float32
    )
    value_part = lax.dot_general(
        group_normed, grad_value, (((0,), (0,)), ((), ())), preferred_element_type=jnp.float32
    )
    normed_term = lax.dot_general(
        grad_query, w_query, (((1,), (1,)), ((), ())), preferred_element_type=jnp.float32
    )
    normed_term = normed_term + lax.dot_general(
        grad_key, w_key, (((1,), (1,)), ((), ())), preferred_element_type=jnp.float32
    )
    normed_term = normed_term + lax.dot_general(
        grad_value, w_value, (((1,), (1,)), ((), ())), preferred_element_type=jnp.float32
    )
    grad_normed, weight_sums, middle = sum_last(
        normed_term.astype(jnp.bfloat16),
        jnp.stack(
            output_parts + [part.astype(jnp.bfloat16) for part in (query_part, key_part, value_part)]
        ),
        middle,
    )
    layer_out = (middle + moe_local.astype(jnp.float32)).astype(jnp.bfloat16)[None]
    pre_gain_part = jnp.sum(grad_normed * residual * inv_pre, 0)
    input_grad = (grad_middle + norm_back(grad_normed, residual, inv_pre, pre_gain, D)).astype(
        jnp.bfloat16
    )[None]
    gains = jnp.concatenate([query_gain_part, key_gain_part], 1).reshape(mesh_dp, 1, -1, 2 * heads)
    mine = jnp.arange(n)[None, :, None, None] == lax.axis_index("tensor")
    gains = jnp.pad(
        jnp.where(mine, gains, 0.0),
        ((0, 0), (0, 0), (0, max(router.shape[0] - HD // mesh_dp, 0)), (0, 0)),
    ).reshape(D, 2 * heads)
    own = router.shape[0]
    block = jnp.concatenate(
        [router_part, gains, jnp.zeros((D, 128 - E - 2 * heads), jnp.float32)], 1
    )
    block = jnp.pad(block.reshape(-1, own, 128), ((0, 0), (0, 8), (0, 0)))
    block = block.at[:, own, :own].set(post_gain_part.reshape(-1, own))
    small = sum_spread(block.at[:, own + 1, :own].set(pre_gain_part.reshape(-1, own)))
    gain_grads = small[: HD // mesh_dp, E : E + 2 * heads]
    return (
        layer_out,
        input_grad,
        small[own + 1, :own],
        gain_grads[:, :heads],
        gain_grads[:, heads : 2 * heads],
        weight_sums[1],
        weight_sums[2],
        weight_sums[3],
        weight_sums[0],
        small[own, :own],
        small[:own, :E],
        gate_weight_grad,
        up_weight_grad,
        down_weight_grad,
    )


def solution(mesh):
    in_specs = (
        P("dp", "tensor", None),
        P("dp", "tensor", None),
        P("dp", None),
        P("dp", None, None),
        P(("dp", "tensor")),
        P("dp", "tensor"),
        P("dp", "tensor"),
        P("dp", "tensor"),
        P("dp", "tensor"),
        P("dp", "tensor"),
        P("dp", "tensor"),
        P(("dp", "tensor")),
        P(("dp", "tensor"), None),
        P("dp", None, "tensor"),
        P("dp", None, "tensor"),
        P("dp", None, "tensor"),
    )
    out_specs = (
        P("dp", "tensor", None),
        P("dp", "tensor", None),
        P(("dp", "tensor")),
        P("dp", "tensor"),
        P("dp", "tensor"),
        P("dp", "tensor"),
        P("dp", "tensor"),
        P("dp", "tensor"),
        P("dp", "tensor"),
        P(("dp", "tensor")),
        P(("dp", "tensor"), None),
        P("dp", None, "tensor"),
        P("dp", None, "tensor"),
        P("dp", None, "tensor"),
    )
    return jax.shard_map(body, mesh=mesh, in_specs=in_specs, out_specs=out_specs, check_vma=False)
```

```python
import functools

import jax
import jax.numpy as jnp
from jax import lax
from jax.experimental import pallas as pl
from jax.experimental.pallas import tpu as pltpu
from jax.sharding import PartitionSpec as P

D = 2048
HD = 128
E = 64
TOP = 8
CG = 192


epsilon = 1e-05
masked_score = -1000000000.0


def rope_tables(length, width):
    positions = jnp.arange(length).astype(jnp.float32)
    rates = 10000.0 ** (-jnp.arange(0, width, 2).astype(jnp.float32) / width)
    angles = positions[:, None] * rates[None, :]
    return (jnp.concatenate([jnp.cos(angles)] * 2, -1), jnp.concatenate([jnp.sin(angles)] * 2, -1))


def rotate(tensor):
    half = tensor.shape[-1] // 2
    return jnp.concatenate([-tensor[..., half:], tensor[..., :half]], -1)


def rotate_back(tensor):
    half = tensor.shape[-1] // 2
    return jnp.concatenate([tensor[..., half:], -tensor[..., :half]], -1)


def sum_heads(parts):
    return lax.psum((parts[0], parts[1]), "tensor")


def norm_back(grad, value, inverse, gain, width):
    scaled = grad * gain
    inner = jnp.sum(scaled * value, -1, keepdims=True)
    return inverse * scaled - value * inverse**3 * inner / width


def block_scores(query, keys, documents, start, block, scale):
    row_place = start + jnp.arange(block)
    col_place = jnp.arange(documents.shape[0])
    allowed = (documents[:, None] == documents[None, :]) & (
        row_place[:, None] >= col_place[None, :]
    )
    scores = jnp.einsum("qhd,khd->hqk", query, keys, preferred_element_type=jnp.float32) * scale
    return (jnp.where(allowed[None], scores, masked_score), query)


def attend_forward(query, keys, values, documents, block, scale):
    count = query.shape[0] // block

    def one(index):
        scores, rows = block_scores(query, keys, documents, index * block, block, scale)
        peak = jnp.max(scores, -1, keepdims=True)
        weights = jnp.exp(scores - peak)
        total = jnp.sum(weights, -1, keepdims=True)
        portion = (weights / total).astype(jnp.bfloat16)
        mixed = jnp.einsum("hqk,khd->qhd", portion, values, preferred_element_type=jnp.float32)
        return (mixed.astype(jnp.bfloat16), peak + jnp.log(total))

    mixed, logsum = lax.map(one, jnp.arange(count))
    return (mixed.reshape(query.shape), logsum)


def attend_backward(query, keys, values, documents, logsum, grad_mixed, block, scale):
    count = query.shape[0] // block

    def one(index):
        start = index * block
        scores, rows = block_scores(query, keys, documents, start, block, scale)
        portion = jnp.exp(scores - logsum[index])
        grad_portion = jnp.einsum(
            "qhd,khd->hqk", grad_mixed, values, preferred_element_type=jnp.float32
        )
        center = jnp.sum(portion * grad_portion, -1, keepdims=True)
        grad_scores = (portion * (grad_portion - center)).astype(jnp.bfloat16)
        grad_values = jnp.einsum(
            "hqk,qhd->khd",
            portion.astype(jnp.bfloat16),
            grad_mixed,
            preferred_element_type=jnp.float32,
        )
        grad_query = (
            jnp.einsum("hqk,khd->qhd", grad_scores, keys, preferred_element_type=jnp.float32)
            * scale
        )
        grad_keys = (
            jnp.einsum("hqk,qhd->khd", grad_scores, rows, preferred_element_type=jnp.float32)
            * scale
        )
        return (grad_query, grad_keys, grad_values)

    grad_query, grad_keys, grad_values = lax.map(one, jnp.arange(count))
    return (grad_query.reshape(query.shape), jnp.sum(grad_keys, 0), jnp.sum(grad_values, 0))


MESH = pl.DeviceIdType.MESH
VMEM = 60 * 1024 * 1024


def transfer(microseconds):
    return pl.CostEstimate(flops=0, bytes_accessed=microseconds * 3_000_000, transcendentals=0)


def flip(index, bit):
    return index + bit - 2 * bit * ((index // bit) % 2)


def send(source, target, send_sem, recv_sem, device):
    return pltpu.make_async_remote_copy(
        src_ref=source,
        dst_ref=target,
        send_sem=send_sem,
        recv_sem=recv_sem,
        device_id=device,
        device_id_type=MESH,
    )


def greet(devices, extra=()):
    barrier = pltpu.get_barrier_semaphore()
    for device in devices:
        pl.semaphore_signal(barrier, inc=1, device_id=device, device_id_type=MESH)
    for there, device in extra:

        @pl.when(there)
        def _(device=device):
            pl.semaphore_signal(barrier, inc=1, device_id=device, device_id_type=MESH)

    count = len(devices)
    for there, _ in extra:
        count = count + jnp.where(there, 1, 0)
    pl.semaphore_wait(barrier, count)


def both_ways(n):
    spot = lax.axis_index("tensor")
    return spot, (
        (spot < n - 1, {"tensor": jnp.minimum(spot + 1, n - 1)}),
        (spot > 0, {"tensor": jnp.maximum(spot - 1, 0)}),
    )


def shard_at(spot, way, distance, n):
    number = spot - distance if way == 0 else spot + distance
    return (number >= 0) & (number < n), jnp.clip(number, 0, n - 1)


def chain_gather_kernel(n, pieces, passing, own, *refs):
    refs = refs[passing:]
    if len(refs) > passing + 4:
        small, out, everything, *sems = refs[0], refs[1], refs[2 + passing], *refs[3 + passing :]
        local_sem, send_sem, recv_sem, all_send, all_recv = sems
        finish = spread_start(n, small, everything, all_send, all_recv)
    else:
        out, (local_sem, send_sem, recv_sem) = refs[0], refs[1 + passing :]
        finish = None
    spot, sides = both_ways(n)
    rows = own.shape[0] // pieces
    if finish is None:
        greet([], sides)
    keep = pltpu.make_async_copy(own, out.at[spot], local_sem)
    keep.start()

    def copy(way, distance, piece):
        there, number = shard_at(spot, way, distance, n)
        part = pl.ds(piece * rows, rows)
        source = own.at[part] if distance == 0 else out.at[number, part]
        return there & sides[way][0], send(
            source,
            out.at[number, part],
            send_sem.at[way, distance, piece],
            recv_sem.at[way, distance, piece],
            sides[way][1],
        )

    def arrived(way, distance, piece):
        there, number = shard_at(spot, way, distance, n)
        part = pl.ds(piece * rows, rows)

        @pl.when(there)
        def _():
            send(
                out.at[number, part],
                out.at[number, part],
                send_sem.at[way, distance - 1, piece],
                recv_sem.at[way, distance - 1, piece],
                sides[way][1],
            ).wait_recv()

    for distance in range(n):
        for piece in range(pieces):
            for way in (0, 1):
                if distance:
                    arrived(way, distance, piece)
                if distance < n - 1:
                    go, one = copy(way, distance, piece)

                    @pl.when(go)
                    def _(one=one):
                        one.start()

    keep.wait()
    for distance in range(n - 1):
        for piece in range(pieces):
            for way in (0, 1):
                go, one = copy(way, distance, piece)

                @pl.when(go)
                def _(one=one):
                    one.wait_send()

    if finish is not None:
        finish()


def chain_gather(own, later, number, small=None, pieces=4):
    n = lax.axis_size("tensor")
    rows, width = own.shape
    anywhere = pl.BlockSpec(memory_space=pl.ANY)
    inside = pl.BlockSpec(memory_space=pltpu.VMEM)
    sem = pltpu.SemaphoreType.DMA
    outs = [jax.ShapeDtypeStruct((n, rows, width), own.dtype)]
    outs += [jax.ShapeDtypeStruct(one.shape, one.dtype) for one in later]
    more, sems = [], []
    if small is not None:
        count = lax.axis_size("dp") * n
        outs.append(jax.ShapeDtypeStruct((count,) + small.shape, small.dtype))
        more, sems = [small], [sem((count,)), sem((count,))]
    plain = [anywhere] * (1 + len(later)) + [inside] * len(more)
    out, *rest = pl.pallas_call(
        functools.partial(chain_gather_kernel, n, pieces, len(later)),
        out_shape=outs,
        in_specs=plain,
        out_specs=plain,
        input_output_aliases={1 + index: 1 + index for index in range(len(later))},
        scratch_shapes=[sem, sem((2, n - 1, pieces)), sem((2, n - 1, pieces))] + sems,
        compiler_params=pltpu.CompilerParams(
            collective_id=number, has_side_effects=True, vmem_limit_bytes=VMEM
        ),
        cost_estimate=transfer(65),
        name="chain_gather",
    )(own, *later, *more)
    return (out.reshape(n * rows, width), *rest)


def add_into(target, source, rows, start=0, source_start=0):
    step = 16

    def body(index, carry):
        at = pl.ds(pl.multiple_of(start + index * step, step), step)
        come = pl.ds(pl.multiple_of(source_start + index * step, step), step)
        target[at, :] = (
            target[at, :].astype(jnp.float32) + source[come, :].astype(jnp.float32)
        ).astype(target.dtype)
        return carry

    lax.fori_loop(0, rows // step, body, 0)


def chain_sum_kernel(n, pieces, part, _later, out, _passed, held, send_sem, recv_sem):
    spot, sides = both_ways(n)
    greet([], sides)
    onward, finish, drain = chain_steps(n, pieces, part, out, held, send_sem, recv_sem)
    for far in range(n - 1, 0, -1):
        onward(far)
    finish()
    drain()


def chain_steps(n, pieces, part, out, held, send_sem, recv_sem):
    spot, sides = both_ways(n)
    rows = out.shape[0] // pieces

    def copy(way, far, piece, mine):
        number = spot + far if way == 0 else spot - far
        there = (number >= 0) & (number < n)
        number = jnp.clip(number, 0, n - 1)
        at = pl.ds(piece * rows, rows)
        source = part.at[number, at]
        return there, number, send(
            source if mine else held.at[way, far, at],
            held.at[way, far - 1, at],
            send_sem.at[way, far - 1, piece],
            recv_sem.at[way, far - 1, piece],
            sides[way][1],
        )

    def arrived(way, far, piece):
        at = pl.ds(piece * rows, rows)
        send(
            held.at[way, far, at],
            held.at[way, far, at],
            send_sem.at[way, far, piece],
            recv_sem.at[way, far, piece],
            sides[way][1],
        ).wait_recv()

    def onward(far):
        for piece in range(pieces):
            for way in (0, 1):
                behind = sides[1 - way][0]
                there, number, first = copy(way, far, piece, True)

                @pl.when(there & jnp.logical_not(behind))
                def _(first=first):
                    first.start()

                if far < n - 1:
                    _, _, again = copy(way, far, piece, False)

                    @pl.when(there & behind)
                    def _(way=way, piece=piece, number=number, again=again):
                        arrived(way, far, piece)
                        add_into(
                            held.at[way, far], part.at[number], rows, piece * rows, piece * rows
                        )
                        again.start()

    def finish():
        for piece in range(pieces):

            def body(index, carry, piece=piece):
                here = pl.ds(pl.multiple_of(piece * rows + index * 16, 16), 16)
                out[here, :] = part[spot, here, :].astype(jnp.float32)
                return carry

            lax.fori_loop(0, rows // 16, body, 0)
            for way in (0, 1):

                @pl.when(sides[1 - way][0])
                def _(way=way, piece=piece):
                    arrived(way, 0, piece)
                    add_into(out, held.at[way, 0], rows, piece * rows, piece * rows)

    def drain():
        for far in range(n - 1, 0, -1):
            for piece in range(pieces):
                for way in (0, 1):
                    there, _, one = copy(way, far, piece, True)

                    @pl.when(there)
                    def _(one=one):
                        one.wait_send()

    return onward, finish, drain


def chain_sum(part, later, number, pieces=4):
    n = lax.axis_size("tensor")
    width = part.shape[1]
    rows = part.shape[0] // n
    anywhere = pl.BlockSpec(memory_space=pl.ANY)
    inside = pl.BlockSpec(memory_space=pltpu.VMEM)
    return pl.pallas_call(
        functools.partial(chain_sum_kernel, n, pieces),
        out_shape=[
            jax.ShapeDtypeStruct((rows, width), jnp.float32),
            jax.ShapeDtypeStruct(later.shape, later.dtype),
        ],
        in_specs=[inside, anywhere],
        out_specs=[inside, anywhere],
        input_output_aliases={1: 1},
        scratch_shapes=[
            pltpu.VMEM((2, n - 1, rows, width), part.dtype),
            pltpu.SemaphoreType.DMA((2, n - 1, pieces)),
            pltpu.SemaphoreType.DMA((2, n - 1, pieces)),
        ],
        compiler_params=pltpu.CompilerParams(
            collective_id=number, has_side_effects=True, vmem_limit_bytes=VMEM
        ),
        cost_estimate=transfer(65),
        name="chain_sum",
    )(part.reshape(n, rows, width), later)


def box_devices():
    me = lax.axis_index("dp")
    return me, {bit: {"dp": flip(me, bit)} for bit in (1, 2, 4)}


def box_gather_kernel(n, own, out, local_sem, z_send, z_recv, near_send, near_recv, on_send, on_recv, side_send, side_recv):
    spot, sides = both_ways(n)
    me, near = box_devices()
    half = own.shape[0] // 2
    greet([near[1], near[2], near[4]], sides)
    keep = pltpu.make_async_copy(own, out.at[me, spot], local_sem)
    keep.start()
    sends = []

    def piece(seq, shard, part):
        return out.at[seq, shard, pl.ds(part * half, half)]

    def start(condition, one):
        sends.append((condition, one))

        @pl.when(condition)
        def _():
            one.start()

    def await_piece(condition, target, recv):
        @pl.when(condition)
        def _():
            send(target, target, side_send.at[0, 0, 0], recv, near[1]).wait_recv()

    def to_side(condition, slot, seq, shard, part, source):
        start(condition, send(source, piece(seq, shard, part), side_send.at[slot, shard, part], side_recv.at[slot, shard, part], near[1]))

    def mine(way, distance):
        there, shard = shard_at(spot, way, distance, n)
        for part in (0, 1):
            if distance:
                await_piece(there, piece(me, shard, part), z_recv.at[way, distance - 1, part])
            source = piece(me, shard, part) if distance else own.at[pl.ds(part * half, half)]
            for out_way in (0, 1) if distance == 0 else (way,):
                if distance < n - 1:
                    start(there & sides[out_way][0], send(source, piece(me, shard, part), z_send.at[out_way, distance, part], z_recv.at[out_way, distance, part], sides[out_way][1]))
            for axis, bit in ((0, 2), (1, 4)):
                start(there, send(source, piece(me, shard, part), near_send.at[axis, shard, part], near_recv.at[axis, shard, part], near[bit]))
            to_side(there, 0, me, shard, part, source)

    def nearby(way, distance):
        there, shard = shard_at(spot, way, distance, n)
        for part in (0, 1):
            for axis, bit in ((0, 2), (1, 4)):
                seq = flip(me, bit)
                source = piece(seq, shard, part)
                await_piece(there, source, near_recv.at[axis, shard, part])
                if part == axis:
                    start(there, send(source, source, on_send.at[1 - axis, shard], on_recv.at[1 - axis, shard], near[6 - bit]))
                to_side(there, 1 + axis, seq, shard, part, source)

    def far(way, distance):
        there, shard = shard_at(spot, way, distance, n)
        seq = flip(flip(me, 2), 4)
        for part in (0, 1):
            source = piece(seq, shard, part)
            await_piece(there, source, on_recv.at[1 - part, shard])
            to_side(there, 3, seq, shard, part, source)

    for step in range(n + 2):
        for task, delay in ((mine, 0), (nearby, 1), (far, 2)):
            distance = step - delay
            if 0 <= distance < n:
                for way in (0, 1) if distance else (0,):
                    task(way, distance)
    for shard in range(n):
        for part in (0, 1):
            for slot, bit in enumerate((0, 2, 4, 6)):
                seq = flip(me, 1)
                for one in (2, 4):
                    if bit & one:
                        seq = flip(seq, one)
                await_piece(spot >= 0, piece(seq, shard, part), side_recv.at[slot, shard, part])
    keep.wait()
    for condition, one in sends:

        @pl.when(condition)
        def _(one=one):
            one.wait_send()


def box_gather(own):
    n = lax.axis_size("tensor")
    rows, width = own.shape
    sem = pltpu.SemaphoreType.DMA
    out = pl.pallas_call(
        functools.partial(box_gather_kernel, n),
        out_shape=jax.ShapeDtypeStruct((8, n, rows, width), own.dtype),
        in_specs=[pl.BlockSpec(memory_space=pl.ANY)],
        out_specs=pl.BlockSpec(memory_space=pl.ANY),
        scratch_shapes=[sem]
        + [sem((2, n - 1, 2))] * 2
        + [sem((2, n, 2))] * 2
        + [sem((2, n))] * 2
        + [sem((4, n, 2))] * 2,
        compiler_params=pltpu.CompilerParams(collective_id=3, has_side_effects=True),
        cost_estimate=transfer(2),
        name="box_gather",
    )(own)
    return out.reshape(8 * n * rows, width)


def order_of(spot, n):
    table = [sorted(range(n), key=lambda s: -abs(s - j)) for j in range(n)]
    result = []
    for step in range(n):
        value = jnp.int32(table[0][step])
        for j in range(1, n):
            value = jnp.where(spot == j, table[j][step], value)
        result.append(value)
    return result


def box_steps(n, pieces, part_at, final, side, local, on, near, chain, local_sem, side_send, side_recv, on_send, on_recv, near_send, near_recv, z_send, z_recv):
    spot, sides = both_ways(n)
    me, close = box_devices()
    rows = side.shape[2]
    half = rows // 2
    bits = (6, 2, 4, 0)
    sends = []

    def seq_of(index, bit):
        for one in (2, 4):
            if bit & one:
                index = flip(index, one)
        return index

    def start(one, condition=None):
        sends.append((condition, one))
        if condition is None:
            one.start()
        else:

            @pl.when(condition)
            def _():
                one.start()

    def await_at(target, recv):
        send(target, target, side_send.at[0, 0], recv, close[1]).wait_recv()

    def loads(chip, shard):
        return pltpu.make_async_copy(
            part_at(seq_of(me, bits[chip]), shard), local.at[chip, shard], local_sem.at[chip, shard]
        )

    def merge(chip, shard):
        await_at(side.at[chip, shard], side_recv.at[chip, shard])
        loads(chip, shard).wait()
        add_into(side.at[chip, shard], local.at[chip, shard], rows)

    def begin():
        for shard, _ in pieces:
            for chip in range(4):
                start(
                    send(
                        part_at(seq_of(flip(me, 1), bits[chip]), shard),
                        side.at[chip, shard],
                        side_send.at[chip, shard],
                        side_recv.at[chip, shard],
                        close[1],
                    )
                )
                loads(chip, shard).start()

    def first(step):
        shard = pieces[step][0]
        merge(0, shard)
        for axis, bit in ((0, 2), (1, 4)):
            start(
                send(
                    side.at[0, shard, pl.ds(axis * half, half)],
                    on.at[axis, shard],
                    on_send.at[axis, shard],
                    on_recv.at[axis, shard],
                    close[bit],
                )
            )
        merge(1, shard)
        merge(2, shard)

    def second(step):
        shard = pieces[step][0]
        for axis, bit in ((0, 2), (1, 4)):
            other = 2 - axis
            await_at(on.at[axis, shard], on_recv.at[axis, shard])
            add_into(side.at[other, shard], on.at[axis, shard], half, axis * half, 0)
            start(
                send(
                    side.at[other, shard],
                    near.at[1 - axis, shard],
                    near_send.at[1 - axis, shard],
                    near_recv.at[1 - axis, shard],
                    close[6 - bit],
                )
            )
        merge(3, shard)

    def third(step):
        shard = pieces[step][0]
        for axis in (0, 1):
            await_at(near.at[axis, shard], near_recv.at[axis, shard])
            add_into(side.at[3, shard], near.at[axis, shard], rows)

    def fourth(step):
        shard, kind = pieces[step]
        if kind == "far":
            for way in (0, 1):
                ahead = shard > spot if way == 0 else shard < spot
                distance = jnp.clip(shard - spot if way == 0 else spot - shard, 1, n - 1)

                @pl.when(ahead & sides[1 - way][0])
                def _(way=way, distance=distance):
                    slot = jnp.minimum(distance, n - 2)
                    await_at(chain.at[way, slot], z_recv.at[way, slot])
                    add_into(side.at[3, shard], chain.at[way, slot], rows)

                start(
                    send(
                        side.at[3, shard],
                        chain.at[way, distance - 1],
                        z_send.at[way, distance - 1],
                        z_recv.at[way, distance - 1],
                        sides[way][1],
                    ),
                    ahead,
                )
            return
        out = final(step)

        def body(index, carry):
            at = pl.ds(pl.multiple_of(index * 16, 16), 16)
            out[at, :] = side[3, shard, at, :].astype(jnp.float32)
            return carry

        lax.fori_loop(0, rows // 16, body, 0)
        if kind == "own":
            for way in (0, 1):

                @pl.when(sides[1 - way][0])
                def _(way=way):
                    await_at(chain.at[way, 0], z_recv.at[way, 0])
                    add_into(out, chain.at[way, 0], rows)

    def drain():
        for condition, one in sends:
            if condition is None:
                one.wait_send()
            else:

                @pl.when(condition)
                def _(one=one):
                    one.wait_send()

    return begin, first, second, third, fourth, drain


def greet_box(n):
    _, sides = both_ways(n)
    _, close = box_devices()
    greet([close[1], close[2], close[4]], sides)


def box_scratch(n, pieces, rows, width, kind):
    sem = pltpu.SemaphoreType.DMA
    return [
        pltpu.VMEM((4, pieces, rows, width), kind),
        pltpu.VMEM((4, pieces, rows, width), kind),
        pltpu.VMEM((2, pieces, rows // 2, width), kind),
        pltpu.VMEM((2, pieces, rows, width), kind),
        pltpu.VMEM((2, n - 1, rows, width), kind),
        sem((4, pieces)),
        sem((4, pieces)),
        sem((4, pieces)),
        sem((2, pieces)),
        sem((2, pieces)),
        sem((2, pieces)),
        sem((2, pieces)),
        sem((2, n - 1)),
        sem((2, n - 1)),
    ]


def box_sum_kernel(n, passing, part, tokens, *refs):
    out, token_out = refs[passing : passing + 2]
    held, send_sem, recv_sem, *scratch = refs[2 * passing + 2 :]
    onward, finish, end = chain_steps(n, 4, tokens, token_out, held, send_sem, recv_sem)
    spot, _ = both_ways(n)
    greet_box(n)
    order = order_of(spot, n)
    pieces = [(shard, "far") for shard in order[:-1]] + [(order[-1], "own")]
    begin, *tasks, drain = box_steps(
        n, pieces, lambda seq, shard: part.at[seq, shard], lambda step: out, *scratch
    )
    begin()
    for step in range(n + 3):
        if step < n - 1:
            onward(n - 1 - step)
        for delay, task in enumerate(tasks):
            if 0 <= step - delay < n:
                task(step - delay)
    finish()
    end()
    drain()


def closing_kernel(n, tokens, part, _later, out, weights, _passed, *scratch):
    spot, _ = both_ways(n)
    greet_box(n)
    held, send_sem, recv_sem = scratch[:3]
    onward, finish, end = chain_steps(n, 4, tokens, out, held, send_sem, recv_sem)
    order = order_of(spot, n)
    flat = weights.shape[0] - 1
    pieces = [(shard, "far") for shard in order[:-1]]
    pieces += [(n + index, "flat") for index in range(flat)] + [(order[-1], "own")]
    targets = [None] * (n - 1) + [weights.at[1 + index] for index in range(flat)] + [weights.at[0]]
    begin, first, second, third, fourth, drain = box_steps(
        n, pieces, lambda seq, shard: part.at[shard, seq], lambda step: targets[step], *scratch[3:]
    )
    begin()
    onward(n - 1)
    count = len(pieces)
    far = n - 2
    for task in (first, second, third, fourth):
        for step in range(count):
            task(step)
        if far:
            onward(far)
            far -= 1
    for left in range(far, 0, -1):
        onward(left)
    finish()
    end()
    drain()


def closing(tokens, part, later):
    n = lax.axis_size("tensor")
    pieces, _, rows, width = part.shape
    sem = pltpu.SemaphoreType.DMA
    inside = pl.BlockSpec(memory_space=pltpu.VMEM)
    anywhere = pl.BlockSpec(memory_space=pl.ANY)
    return pl.pallas_call(
        functools.partial(closing_kernel, n),
        out_shape=[
            jax.ShapeDtypeStruct(tokens.shape[1:], jnp.float32),
            jax.ShapeDtypeStruct((pieces - n + 1, rows, width), jnp.float32),
            jax.ShapeDtypeStruct(later.shape, later.dtype),
        ],
        in_specs=[inside, anywhere, anywhere],
        out_specs=[inside, inside, anywhere],
        input_output_aliases={2: 2},
        scratch_shapes=[
            pltpu.VMEM((2, n - 1) + tokens.shape[1:], tokens.dtype),
            sem((2, n - 1, 4)),
            sem((2, n - 1, 4)),
        ]
        + box_scratch(n, pieces, rows, width, part.dtype),
        compiler_params=pltpu.CompilerParams(
            collective_id=8, has_side_effects=True, vmem_limit_bytes=VMEM
        ),
        cost_estimate=transfer(80),
        name="closing",
    )(tokens, part, later)


def swap_kernel(n, part, _later, out, _passed, local_sem, send_sem, recv_sem):
    spot = lax.axis_index("tensor")
    greet([{"tensor": lax.rem(spot + step, n)} for step in range(1, n)])
    keep = pltpu.make_async_copy(part.at[spot], out.at[spot], local_sem)
    keep.start()

    def copy(step):
        to = lax.rem(spot + step, n)
        return send(
            part.at[to], out.at[spot], send_sem.at[step], recv_sem.at[step], {"tensor": to}
        )

    for step in range(1, n):
        copy(step).start()
    keep.wait()
    for step in range(1, n):
        come = lax.rem(spot - step + n, n)
        send(
            part.at[come], out.at[come], send_sem.at[step], recv_sem.at[step], {"tensor": come}
        ).wait_recv()
        copy(step).wait_send()


def swap(part, later, number):
    n = lax.axis_size("tensor")
    sem = pltpu.SemaphoreType.DMA
    anywhere = pl.BlockSpec(memory_space=pl.ANY)
    return pl.pallas_call(
        functools.partial(swap_kernel, n),
        out_shape=[
            jax.ShapeDtypeStruct(part.shape, part.dtype),
            jax.ShapeDtypeStruct(later.shape, later.dtype),
        ],
        in_specs=[anywhere] * 2,
        out_specs=[anywhere] * 2,
        input_output_aliases={1: 1},
        scratch_shapes=[sem, sem((n,)), sem((n,))],
        compiler_params=pltpu.CompilerParams(
            collective_id=number, has_side_effects=True, vmem_limit_bytes=VMEM
        ),
        cost_estimate=transfer(25),
        name="swap",
    )(part, later)


def box_sum(part, tokens, later):
    n = lax.axis_size("tensor")
    width = part.shape[1]
    rows = part.shape[0] // (8 * n)
    kind = part.dtype
    anywhere = pl.BlockSpec(memory_space=pl.ANY)
    inside = pl.BlockSpec(memory_space=pltpu.VMEM)
    tokens = tokens.reshape(n, -1, width)
    sem = pltpu.SemaphoreType.DMA
    out, token_out, *later = pl.pallas_call(
        functools.partial(box_sum_kernel, n, len(later)),
        out_shape=[
            jax.ShapeDtypeStruct((rows, width), jnp.float32),
            jax.ShapeDtypeStruct(tokens.shape[1:], jnp.float32),
        ]
        + [jax.ShapeDtypeStruct(one.shape, one.dtype) for one in later],
        in_specs=[anywhere, inside] + [anywhere] * len(later),
        out_specs=[inside] * 2 + [anywhere] * len(later),
        input_output_aliases={2 + index: 2 + index for index in range(len(later))},
        scratch_shapes=[
            pltpu.VMEM((2, n - 1) + tokens.shape[1:], tokens.dtype),
            sem((2, n - 1, 4)),
            sem((2, n - 1, 4)),
        ]
        + box_scratch(n, n, rows, width, kind),
        compiler_params=pltpu.CompilerParams(
            collective_id=4, has_side_effects=True, vmem_limit_bytes=VMEM
        ),
        cost_estimate=transfer(90),
        name="box_sum",
    )(part.reshape(8, n, rows, width), tokens, *later)
    return out, token_out, later


def everyone(n):
    count = lax.axis_size("dp") * n
    me = lax.axis_index("dp") * n + lax.axis_index("tensor")

    def device(number):
        return {"dp": number // n, "tensor": number % n}

    return count, me, device


def greet_all(count, me, device):
    barrier = pltpu.get_barrier_semaphore()

    def signal(step, carry):
        pl.semaphore_signal(barrier, inc=1, device_id=device(lax.rem(me + step, count)), device_id_type=MESH)
        return carry

    lax.fori_loop(1, count, signal, 0)
    pl.semaphore_wait(barrier, count - 1)


def spread_start(n, own, out, send_sem, recv_sem):
    count, me, device = everyone(n)
    greet_all(count, me, device)
    out[me] = own[...]

    def copy(step):
        to = device(lax.rem(me + step, count))
        return send(own, out.at[me], send_sem.at[step], recv_sem.at[step], to)

    def go(step, carry):
        copy(step).start()
        return carry

    def end(step, carry):
        copy(step).wait_send()
        come = lax.rem(me - step + count, count)
        send(own, out.at[come], send_sem.at[step], recv_sem.at[step], device(come)).wait_recv()
        return carry

    lax.fori_loop(1, count, go, 0)
    return lambda: lax.fori_loop(1, count, end, 0)


def sum_spread_kernel(n, part, out, held, send_sem, recv_sem):
    count, me, device = everyone(n)
    greet_all(count, me, device)
    out[...] = part[me]

    def copy(step):
        to = lax.rem(me + step, count)
        return send(part.at[to], held.at[me], send_sem.at[step], recv_sem.at[step], device(to))

    def go(step, carry):
        copy(step).start()
        return carry

    def end(step, carry):
        come = lax.rem(me - step + count, count)
        send(part.at[0], held.at[come], send_sem.at[step], recv_sem.at[step], device(come)).wait_recv()
        out[...] += held[come]
        copy(step).wait_send()
        return carry

    lax.fori_loop(1, count, go, 0)
    lax.fori_loop(1, count, end, 0)


def sum_spread(part):
    n = lax.axis_size("tensor")
    count = lax.axis_size("dp") * n
    sem = pltpu.SemaphoreType.DMA
    return pl.pallas_call(
        functools.partial(sum_spread_kernel, n),
        out_shape=jax.ShapeDtypeStruct(part.shape[1:], part.dtype),
        in_specs=[pl.BlockSpec(memory_space=pltpu.VMEM)],
        out_specs=pl.BlockSpec(memory_space=pltpu.VMEM),
        scratch_shapes=[pltpu.VMEM(part.shape, part.dtype), sem((count,)), sem((count,))],
        compiler_params=pltpu.CompilerParams(
            collective_id=6, has_side_effects=True, vmem_limit_bytes=VMEM
        ),
        cost_estimate=transfer(20),
        name="sum_spread",
    )(part)


TB = 256
GR = 16
TILE = 256
EXTRA = 2 * E
def ceil_to(value, unit):
    return (value + unit - 1) // unit * unit


def nt_dot(a, b):
    return lax.dot_general(a, b, (((1,), (1,)), ((), ())), preferred_element_type=jnp.float32)


def tn_dot(a, b):
    return lax.dot_general(a, b, (((0,), (0,)), ((), ())), preferred_element_type=jnp.float32)


def nn_dot(a, b):
    return jnp.dot(a, b, preferred_element_type=jnp.float32)


def pair(value):
    high = value.astype(jnp.bfloat16)
    low = (value - high.astype(jnp.float32)).astype(jnp.bfloat16)
    return high, low


def unpair(value):
    value = value.astype(jnp.float32)
    return value[:, :E] + value[:, E:]


def excl_cumsum(value, axis):
    return jnp.cumsum(value, axis) - value


class Plan:
    def __init__(self, tokens, seq_len, local):
        seqs = tokens // seq_len
        self.tokens, self.local = tokens, local
        self.blocks = tokens // TB
        per_seq = seq_len // TB
        worst = min(CG + (GR - 1) * per_seq, seq_len)
        self.cap = ceil_to(seqs * worst // GR * GR, TILE)
        groups = (seqs * local * CG + self.blocks * local * (GR - 1)) // GR
        self.slots = ceil_to(TB * TOP * local // E + local * GR, 64)
        self.items = groups * GR // self.slots + self.blocks
        self.tiles = self.cap // TILE


def pick_at(here, table):
    return jnp.sum(jnp.where(here, table[None, :], 0), 1)


def steps_of(size, steps):
    first = excl_cumsum(steps, 0)
    used = jnp.sum(steps)
    index = jnp.minimum(jnp.arange(size), used - 1)
    owner = jnp.sum((first[None, :] <= index[:, None]).astype(jnp.int32), 1) - 1
    here = owner[:, None] == jnp.arange(steps.shape[0])[None, :]
    part = index - pick_at(here, first)
    last = (part == pick_at(here, steps) - 1).astype(jnp.int32)
    return first, used, owner, part, last, here


def routing(plan, routes, base):
    local, blocks = plan.local, plan.blocks
    mine = base + jnp.arange(local)
    picked = jnp.any(routes[:, :, None] == mine[None, None, :], 1)
    grid = picked.reshape(blocks, TB, local)
    ones = grid.astype(jnp.bfloat16)
    earlier = (jnp.arange(TB)[:, None] > jnp.arange(TB)[None, :]).astype(jnp.bfloat16)
    rank = jnp.einsum("ts,bse->bte", earlier, ones, preferred_element_type=jnp.float32).astype(
        jnp.int32
    )
    count = jnp.sum(grid.astype(jnp.int32), 1)
    groups = (count + GR - 1) // GR
    inner = excl_cumsum(groups, 1)
    total = jnp.sum(groups, 1)
    outer = excl_cumsum(groups, 0)
    expert_rows = jnp.sum(groups, 0) * GR
    place = jnp.where(grid, inner[:, None, :] * GR + rank, -1)
    items = jnp.maximum((total * GR + plan.slots - 1) // plan.slots, 1)
    first, used, block, part, last, here = steps_of(plan.items, items)
    wide, slots = plan.slots // GR, plan.cap // GR
    spot = jnp.arange(slots)[None, :, None]
    low = outer.T[:, None, :]
    inside = (spot >= low) & (spot < low + groups.T[:, None, :])
    origin = first[None, :] * wide + inner.T
    source = jnp.sum(jnp.where(inside, origin[:, None, :] + spot - low, 0), 2)
    tiles = jnp.maximum((expert_rows + TILE - 1) // TILE, 1)
    _, tiles_used, owner, tile, tile_last, _ = steps_of(local * plan.tiles, tiles)

    def at_block(table):
        return jnp.sum(jnp.where(here[:, :, None], table[None], 0), 1)[:, None, :]

    spot = (part[:, None] * wide + jnp.arange(wide)[None, :])[:, :, None]
    low, many, begin = at_block(inner), at_block(groups), at_block(outer)
    inside = (spot >= low) & (spot < low + many)
    target = jnp.sum(
        jnp.where(inside, (jnp.arange(local) * slots)[None, None, :] + begin + spot - low, 0), 2
    )
    return dict(
        place=place,
        used=used[None],
        block=block,
        part=part,
        last=last,
        source=source.reshape(-1),
        filled=expert_rows,
        tiles_used=tiles_used[None],
        owner=owner,
        tile=tile,
        tile_last=tile_last,
        target=target.reshape(-1),
    )


def while_used(step, used, *refs):
    @pl.when(pl.program_id(0) < used[0])
    def _():
        step(used, *refs)


def dispatch_step(used, block, part, post, grad, router, place, *refs):
    rows, share, held = refs[len(refs) // 2 - 1], refs[len(refs) // 2], refs[-1]
    step = pl.program_id(0)
    local = place.shape[1]
    slots = rows.shape[0]

    @pl.when(part[step] == 0)
    def _():
        portion = jax.nn.softmax(nn_dot(post[...], router[...]), -1)
        high, low = pair(portion)
        both = jnp.concatenate([high, low], 1)
        held[...] = both
        share[...] = both

    slot = lax.broadcasted_iota(jnp.int32, (slots, TB), 0) + part[step] * slots
    hit = slot == place[0, 0:1, :]
    for one in range(1, local):
        hit = hit | (slot == place[0, one : one + 1, :])
    pick = jnp.where(hit, 1.0, 0.0).astype(jnp.bfloat16)
    rows[:, :D] = nn_dot(pick, post[...]).astype(jnp.bfloat16)
    rows[:, D : 2 * D] = nn_dot(pick, grad[...]).astype(jnp.bfloat16)
    rows[:, 2 * D :] = nn_dot(pick, held[...]).astype(jnp.bfloat16)


def dispatch(plan, route, post, grad, router, later):
    wide = 2 * D + EXTRA
    place = route["place"].transpose(0, 2, 1)

    def at_block(step, used, block, part):
        return (block[step], 0)

    return pl.pallas_call(
        functools.partial(while_used, dispatch_step),
        grid_spec=pltpu.PrefetchScalarGridSpec(
            num_scalar_prefetch=3,
            grid=(plan.items,),
            in_specs=[
                pl.BlockSpec((TB, D), at_block),
                pl.BlockSpec((TB, D), at_block),
                pl.BlockSpec((D, E), lambda step, used, block, part: (0, 0)),
                pl.BlockSpec((1, plan.local, TB), lambda step, used, block, part: (block[step], 0, 0)),
            ]
            + [pl.BlockSpec(memory_space=pl.ANY)] * len(later),
            out_specs=[
                pl.BlockSpec((plan.slots, wide), lambda step, used, block, part: (jnp.minimum(step, used[0] - 1), 0)),
                pl.BlockSpec((TB, EXTRA), at_block),
            ]
            + [pl.BlockSpec(memory_space=pl.ANY)] * len(later),
            scratch_shapes=[pltpu.VMEM((TB, EXTRA), jnp.bfloat16)],
        ),
        out_shape=[
            jax.ShapeDtypeStruct((plan.items * plan.slots, wide), jnp.bfloat16),
            jax.ShapeDtypeStruct((plan.tokens, EXTRA), jnp.bfloat16),
        ]
        + [jax.ShapeDtypeStruct(one.shape, one.dtype) for one in later],
        input_output_aliases={7 + index: 2 + index for index in range(len(later))},
        compiler_params=pltpu.CompilerParams(vmem_limit_bytes=VMEM),
        cost_estimate=transfer(2),
        name="dispatch",
    )(route["used"], route["block"], route["part"], post, grad, router, place, *later)


def fetch_groups(table, rows, held, sems, step, count):
    slot = lax.rem(step, 2)
    for index in range(count):
        group = table[step * count + index]
        pltpu.make_async_copy(
            rows.at[pl.ds(pl.multiple_of(group * GR, GR), GR)],
            held.at[slot, pl.ds(index * GR, GR)],
            sems.at[slot],
        ).start()


def await_groups(rows, held, sems, step, count):
    slot = lax.rem(step, 2)
    pltpu.make_async_copy(rows.at[pl.ds(0, count * GR)], held.at[slot], sems.at[slot]).wait()


def next_groups(used, table, rows, held, sems, count):
    step = pl.program_id(0)

    @pl.when(step == 0)
    def _():
        fetch_groups(table, rows, held, sems, step, count)

    @pl.when(step + 1 < used[0])
    def _():
        fetch_groups(table, rows, held, sems, step + 1, count)

    await_groups(rows, held, sems, step, count)
    return lax.rem(step, 2)


def expert_step(
    used, source, owner, tile, last, filled, base, all_rows, w_gate, w_up, w_down, *refs
):
    *before, result, gate_out, up_out, down_out, held, sems, gate_sum, up_sum, down_sum = refs
    step = pl.program_id(0)
    count = TILE // GR
    slot = next_groups(used, source, all_rows, held, sems, count)
    expert, part = owner[step], tile[step]

    @pl.when(part == 0)
    def _():
        gate_sum[...] = jnp.zeros_like(gate_sum)
        up_sum[...] = jnp.zeros_like(up_sum)
        down_sum[...] = jnp.zeros_like(down_sum)

    @pl.when(last[step] == 1)
    def _():
        def clear(index, carry):
            at = pl.ds(pl.multiple_of(index * GR, GR), GR)
            held[slot, at, :] = jnp.zeros((GR, held.shape[2]), held.dtype)
            return carry

        lax.fori_loop((filled[expert] - part * TILE) // GR, count, clear, 0)

    number = base[0] + expert
    rows, upstream = held[slot, :, :D], held[slot, :, D : 2 * D]
    shares = held[slot, :, 2 * D :]
    lane = lax.broadcasted_iota(jnp.int32, (TILE, EXTRA), 1)
    own = (lane == number) | (lane == number + E)
    gate = jnp.sum(jnp.where(own, shares.astype(jnp.float32), 0.0), -1, keepdims=True)
    gate_pre = nn_dot(rows, w_gate[0])
    up_pre = nn_dot(rows, w_up[0])
    plain = nn_dot(upstream, w_down[0])
    squash = jax.nn.sigmoid(gate_pre)
    swish = gate_pre * squash
    active = (swish * up_pre).astype(jnp.bfloat16).astype(jnp.float32)
    change = jnp.sum(active * plain, -1, keepdims=True)
    grad_active = gate * plain
    grad_gate = (grad_active * up_pre * squash * (1.0 + gate_pre * (1.0 - squash))).astype(
        jnp.bfloat16
    )
    grad_up = (grad_active * swish).astype(jnp.bfloat16)
    scaled = (gate * active).astype(jnp.bfloat16)
    result[:, :D] = nt_dot(scaled, w_down[0]).astype(jnp.bfloat16)
    result[:, D : 2 * D] = (nt_dot(grad_gate, w_gate[0]) + nt_dot(grad_up, w_up[0])).astype(
        jnp.bfloat16
    )
    high, low = pair(change)
    result[:, 2 * D :] = jnp.where(
        lane == number,
        high.astype(jnp.float32),
        jnp.where(lane == number + E, low.astype(jnp.float32), 0.0),
    ).astype(jnp.bfloat16)
    gate_sum[...] += tn_dot(grad_gate, rows)
    up_sum[...] += tn_dot(grad_up, rows)
    down_sum[...] += tn_dot(scaled, upstream)

    @pl.when(last[step] == 1)
    def _():
        for index, (out, total) in enumerate(
            ((gate_out, gate_sum), (up_out, up_sum), (down_out, down_sum))
        ):
            out[0] = total[...].T + before[index][0] if before else total[...].T


def experts(plan, route, base, rows, w_gate, w_up, w_down, before):
    wide = 2 * D + EXTRA
    width = w_gate.shape[2]
    slots, count = plan.cap // GR, TILE // GR
    table = route["source"].reshape(plan.local * plan.tiles, count)
    number = route["owner"] * (slots // count) + route["tile"]
    table = table[number].reshape(-1)

    def whole(step, used, table, owner, tile, last, filled, base):
        return (owner[step], 0, 0)

    def tile_at(step, used, table, owner, tile, last, filled, base):
        return (owner[step] * plan.tiles + tile[step], 0)

    weight = pl.BlockSpec((1, D, width), whole)
    total = plan.local * plan.cap
    return pl.pallas_call(
        functools.partial(while_used, expert_step),
        grid_spec=pltpu.PrefetchScalarGridSpec(
            num_scalar_prefetch=7,
            grid=(plan.local * plan.tiles,),
            in_specs=[pl.BlockSpec(memory_space=pl.ANY)] + [weight] * (3 + len(before)),
            out_specs=[pl.BlockSpec((TILE, wide), tile_at)] + [weight] * 3,
            scratch_shapes=[
                pltpu.VMEM((2, TILE, wide), jnp.bfloat16),
                pltpu.SemaphoreType.DMA((2,)),
            ]
            + [pltpu.VMEM((width, D), jnp.float32)] * 3,
        ),
        out_shape=[jax.ShapeDtypeStruct((total, wide), jnp.bfloat16)]
        + [jax.ShapeDtypeStruct((plan.local, D, width), jnp.float32)] * 3,
        compiler_params=pltpu.CompilerParams(vmem_limit_bytes=VMEM),
        input_output_aliases={11 + index: 1 + index for index in range(len(before))},
        cost_estimate=transfer(2),
        name="experts",
    )(
        route["tiles_used"],
        table,
        route["owner"],
        route["tile"],
        route["tile_last"],
        route["filled"],
        base[None],
        rows,
        w_gate,
        w_up,
        w_down,
        *before,
    )


def combine_step(
    used, target, block, part, last, results, place, share, post, router, *refs
):
    held, sems, sums = refs[-3:]
    passing = (len(refs) - 6) // 2
    out, grad, router_out = refs[passing : passing + 3]
    step = pl.program_id(0)
    local = place.shape[1]
    slots = held.shape[1]

    at = next_groups(used, target, results, held, sems, slots // GR)

    @pl.when(step == 0)
    def _():
        router_out[...] = jnp.zeros_like(router_out)

    slot = lax.broadcasted_iota(jnp.int32, (TB, slots), 1) + part[step] * slots
    hit = slot == place[:, 0:1]
    for one in range(1, local):
        hit = hit | (slot == place[:, one : one + 1])
    pick = jnp.where(hit, 1.0, 0.0).astype(jnp.bfloat16)

    def term(begin, end):
        return nn_dot(pick, held[at, :, begin:end])

    def finish(value):
        change = unpair(value(2 * D, 2 * D + EXTRA))
        portion = unpair(share[...])
        moved = portion * (change - jnp.sum(change * portion, -1, keepdims=True))
        moved = moved.astype(jnp.bfloat16)
        out[...] = value(0, D).astype(jnp.bfloat16)
        grad[...] = (value(D, 2 * D) + nt_dot(moved, router[...])).astype(jnp.bfloat16)
        router_out[...] += tn_dot(moved, post[...])

    single = (part[step] == 0) & (last[step] == 1)

    @pl.when(single)
    def _():
        finish(term)

    @pl.when(jnp.logical_not(single))
    def _():
        @pl.when(part[step] == 0)
        def _():
            sums[...] = jnp.zeros_like(sums)

        sums[...] += term(0, 2 * D + EXTRA)

        @pl.when(last[step] == 1)
        def _():
            finish(lambda begin, end: sums[:, begin:end])


def combine(plan, route, results, share, post, router, later):
    wide = 2 * D + EXTRA

    def at_block(step, used, target, block, part, last):
        return (block[step], 0)

    def fixed(step, used, target, block, part, last):
        return (0, 0)

    return pl.pallas_call(
        functools.partial(while_used, combine_step),
        grid_spec=pltpu.PrefetchScalarGridSpec(
            num_scalar_prefetch=5,
            grid=(plan.items,),
            in_specs=[
                pl.BlockSpec(memory_space=pl.ANY),
                pl.BlockSpec((TB, plan.local), at_block),
                pl.BlockSpec((TB, EXTRA), at_block),
                pl.BlockSpec((TB, D), at_block),
                pl.BlockSpec((D, E), fixed),
            ]
            + [pl.BlockSpec(memory_space=pl.ANY)] * len(later),
            out_specs=[
                pl.BlockSpec((TB, D), at_block),
                pl.BlockSpec((TB, D), at_block),
                pl.BlockSpec((E, D), fixed),
            ]
            + [pl.BlockSpec(memory_space=pl.ANY)] * len(later),
            scratch_shapes=[
                pltpu.VMEM((2, plan.slots, wide), jnp.bfloat16),
                pltpu.SemaphoreType.DMA((2,)),
                pltpu.VMEM((TB, wide), jnp.float32),
            ],
        ),
        out_shape=[
            jax.ShapeDtypeStruct((plan.tokens, D), jnp.bfloat16),
            jax.ShapeDtypeStruct((plan.tokens, D), jnp.bfloat16),
            jax.ShapeDtypeStruct((E, D), jnp.float32),
        ]
        + [jax.ShapeDtypeStruct(one.shape, one.dtype) for one in later],
        input_output_aliases={10 + index: 3 + index for index in range(len(later))},
        compiler_params=pltpu.CompilerParams(vmem_limit_bytes=VMEM),
        cost_estimate=transfer(2),
        name="combine",
    )(
        route["used"],
        route["target"],
        route["block"],
        route["part"],
        route["last"],
        results,
        route["place"].reshape(plan.tokens, plan.local),
        share,
        post,
        router,
        *later,
    )


def gather_all(own):
    if lax.axis_size("dp") == 8:
        return box_gather(own)
    return lax.all_gather(
        lax.all_gather(own, "tensor", axis=0, tiled=True), "dp", axis=0, tiled=True
    )


def gather_slowly(own):
    if lax.axis_size("dp") == 8:
        return lax.all_gather(own, ("dp", "tensor"), axis=0, tiled=True)
    return gather_all(own)


def gather_output(own):
    n = lax.axis_size("tensor")
    if lax.axis_size("dp") == 8:
        everything = lax.all_gather(own, ("dp", "tensor"), axis=0, tiled=False)
        everything = everything.reshape((8, n) + own.shape).transpose(1, 0, 2, 3)
        return everything.reshape(n, -1, own.shape[1])
    part = lax.all_gather(own, "dp", axis=0, tiled=True)
    return lax.all_gather(part, "tensor", axis=0, tiled=False)


def sum_last(tokens, parts, later):
    n = lax.axis_size("tensor")
    if lax.axis_size("dp") == 8:
        return closing(
            tokens.reshape(n, -1, tokens.shape[1]),
            parts.reshape(parts.shape[0], 8, -1, parts.shape[2]),
            later,
        )
    tokens, later = chain_sum(tokens, later, 8)
    parts = lax.psum_scatter(parts, "dp", scatter_dimension=1, tiled=True)
    own = lax.psum_scatter(parts[:n], "tensor", scatter_dimension=0, tiled=True)
    return tokens, jnp.concatenate([own, parts[n:]]).astype(jnp.float32), later


def sum_all(part, tokens, later):
    if lax.axis_size("dp") == 8:
        return box_sum(part, tokens, later)
    tokens = lax.psum_scatter(tokens, "tensor", scatter_dimension=0, tiled=True)
    return sum_slowly(part).astype(jnp.float32), tokens.astype(jnp.float32), later


def sum_slowly(part):
    part = lax.psum_scatter(part, "dp", scatter_dimension=0, tiled=True)
    return lax.psum_scatter(part, "tensor", scatter_dimension=0, tiled=True)


def fill(value, rows, columns):
    return jnp.pad(value, ((0, rows - value.shape[0]), (0, columns - value.shape[1])))


def pack_small(router, prenorm, postnorm, querynorm, keynorm, routes):
    n = lax.axis_size("tensor")
    rank = lax.axis_index("tensor")
    rows = router.shape[0]
    head = ceil_to(max(rows, querynorm.shape[0]), 16)
    heads = querynorm.shape[1]
    block = jnp.concatenate(
        [
            fill(router, head, E),
            fill(prenorm[:, None], head, 1),
            fill(postnorm[:, None], head, 1),
            fill(querynorm, head, heads),
            fill(keynorm, head, heads),
        ],
        1,
    )
    part = routes.shape[0] // n
    own = lax.dynamic_slice_in_dim(routes, rank * part, part, 0)
    own = own.astype(jnp.bfloat16).reshape(-1, 128)
    tail = ceil_to(own.shape[0], 16)
    return jnp.concatenate([fill(block, head, 128), fill(own, tail, 128)], 0)


def unpack_small(everything, router, querynorm, routes):
    n = lax.axis_size("tensor")
    rank = lax.axis_index("tensor")
    rows, heads = router.shape[0], querynorm.shape[1]
    head = ceil_to(max(rows, querynorm.shape[0]), 16)
    part = routes.size // n // 128
    total = everything.shape[1]
    mine = everything.reshape(-1, n, total, 128)[:, rank]
    at = E + 2
    return (
        everything[:, :rows, :E].reshape(-1, E),
        everything[:, :rows, E].reshape(-1).astype(jnp.float32),
        everything[:, :rows, E + 1].reshape(-1).astype(jnp.float32),
        mine[:, : querynorm.shape[0], at : at + heads].reshape(-1, heads),
        mine[:, : querynorm.shape[0], at + heads : at + 2 * heads].reshape(-1, heads),
        everything[:, head : head + part].reshape(-1, TOP).astype(jnp.int32),
    )


def body(
    hidden_in,
    out_grad,
    doc_ids,
    expert_ids,
    prenorm,
    querynorm,
    keynorm,
    query_proj,
    key_proj,
    value_proj,
    output_proj,
    postnorm,
    router,
    gate_proj,
    up_proj,
    down_proj,
):
    residual = hidden_in[0].astype(jnp.float32)
    upstream = out_grad[0]
    documents = doc_ids[0]
    routes = expert_ids[0]
    shard = residual.shape[0]
    seq_len = documents.shape[0]
    mesh_dp = lax.axis_size("dp")
    block = min(seq_len, 1024)
    scale = HD ** (-0.5)
    cosine, sine = rope_tables(seq_len, HD)
    small = pack_small(router, prenorm, postnorm, querynorm, keynorm, routes)
    group_hidden, later, output_late, everything = chain_gather(
        hidden_in[0], [upstream[: shard // 2], output_proj], 1, small
    )
    router_full, pre_gain, post_gain, gain_query, gain_key, all_routes = unpack_small(
        everything, router, querynorm, routes
    )
    weights = lax.all_gather(
        jnp.concatenate([query_proj, key_proj, value_proj], 1),
        "dp",
        axis=0,
        tiled=True,
    )
    w_query, w_key, w_value = jnp.split(weights, 3, 1)
    w_output = gather_output(output_late)
    heads = w_query.shape[1] // HD
    query_scale = gain_query.astype(jnp.float32).T.reshape(-1)
    key_scale = gain_key.astype(jnp.float32).T.reshape(-1)
    inv_pre = lax.rsqrt(jnp.mean(residual * residual, -1, keepdims=True) + epsilon)
    group_hidden = group_hidden.astype(jnp.float32)
    group_inv = lax.rsqrt(jnp.mean(group_hidden * group_hidden, -1, keepdims=True) + epsilon)
    group_normed = (group_hidden * group_inv * pre_gain).astype(jnp.bfloat16)
    n = lax.axis_size("tensor")
    few = shard // 2
    plan = Plan(mesh_dp * n * few, n * few, gate_proj.shape[0])
    base = (lax.axis_index("dp") * plan.local).astype(jnp.int32)
    all_routes = all_routes.reshape(mesh_dp, n, 2, few, TOP)
    both = jnp.moveaxis(all_routes, 2, 0).reshape(2, -1, TOP)
    both = jax.vmap(lambda routes: routing(plan, routes, base))(both)
    route = [{name: value[index] for name, value in both.items()} for index in range(2)]
    all_grad = [gather_slowly(later)]
    query = jnp.dot(group_normed, w_query, preferred_element_type=jnp.float32)
    keys = jnp.dot(group_normed, w_key, preferred_element_type=jnp.float32)
    values = jnp.dot(group_normed, w_value, preferred_element_type=jnp.float32).astype(jnp.bfloat16)
    query_sq, key_sq = sum_heads(
        (jnp.sum(query * query, -1, keepdims=True), jnp.sum(keys * keys, -1, keepdims=True))
    )
    inv_query = lax.rsqrt(query_sq / D + epsilon)
    inv_key = lax.rsqrt(key_sq / D + epsilon)
    query_heads = (query * inv_query * query_scale).reshape(seq_len, heads, HD)
    key_heads = (keys * inv_key * key_scale).reshape(seq_len, heads, HD)
    query_rot = (query_heads * cosine[:, None] + rotate(query_heads) * sine[:, None]).astype(
        jnp.bfloat16
    )
    key_rot = (key_heads * cosine[:, None] + rotate(key_heads) * sine[:, None]).astype(jnp.bfloat16)
    value_heads = values.reshape(seq_len, heads, HD)
    mixed, logsum = attend_forward(query_rot, key_rot, value_heads, documents, block, scale)
    mixed_flat = mixed.reshape(seq_len, heads * HD)
    mixed_own, later = swap(mixed_flat.reshape(n, shard, heads * HD), upstream[few:], 7)
    all_grad.append(gather_slowly(later))
    attn_local = sum(nt_dot(mixed_own[index], w_output[index]) for index in range(n))
    middle = residual + attn_local
    inv_post = lax.rsqrt(jnp.mean(middle * middle, -1, keepdims=True) + epsilon)
    post_normed = (middle * inv_post * post_gain).astype(jnp.bfloat16)
    all_post = [gather_all(post_normed[:few]), gather_slowly(post_normed[few:])]
    grads, outs, backs, router_parts = [], [], [], []
    for index in range(2):
        rows, portion, *outs = dispatch(
            plan, route[index], all_post[index], all_grad[index], router_full, outs
        )
        results, *grads = experts(
            plan, route[index], base, rows, gate_proj, up_proj, down_proj, grads
        )
        later = []
        if index == 1:
            later = [lax.psum_scatter(backs[0], "dp", scatter_dimension=0, tiled=True)]
        out, back, router_part, *later = combine(
            plan, route[index], results, portion, all_post[index], router_full, later
        )
        if index == 1:
            early = later[0]
        outs.append(out)
        backs.append(back)
        router_parts.append(router_part)
    gate_weight_grad, up_weight_grad, down_weight_grad = grads
    first_out = lax.psum_scatter(outs[0], "dp", scatter_dimension=0, tiled=True)
    late, early, outs = sum_all(backs[1], early, outs[1:])
    grad_post = jnp.concatenate([early, late], 0)
    second_out = lax.psum_scatter(outs[0], "dp", scatter_dimension=0, tiled=True)
    router_part = router_parts[0] + router_parts[1]
    router_part = router_part.T
    post_gain_part = jnp.sum(grad_post * middle * inv_post, 0)
    grad_middle = upstream.astype(jnp.float32) + norm_back(
        grad_post, middle, inv_post, post_gain, D
    )
    change = grad_middle.astype(jnp.bfloat16)
    grad_mixed, first_out = swap(
        jnp.stack([nn_dot(change, w_output[index]).astype(jnp.bfloat16) for index in range(n)]),
        first_out,
        2,
    )
    moe_local = lax.psum_scatter(
        jnp.concatenate(
            [first_out.reshape(n, few, D), second_out.reshape(n, few, D)], 1
        ).reshape(-1, D),
        "tensor",
        scatter_dimension=0,
        tiled=True,
    )
    output_parts = [tn_dot(change, mixed_own[index]).astype(jnp.bfloat16) for index in range(n)]
    grad_query_rot, grad_key_rot, grad_value_heads = attend_backward(
        query_rot,
        key_rot,
        value_heads,
        documents,
        logsum,
        grad_mixed.reshape(seq_len, heads, HD),
        block,
        scale,
    )
    grad_query_flat = (
        grad_query_rot * cosine[:, None] + rotate_back(grad_query_rot * sine[:, None])
    ).reshape(seq_len, -1)
    grad_key_flat = (
        grad_key_rot * cosine[:, None] + rotate_back(grad_key_rot * sine[:, None])
    ).reshape(seq_len, -1)
    query_inner, key_inner = sum_heads(
        (
            jnp.sum(grad_query_flat * query_scale * query, -1, keepdims=True),
            jnp.sum(grad_key_flat * key_scale * keys, -1, keepdims=True),
        )
    )
    grad_query = (
        inv_query * query_scale * grad_query_flat - query * inv_query**3 * query_inner / D
    ).astype(jnp.bfloat16)
    grad_key = (inv_key * key_scale * grad_key_flat - keys * inv_key**3 * key_inner / D).astype(
        jnp.bfloat16
    )
    query_gain_part = jnp.sum(grad_query_flat * query * inv_query, 0).reshape(heads, HD).T
    key_gain_part = jnp.sum(grad_key_flat * keys * inv_key, 0).reshape(heads, HD).T
    grad_value = grad_value_heads.reshape(seq_len, -1).astype(jnp.bfloat16)
    query_part = lax.dot_general(
        group_normed, grad_query, (((0,), (0,)), ((), ())), preferred_element_type=jnp.float32
    )
    key_part = lax.dot_general(
        group_normed, grad_key, (((0,), (0,)), ((), ())), preferred_element_type=jnp.float32
    )
    value_part = lax.dot_general(
        group_normed, grad_value, (((0,), (0,)), ((), ())), preferred_element_type=jnp.float32
    )
    normed_term = lax.dot_general(
        grad_query, w_query, (((1,), (1,)), ((), ())), preferred_element_type=jnp.float32
    )
    normed_term = normed_term + lax.dot_general(
        grad_key, w_key, (((1,), (1,)), ((), ())), preferred_element_type=jnp.float32
    )
    normed_term = normed_term + lax.dot_general(
        grad_value, w_value, (((1,), (1,)), ((), ())), preferred_element_type=jnp.float32
    )
    grad_normed, weight_sums, middle = sum_last(
        normed_term.astype(jnp.bfloat16),
        jnp.stack(
            output_parts + [part.astype(jnp.bfloat16) for part in (query_part, key_part, value_part)]
        ),
        middle,
    )
    layer_out = (middle + moe_local.astype(jnp.float32)).astype(jnp.bfloat16)[None]
    pre_gain_part = jnp.sum(grad_normed * residual * inv_pre, 0)
    input_grad = (grad_middle + norm_back(grad_normed, residual, inv_pre, pre_gain, D)).astype(
        jnp.bfloat16
    )[None]
    gains = jnp.concatenate([query_gain_part, key_gain_part], 1).reshape(mesh_dp, 1, -1, 2 * heads)
    mine = jnp.arange(n)[None, :, None, None] == lax.axis_index("tensor")
    gains = jnp.pad(
        jnp.where(mine, gains, 0.0),
        ((0, 0), (0, 0), (0, max(router.shape[0] - HD // mesh_dp, 0)), (0, 0)),
    ).reshape(D, 2 * heads)
    own = router.shape[0]
    block = jnp.concatenate(
        [router_part, gains, jnp.zeros((D, 128 - E - 2 * heads), jnp.float32)], 1
    )
    block = jnp.pad(block.reshape(-1, own, 128), ((0, 0), (0, 8), (0, 0)))
    block = block.at[:, own, :own].set(post_gain_part.reshape(-1, own))
    small = sum_spread(block.at[:, own + 1, :own].set(pre_gain_part.reshape(-1, own)))
    gain_grads = small[: HD // mesh_dp, E : E + 2 * heads]
    return (
        layer_out,
        input_grad,
        small[own + 1, :own],
        gain_grads[:, :heads],
        gain_grads[:, heads : 2 * heads],
        weight_sums[1],
        weight_sums[2],
        weight_sums[3],
        weight_sums[0],
        small[own, :own],
        small[:own, :E],
        gate_weight_grad,
        up_weight_grad,
        down_weight_grad,
    )


def solution(mesh):
    in_specs = (
        P("dp", "tensor", None),
        P("dp", "tensor", None),
        P("dp", None),
        P("dp", None, None),
        P(("dp", "tensor")),
        P("dp", "tensor"),
        P("dp", "tensor"),
        P("dp", "tensor"),
        P("dp", "tensor"),
        P("dp", "tensor"),
        P("dp", "tensor"),
        P(("dp", "tensor")),
        P(("dp", "tensor"), None),
        P("dp", None, "tensor"),
        P("dp", None, "tensor"),
        P("dp", None, "tensor"),
    )
    out_specs = (
        P("dp", "tensor", None),
        P("dp", "tensor", None),
        P(("dp", "tensor")),
        P("dp", "tensor"),
        P("dp", "tensor"),
        P("dp", "tensor"),
        P("dp", "tensor"),
        P("dp", "tensor"),
        P("dp", "tensor"),
        P(("dp", "tensor")),
        P(("dp", "tensor"), None),
        P("dp", None, "tensor"),
        P("dp", None, "tensor"),
        P("dp", None, "tensor"),
    )
    return jax.shard_map(body, mesh=mesh, in_specs=in_specs, out_specs=out_specs, check_vma=False)
```

```python
import functools

import jax
import jax.numpy as jnp
from jax import lax
from jax.experimental import pallas as pl
from jax.experimental.pallas import tpu as pltpu
from jax.sharding import PartitionSpec as P

D = 2048
HD = 128
E = 64
TOP = 8
CG = 192


epsilon = 1e-05
masked_score = -1000000000.0


def rope_tables(length, width):
    positions = jnp.arange(length).astype(jnp.float32)
    rates = 10000.0 ** (-jnp.arange(0, width, 2).astype(jnp.float32) / width)
    angles = positions[:, None] * rates[None, :]
    return (jnp.concatenate([jnp.cos(angles)] * 2, -1), jnp.concatenate([jnp.sin(angles)] * 2, -1))


def rotate(tensor):
    half = tensor.shape[-1] // 2
    return jnp.concatenate([-tensor[..., half:], tensor[..., :half]], -1)


def rotate_back(tensor):
    half = tensor.shape[-1] // 2
    return jnp.concatenate([tensor[..., half:], -tensor[..., :half]], -1)


def sum_heads(parts):
    return lax.psum((parts[0], parts[1]), "tensor")


def norm_back(grad, value, inverse, gain, width):
    scaled = grad * gain
    inner = jnp.sum(scaled * value, -1, keepdims=True)
    return inverse * scaled - value * inverse**3 * inner / width


def block_scores(query, keys, documents, start, block, scale):
    row_place = start + jnp.arange(block)
    col_place = jnp.arange(documents.shape[0])
    allowed = (documents[:, None] == documents[None, :]) & (
        row_place[:, None] >= col_place[None, :]
    )
    scores = jnp.einsum("qhd,khd->hqk", query, keys, preferred_element_type=jnp.float32) * scale
    return (jnp.where(allowed[None], scores, masked_score), query)


def attend_forward(query, keys, values, documents, block, scale):
    count = query.shape[0] // block

    def one(index):
        scores, rows = block_scores(query, keys, documents, index * block, block, scale)
        peak = jnp.max(scores, -1, keepdims=True)
        weights = jnp.exp(scores - peak)
        total = jnp.sum(weights, -1, keepdims=True)
        portion = (weights / total).astype(jnp.bfloat16)
        mixed = jnp.einsum("hqk,khd->qhd", portion, values, preferred_element_type=jnp.float32)
        return (mixed.astype(jnp.bfloat16), peak + jnp.log(total))

    mixed, logsum = lax.map(one, jnp.arange(count))
    return (mixed.reshape(query.shape), logsum)


def attend_backward(query, keys, values, documents, logsum, grad_mixed, block, scale):
    count = query.shape[0] // block

    def one(index):
        start = index * block
        scores, rows = block_scores(query, keys, documents, start, block, scale)
        portion = jnp.exp(scores - logsum[index])
        grad_portion = jnp.einsum(
            "qhd,khd->hqk", grad_mixed, values, preferred_element_type=jnp.float32
        )
        center = jnp.sum(portion * grad_portion, -1, keepdims=True)
        grad_scores = (portion * (grad_portion - center)).astype(jnp.bfloat16)
        grad_values = jnp.einsum(
            "hqk,qhd->khd",
            portion.astype(jnp.bfloat16),
            grad_mixed,
            preferred_element_type=jnp.float32,
        )
        grad_query = (
            jnp.einsum("hqk,khd->qhd", grad_scores, keys, preferred_element_type=jnp.float32)
            * scale
        )
        grad_keys = (
            jnp.einsum("hqk,qhd->khd", grad_scores, rows, preferred_element_type=jnp.float32)
            * scale
        )
        return (grad_query, grad_keys, grad_values)

    grad_query, grad_keys, grad_values = lax.map(one, jnp.arange(count))
    return (grad_query.reshape(query.shape), jnp.sum(grad_keys, 0), jnp.sum(grad_values, 0))


MESH = pl.DeviceIdType.MESH
VMEM = 60 * 1024 * 1024


def transfer(microseconds):
    return pl.CostEstimate(flops=0, bytes_accessed=microseconds * 3_000_000, transcendentals=0)


def flip(index, bit):
    return index + bit - 2 * bit * ((index // bit) % 2)


def send(source, target, send_sem, recv_sem, device):
    return pltpu.make_async_remote_copy(
        src_ref=source,
        dst_ref=target,
        send_sem=send_sem,
        recv_sem=recv_sem,
        device_id=device,
        device_id_type=MESH,
    )


def greet(devices, extra=()):
    barrier = pltpu.get_barrier_semaphore()
    for device in devices:
        pl.semaphore_signal(barrier, inc=1, device_id=device, device_id_type=MESH)
    for there, device in extra:

        @pl.when(there)
        def _(device=device):
            pl.semaphore_signal(barrier, inc=1, device_id=device, device_id_type=MESH)

    count = len(devices)
    for there, _ in extra:
        count = count + jnp.where(there, 1, 0)
    pl.semaphore_wait(barrier, count)


def both_ways(n):
    spot = lax.axis_index("tensor")
    return spot, (
        (spot < n - 1, {"tensor": jnp.minimum(spot + 1, n - 1)}),
        (spot > 0, {"tensor": jnp.maximum(spot - 1, 0)}),
    )


def shard_at(spot, way, distance, n):
    number = spot - distance if way == 0 else spot + distance
    return (number >= 0) & (number < n), jnp.clip(number, 0, n - 1)


def chain_gather_kernel(n, pieces, passing, own, *refs):
    refs = refs[passing:]
    if len(refs) > passing + 4:
        small, out, everything, *sems = refs[0], refs[1], refs[2 + passing], *refs[3 + passing :]
        local_sem, send_sem, recv_sem, all_send, all_recv = sems
        finish = spread_start(n, small, everything, all_send, all_recv)
    else:
        out, (local_sem, send_sem, recv_sem) = refs[0], refs[1 + passing :]
        finish = None
    spot, sides = both_ways(n)
    rows = own.shape[0] // pieces
    if finish is None:
        greet([], sides)
    keep = pltpu.make_async_copy(own, out.at[spot], local_sem)
    keep.start()

    def copy(way, distance, piece):
        there, number = shard_at(spot, way, distance, n)
        part = pl.ds(piece * rows, rows)
        source = own.at[part] if distance == 0 else out.at[number, part]
        return there & sides[way][0], send(
            source,
            out.at[number, part],
            send_sem.at[way, distance, piece],
            recv_sem.at[way, distance, piece],
            sides[way][1],
        )

    def arrived(way, distance, piece):
        there, number = shard_at(spot, way, distance, n)
        part = pl.ds(piece * rows, rows)

        @pl.when(there)
        def _():
            send(
                out.at[number, part],
                out.at[number, part],
                send_sem.at[way, distance - 1, piece],
                recv_sem.at[way, distance - 1, piece],
                sides[way][1],
            ).wait_recv()

    for distance in range(n):
        for piece in range(pieces):
            for way in (0, 1):
                if distance:
                    arrived(way, distance, piece)
                if distance < n - 1:
                    go, one = copy(way, distance, piece)

                    @pl.when(go)
                    def _(one=one):
                        one.start()

    keep.wait()
    for distance in range(n - 1):
        for piece in range(pieces):
            for way in (0, 1):
                go, one = copy(way, distance, piece)

                @pl.when(go)
                def _(one=one):
                    one.wait_send()

    if finish is not None:
        finish()


def chain_gather(own, later, number, small=None, pieces=4):
    n = lax.axis_size("tensor")
    rows, width = own.shape
    anywhere = pl.BlockSpec(memory_space=pl.ANY)
    inside = pl.BlockSpec(memory_space=pltpu.VMEM)
    sem = pltpu.SemaphoreType.DMA
    outs = [jax.ShapeDtypeStruct((n, rows, width), own.dtype)]
    outs += [jax.ShapeDtypeStruct(one.shape, one.dtype) for one in later]
    more, sems = [], []
    if small is not None:
        count = lax.axis_size("dp") * n
        outs.append(jax.ShapeDtypeStruct((count,) + small.shape, small.dtype))
        more, sems = [small], [sem((count,)), sem((count,))]
    plain = [anywhere] * (1 + len(later)) + [inside] * len(more)
    out, *rest = pl.pallas_call(
        functools.partial(chain_gather_kernel, n, pieces, len(later)),
        out_shape=outs,
        in_specs=plain,
        out_specs=plain,
        input_output_aliases={1 + index: 1 + index for index in range(len(later))},
        scratch_shapes=[sem, sem((2, n - 1, pieces)), sem((2, n - 1, pieces))] + sems,
        compiler_params=pltpu.CompilerParams(
            collective_id=number, has_side_effects=True, vmem_limit_bytes=VMEM
        ),
        cost_estimate=transfer(65),
        name="chain_gather",
    )(own, *later, *more)
    return (out.reshape(n * rows, width), *rest)


def add_into(target, source, rows, start=0, source_start=0):
    step = 16

    def body(index, carry):
        at = pl.ds(pl.multiple_of(start + index * step, step), step)
        come = pl.ds(pl.multiple_of(source_start + index * step, step), step)
        target[at, :] = (
            target[at, :].astype(jnp.float32) + source[come, :].astype(jnp.float32)
        ).astype(target.dtype)
        return carry

    lax.fori_loop(0, rows // step, body, 0)


def chain_sum_kernel(n, pieces, part, _later, out, _passed, held, send_sem, recv_sem):
    spot, sides = both_ways(n)
    greet([], sides)
    onward, finish, drain = chain_steps(n, pieces, part, out, held, send_sem, recv_sem)
    for far in range(n - 1, 0, -1):
        onward(far)
    finish()
    drain()


def chain_steps(n, pieces, part, out, held, send_sem, recv_sem):
    spot, sides = both_ways(n)
    rows = out.shape[0] // pieces

    def copy(way, far, piece, mine):
        number = spot + far if way == 0 else spot - far
        there = (number >= 0) & (number < n)
        number = jnp.clip(number, 0, n - 1)
        at = pl.ds(piece * rows, rows)
        source = part.at[number, at]
        return there, number, send(
            source if mine else held.at[way, far, at],
            held.at[way, far - 1, at],
            send_sem.at[way, far - 1, piece],
            recv_sem.at[way, far - 1, piece],
            sides[way][1],
        )

    def arrived(way, far, piece):
        at = pl.ds(piece * rows, rows)
        send(
            held.at[way, far, at],
            held.at[way, far, at],
            send_sem.at[way, far, piece],
            recv_sem.at[way, far, piece],
            sides[way][1],
        ).wait_recv()

    def onward(far):
        for piece in range(pieces):
            for way in (0, 1):
                behind = sides[1 - way][0]
                there, number, first = copy(way, far, piece, True)

                @pl.when(there & jnp.logical_not(behind))
                def _(first=first):
                    first.start()

                if far < n - 1:
                    _, _, again = copy(way, far, piece, False)

                    @pl.when(there & behind)
                    def _(way=way, piece=piece, number=number, again=again):
                        arrived(way, far, piece)
                        add_into(
                            held.at[way, far], part.at[number], rows, piece * rows, piece * rows
                        )
                        again.start()

    def finish():
        for piece in range(pieces):

            def body(index, carry, piece=piece):
                here = pl.ds(pl.multiple_of(piece * rows + index * 16, 16), 16)
                out[here, :] = part[spot, here, :].astype(jnp.float32)
                return carry

            lax.fori_loop(0, rows // 16, body, 0)
            for way in (0, 1):

                @pl.when(sides[1 - way][0])
                def _(way=way, piece=piece):
                    arrived(way, 0, piece)
                    add_into(out, held.at[way, 0], rows, piece * rows, piece * rows)

    def drain():
        for far in range(n - 1, 0, -1):
            for piece in range(pieces):
                for way in (0, 1):
                    there, _, one = copy(way, far, piece, True)

                    @pl.when(there)
                    def _(one=one):
                        one.wait_send()

    return onward, finish, drain


def chain_sum(part, later, number, pieces=4):
    n = lax.axis_size("tensor")
    width = part.shape[1]
    rows = part.shape[0] // n
    anywhere = pl.BlockSpec(memory_space=pl.ANY)
    inside = pl.BlockSpec(memory_space=pltpu.VMEM)
    return pl.pallas_call(
        functools.partial(chain_sum_kernel, n, pieces),
        out_shape=[
            jax.ShapeDtypeStruct((rows, width), jnp.float32),
            jax.ShapeDtypeStruct(later.shape, later.dtype),
        ],
        in_specs=[inside, anywhere],
        out_specs=[inside, anywhere],
        input_output_aliases={1: 1},
        scratch_shapes=[
            pltpu.VMEM((2, n - 1, rows, width), part.dtype),
            pltpu.SemaphoreType.DMA((2, n - 1, pieces)),
            pltpu.SemaphoreType.DMA((2, n - 1, pieces)),
        ],
        compiler_params=pltpu.CompilerParams(
            collective_id=number, has_side_effects=True, vmem_limit_bytes=VMEM
        ),
        cost_estimate=transfer(65),
        name="chain_sum",
    )(part.reshape(n, rows, width), later)


def box_devices():
    me = lax.axis_index("dp")
    return me, {bit: {"dp": flip(me, bit)} for bit in (1, 2, 4)}


def box_gather_kernel(n, own, out, local_sem, z_send, z_recv, near_send, near_recv, on_send, on_recv, side_send, side_recv):
    spot, sides = both_ways(n)
    me, near = box_devices()
    half = own.shape[0] // 2
    greet([near[1], near[2], near[4]], sides)
    keep = pltpu.make_async_copy(own, out.at[me, spot], local_sem)
    keep.start()
    sends = []

    def piece(seq, shard, part):
        return out.at[seq, shard, pl.ds(part * half, half)]

    def start(condition, one):
        sends.append((condition, one))

        @pl.when(condition)
        def _():
            one.start()

    def await_piece(condition, target, recv):
        @pl.when(condition)
        def _():
            send(target, target, side_send.at[0, 0, 0], recv, near[1]).wait_recv()

    def to_side(condition, slot, seq, shard, part, source):
        start(condition, send(source, piece(seq, shard, part), side_send.at[slot, shard, part], side_recv.at[slot, shard, part], near[1]))

    def mine(way, distance):
        there, shard = shard_at(spot, way, distance, n)
        for part in (0, 1):
            if distance:
                await_piece(there, piece(me, shard, part), z_recv.at[way, distance - 1, part])
            source = piece(me, shard, part) if distance else own.at[pl.ds(part * half, half)]
            for out_way in (0, 1) if distance == 0 else (way,):
                if distance < n - 1:
                    start(there & sides[out_way][0], send(source, piece(me, shard, part), z_send.at[out_way, distance, part], z_recv.at[out_way, distance, part], sides[out_way][1]))
            for axis, bit in ((0, 2), (1, 4)):
                start(there, send(source, piece(me, shard, part), near_send.at[axis, shard, part], near_recv.at[axis, shard, part], near[bit]))
            to_side(there, 0, me, shard, part, source)

    def nearby(way, distance):
        there, shard = shard_at(spot, way, distance, n)
        for part in (0, 1):
            for axis, bit in ((0, 2), (1, 4)):
                seq = flip(me, bit)
                source = piece(seq, shard, part)
                await_piece(there, source, near_recv.at[axis, shard, part])
                if part == axis:
                    start(there, send(source, source, on_send.at[1 - axis, shard], on_recv.at[1 - axis, shard], near[6 - bit]))
                to_side(there, 1 + axis, seq, shard, part, source)

    def far(way, distance):
        there, shard = shard_at(spot, way, distance, n)
        seq = flip(flip(me, 2), 4)
        for part in (0, 1):
            source = piece(seq, shard, part)
            await_piece(there, source, on_recv.at[1 - part, shard])
            to_side(there, 3, seq, shard, part, source)

    for step in range(n + 2):
        for task, delay in ((mine, 0), (nearby, 1), (far, 2)):
            distance = step - delay
            if 0 <= distance < n:
                for way in (0, 1) if distance else (0,):
                    task(way, distance)
    for shard in range(n):
        for part in (0, 1):
            for slot, bit in enumerate((0, 2, 4, 6)):
                seq = flip(me, 1)
                for one in (2, 4):
                    if bit & one:
                        seq = flip(seq, one)
                await_piece(spot >= 0, piece(seq, shard, part), side_recv.at[slot, shard, part])
    keep.wait()
    for condition, one in sends:

        @pl.when(condition)
        def _(one=one):
            one.wait_send()


def box_gather(own):
    n = lax.axis_size("tensor")
    rows, width = own.shape
    sem = pltpu.SemaphoreType.DMA
    out = pl.pallas_call(
        functools.partial(box_gather_kernel, n),
        out_shape=jax.ShapeDtypeStruct((8, n, rows, width), own.dtype),
        in_specs=[pl.BlockSpec(memory_space=pl.ANY)],
        out_specs=pl.BlockSpec(memory_space=pl.ANY),
        scratch_shapes=[sem]
        + [sem((2, n - 1, 2))] * 2
        + [sem((2, n, 2))] * 2
        + [sem((2, n))] * 2
        + [sem((4, n, 2))] * 2,
        compiler_params=pltpu.CompilerParams(collective_id=3, has_side_effects=True),
        cost_estimate=transfer(2),
        name="box_gather",
    )(own)
    return out.reshape(8 * n * rows, width)


def order_of(spot, n):
    table = [sorted(range(n), key=lambda s: -abs(s - j)) for j in range(n)]
    result = []
    for step in range(n):
        value = jnp.int32(table[0][step])
        for j in range(1, n):
            value = jnp.where(spot == j, table[j][step], value)
        result.append(value)
    return result


def box_steps(n, pieces, part_at, final, side, local, on, near, chain, local_sem, side_send, side_recv, on_send, on_recv, near_send, near_recv, z_send, z_recv):
    spot, sides = both_ways(n)
    me, close = box_devices()
    rows = side.shape[2]
    half = rows // 2
    bits = (6, 2, 4, 0)
    sends = []

    def seq_of(index, bit):
        for one in (2, 4):
            if bit & one:
                index = flip(index, one)
        return index

    def start(one, condition=None):
        sends.append((condition, one))
        if condition is None:
            one.start()
        else:

            @pl.when(condition)
            def _():
                one.start()

    def await_at(target, recv):
        send(target, target, side_send.at[0, 0], recv, close[1]).wait_recv()

    def loads(chip, shard):
        return pltpu.make_async_copy(
            part_at(seq_of(me, bits[chip]), shard), local.at[chip, shard], local_sem.at[chip, shard]
        )

    def merge(chip, shard):
        await_at(side.at[chip, shard], side_recv.at[chip, shard])
        loads(chip, shard).wait()
        add_into(side.at[chip, shard], local.at[chip, shard], rows)

    def begin():
        for shard, _ in pieces:
            for chip in range(4):
                start(
                    send(
                        part_at(seq_of(flip(me, 1), bits[chip]), shard),
                        side.at[chip, shard],
                        side_send.at[chip, shard],
                        side_recv.at[chip, shard],
                        close[1],
                    )
                )
                loads(chip, shard).start()

    def first(step):
        shard = pieces[step][0]
        merge(0, shard)
        for axis, bit in ((0, 2), (1, 4)):
            start(
                send(
                    side.at[0, shard, pl.ds(axis * half, half)],
                    on.at[axis, shard],
                    on_send.at[axis, shard],
                    on_recv.at[axis, shard],
                    close[bit],
                )
            )
        merge(1, shard)
        merge(2, shard)

    def second(step):
        shard = pieces[step][0]
        for axis, bit in ((0, 2), (1, 4)):
            other = 2 - axis
            await_at(on.at[axis, shard], on_recv.at[axis, shard])
            add_into(side.at[other, shard], on.at[axis, shard], half, axis * half, 0)
            start(
                send(
                    side.at[other, shard],
                    near.at[1 - axis, shard],
                    near_send.at[1 - axis, shard],
                    near_recv.at[1 - axis, shard],
                    close[6 - bit],
                )
            )
        merge(3, shard)

    def third(step):
        shard = pieces[step][0]
        for axis in (0, 1):
            await_at(near.at[axis, shard], near_recv.at[axis, shard])
            add_into(side.at[3, shard], near.at[axis, shard], rows)

    def fourth(step):
        shard, kind = pieces[step]
        if kind == "far":
            for way in (0, 1):
                ahead = shard > spot if way == 0 else shard < spot
                distance = jnp.clip(shard - spot if way == 0 else spot - shard, 1, n - 1)

                @pl.when(ahead & sides[1 - way][0])
                def _(way=way, distance=distance):
                    slot = jnp.minimum(distance, n - 2)
                    await_at(chain.at[way, slot], z_recv.at[way, slot])
                    add_into(side.at[3, shard], chain.at[way, slot], rows)

                start(
                    send(
                        side.at[3, shard],
                        chain.at[way, distance - 1],
                        z_send.at[way, distance - 1],
                        z_recv.at[way, distance - 1],
                        sides[way][1],
                    ),
                    ahead,
                )
            return
        out = final(step)

        def body(index, carry):
            at = pl.ds(pl.multiple_of(index * 16, 16), 16)
            out[at, :] = side[3, shard, at, :].astype(jnp.float32)
            return carry

        lax.fori_loop(0, rows // 16, body, 0)
        if kind == "own":
            for way in (0, 1):

                @pl.when(sides[1 - way][0])
                def _(way=way):
                    await_at(chain.at[way, 0], z_recv.at[way, 0])
                    add_into(out, chain.at[way, 0], rows)

    def drain():
        for condition, one in sends:
            if condition is None:
                one.wait_send()
            else:

                @pl.when(condition)
                def _(one=one):
                    one.wait_send()

    return begin, first, second, third, fourth, drain


def greet_box(n):
    _, sides = both_ways(n)
    _, close = box_devices()
    greet([close[1], close[2], close[4]], sides)


def box_scratch(n, pieces, rows, width, kind):
    sem = pltpu.SemaphoreType.DMA
    return [
        pltpu.VMEM((4, pieces, rows, width), kind),
        pltpu.VMEM((4, pieces, rows, width), kind),
        pltpu.VMEM((2, pieces, rows // 2, width), kind),
        pltpu.VMEM((2, pieces, rows, width), kind),
        pltpu.VMEM((2, n - 1, rows, width), kind),
        sem((4, pieces)),
        sem((4, pieces)),
        sem((4, pieces)),
        sem((2, pieces)),
        sem((2, pieces)),
        sem((2, pieces)),
        sem((2, pieces)),
        sem((2, n - 1)),
        sem((2, n - 1)),
    ]


def box_sum_kernel(n, passing, part, tokens, *refs):
    out, token_out = refs[passing : passing + 2]
    held, send_sem, recv_sem, *scratch = refs[2 * passing + 2 :]
    onward, finish, end = chain_steps(n, 4, tokens, token_out, held, send_sem, recv_sem)
    spot, _ = both_ways(n)
    greet_box(n)
    order = order_of(spot, n)
    pieces = [(shard, "far") for shard in order[:-1]] + [(order[-1], "own")]
    begin, *tasks, drain = box_steps(
        n, pieces, lambda seq, shard: part.at[seq, shard], lambda step: out, *scratch
    )
    begin()
    for step in range(n + 3):
        if step < n - 1:
            onward(n - 1 - step)
        for delay, task in enumerate(tasks):
            if 0 <= step - delay < n:
                task(step - delay)
    finish()
    end()
    drain()


def closing_kernel(n, tokens, part, _later, out, weights, _passed, *scratch):
    spot, _ = both_ways(n)
    greet_box(n)
    held, send_sem, recv_sem = scratch[:3]
    onward, finish, end = chain_steps(n, 4, tokens, out, held, send_sem, recv_sem)
    order = order_of(spot, n)
    flat = weights.shape[0] - 1
    pieces = [(shard, "far") for shard in order[:-1]]
    pieces += [(n + index, "flat") for index in range(flat)] + [(order[-1], "own")]
    targets = [None] * (n - 1) + [weights.at[1 + index] for index in range(flat)] + [weights.at[0]]
    begin, first, second, third, fourth, drain = box_steps(
        n, pieces, lambda seq, shard: part.at[shard, seq], lambda step: targets[step], *scratch[3:]
    )
    begin()
    onward(n - 1)
    count = len(pieces)
    far = n - 2
    for task in (first, second, third, fourth):
        for step in range(count):
            task(step)
        if far:
            onward(far)
            far -= 1
    for left in range(far, 0, -1):
        onward(left)
    finish()
    end()
    drain()


def closing(tokens, part, later):
    n = lax.axis_size("tensor")
    pieces, _, rows, width = part.shape
    sem = pltpu.SemaphoreType.DMA
    inside = pl.BlockSpec(memory_space=pltpu.VMEM)
    anywhere = pl.BlockSpec(memory_space=pl.ANY)
    return pl.pallas_call(
        functools.partial(closing_kernel, n),
        out_shape=[
            jax.ShapeDtypeStruct(tokens.shape[1:], jnp.float32),
            jax.ShapeDtypeStruct((pieces - n + 1, rows, width), jnp.float32),
            jax.ShapeDtypeStruct(later.shape, later.dtype),
        ],
        in_specs=[inside, anywhere, anywhere],
        out_specs=[inside, inside, anywhere],
        input_output_aliases={2: 2},
        scratch_shapes=[
            pltpu.VMEM((2, n - 1) + tokens.shape[1:], tokens.dtype),
            sem((2, n - 1, 4)),
            sem((2, n - 1, 4)),
        ]
        + box_scratch(n, pieces, rows, width, part.dtype),
        compiler_params=pltpu.CompilerParams(
            collective_id=8, has_side_effects=True, vmem_limit_bytes=VMEM
        ),
        cost_estimate=transfer(300),
        name="closing",
    )(tokens, part, later)


def swap_kernel(n, part, _later, out, _passed, local_sem, send_sem, recv_sem):
    spot = lax.axis_index("tensor")
    greet([{"tensor": lax.rem(spot + step, n)} for step in range(1, n)])
    keep = pltpu.make_async_copy(part.at[spot], out.at[spot], local_sem)
    keep.start()

    def copy(step):
        to = lax.rem(spot + step, n)
        return send(
            part.at[to], out.at[spot], send_sem.at[step], recv_sem.at[step], {"tensor": to}
        )

    for step in range(1, n):
        copy(step).start()
    keep.wait()
    for step in range(1, n):
        come = lax.rem(spot - step + n, n)
        send(
            part.at[come], out.at[come], send_sem.at[step], recv_sem.at[step], {"tensor": come}
        ).wait_recv()
        copy(step).wait_send()


def swap(part, later, number):
    n = lax.axis_size("tensor")
    sem = pltpu.SemaphoreType.DMA
    anywhere = pl.BlockSpec(memory_space=pl.ANY)
    return pl.pallas_call(
        functools.partial(swap_kernel, n),
        out_shape=[
            jax.ShapeDtypeStruct(part.shape, part.dtype),
            jax.ShapeDtypeStruct(later.shape, later.dtype),
        ],
        in_specs=[anywhere] * 2,
        out_specs=[anywhere] * 2,
        input_output_aliases={1: 1},
        scratch_shapes=[sem, sem((n,)), sem((n,))],
        compiler_params=pltpu.CompilerParams(
            collective_id=number, has_side_effects=True, vmem_limit_bytes=VMEM
        ),
        cost_estimate=transfer(25),
        name="swap",
    )(part, later)


def box_sum(part, tokens, later):
    n = lax.axis_size("tensor")
    width = part.shape[1]
    rows = part.shape[0] // (8 * n)
    kind = part.dtype
    anywhere = pl.BlockSpec(memory_space=pl.ANY)
    inside = pl.BlockSpec(memory_space=pltpu.VMEM)
    tokens = tokens.reshape(n, -1, width)
    sem = pltpu.SemaphoreType.DMA
    out, token_out, *later = pl.pallas_call(
        functools.partial(box_sum_kernel, n, len(later)),
        out_shape=[
            jax.ShapeDtypeStruct((rows, width), jnp.float32),
            jax.ShapeDtypeStruct(tokens.shape[1:], jnp.float32),
        ]
        + [jax.ShapeDtypeStruct(one.shape, one.dtype) for one in later],
        in_specs=[anywhere, inside] + [anywhere] * len(later),
        out_specs=[inside] * 2 + [anywhere] * len(later),
        input_output_aliases={2 + index: 2 + index for index in range(len(later))},
        scratch_shapes=[
            pltpu.VMEM((2, n - 1) + tokens.shape[1:], tokens.dtype),
            sem((2, n - 1, 4)),
            sem((2, n - 1, 4)),
        ]
        + box_scratch(n, n, rows, width, kind),
        compiler_params=pltpu.CompilerParams(
            collective_id=4, has_side_effects=True, vmem_limit_bytes=VMEM
        ),
        cost_estimate=transfer(90),
        name="box_sum",
    )(part.reshape(8, n, rows, width), tokens, *later)
    return out, token_out, later


def everyone(n):
    count = lax.axis_size("dp") * n
    me = lax.axis_index("dp") * n + lax.axis_index("tensor")

    def device(number):
        return {"dp": number // n, "tensor": number % n}

    return count, me, device


def greet_all(count, me, device):
    barrier = pltpu.get_barrier_semaphore()

    def signal(step, carry):
        pl.semaphore_signal(barrier, inc=1, device_id=device(lax.rem(me + step, count)), device_id_type=MESH)
        return carry

    lax.fori_loop(1, count, signal, 0)
    pl.semaphore_wait(barrier, count - 1)


def spread_start(n, own, out, send_sem, recv_sem):
    count, me, device = everyone(n)
    greet_all(count, me, device)
    out[me] = own[...]

    def copy(step):
        to = device(lax.rem(me + step, count))
        return send(own, out.at[me], send_sem.at[step], recv_sem.at[step], to)

    def go(step, carry):
        copy(step).start()
        return carry

    def end(step, carry):
        copy(step).wait_send()
        come = lax.rem(me - step + count, count)
        send(own, out.at[come], send_sem.at[step], recv_sem.at[step], device(come)).wait_recv()
        return carry

    lax.fori_loop(1, count, go, 0)
    return lambda: lax.fori_loop(1, count, end, 0)


def sum_spread_kernel(n, part, out, held, send_sem, recv_sem):
    count, me, device = everyone(n)
    greet_all(count, me, device)
    out[...] = part[me]

    def copy(step):
        to = lax.rem(me + step, count)
        return send(part.at[to], held.at[me], send_sem.at[step], recv_sem.at[step], device(to))

    def go(step, carry):
        copy(step).start()
        return carry

    def end(step, carry):
        come = lax.rem(me - step + count, count)
        send(part.at[0], held.at[come], send_sem.at[step], recv_sem.at[step], device(come)).wait_recv()
        out[...] += held[come]
        copy(step).wait_send()
        return carry

    lax.fori_loop(1, count, go, 0)
    lax.fori_loop(1, count, end, 0)


def sum_spread(part):
    n = lax.axis_size("tensor")
    count = lax.axis_size("dp") * n
    sem = pltpu.SemaphoreType.DMA
    return pl.pallas_call(
        functools.partial(sum_spread_kernel, n),
        out_shape=jax.ShapeDtypeStruct(part.shape[1:], part.dtype),
        in_specs=[pl.BlockSpec(memory_space=pltpu.VMEM)],
        out_specs=pl.BlockSpec(memory_space=pltpu.VMEM),
        scratch_shapes=[pltpu.VMEM(part.shape, part.dtype), sem((count,)), sem((count,))],
        compiler_params=pltpu.CompilerParams(
            collective_id=6, has_side_effects=True, vmem_limit_bytes=VMEM
        ),
        cost_estimate=transfer(20),
        name="sum_spread",
    )(part)


TB = 256
GR = 16
TILE = 256
EXTRA = 2 * E
def ceil_to(value, unit):
    return (value + unit - 1) // unit * unit


def nt_dot(a, b):
    return lax.dot_general(a, b, (((1,), (1,)), ((), ())), preferred_element_type=jnp.float32)


def tn_dot(a, b):
    return lax.dot_general(a, b, (((0,), (0,)), ((), ())), preferred_element_type=jnp.float32)


def nn_dot(a, b):
    return jnp.dot(a, b, preferred_element_type=jnp.float32)


def pair(value):
    high = value.astype(jnp.bfloat16)
    low = (value - high.astype(jnp.float32)).astype(jnp.bfloat16)
    return high, low


def unpair(value):
    value = value.astype(jnp.float32)
    return value[:, :E] + value[:, E:]


def excl_cumsum(value, axis):
    return jnp.cumsum(value, axis) - value


class Plan:
    def __init__(self, tokens, seq_len, local):
        seqs = tokens // seq_len
        self.tokens, self.local = tokens, local
        self.blocks = tokens // TB
        per_seq = seq_len // TB
        worst = min(CG + (GR - 1) * per_seq, seq_len)
        self.cap = ceil_to(seqs * worst // GR * GR, TILE)
        groups = (seqs * local * CG + self.blocks * local * (GR - 1)) // GR
        self.slots = ceil_to(TB * TOP * local // E + local * GR, 64)
        self.items = groups * GR // self.slots + self.blocks
        self.tiles = self.cap // TILE


def pick_at(here, table):
    return jnp.sum(jnp.where(here, table[None, :], 0), 1)


def steps_of(size, steps):
    first = excl_cumsum(steps, 0)
    used = jnp.sum(steps)
    index = jnp.minimum(jnp.arange(size), used - 1)
    owner = jnp.sum((first[None, :] <= index[:, None]).astype(jnp.int32), 1) - 1
    here = owner[:, None] == jnp.arange(steps.shape[0])[None, :]
    part = index - pick_at(here, first)
    last = (part == pick_at(here, steps) - 1).astype(jnp.int32)
    return first, used, owner, part, last, here


def routing(plan, routes, base):
    local, blocks = plan.local, plan.blocks
    mine = base + jnp.arange(local)
    picked = jnp.any(routes[:, :, None] == mine[None, None, :], 1)
    grid = picked.reshape(blocks, TB, local)
    ones = grid.astype(jnp.bfloat16)
    earlier = (jnp.arange(TB)[:, None] > jnp.arange(TB)[None, :]).astype(jnp.bfloat16)
    rank = jnp.einsum("ts,bse->bte", earlier, ones, preferred_element_type=jnp.float32).astype(
        jnp.int32
    )
    count = jnp.sum(grid.astype(jnp.int32), 1)
    groups = (count + GR - 1) // GR
    inner = excl_cumsum(groups, 1)
    total = jnp.sum(groups, 1)
    outer = excl_cumsum(groups, 0)
    expert_rows = jnp.sum(groups, 0) * GR
    place = jnp.where(grid, inner[:, None, :] * GR + rank, -1)
    items = jnp.maximum((total * GR + plan.slots - 1) // plan.slots, 1)
    first, used, block, part, last, here = steps_of(plan.items, items)
    wide, slots = plan.slots // GR, plan.cap // GR
    spot = jnp.arange(slots)[None, :, None]
    low = outer.T[:, None, :]
    inside = (spot >= low) & (spot < low + groups.T[:, None, :])
    origin = first[None, :] * wide + inner.T
    source = jnp.sum(jnp.where(inside, origin[:, None, :] + spot - low, 0), 2)
    tiles = jnp.maximum((expert_rows + TILE - 1) // TILE, 1)
    _, tiles_used, owner, tile, tile_last, _ = steps_of(local * plan.tiles, tiles)

    def at_block(table):
        return jnp.sum(jnp.where(here[:, :, None], table[None], 0), 1)[:, None, :]

    spot = (part[:, None] * wide + jnp.arange(wide)[None, :])[:, :, None]
    low, many, begin = at_block(inner), at_block(groups), at_block(outer)
    inside = (spot >= low) & (spot < low + many)
    target = jnp.sum(
        jnp.where(inside, (jnp.arange(local) * slots)[None, None, :] + begin + spot - low, 0), 2
    )
    return dict(
        place=place,
        used=used[None],
        block=block,
        part=part,
        last=last,
        source=source.reshape(-1),
        filled=expert_rows,
        tiles_used=tiles_used[None],
        owner=owner,
        tile=tile,
        tile_last=tile_last,
        target=target.reshape(-1),
    )


def while_used(step, used, *refs):
    @pl.when(pl.program_id(0) < used[0])
    def _():
        step(used, *refs)


def dispatch_step(used, block, part, post, grad, router, place, *refs):
    rows, share, held = refs[len(refs) // 2 - 1], refs[len(refs) // 2], refs[-1]
    step = pl.program_id(0)
    local = place.shape[1]
    slots = rows.shape[0]

    @pl.when(part[step] == 0)
    def _():
        portion = jax.nn.softmax(nn_dot(post[...], router[...]), -1)
        high, low = pair(portion)
        both = jnp.concatenate([high, low], 1)
        held[...] = both
        share[...] = both

    slot = lax.broadcasted_iota(jnp.int32, (slots, TB), 0) + part[step] * slots
    hit = slot == place[0, 0:1, :]
    for one in range(1, local):
        hit = hit | (slot == place[0, one : one + 1, :])
    pick = jnp.where(hit, 1.0, 0.0).astype(jnp.bfloat16)
    rows[:, :D] = nn_dot(pick, post[...]).astype(jnp.bfloat16)
    rows[:, D : 2 * D] = nn_dot(pick, grad[...]).astype(jnp.bfloat16)
    rows[:, 2 * D :] = nn_dot(pick, held[...]).astype(jnp.bfloat16)


def dispatch(plan, route, post, grad, router, later):
    wide = 2 * D + EXTRA
    place = route["place"].transpose(0, 2, 1)

    def at_block(step, used, block, part):
        return (block[step], 0)

    return pl.pallas_call(
        functools.partial(while_used, dispatch_step),
        grid_spec=pltpu.PrefetchScalarGridSpec(
            num_scalar_prefetch=3,
            grid=(plan.items,),
            in_specs=[
                pl.BlockSpec((TB, D), at_block),
                pl.BlockSpec((TB, D), at_block),
                pl.BlockSpec((D, E), lambda step, used, block, part: (0, 0)),
                pl.BlockSpec((1, plan.local, TB), lambda step, used, block, part: (block[step], 0, 0)),
            ]
            + [pl.BlockSpec(memory_space=pl.ANY)] * len(later),
            out_specs=[
                pl.BlockSpec((plan.slots, wide), lambda step, used, block, part: (jnp.minimum(step, used[0] - 1), 0)),
                pl.BlockSpec((TB, EXTRA), at_block),
            ]
            + [pl.BlockSpec(memory_space=pl.ANY)] * len(later),
            scratch_shapes=[pltpu.VMEM((TB, EXTRA), jnp.bfloat16)],
        ),
        out_shape=[
            jax.ShapeDtypeStruct((plan.items * plan.slots, wide), jnp.bfloat16),
            jax.ShapeDtypeStruct((plan.tokens, EXTRA), jnp.bfloat16),
        ]
        + [jax.ShapeDtypeStruct(one.shape, one.dtype) for one in later],
        input_output_aliases={7 + index: 2 + index for index in range(len(later))},
        compiler_params=pltpu.CompilerParams(vmem_limit_bytes=VMEM),
        cost_estimate=transfer(2),
        name="dispatch",
    )(route["used"], route["block"], route["part"], post, grad, router, place, *later)


def fetch_groups(table, rows, held, sems, step, count):
    slot = lax.rem(step, 2)
    for index in range(count):
        group = table[step * count + index]
        pltpu.make_async_copy(
            rows.at[pl.ds(pl.multiple_of(group * GR, GR), GR)],
            held.at[slot, pl.ds(index * GR, GR)],
            sems.at[slot],
        ).start()


def await_groups(rows, held, sems, step, count):
    slot = lax.rem(step, 2)
    pltpu.make_async_copy(rows.at[pl.ds(0, count * GR)], held.at[slot], sems.at[slot]).wait()


def next_groups(used, table, rows, held, sems, count):
    step = pl.program_id(0)

    @pl.when(step == 0)
    def _():
        fetch_groups(table, rows, held, sems, step, count)

    @pl.when(step + 1 < used[0])
    def _():
        fetch_groups(table, rows, held, sems, step + 1, count)

    await_groups(rows, held, sems, step, count)
    return lax.rem(step, 2)


def expert_step(
    used, source, owner, tile, last, filled, base, all_rows, w_gate, w_up, w_down, *refs
):
    *before, result, gate_out, up_out, down_out, held, sems, gate_sum, up_sum, down_sum = refs
    step = pl.program_id(0)
    count = TILE // GR
    slot = next_groups(used, source, all_rows, held, sems, count)
    expert, part = owner[step], tile[step]

    @pl.when(part == 0)
    def _():
        gate_sum[...] = jnp.zeros_like(gate_sum)
        up_sum[...] = jnp.zeros_like(up_sum)
        down_sum[...] = jnp.zeros_like(down_sum)

    @pl.when(last[step] == 1)
    def _():
        def clear(index, carry):
            at = pl.ds(pl.multiple_of(index * GR, GR), GR)
            held[slot, at, :] = jnp.zeros((GR, held.shape[2]), held.dtype)
            return carry

        lax.fori_loop((filled[expert] - part * TILE) // GR, count, clear, 0)

    number = base[0] + expert
    rows, upstream = held[slot, :, :D], held[slot, :, D : 2 * D]
    shares = held[slot, :, 2 * D :]
    lane = lax.broadcasted_iota(jnp.int32, (TILE, EXTRA), 1)
    own = (lane == number) | (lane == number + E)
    gate = jnp.sum(jnp.where(own, shares.astype(jnp.float32), 0.0), -1, keepdims=True)
    gate_pre = nn_dot(rows, w_gate[0])
    up_pre = nn_dot(rows, w_up[0])
    plain = nn_dot(upstream, w_down[0])
    squash = jax.nn.sigmoid(gate_pre)
    swish = gate_pre * squash
    active = (swish * up_pre).astype(jnp.bfloat16).astype(jnp.float32)
    change = jnp.sum(active * plain, -1, keepdims=True)
    grad_active = gate * plain
    grad_gate = (grad_active * up_pre * squash * (1.0 + gate_pre * (1.0 - squash))).astype(
        jnp.bfloat16
    )
    grad_up = (grad_active * swish).astype(jnp.bfloat16)
    scaled = (gate * active).astype(jnp.bfloat16)
    result[:, :D] = nt_dot(scaled, w_down[0]).astype(jnp.bfloat16)
    result[:, D : 2 * D] = (nt_dot(grad_gate, w_gate[0]) + nt_dot(grad_up, w_up[0])).astype(
        jnp.bfloat16
    )
    high, low = pair(change)
    result[:, 2 * D :] = jnp.where(
        lane == number,
        high.astype(jnp.float32),
        jnp.where(lane == number + E, low.astype(jnp.float32), 0.0),
    ).astype(jnp.bfloat16)
    gate_sum[...] += tn_dot(grad_gate, rows)
    up_sum[...] += tn_dot(grad_up, rows)
    down_sum[...] += tn_dot(scaled, upstream)

    @pl.when(last[step] == 1)
    def _():
        for index, (out, total) in enumerate(
            ((gate_out, gate_sum), (up_out, up_sum), (down_out, down_sum))
        ):
            out[0] = total[...].T + before[index][0] if before else total[...].T


def experts(plan, route, base, rows, w_gate, w_up, w_down, before):
    wide = 2 * D + EXTRA
    width = w_gate.shape[2]
    slots, count = plan.cap // GR, TILE // GR
    table = route["source"].reshape(plan.local * plan.tiles, count)
    number = route["owner"] * (slots // count) + route["tile"]
    table = table[number].reshape(-1)

    def whole(step, used, table, owner, tile, last, filled, base):
        return (owner[step], 0, 0)

    def tile_at(step, used, table, owner, tile, last, filled, base):
        return (owner[step] * plan.tiles + tile[step], 0)

    weight = pl.BlockSpec((1, D, width), whole)
    total = plan.local * plan.cap
    return pl.pallas_call(
        functools.partial(while_used, expert_step),
        grid_spec=pltpu.PrefetchScalarGridSpec(
            num_scalar_prefetch=7,
            grid=(plan.local * plan.tiles,),
            in_specs=[pl.BlockSpec(memory_space=pl.ANY)] + [weight] * (3 + len(before)),
            out_specs=[pl.BlockSpec((TILE, wide), tile_at)] + [weight] * 3,
            scratch_shapes=[
                pltpu.VMEM((2, TILE, wide), jnp.bfloat16),
                pltpu.SemaphoreType.DMA((2,)),
            ]
            + [pltpu.VMEM((width, D), jnp.float32)] * 3,
        ),
        out_shape=[jax.ShapeDtypeStruct((total, wide), jnp.bfloat16)]
        + [jax.ShapeDtypeStruct((plan.local, D, width), jnp.float32)] * 3,
        compiler_params=pltpu.CompilerParams(vmem_limit_bytes=VMEM),
        input_output_aliases={11 + index: 1 + index for index in range(len(before))},
        cost_estimate=transfer(2),
        name="experts",
    )(
        route["tiles_used"],
        table,
        route["owner"],
        route["tile"],
        route["tile_last"],
        route["filled"],
        base[None],
        rows,
        w_gate,
        w_up,
        w_down,
        *before,
    )


def combine_step(
    used, target, block, part, last, results, place, share, post, router, *refs
):
    held, sems, sums = refs[-3:]
    passing = (len(refs) - 6) // 2
    out, grad, router_out = refs[passing : passing + 3]
    step = pl.program_id(0)
    local = place.shape[1]
    slots = held.shape[1]

    at = next_groups(used, target, results, held, sems, slots // GR)

    @pl.when(step == 0)
    def _():
        router_out[...] = jnp.zeros_like(router_out)

    slot = lax.broadcasted_iota(jnp.int32, (TB, slots), 1) + part[step] * slots
    hit = slot == place[:, 0:1]
    for one in range(1, local):
        hit = hit | (slot == place[:, one : one + 1])
    pick = jnp.where(hit, 1.0, 0.0).astype(jnp.bfloat16)

    def term(begin, end):
        return nn_dot(pick, held[at, :, begin:end])

    def finish(value):
        change = unpair(value(2 * D, 2 * D + EXTRA))
        portion = unpair(share[...])
        moved = portion * (change - jnp.sum(change * portion, -1, keepdims=True))
        moved = moved.astype(jnp.bfloat16)
        out[...] = value(0, D).astype(jnp.bfloat16)
        grad[...] = (value(D, 2 * D) + nt_dot(moved, router[...])).astype(jnp.bfloat16)
        router_out[...] += tn_dot(moved, post[...])

    single = (part[step] == 0) & (last[step] == 1)

    @pl.when(single)
    def _():
        finish(term)

    @pl.when(jnp.logical_not(single))
    def _():
        @pl.when(part[step] == 0)
        def _():
            sums[...] = jnp.zeros_like(sums)

        sums[...] += term(0, 2 * D + EXTRA)

        @pl.when(last[step] == 1)
        def _():
            finish(lambda begin, end: sums[:, begin:end])


def combine(plan, route, results, share, post, router, later):
    wide = 2 * D + EXTRA

    def at_block(step, used, target, block, part, last):
        return (block[step], 0)

    def fixed(step, used, target, block, part, last):
        return (0, 0)

    return pl.pallas_call(
        functools.partial(while_used, combine_step),
        grid_spec=pltpu.PrefetchScalarGridSpec(
            num_scalar_prefetch=5,
            grid=(plan.items,),
            in_specs=[
                pl.BlockSpec(memory_space=pl.ANY),
                pl.BlockSpec((TB, plan.local), at_block),
                pl.BlockSpec((TB, EXTRA), at_block),
                pl.BlockSpec((TB, D), at_block),
                pl.BlockSpec((D, E), fixed),
            ]
            + [pl.BlockSpec(memory_space=pl.ANY)] * len(later),
            out_specs=[
                pl.BlockSpec((TB, D), at_block),
                pl.BlockSpec((TB, D), at_block),
                pl.BlockSpec((E, D), fixed),
            ]
            + [pl.BlockSpec(memory_space=pl.ANY)] * len(later),
            scratch_shapes=[
                pltpu.VMEM((2, plan.slots, wide), jnp.bfloat16),
                pltpu.SemaphoreType.DMA((2,)),
                pltpu.VMEM((TB, wide), jnp.float32),
            ],
        ),
        out_shape=[
            jax.ShapeDtypeStruct((plan.tokens, D), jnp.bfloat16),
            jax.ShapeDtypeStruct((plan.tokens, D), jnp.bfloat16),
            jax.ShapeDtypeStruct((E, D), jnp.float32),
        ]
        + [jax.ShapeDtypeStruct(one.shape, one.dtype) for one in later],
        input_output_aliases={10 + index: 3 + index for index in range(len(later))},
        compiler_params=pltpu.CompilerParams(vmem_limit_bytes=VMEM),
        cost_estimate=transfer(2),
        name="combine",
    )(
        route["used"],
        route["target"],
        route["block"],
        route["part"],
        route["last"],
        results,
        route["place"].reshape(plan.tokens, plan.local),
        share,
        post,
        router,
        *later,
    )


def gather_all(own):
    if lax.axis_size("dp") == 8:
        return box_gather(own)
    return lax.all_gather(
        lax.all_gather(own, "tensor", axis=0, tiled=True), "dp", axis=0, tiled=True
    )


def gather_slowly(own):
    if lax.axis_size("dp") == 8:
        return lax.all_gather(own, ("dp", "tensor"), axis=0, tiled=True)
    return gather_all(own)


def gather_output(own):
    n = lax.axis_size("tensor")
    if lax.axis_size("dp") == 8:
        everything = lax.all_gather(own, ("dp", "tensor"), axis=0, tiled=False)
        everything = everything.reshape((8, n) + own.shape).transpose(1, 0, 2, 3)
        return everything.reshape(n, -1, own.shape[1])
    part = lax.all_gather(own, "dp", axis=0, tiled=True)
    return lax.all_gather(part, "tensor", axis=0, tiled=False)


def sum_last(tokens, parts, later):
    n = lax.axis_size("tensor")
    if lax.axis_size("dp") == 8:
        return closing(
            tokens.reshape(n, -1, tokens.shape[1]),
            parts.reshape(parts.shape[0], 8, -1, parts.shape[2]),
            later,
        )
    tokens, later = chain_sum(tokens, later, 8)
    parts = lax.psum_scatter(parts, "dp", scatter_dimension=1, tiled=True)
    own = lax.psum_scatter(parts[:n], "tensor", scatter_dimension=0, tiled=True)
    return tokens, jnp.concatenate([own, parts[n:]]).astype(jnp.float32), later


def sum_all(part, tokens, later):
    if lax.axis_size("dp") == 8:
        return box_sum(part, tokens, later)
    tokens = lax.psum_scatter(tokens, "tensor", scatter_dimension=0, tiled=True)
    return sum_slowly(part).astype(jnp.float32), tokens.astype(jnp.float32), later


def sum_slowly(part):
    part = lax.psum_scatter(part, "dp", scatter_dimension=0, tiled=True)
    return lax.psum_scatter(part, "tensor", scatter_dimension=0, tiled=True)


def fill(value, rows, columns):
    return jnp.pad(value, ((0, rows - value.shape[0]), (0, columns - value.shape[1])))


def pack_small(router, prenorm, postnorm, querynorm, keynorm, routes):
    n = lax.axis_size("tensor")
    rank = lax.axis_index("tensor")
    rows = router.shape[0]
    head = ceil_to(max(rows, querynorm.shape[0]), 16)
    heads = querynorm.shape[1]
    block = jnp.concatenate(
        [
            fill(router, head, E),
            fill(prenorm[:, None], head, 1),
            fill(postnorm[:, None], head, 1),
            fill(querynorm, head, heads),
            fill(keynorm, head, heads),
        ],
        1,
    )
    part = routes.shape[0] // n
    own = lax.dynamic_slice_in_dim(routes, rank * part, part, 0)
    own = own.astype(jnp.bfloat16).reshape(-1, 128)
    tail = ceil_to(own.shape[0], 16)
    return jnp.concatenate([fill(block, head, 128), fill(own, tail, 128)], 0)


def unpack_small(everything, router, querynorm, routes):
    n = lax.axis_size("tensor")
    rank = lax.axis_index("tensor")
    rows, heads = router.shape[0], querynorm.shape[1]
    head = ceil_to(max(rows, querynorm.shape[0]), 16)
    part = routes.size // n // 128
    total = everything.shape[1]
    mine = everything.reshape(-1, n, total, 128)[:, rank]
    at = E + 2
    return (
        everything[:, :rows, :E].reshape(-1, E),
        everything[:, :rows, E].reshape(-1).astype(jnp.float32),
        everything[:, :rows, E + 1].reshape(-1).astype(jnp.float32),
        mine[:, : querynorm.shape[0], at : at + heads].reshape(-1, heads),
        mine[:, : querynorm.shape[0], at + heads : at + 2 * heads].reshape(-1, heads),
        everything[:, head : head + part].reshape(-1, TOP).astype(jnp.int32),
    )


def body(
    hidden_in,
    out_grad,
    doc_ids,
    expert_ids,
    prenorm,
    querynorm,
    keynorm,
    query_proj,
    key_proj,
    value_proj,
    output_proj,
    postnorm,
    router,
    gate_proj,
    up_proj,
    down_proj,
):
    residual = hidden_in[0].astype(jnp.float32)
    upstream = out_grad[0]
    documents = doc_ids[0]
    routes = expert_ids[0]
    shard = residual.shape[0]
    seq_len = documents.shape[0]
    mesh_dp = lax.axis_size("dp")
    block = min(seq_len, 1024)
    scale = HD ** (-0.5)
    cosine, sine = rope_tables(seq_len, HD)
    small = pack_small(router, prenorm, postnorm, querynorm, keynorm, routes)
    group_hidden, later, output_late, everything = chain_gather(
        hidden_in[0], [upstream[: shard // 2], output_proj], 1, small
    )
    router_full, pre_gain, post_gain, gain_query, gain_key, all_routes = unpack_small(
        everything, router, querynorm, routes
    )
    weights = lax.all_gather(
        jnp.concatenate([query_proj, key_proj, value_proj], 1),
        "dp",
        axis=0,
        tiled=True,
    )
    w_query, w_key, w_value = jnp.split(weights, 3, 1)
    w_output = gather_output(output_late)
    heads = w_query.shape[1] // HD
    query_scale = gain_query.astype(jnp.float32).T.reshape(-1)
    key_scale = gain_key.astype(jnp.float32).T.reshape(-1)
    inv_pre = lax.rsqrt(jnp.mean(residual * residual, -1, keepdims=True) + epsilon)
    group_hidden = group_hidden.astype(jnp.float32)
    group_inv = lax.rsqrt(jnp.mean(group_hidden * group_hidden, -1, keepdims=True) + epsilon)
    group_normed = (group_hidden * group_inv * pre_gain).astype(jnp.bfloat16)
    n = lax.axis_size("tensor")
    few = shard // 2
    plan = Plan(mesh_dp * n * few, n * few, gate_proj.shape[0])
    base = (lax.axis_index("dp") * plan.local).astype(jnp.int32)
    all_routes = all_routes.reshape(mesh_dp, n, 2, few, TOP)
    both = jnp.moveaxis(all_routes, 2, 0).reshape(2, -1, TOP)
    both = jax.vmap(lambda routes: routing(plan, routes, base))(both)
    route = [{name: value[index] for name, value in both.items()} for index in range(2)]
    all_grad = [gather_slowly(later)]
    query = jnp.dot(group_normed, w_query, preferred_element_type=jnp.float32)
    keys = jnp.dot(group_normed, w_key, preferred_element_type=jnp.float32)
    values = jnp.dot(group_normed, w_value, preferred_element_type=jnp.float32).astype(jnp.bfloat16)
    query_sq, key_sq = sum_heads(
        (jnp.sum(query * query, -1, keepdims=True), jnp.sum(keys * keys, -1, keepdims=True))
    )
    inv_query = lax.rsqrt(query_sq / D + epsilon)
    inv_key = lax.rsqrt(key_sq / D + epsilon)
    query_heads = (query * inv_query * query_scale).reshape(seq_len, heads, HD)
    key_heads = (keys * inv_key * key_scale).reshape(seq_len, heads, HD)
    query_rot = (query_heads * cosine[:, None] + rotate(query_heads) * sine[:, None]).astype(
        jnp.bfloat16
    )
    key_rot = (key_heads * cosine[:, None] + rotate(key_heads) * sine[:, None]).astype(jnp.bfloat16)
    value_heads = values.reshape(seq_len, heads, HD)
    mixed, logsum = attend_forward(query_rot, key_rot, value_heads, documents, block, scale)
    mixed_flat = mixed.reshape(seq_len, heads * HD)
    mixed_own, later = swap(mixed_flat.reshape(n, shard, heads * HD), upstream[few:], 7)
    all_grad.append(gather_slowly(later))
    attn_local = sum(nt_dot(mixed_own[index], w_output[index]) for index in range(n))
    middle = residual + attn_local
    inv_post = lax.rsqrt(jnp.mean(middle * middle, -1, keepdims=True) + epsilon)
    post_normed = (middle * inv_post * post_gain).astype(jnp.bfloat16)
    all_post = [gather_all(post_normed[:few]), gather_slowly(post_normed[few:])]
    grads, outs, backs, router_parts = [], [], [], []
    for index in range(2):
        rows, portion, *outs = dispatch(
            plan, route[index], all_post[index], all_grad[index], router_full, outs
        )
        results, *grads = experts(
            plan, route[index], base, rows, gate_proj, up_proj, down_proj, grads
        )
        later = []
        if index == 1:
            later = [lax.psum_scatter(backs[0], "dp", scatter_dimension=0, tiled=True)]
        out, back, router_part, *later = combine(
            plan, route[index], results, portion, all_post[index], router_full, later
        )
        if index == 1:
            early = later[0]
        outs.append(out)
        backs.append(back)
        router_parts.append(router_part)
    gate_weight_grad, up_weight_grad, down_weight_grad = grads
    first_out = lax.psum_scatter(outs[0], "dp", scatter_dimension=0, tiled=True)
    late, early, outs = sum_all(backs[1], early, outs[1:])
    grad_post = jnp.concatenate([early, late], 0)
    second_out = lax.psum_scatter(outs[0], "dp", scatter_dimension=0, tiled=True)
    router_part = router_parts[0] + router_parts[1]
    router_part = router_part.T
    post_gain_part = jnp.sum(grad_post * middle * inv_post, 0)
    grad_middle = upstream.astype(jnp.float32) + norm_back(
        grad_post, middle, inv_post, post_gain, D
    )
    change = grad_middle.astype(jnp.bfloat16)
    grad_mixed, first_out = swap(
        jnp.stack([nn_dot(change, w_output[index]).astype(jnp.bfloat16) for index in range(n)]),
        first_out,
        2,
    )
    moe_local = lax.psum_scatter(
        jnp.concatenate(
            [first_out.reshape(n, few, D), second_out.reshape(n, few, D)], 1
        ).reshape(-1, D),
        "tensor",
        scatter_dimension=0,
        tiled=True,
    )
    output_parts = [tn_dot(change, mixed_own[index]).astype(jnp.bfloat16) for index in range(n)]
    grad_query_rot, grad_key_rot, grad_value_heads = attend_backward(
        query_rot,
        key_rot,
        value_heads,
        documents,
        logsum,
        grad_mixed.reshape(seq_len, heads, HD),
        block,
        scale,
    )
    grad_query_flat = (
        grad_query_rot * cosine[:, None] + rotate_back(grad_query_rot * sine[:, None])
    ).reshape(seq_len, -1)
    grad_key_flat = (
        grad_key_rot * cosine[:, None] + rotate_back(grad_key_rot * sine[:, None])
    ).reshape(seq_len, -1)
    query_inner, key_inner = sum_heads(
        (
            jnp.sum(grad_query_flat * query_scale * query, -1, keepdims=True),
            jnp.sum(grad_key_flat * key_scale * keys, -1, keepdims=True),
        )
    )
    grad_query = (
        inv_query * query_scale * grad_query_flat - query * inv_query**3 * query_inner / D
    ).astype(jnp.bfloat16)
    grad_key = (inv_key * key_scale * grad_key_flat - keys * inv_key**3 * key_inner / D).astype(
        jnp.bfloat16
    )
    query_gain_part = jnp.sum(grad_query_flat * query * inv_query, 0).reshape(heads, HD).T
    key_gain_part = jnp.sum(grad_key_flat * keys * inv_key, 0).reshape(heads, HD).T
    grad_value = grad_value_heads.reshape(seq_len, -1).astype(jnp.bfloat16)
    query_part = lax.dot_general(
        group_normed, grad_query, (((0,), (0,)), ((), ())), preferred_element_type=jnp.float32
    )
    key_part = lax.dot_general(
        group_normed, grad_key, (((0,), (0,)), ((), ())), preferred_element_type=jnp.float32
    )
    value_part = lax.dot_general(
        group_normed, grad_value, (((0,), (0,)), ((), ())), preferred_element_type=jnp.float32
    )
    normed_term = lax.dot_general(
        grad_query, w_query, (((1,), (1,)), ((), ())), preferred_element_type=jnp.float32
    )
    normed_term = normed_term + lax.dot_general(
        grad_key, w_key, (((1,), (1,)), ((), ())), preferred_element_type=jnp.float32
    )
    normed_term = normed_term + lax.dot_general(
        grad_value, w_value, (((1,), (1,)), ((), ())), preferred_element_type=jnp.float32
    )
    grad_normed, weight_sums, middle = sum_last(
        normed_term.astype(jnp.bfloat16),
        jnp.stack(
            output_parts + [part.astype(jnp.bfloat16) for part in (query_part, key_part, value_part)]
        ),
        middle,
    )
    layer_out = (middle + moe_local.astype(jnp.float32)).astype(jnp.bfloat16)[None]
    pre_gain_part = jnp.sum(grad_normed * residual * inv_pre, 0)
    input_grad = (grad_middle + norm_back(grad_normed, residual, inv_pre, pre_gain, D)).astype(
        jnp.bfloat16
    )[None]
    gains = jnp.concatenate([query_gain_part, key_gain_part], 1).reshape(mesh_dp, 1, -1, 2 * heads)
    mine = jnp.arange(n)[None, :, None, None] == lax.axis_index("tensor")
    gains = jnp.pad(
        jnp.where(mine, gains, 0.0),
        ((0, 0), (0, 0), (0, max(router.shape[0] - HD // mesh_dp, 0)), (0, 0)),
    ).reshape(D, 2 * heads)
    own = router.shape[0]
    block = jnp.concatenate(
        [router_part, gains, jnp.zeros((D, 128 - E - 2 * heads), jnp.float32)], 1
    )
    block = jnp.pad(block.reshape(-1, own, 128), ((0, 0), (0, 8), (0, 0)))
    block = block.at[:, own, :own].set(post_gain_part.reshape(-1, own))
    small = sum_spread(block.at[:, own + 1, :own].set(pre_gain_part.reshape(-1, own)))
    gain_grads = small[: HD // mesh_dp, E : E + 2 * heads]
    return (
        layer_out,
        input_grad,
        small[own + 1, :own],
        gain_grads[:, :heads],
        gain_grads[:, heads : 2 * heads],
        weight_sums[1],
        weight_sums[2],
        weight_sums[3],
        weight_sums[0],
        small[own, :own],
        small[:own, :E],
        gate_weight_grad,
        up_weight_grad,
        down_weight_grad,
    )


def solution(mesh):
    in_specs = (
        P("dp", "tensor", None),
        P("dp", "tensor", None),
        P("dp", None),
        P("dp", None, None),
        P(("dp", "tensor")),
        P("dp", "tensor"),
        P("dp", "tensor"),
        P("dp", "tensor"),
        P("dp", "tensor"),
        P("dp", "tensor"),
        P("dp", "tensor"),
        P(("dp", "tensor")),
        P(("dp", "tensor"), None),
        P("dp", None, "tensor"),
        P("dp", None, "tensor"),
        P("dp", None, "tensor"),
    )
    out_specs = (
        P("dp", "tensor", None),
        P("dp", "tensor", None),
        P(("dp", "tensor")),
        P("dp", "tensor"),
        P("dp", "tensor"),
        P("dp", "tensor"),
        P("dp", "tensor"),
        P("dp", "tensor"),
        P("dp", "tensor"),
        P(("dp", "tensor")),
        P(("dp", "tensor"), None),
        P("dp", None, "tensor"),
        P("dp", None, "tensor"),
        P("dp", None, "tensor"),
    )
    return jax.shard_map(body, mesh=mesh, in_specs=in_specs, out_specs=out_specs, check_vma=False)
```
